32 devices in a mesh: seq: 8 (over y, x, core), batch: 4 (over z).
Axes of the slice: x: 2, y: 2, z: 4, core: 2. Of those that a mesh axis runs over, the one named last changes fastest.
Arguments:
- layer_input: bfloat16 [4, 2048, 768], P('batch', 'seq'), may hold values from -6 to 6
- segments: int32 [4, 2048], P('batch', 'seq'), may hold values from 0 to 7, never falling along the last dimension, each value on 1 to 800 neighbouring positions
- rand_blocks: int32 [4, 32, 12, 3], P('batch', 'seq'), may hold values from 0 to 31, as said below
- w_qkv: bfloat16 [2, 768, 2304], P(None, ('seq', 'batch')), may hold values from -0.21875 to 0.21875
- w_out: bfloat16 [2, 768, 768], P(None, ('seq', 'batch')), may hold values from -2.5 to 2.5
- w_up: bfloat16 [2, 768, 3072], P(None, ('seq', 'batch')), may hold values from -0.21875 to 0.21875
- w_down: bfloat16 [2, 3072, 768], P(None, ('seq', 'batch')), may hold values from -0.109375 to 0.109375
- gains: bfloat16 [2, 2, 768], P(None, None, ('seq', 'batch')), may hold values from 0.5 to 1.5
- biases: bfloat16 [2, 6, 768], P(None, None, ('seq', 'batch')), may hold values from -2 to 2
- up_bias: bfloat16 [2, 3072], P(None, ('seq', 'batch')), may hold values from -2 to 2
- d_out: bfloat16 [4, 2048, 768], P('batch', 'seq'), may hold values from -6 to 6
Outputs:
- output: bfloat16 [4, 2048, 768], P('batch', 'seq')
- d_input: float32 [4, 2048, 768], P('batch', 'seq')
- grad_w_qkv: float32 [2, 768, 2304], P(None, ('seq', 'batch'))
- grad_w_out: float32 [2, 768, 768], P(None, ('seq', 'batch'))
- grad_w_up: float32 [2, 768, 3072], P(None, ('seq', 'batch'))
- grad_w_down: float32 [2, 3072, 768], P(None, ('seq', 'batch'))
- grad_gains: float32 [2, 2, 768], P(None, None, ('seq', 'batch'))
- grad_biases: float32 [2, 6, 768], P(None, None, ('seq', 'batch'))
- grad_up_bias: float32 [2, 3072], P(None, ('seq', 'batch'))
The draws below stay inside these ranges and needn't reach their ends.
Inputs may be any that keep to these rules, and one draw needn't show every extreme that they name: `rand_blocks`: for each sequence and each index of seq, the entries of the 4 query blocks held there (all heads and draws) name blocks held by each index of seq between 17 and 18 times, and some index exactly 18 times.
All inputs are finite; a program needn't handle non-finite values.
Results may differ from the reference program's by a relative error of at most 0.02.
Values may be sent and summed in bfloat16 or wider, within the bound.
A program may use at most 256 MiB of HBM per device.

```python
import math
import jax
import jax.numpy as jnp
import numpy as np
from jax import lax

D = 768
H = 12
DH = 64
FF = 3072
BLK = 64
R = 3
GLOB = 2
L = 2
LEN = 2048
NB = 32
BPD = 4
SEQS = 4
N_SEQ = 8


def draw_rand_blocks(key, part):
    per_group = BPD * H * R

    def draw_group(index_key):
        offset_key, ordering_key, block_key = jax.random.split(index_key, 3)
        offset = jax.random.randint(offset_key, (), 0, N_SEQ)
        ordering = jax.random.permutation(ordering_key, per_group)
        owners = (offset + ordering) % N_SEQ
        inner_block = jax.random.randint(block_key, (per_group,), 0, BPD)
        return (owners * BPD + inner_block).reshape(BPD, H, R)
    group_keys = jax.random.split(jax.random.fold_in(key, 17), SEQS * N_SEQ)
    chosen = jax.vmap(draw_group)(group_keys)
    return chosen.reshape(SEQS, NB, H, R).astype(jnp.int32)


def level_of(rng, dims, cuts, least, top_value):
    factor_of = 1.0
    for dim, shards_of in cuts:
        draws = jax.random.uniform(jax.random.fold_in(jax.random.fold_in(rng, 6), dim), (shards_of,), jnp.float32, least / len(cuts), top_value / len(cuts))
        factor_of = factor_of * jnp.repeat(jnp.exp(draws), dims[dim] // shards_of).reshape((-1,) + (1,) * (len(dims) - 1 - dim))
    return factor_of


def split_up(count, total, reach, lean):
    portions = [(1 << 20) // math.isqrt(rank ** lean) + 1 for rank in range(2, count + 1)]
    rest, holding = total - reach - (count - 1), [1] * (count - 1)
    while rest > 0:
        candidates = [i for i in range(count - 1) if holding[i] < reach]
        pool, budget = sum([portions[i] for i in candidates]), rest
        for i in candidates:
            more = min(reach - holding[i], max(1, budget * portions[i] // pool), rest)
            holding[i] = holding[i] + more
            rest = rest - more
    return np.array([reach] + holding)


def ragged_sizes(key, amount, total, most, lean):
    if amount == 2:
        one = jax.random.randint(key, (), max(1, total - most), min(most, total - 1) + 1)
        return jnp.stack([one, total - one])
    lengths = jnp.asarray(split_up(amount, total, most, lean), jnp.int32)
    pairs = (amount - 1) // 2
    giver, receiver = lengths[1:1 + 2 * pairs:2], lengths[2:2 + 2 * pairs:2]
    margin = jnp.minimum(giver - 1, most - receiver)
    moved = jax.random.randint(jax.random.fold_in(key, 1), (pairs,), 0, 1 << 20) % (margin + 1)
    lengths = lengths.at[1:1 + 2 * pairs:2].set(giver - moved).at[2:2 + 2 * pairs:2].set(receiver + moved)
    return lengths[jax.random.permutation(jax.random.fold_in(key, 2), amount)]


def noise(rng, dims, scale, reach, cuts=(), kind=jnp.bfloat16):
    drawn = scale * jax.random.normal(rng, dims, jnp.float32)
    if cuts:
        drawn = drawn * level_of(rng, dims, cuts, -0.22, 0.18)
    return jnp.clip(drawn, -reach, reach).astype(kind)


def setup_inputs(seed: int = 0) -> dict:
    key_list = jax.random.split(jax.random.key(seed), 12)
    layer_input = noise(key_list[0], (SEQS, LEN, D), 1.0, 6.0, ((0, 4), (1, 8)))
    segments = jax.vmap(lambda own: jnp.searchsorted(jnp.cumsum(ragged_sizes(own, max(4, LEN // 256), LEN, min(800, LEN // 2), 1)), jnp.arange(LEN), side="right"))(jax.random.split(key_list[1], SEQS)).reshape((SEQS, LEN)).astype(jnp.int32)
    rand_blocks = draw_rand_blocks(jax.random.fold_in(key_list[11], 71), 0)
    w_qkv = noise(key_list[3], (L, D, 3 * D), D ** -0.5, 0.21875, ((1, 32),))
    w_out = noise(key_list[4], (L, D, D), (D // 128) ** -0.5, 2.5, ((1, 32),))
    w_up = noise(key_list[5], (L, D, FF), D ** -0.5, 0.21875, ((1, 32),))
    w_down = noise(key_list[6], (L, FF, D), FF ** -0.5, 0.109375, ((1, 32),))
    gains = jnp.clip(1.0 + 0.1 * jax.random.normal(key_list[7], (L, 2, D), jnp.float32), 0.5, 1.5).astype(jnp.bfloat16)
    biases = noise(key_list[8], (L, 6, D), 0.3, 2.0, ((2, 32),))
    up_bias = noise(key_list[9], (L, FF), 0.3, 2.0, ((1, 32),))
    d_out = noise(key_list[10], (SEQS, LEN, D), 1.0, 6.0, ((0, 4), (1, 8)))
    return dict(layer_input=layer_input, segments=segments, rand_blocks=rand_blocks, w_qkv=w_qkv, w_out=w_out, w_up=w_up, w_down=w_down, gains=gains, biases=biases, up_bias=up_bias, d_out=d_out)


@jax.custom_vjp
def low(v):
    return lax.optimization_barrier(v.astype(jnp.bfloat16)).astype(jnp.float32)

@jax.custom_vjp
def low_back(v):
    return v

def low_keep(v):
    return (low(v), None)

def low_pass(kept, grad):
    return (grad,)

def back_keep(v):
    return (v, None)

def back_low(kept, grad):
    return (low(grad),)
low.defvjp(low_keep, low_pass)
low_back.defvjp(back_keep, back_low)
layer_eps = 1e-06
highest = lax.Precision.HIGHEST

def product(left, right):
    return jnp.dot(left, right, precision=highest)

def norm_rows(resid, gain, shift):
    center = resid - lax.optimization_barrier(jnp.mean(resid, axis=-1, keepdims=True))
    inv_std = lax.rsqrt(lax.optimization_barrier(jnp.mean(center * center, axis=-1, keepdims=True)) + layer_eps)
    return center * inv_std * gain + shift

def attend(queries, key_rows, values, seg_ids, picks):
    global_width = GLOB * BLK
    score_scale = DH ** (-0.5)
    query_blocks = queries.reshape(NB, BLK, H, DH)
    key_blocks = key_rows.reshape(NB, BLK, H, DH)
    value_blocks = values.reshape(NB, BLK, H, DH)
    padding = jnp.zeros((1, BLK, H, DH), jnp.float32)
    key_padded = jnp.concatenate([padding, key_blocks, padding], 0)
    value_padded = jnp.concatenate([padding, value_blocks, padding], 0)
    key_window = jnp.concatenate([key_padded[0:NB], key_padded[1:NB + 1], key_padded[2:NB + 2]], 1)
    value_window = jnp.concatenate([value_padded[0:NB], value_padded[1:NB + 1], value_padded[2:NB + 2]], 1)
    head_ids = jnp.arange(H, dtype=jnp.int32)[None, :, None]
    key_drawn = key_blocks[picks, :, head_ids, :]
    value_drawn = value_blocks[picks, :, head_ids, :]
    key_shared = key_rows[0:global_width]
    value_shared = values[0:global_width]
    shared_scores = jnp.einsum('bqhd,khd->bhqk', query_blocks, key_shared, precision=highest)
    window_scores = jnp.einsum('bqhd,bkhd->bhqk', query_blocks, key_window, precision=highest)
    drawn_scores = jnp.einsum('bqhd,bhrkd->bhqrk', query_blocks, key_drawn, precision=highest).reshape(NB, H, BLK, R * BLK)
    products = low_back(jnp.concatenate([shared_scores, window_scores, drawn_scores], -1))
    positions = jnp.arange(NB, dtype=jnp.int32)[:, None] * BLK - BLK + jnp.arange(3 * BLK, dtype=jnp.int32)[None, :]
    seg_padded = jnp.concatenate([jnp.full((BLK,), -1, jnp.int32), seg_ids, jnp.full((BLK,), -1, jnp.int32)])
    seg_window = seg_padded[positions + BLK]
    seg_query = seg_ids.reshape(NB, BLK)
    inside = (positions >= global_width) & (positions < LEN)
    window_allowed = inside[:, None, :] & (seg_window[:, None, :] == seg_query[:, :, None])
    allowed = jnp.concatenate([jnp.ones((NB, BLK, global_width), jnp.bool_), window_allowed, jnp.ones((NB, BLK, R * BLK), jnp.bool_)], -1)[:, None]
    weights = jax.nn.softmax(jnp.where(allowed, products * score_scale, -1e+30), axis=-1)
    rounded = low(weights)
    blended = jnp.einsum('bhqk,khd->bqhd', rounded[..., :global_width], value_shared, precision=highest) + jnp.einsum('bhqk,bkhd->bqhd', rounded[..., global_width:global_width + 3 * BLK], value_window, precision=highest) + jnp.einsum('bhqrk,bhrkd->bqhd', rounded[..., global_width + 3 * BLK:].reshape(NB, H, BLK, R, BLK), value_drawn, precision=highest)
    blended = blended.reshape(LEN, H, DH)
    global_scores = low_back(jnp.einsum('qhd,khd->hqk', queries[0:global_width], key_rows, precision=highest))
    global_weights = low(jax.nn.softmax(global_scores * score_scale, axis=-1))
    global_out = jnp.einsum('hqk,khd->qhd', global_weights, values, precision=highest)
    return jnp.concatenate([global_out, blended[global_width:]], 0).reshape(LEN, D)

def run_layer(resid, seg_ids, picks, weights_now):
    mat_qkv, mat_out, mat_up, mat_down, gain_rows, bias_rows, up_shift = weights_now
    inputs_low = low(resid)
    projected = low_back(product(inputs_low, mat_qkv))
    queries = low(projected[:, :D] + bias_rows[0])
    key_rows = low(projected[:, D:2 * D])
    values = low(projected[:, 2 * D:] + bias_rows[1])
    attended = low_back(low(attend(queries.reshape(LEN, H, DH), key_rows.reshape(LEN, H, DH), values.reshape(LEN, H, DH), seg_ids, picks)))
    resid_one = resid + low_back(product(attended, mat_out)) + bias_rows[2]
    middle = norm_rows(resid_one, gain_rows[0], bias_rows[3])
    hidden = low_back(product(low(middle), mat_up)) + up_shift
    resid_two = middle + low_back(product(low(jax.nn.gelu(hidden, approximate=False)), mat_down)) + bias_rows[4]
    return norm_rows(resid_two, gain_rows[1], bias_rows[5])

def reference(layer_input, segments, rand_blocks, w_qkv, w_out, w_up, w_down, gains, biases, up_bias, d_out):
    params = tuple((member.astype(jnp.float32) for member in (w_qkv, w_out, w_up, w_down, gains, biases, up_bias)))
    inputs_float = layer_input.astype(jnp.float32)

    def sequence(resid, seg_ids, picks, weights_all):
        for layer_index in range(L):
            resid = run_layer(resid, seg_ids, picks, tuple((member[layer_index] for member in weights_all)))
        return resid
    saved_sequence = jax.checkpoint(sequence)

    def whole_run(inputs_all, *weights_all):
        return lax.map(lambda packed: saved_sequence(packed[0], packed[1], packed[2], weights_all), (inputs_all, segments, rand_blocks))
    result, pull_back = jax.vjp(whole_run, inputs_float, *params)
    gradients = pull_back(d_out.astype(jnp.float32))
    return (result.astype(jnp.bfloat16), gradients[0], gradients[1], gradients[2], gradients[3], gradients[4], gradients[5], gradients[6], gradients[7])
```

```python
import functools
import itertools
from functools import partial

import jax
import jax.numpy as jnp
from jax import lax
from jax.experimental import pallas as pl
from jax.experimental.pallas import tpu as pltpu
from jax.sharding import PartitionSpec as P

MESH = pl.DeviceIdType.MESH


def place():
    s = lax.axis_index("seq")
    return {"y": s // 4, "x": (s // 2) % 2, "c": s % 2, "z": lax.axis_index("batch")}


def device_of(p):
    return ((p["y"] * 2 + p["x"]) * 2 + p["c"], p["z"])


def moved(p, axis, d):
    p = dict(p)
    if d:
        p[axis] = p[axis] + d if axis == "z" else 1 - p[axis]
    return p


def holds(p, depth):
    return (p["z"] >= 0) & (p["z"] < depth)


def when(cond, action):
    if cond is None:
        action()
    else:
        pl.when(cond)(action)


def both(one, other):
    return other if one is None else one if other is None else one & other


def offsets(order, depth):
    return list(
        itertools.product(*[range(1 - depth, depth) if a == "z" else (0, 1) for a in order])
    )


def last_move(offset):
    return max([-1] + [i for i, d in enumerate(offset) if d])


def onward(order, offset):
    last = last_move(offset)
    moves = []
    if last >= 0 and order[last] == "z":
        moves.append(("on", "z", -1 if offset[last] > 0 else 1))
    for axis in order[last + 1 :]:
        moves += [("start", axis, d) for d in ((1, -1) if axis == "z" else (1,))]
    moves.append(("core", "c", 1))
    return moves


def greet(axes, depth, from_first=0):
    me = place()
    barrier = pltpu.get_barrier_semaphore()
    count = 0
    for axis in axes + ("c",):
        for d in (1, -1) if axis == "z" else (1,):
            peer = moved(me, axis, d)
            cond = holds(peer, depth) if axis == "z" else None
            when(
                cond,
                lambda peer=peer: pl.semaphore_signal(
                    barrier, inc=1, device_id=device_of(peer), device_id_type=MESH
                ),
            )
            count = count + (1 if cond is None else cond.astype(jnp.int32))
    if from_first:
        seq = lax.axis_index("seq")

        @pl.when(seq != 0)
        def _():
            pl.semaphore_signal(
                barrier, inc=1, device_id=(0, lax.axis_index("batch")), device_id_type=MESH
            )

        count = count + jnp.where(seq == 0, from_first, 0)
    pl.semaphore_wait(barrier, count)


class Gather:
    def __init__(self, source, target, number, order, depth, send, recv, send_at):
        self.source, self.target, self.number = source, target, number
        self.order, self.depth, self.send, self.recv = order, depth, send, recv
        self.send_at = send_at
        self.me = place()
        self.sent = []

    @staticmethod
    def sends(order, depth):
        return sum(len(onward(order, t)) for t in offsets(order, depth))

    def origin(self, offset):
        p = self.me
        for axis, d in zip(self.order, offset):
            p = moved(p, axis, d)
        cond = None
        if "z" in self.order and offset[self.order.index("z")]:
            cond = holds(p, self.depth)
        return p, cond

    def arrival(self, p):
        ref = self.target(p)
        return pltpu.make_async_remote_copy(
            src_ref=ref, dst_ref=ref, send_sem=self.send.at[self.send_at],
            recv_sem=self.recv.at[self.number(p)], device_id=device_of(self.me), device_id_type=MESH,
        )

    def handle(self, offset):
        p, cond = self.origin(offset)
        own = not any(offset)
        plans = []
        for kind, axis, d in onward(self.order, offset):
            peer = moved(self.me, axis, d)
            also = holds(peer, self.depth) if axis == "z" else None
            plans.append((peer, also, self.send_at))
            self.send_at += 1

        def act():
            if not own:
                self.arrival(p).wait_recv()
            for peer, also, slot in plans:
                copy = pltpu.make_async_remote_copy(
                    src_ref=self.source if own else self.target(p), dst_ref=self.target(p),
                    send_sem=self.send.at[slot], recv_sem=self.recv.at[self.number(p)],
                    device_id=device_of(peer), device_id_type=MESH,
                )
                when(also, copy.start)

        when(cond, act)
        for peer, also, slot in plans:
            self.sent.append((both(cond, also), slot))

    def events(self):
        marks = sorted(
            (t for t in offsets(self.order, self.depth) if any(t)),
            key=lambda t: (sum(abs(d) for d in t), t),
        )
        return [(sum(abs(d) for d in t), partial(self.handle, t)) for t in marks]

    def siblings(self):
        for t in offsets(self.order, self.depth):
            p, cond = self.origin(t)
            p = moved(p, "c", 1)
            when(cond, lambda p=p: self.arrival(p).wait_recv())

    def drain(self):
        for cond, slot in self.sent:
            copy = pltpu.make_async_remote_copy(
                src_ref=self.source, dst_ref=self.target(self.me), send_sem=self.send.at[slot],
                recv_sem=self.recv.at[self.number(self.me)], device_id=device_of(self.me), device_id_type=MESH,
            )
            when(cond, copy.wait_send)


def run_gathers(jobs):
    for job in jobs:
        job.handle((0,) * len(job.order))
    todo = []
    for i, job in enumerate(jobs):
        todo += [(when_, i, k, act) for k, (when_, act) in enumerate(job.events())]
    for _, _, _, act in sorted(todo, key=lambda e: e[:3]):
        act()
    for job in jobs:
        job.siblings()
    for job in jobs:
        job.drain()


class Reduce:
    def __init__(self, partial_of, inbox, number, order, depth, send, recv):
        self.partial_of, self.inbox, self.number = partial_of, inbox, number
        self.order, self.depth, self.send, self.recv = order, depth, send, recv
        self.me = place()
        self.edges = self.edge_table(order, depth)
        self.sent = []

    @staticmethod
    def edge_table(order, depth):
        table = {}
        for t in offsets(order, depth):
            for move in onward(order, t):
                table[(t, move)] = len(table)
        return table

    def owner(self, offset):
        p = self.me
        for axis, d in zip(self.order, offset):
            p = moved(p, axis, d)
        cond = None
        if "z" in self.order and offset[self.order.index("z")]:
            cond = holds(p, self.depth)
        return p, cond

    def copy(self, source, edge, slot, peer):
        return pltpu.make_async_remote_copy(
            src_ref=source, dst_ref=self.inbox.at[edge], send_sem=self.send.at[slot],
            recv_sem=self.recv.at[edge], device_id=device_of(peer), device_id_type=MESH,
        )

    def slots(self):
        return {t: i for i, t in enumerate(offsets(self.order, self.depth))}

    def start(self, offset):
        p, cond = self.owner(offset)
        q = moved(p, "c", 1)
        slot = self.slots()[offset]
        edge = self.edges[(offset, ("core", "c", 1))]
        when(cond, lambda: self.copy(self.partial_of(q), edge, slot, moved(self.me, "c", 1)).start())
        self.sent.append((cond, slot))

    def children(self, offset):
        found = []
        for kind, axis, d in onward(self.order, offset):
            cond = None
            if axis == "z":
                cond = holds(moved(self.me, "z", d), self.depth)
            found.append((self.edges[(offset, (kind, axis, d))], cond, kind))
        return found

    def upward(self, offset):
        k = last_move(offset)
        axis, d = self.order[k], offset[k]
        step = 1 if d > 0 else -1
        parent = list(offset)
        parent[k] = d - step if axis == "z" else 0
        if axis == "z" and parent[k]:
            kind, back = "on", -step
        else:
            kind, back = "start", -step if axis == "z" else 1
        edge = self.edges[(tuple(parent), (kind, axis, back))]
        return edge, moved(self.me, axis, step)

    def handle(self, offset, add, finish):
        p, cond = self.owner(offset)
        kids = self.children(offset)
        core = [e for e, c, kind in kids if kind == "core"][0]
        slot = len(self.slots()) + self.slots()[offset]

        def act():
            for edge, also, _ in kids:
                when(also, lambda edge=edge: self.copy(self.inbox.at[edge], edge, slot, self.me).wait_recv())
            if any(offset):
                add(self.partial_of(p), [(self.inbox.at[e], c) for e, c, _ in kids], self.inbox.at[core])
                edge, peer = self.upward(offset)
                self.copy(self.inbox.at[core], edge, slot, peer).start()
            else:
                finish(self.partial_of(p), [(self.inbox.at[e], c) for e, c, _ in kids])

        when(cond, act)
        if any(offset):
            self.sent.append((cond, slot))

    def marks(self):
        return sorted(offsets(self.order, self.depth), key=lambda t: (-sum(abs(d) for d in t), t))

    def drain(self):
        for cond, slot in self.sent:
            when(cond, self.copy(self.inbox.at[0], 0, slot, self.me).wait_send)

D = 768
H = 12
DH = 64
BLK = 64
R = 3
GLOB = 2
L = 2
PAIRS = H // 2
WIDE = 2 * DH
SHARED = GLOB * BLK
SHARE = 16
HELPERS = SHARED // SHARE
VMEM_LIMIT = 60 * 1024 * 1024

layer_eps = 1e-06
masked_score = -1e30

Z_Y_X, Z_X_Y, X_Y_Z, Y_X_Z = ("z", "y", "x"), ("z", "x", "y"), ("x", "y", "z"), ("y", "x", "z")
Y_X, X_Y = ("y", "x"), ("x", "y")
ANYWHERE = pl.BlockSpec(memory_space=pl.ANY)
IN_VMEM = pl.BlockSpec(memory_space=pltpu.VMEM)


def number_in(depth):
    return lambda p: device_of(p)[0] * depth + p["z"]


def dma(*shape):
    return pltpu.SemaphoreType.DMA(shape)


def gather_weights_kernel(depth, orders, *refs):
    n = len(orders)
    sources, targets = refs[:n], refs[n : 2 * n]
    send, recv, local = refs[2 * n :]
    greet(("y", "x", "z"), depth)
    me = place()
    number = number_in(depth)
    jobs, own, at = [], [], 0
    for i, order in enumerate(orders):
        copy = pltpu.make_async_copy(sources[i], targets[i].at[number(me)], local.at[i])
        copy.start()
        own.append(copy)
        jobs.append(
            Gather(
                sources[i], lambda p, i=i: targets[i].at[number(p)], number, order, depth,
                send, recv.at[i], at,
            )
        )
        at += Gather.sends(order, depth)
    run_gathers(jobs)
    for copy in own:
        copy.wait()


def gather_weights(arrays, orders, depth, n_dev, cid):
    total = sum(Gather.sends(order, depth) for order in orders)
    n = len(arrays)
    return pl.pallas_call(
        partial(gather_weights_kernel, depth, orders),
        out_shape=[jax.ShapeDtypeStruct((n_dev,) + a.shape, a.dtype) for a in arrays],
        in_specs=[ANYWHERE] * n,
        out_specs=[ANYWHERE] * n,
        scratch_shapes=[dma(total), dma(n, n_dev), dma(n)],
        compiler_params=pltpu.CompilerParams(collective_id=cid, has_side_effects=True),
        name="gather_weights",
    )(*arrays)


def fetch_layer(layer, w_qkv, w_out, w_up, w_down, seq_count, depth):
    if seq_count != 8:
        gathered = [
            lax.all_gather(w[layer], ("seq", "batch"), axis=0, tiled=True)
            for w in (w_qkv, w_out, w_up, w_down)
        ]
        return tuple(gathered)
    n_dev = seq_count * depth
    rows = w_down.shape[1] * 2 // 3
    got = gather_weights(
        [w_qkv[layer], w_out[layer], w_up[layer], w_down[layer]],
        [Z_Y_X, Z_X_Y, Z_X_Y, X_Y_Z],
        depth, n_dev, layer,
    )
    return tuple(g.reshape(-1, g.shape[-1]) for g in got)


def to_helpers(depth, source, target, send, recv):
    seq, z = lax.axis_index("seq"), lax.axis_index("batch")

    def copy(j):
        return pltpu.make_async_remote_copy(
            src_ref=source.at[pl.ds(j * SHARE, SHARE)], dst_ref=target, send_sem=send.at[j],
            recv_sem=recv, device_id=(j, z), device_id_type=MESH,
        )

    def begin():
        for j in range(1, HELPERS):
            copy(j).start()

    def own():
        pltpu.sync_copy(source.at[pl.ds(0, SHARE)], target)
        for j in range(1, HELPERS):
            copy(j).wait_send()

    def end():
        pl.when(seq == 0)(own)
        pl.when(seq != 0)(lambda: copy(1).wait_recv())

    pl.when(seq == 0)(begin)
    return end


def to_first(source, target, send, recv):
    seq, z = lax.axis_index("seq"), lax.axis_index("batch")

    def copy(j):
        return pltpu.make_async_remote_copy(
            src_ref=source, dst_ref=target.at[pl.ds(j * SHARE, SHARE)], send_sem=send,
            recv_sem=recv.at[j], device_id=(0, z), device_id_type=MESH,
        )

    for j in range(1, HELPERS):
        pl.when(seq == j)(copy(j).start)

    def end():
        def mine():
            pltpu.sync_copy(source, target.at[pl.ds(0, SHARE)])
            for j in range(1, HELPERS):
                copy(j).wait_recv()

        pl.when(seq == 0)(mine)
        pl.when(seq != 0)(lambda: copy(1).wait_send())

    return end


def greet_first():
    seq, z = lax.axis_index("seq"), lax.axis_index("batch")
    barrier = pltpu.get_barrier_semaphore()

    @pl.when(seq != 0)
    def _():
        pl.semaphore_signal(barrier, inc=1, device_id=(0, z), device_id_type=MESH)

    @pl.when(seq == 0)
    def _():
        pl.semaphore_wait(barrier, HELPERS - 1)


def greet_helpers():
    seq, z = lax.axis_index("seq"), lax.axis_index("batch")
    barrier = pltpu.get_barrier_semaphore()

    @pl.when(seq == 0)
    def _():
        for j in range(1, HELPERS):
            pl.semaphore_signal(barrier, inc=1, device_id=(j, z), device_id_type=MESH)

    @pl.when(seq != 0)
    def _():
        pl.semaphore_wait(barrier, 1)


def number_in_sequence(p):
    return device_of(p)[0]


def gather_rows_kernel(depth, kv_ref, q_ref, all_ref, part_ref, send, recv, local, give, take):
    greet(("y", "x"), depth, HELPERS - 1)
    me = place()
    end = to_helpers(depth, q_ref, part_ref, give, take)
    own = pltpu.make_async_copy(kv_ref, all_ref.at[number_in_sequence(me)], local)
    own.start()
    rows, half = kv_ref.shape[0] // 2, kv_ref.shape[1] // 2
    jobs, at = [], 0
    for i in range(4):
        window = (pl.ds(i // 2 * rows, rows), pl.ds(i % 2 * half, half))
        order = (X_Y, Y_X)[i % 2]
        jobs.append(
            Gather(
                kv_ref.at[window], lambda p, window=window: all_ref.at[(number_in_sequence(p),) + window],
                number_in_sequence, order, depth, send, recv.at[i], at,
            )
        )
        at += Gather.sends(order, depth)
    run_gathers(jobs)
    own.wait()
    end()


def gather_rows(kv, queries, seq_count, depth, cid):
    if seq_count != 8:
        every = lax.all_gather(kv, "seq", axis=0, tiled=True)
        first = lax.all_gather(queries[:SHARED], "seq", axis=0)[0]
        own = jnp.minimum(lax.axis_index("seq"), HELPERS - 1) * SHARE
        return every, lax.dynamic_slice_in_dim(first, own, SHARE, axis=0)
    every, share = pl.pallas_call(
        partial(gather_rows_kernel, depth),
        out_shape=[
            jax.ShapeDtypeStruct((seq_count,) + kv.shape, kv.dtype),
            jax.ShapeDtypeStruct((SHARE, D), queries.dtype),
        ],
        in_specs=[ANYWHERE] * 2,
        out_specs=[ANYWHERE] * 2,
        scratch_shapes=[
            dma(4 * Gather.sends(Y_X, depth)), dma(4, seq_count), dma(), dma(HELPERS), dma(),
        ],
        compiler_params=pltpu.CompilerParams(collective_id=cid, has_side_effects=True),
        name="gather_rows",
    )(kv, queries)
    return every.reshape(-1, kv.shape[1]), share


def spread_kernel(depth, source, target, give, take):
    greet_first()
    to_helpers(depth, source, target, give, take)()


def spread(rows, seq_count, depth, cid):
    if seq_count != 8:
        first = lax.all_gather(rows[:SHARED], "seq", axis=0)[0]
        own = jnp.minimum(lax.axis_index("seq"), HELPERS - 1) * SHARE
        return lax.dynamic_slice_in_dim(first, own, SHARE, axis=0)
    return pl.pallas_call(
        partial(spread_kernel, depth),
        out_shape=jax.ShapeDtypeStruct((SHARE, D), rows.dtype),
        in_specs=[ANYWHERE], out_specs=ANYWHERE,
        scratch_shapes=[dma(HELPERS), dma()],
        compiler_params=pltpu.CompilerParams(collective_id=cid, has_side_effects=True),
        name="spread",
    )(rows)


def collect_kernel(source, target, send, recv):
    greet_helpers()
    to_first(source, target, send, recv)()


def collect(part, rows, seq_count, cid):
    own_index = lax.axis_index("seq")
    if seq_count != 8:
        first = lax.all_gather(part, "seq", axis=0)[:HELPERS].reshape(SHARED, D)
    else:
        first = pl.pallas_call(
            collect_kernel,
            out_shape=jax.ShapeDtypeStruct((SHARED, D), part.dtype),
            in_specs=[ANYWHERE], out_specs=ANYWHERE,
            scratch_shapes=[dma(), dma(HELPERS)],
            compiler_params=pltpu.CompilerParams(collective_id=cid, has_side_effects=True),
            name="collect",
        )(part)
    head = jnp.where(own_index == 0, first.astype(rows.dtype), rows[:SHARED])
    return jnp.concatenate([head, rows[SHARED:]], axis=0)


def chunked(shape):
    rows, columns = shape
    width = columns
    while rows * width > 24 * 1024 and width % 256 == 0:
        width //= 2
    if rows * width > 24 * 1024 and width % 384 == 0:
        width //= 3
    return width, columns // width


def total_of(own, kids, window):
    total = own[window].astype(jnp.float32)
    for ref, cond in kids:
        if cond is None:
            total = total + ref[window].astype(jnp.float32)
        else:
            total = total + lax.cond(
                cond,
                lambda ref=ref: ref[window].astype(jnp.float32),
                lambda total=total: jnp.zeros_like(total),
            )
    return total


def over_chunks(shape, act):
    width, count = chunked(shape)

    def step(i, carry):
        act((slice(None), pl.ds(pl.multiple_of(i * width, width), width)))
        return carry

    lax.fori_loop(0, count, step, 0)


def add_up(own, kids, into):
    def act(window):
        into[window] = total_of(own, kids, window).astype(into.dtype)

    over_chunks(into.shape, act)


def write_total(target):
    def finish(own, kids):
        def act(window):
            target[window] = total_of(own, kids, window).astype(target.dtype)

        over_chunks(target.shape, act)

    return finish


def run_reduces(jobs):
    marks = [(k, i, t) for i, (job, _) in enumerate(jobs) for k, t in enumerate(job.marks())]
    marks.sort()
    for _, i, t in marks:
        jobs[i][0].start(t)
    for _, i, t in marks:
        jobs[i][0].handle(t, add_up, write_total(jobs[i][1]))
    for job, _ in jobs:
        job.drain()


def reduce_rows_kernel(depth, dk_ref, dv_ref, out_ref, *scratch):
    inboxes, (send, recv) = scratch[:4], scratch[4:]
    greet(("y", "x"), depth)
    rows, half = out_ref.shape[0] // 2, out_ref.shape[1] // 2
    jobs = []
    for i in range(4):
        source = (dk_ref, dv_ref)[i % 2]
        window = pl.ds(i // 2 * rows, rows)
        order = (X_Y, Y_X)[i % 2]
        jobs.append(
            (
                Reduce(
                    lambda p, source=source, window=window: source.at[number_in_sequence(p), window],
                    inboxes[i], number_in_sequence, order, depth, send.at[i], recv.at[i],
                ),
                out_ref.at[window, pl.ds(i % 2 * half, half)],
            )
        )
    run_reduces(jobs)


def reduce_rows(dk, dv, seq_count, depth, cid):
    if seq_count != 8:
        both_parts = jnp.concatenate([dk, dv], axis=1).astype(jnp.float32)
        return lax.psum_scatter(both_parts, "seq", scatter_dimension=0, tiled=True)
    rows = dk.shape[0] // seq_count
    edges = len(Reduce.edge_table(Y_X, depth))
    slots = 2 * len(offsets(Y_X, depth))
    return pl.pallas_call(
        partial(reduce_rows_kernel, depth),
        out_shape=jax.ShapeDtypeStruct((rows, 2 * D), jnp.float32),
        in_specs=[IN_VMEM] * 2,
        out_specs=IN_VMEM,
        scratch_shapes=[pltpu.VMEM((edges, rows // 2, D), dk.dtype) for _ in range(4)]
        + [dma(4, slots), dma(4, edges)],
        compiler_params=pltpu.CompilerParams(
            collective_id=cid, has_side_effects=True, vmem_limit_bytes=VMEM_LIMIT
        ),
        name="reduce_rows",
    )(dk.reshape(seq_count, rows, D), dv.reshape(seq_count, rows, D))


def reduce_weights_kernel(depth, orders, *refs):
    n = len(orders)
    sources, targets, inboxes = refs[:n], refs[n : 2 * n], refs[2 * n : 3 * n]
    send, recv = refs[3 * n : 4 * n], refs[4 * n :]
    greet(("y", "x", "z"), depth)
    number = number_in(depth)
    run_reduces(
        [
            (
                Reduce(
                    lambda p, i=i: sources[i].at[number(p)], inboxes[i], number, orders[i], depth,
                    send[i], recv[i],
                ),
                targets[i],
            )
            for i in range(n)
        ]
    )


def reduce_weights(parts, orders, depth, cid):
    n = len(parts)
    edges = [len(Reduce.edge_table(order, depth)) for order in orders]
    slots = [2 * len(offsets(order, depth)) for order in orders]
    return pl.pallas_call(
        partial(reduce_weights_kernel, depth, orders),
        out_shape=[jax.ShapeDtypeStruct(a.shape[1:], jnp.float32) for a in parts],
        in_specs=[IN_VMEM] * n,
        out_specs=[IN_VMEM] * n,
        scratch_shapes=[pltpu.VMEM((e,) + a.shape[1:], a.dtype) for e, a in zip(edges, parts)]
        + [dma(s) for s in slots]
        + [dma(e) for e in edges],
        compiler_params=pltpu.CompilerParams(
            collective_id=cid, has_side_effects=True, vmem_limit_bytes=VMEM_LIMIT
        ),
        name="reduce_weights",
    )(*parts)


def own_layer(parts, seq_count, depth, cid):
    n_dev = seq_count * depth
    if seq_count != 8:
        *matrices, small = parts
        return [
            lax.psum_scatter(a.astype(jnp.float32), ("seq", "batch"), scatter_dimension=0, tiled=True)
            for a in matrices
        ] + [lax.psum_scatter(small, ("seq", "batch"), scatter_dimension=0, tiled=True)[0]]
    cut = [a.astype(jnp.bfloat16).reshape(n_dev, -1, a.shape[-1]) for a in parts[:4]] + [parts[4]]
    return reduce_weights(cut, [Z_Y_X, Z_X_Y, Z_X_Y, X_Y_Z, Z_Y_X], depth, cid)


def product(a, b):
    return lax.dot_general(a, b, (((1,), (0,)), ((), ())), preferred_element_type=jnp.float32)


def product_nt(a, b):
    return lax.dot_general(a, b, (((1,), (1,)), ((), ())), preferred_element_type=jnp.float32)


def product_tn(a, b):
    return lax.dot_general(a, b, (((0,), (0,)), ((), ())), preferred_element_type=jnp.float32)


def head_masks(dtype):
    lane = lax.broadcasted_iota(jnp.int32, (1, WIDE), 1)
    return [(lane < DH).astype(dtype), (lane >= DH).astype(dtype)]


def key_places(picks_ref, first, block, head, blocks_all):
    def row(index):
        return pl.multiple_of(index * BLK, BLK)

    drawn = [row(picks_ref[(block * H + head) * R + r]) for r in range(R)]
    window = [row(jnp.clip(first + block + j - 1, 0, blocks_all - 1)) for j in range(3)]
    return [drawn[0], drawn[1]] + window + [drawn[2]]


def bring(picks_ref, first_ref, pair, pairs, blocks_here):
    for block in range(blocks_here):
        for side in range(2):
            places = key_places(
                picks_ref, first_ref[0], block, 2 * pair + side, pairs[0][0].shape[0] // BLK
            )
            for source, target in pairs:
                for i, at in enumerate(places):
                    target[2 * block + side, i * BLK : (i + 1) * BLK] = source[pl.ds(at, BLK)]


def with_shared(ref, near):
    return jnp.concatenate([ref[0:SHARED], near], axis=0)


def soft(scores):
    top = jnp.max(scores, axis=1, keepdims=True)
    weight = jnp.exp(scores - top)
    return weight * (1.0 / jnp.sum(weight, axis=1, keepdims=True))


def local_scores(q_head, keys, shut):
    scores = product_nt(q_head, keys)
    half = scores.shape[1] // 2
    return jnp.concatenate([scores[:, :half], scores[:, half:] + shut], axis=1)


def attend_kernel(
    picks_ref, first_ref, q_ref, k_ref, v_ref, shut_ref, part_ref, o_ref, po_ref, near_k, near_v
):
    pair = pl.program_id(0)
    blocks_here = q_ref.shape[0] // BLK
    bring(picks_ref, first_ref, pair, [(k_ref, near_k), (v_ref, near_v)], blocks_here)
    masks = head_masks(jnp.bfloat16)
    low_lanes = lax.broadcasted_iota(jnp.int32, (1, WIDE), 1) < DH
    scale = jnp.bfloat16(DH ** (-0.5))
    part = part_ref[...] * scale
    both_heads = jnp.concatenate([part * masks[0], part * masks[1]], axis=0)
    weight = soft(product_nt(both_heads, k_ref[...])).astype(jnp.bfloat16)
    mixed = product(weight, v_ref[...])
    po_ref[...] = jnp.where(low_lanes, mixed[:SHARE], mixed[SHARE:]).astype(po_ref.dtype)
    for block in range(blocks_here):
        q = q_ref[block * BLK : (block + 1) * BLK] * scale
        mixed = []
        for side in range(2):
            at = 2 * block + side
            scores = local_scores(q * masks[side], with_shared(k_ref, near_k[at]), shut_ref[block])
            weight = soft(scores).astype(jnp.bfloat16)
            mixed.append(product(weight, with_shared(v_ref, near_v[at])))
        o_ref[block * BLK : (block + 1) * BLK] = jnp.where(low_lanes, mixed[0], mixed[1]).astype(o_ref.dtype)


def near_rows(rows, dtype):
    return pltpu.VMEM((2 * (rows // BLK), 6 * BLK, WIDE), dtype)


def columns(rows, shift=0):
    return pl.BlockSpec((rows, WIDE), lambda p, *_: (0, p + shift))


def attend(picks, first, queries, kv, shut, part):
    rows, length = queries.shape[0], kv.shape[0]
    return pl.pallas_call(
        attend_kernel,
        grid_spec=pltpu.PrefetchScalarGridSpec(
            num_scalar_prefetch=2,
            grid=(PAIRS,),
            in_specs=[
                columns(rows), columns(length), columns(length, PAIRS),
                pl.BlockSpec(shut.shape, lambda p, *_: (0, 0, 0)), columns(SHARE),
            ],
            out_specs=[columns(rows), columns(SHARE)],
            scratch_shapes=[near_rows(rows, jnp.bfloat16)] * 2,
        ),
        out_shape=[
            jax.ShapeDtypeStruct((rows, D), jnp.bfloat16),
            jax.ShapeDtypeStruct((SHARE, D), jnp.bfloat16),
        ],
        compiler_params=pltpu.CompilerParams(vmem_limit_bytes=VMEM_LIMIT),
        name="attend",
    )(picks, first, queries, kv, kv, shut, part)


def score_grads(weight, cot_head, values):
    grads = product_nt(cot_head, values)
    mean = jnp.sum(weight * grads, axis=1, keepdims=True)
    return (weight * (grads - mean)).astype(jnp.bfloat16)


def attend_back_kernel(
    picks_ref, first_ref, q_ref, k_ref, v_ref, shut_ref, do_ref, part_ref, pdo_ref,
    dq_ref, dk_ref, dv_ref, pdq_ref, sum_k, sum_v, near_k, near_v, grad_k, grad_v,
):
    pair = pl.program_id(0)
    blocks_here, blocks_all = q_ref.shape[0] // BLK, k_ref.shape[0] // BLK
    bring(picks_ref, first_ref, pair, [(k_ref, near_k), (v_ref, near_v)], blocks_here)
    masks = head_masks(jnp.bfloat16)
    low_lanes = lax.broadcasted_iota(jnp.int32, (1, WIDE), 1) < DH
    step = DH ** (-0.5)
    scale = jnp.bfloat16(step)
    part = part_ref[...] * scale
    part = jnp.concatenate([part * masks[0], part * masks[1]], axis=0)
    cot = pdo_ref[...]
    cot = jnp.concatenate([cot * masks[0], cot * masks[1]], axis=0)
    weight = soft(product_nt(part, k_ref[...]))
    grads = score_grads(weight, cot, v_ref[...])
    mixed = product(grads, k_ref[...]) * step
    pdq_ref[...] = jnp.where(low_lanes, mixed[:SHARE], mixed[SHARE:]).astype(pdq_ref.dtype)
    sum_k[...] = product_tn(grads, part)
    sum_v[...] = product_tn(weight.astype(jnp.bfloat16), cot)
    shared_k = jnp.zeros((SHARED, WIDE), jnp.float32)
    shared_v = jnp.zeros((SHARED, WIDE), jnp.float32)
    for block in range(blocks_here):
        here = slice(block * BLK, (block + 1) * BLK)
        q, do = q_ref[here] * scale, do_ref[here]
        mixed = []
        for side in range(2):
            near = 2 * block + side
            keys, values = with_shared(k_ref, near_k[near]), with_shared(v_ref, near_v[near])
            q_head, do_head = q * masks[side], do * masks[side]
            weight = soft(local_scores(q_head, keys, shut_ref[block]))
            grads = score_grads(weight, do_head, values)
            mixed.append(product(grads, keys))
            key_grad = product_tn(grads, q_head)
            value_grad = product_tn(weight.astype(jnp.bfloat16), do_head)
            shared_k = shared_k + key_grad[:SHARED]
            shared_v = shared_v + value_grad[:SHARED]
            grad_k[near] = key_grad[SHARED:]
            grad_v[near] = value_grad[SHARED:]
        dq_ref[here] = (jnp.where(low_lanes, mixed[0], mixed[1]) * step).astype(dq_ref.dtype)
    sum_k[0:SHARED] += shared_k
    sum_v[0:SHARED] += shared_v
    for block in range(blocks_here):
        for side in range(2):
            places = key_places(picks_ref, first_ref[0], block, 2 * pair + side, blocks_all)
            for i, at in enumerate(places):
                source = slice(i * BLK, (i + 1) * BLK)
                sum_k[pl.ds(at, BLK)] += grad_k[2 * block + side, source]
                sum_v[pl.ds(at, BLK)] += grad_v[2 * block + side, source]
    dk_ref[...] = sum_k[...].astype(dk_ref.dtype)
    dv_ref[...] = sum_v[...].astype(dv_ref.dtype)


def attend_back(picks, first, queries, kv, shut, cot, part, part_cot):
    rows, length = queries.shape[0], kv.shape[0]
    return pl.pallas_call(
        attend_back_kernel,
        grid_spec=pltpu.PrefetchScalarGridSpec(
            num_scalar_prefetch=2,
            grid=(PAIRS,),
            in_specs=[
                columns(rows), columns(length), columns(length, PAIRS),
                pl.BlockSpec(shut.shape, lambda p, *_: (0, 0, 0)), columns(rows), columns(SHARE), columns(SHARE),
            ],
            out_specs=[columns(rows), columns(length), columns(length), columns(SHARE)],
            scratch_shapes=[pltpu.VMEM((length, WIDE), jnp.float32)] * 2
            + [near_rows(rows, jnp.bfloat16)] * 2
            + [near_rows(rows, jnp.float32)] * 2,
        ),
        out_shape=[
            jax.ShapeDtypeStruct((rows, D), jnp.bfloat16),
            jax.ShapeDtypeStruct((length, D), jnp.bfloat16),
            jax.ShapeDtypeStruct((length, D), jnp.bfloat16),
            jax.ShapeDtypeStruct((SHARE, D), jnp.bfloat16),
        ],
        compiler_params=pltpu.CompilerParams(vmem_limit_bytes=VMEM_LIMIT),
        name="attend_back",
    )(picks, first, queries, kv, kv, shut, cot, part, part_cot)


def norm_rows(resid, gain, shift):
    center = resid - jnp.mean(resid, axis=-1, keepdims=True)
    inv_std = lax.rsqrt(jnp.mean(center * center, axis=-1, keepdims=True) + layer_eps)
    normed = center * inv_std
    return (normed * gain + shift, normed, inv_std)


def norm_back(grad_rows, normed, inv_std, gain):
    scaled = grad_rows * gain
    return (
        scaled
        - jnp.mean(scaled, axis=-1, keepdims=True)
        - normed * jnp.mean(scaled * normed, axis=-1, keepdims=True)
    ) * inv_std


def dot32(a, b):
    return jnp.dot(a, b, preferred_element_type=jnp.float32)


def on_device(
    layer_input, segments, rand_blocks, w_qkv, w_out, w_up, w_down, gains, biases, up_bias, d_out
):
    seq_count, depth = lax.axis_size("seq"), lax.axis_size("batch")
    n_dev = seq_count * depth
    own_index = lax.axis_index("seq")
    rows = layer_input.shape[1]
    blocks_here, length = rows // BLK, rows * seq_count
    picks = rand_blocks.reshape(-1)
    first = (own_index * blocks_here).reshape(1)

    piece = D // n_dev
    small = jnp.concatenate(
        [biases.reshape(L, -1), gains.reshape(L, -1), up_bias], axis=1
    )
    small = lax.all_gather(small, ("seq", "batch"), axis=0).astype(jnp.float32)
    vectors = jnp.moveaxis(small[:, :, : 8 * piece].reshape(n_dev, L, 8, piece), 0, 2).reshape(L, 8, D)
    hidden_shifts = jnp.moveaxis(small[:, :, 8 * piece :], 0, 1).reshape(L, -1)

    segs_all = lax.all_gather(segments[0], "seq", axis=0, tiled=True)
    padding = jnp.full((BLK,), -1, jnp.int32)
    segs_all = jnp.concatenate([padding, segs_all, padding]).reshape(-1, BLK)
    segs_near = lax.dynamic_slice_in_dim(segs_all, first[0], blocks_here + 2, axis=0)
    seg_window = jnp.concatenate([segs_near[j : j + blocks_here] for j in range(3)], axis=1)
    spot = (first[0] - 1 + jnp.arange(blocks_here)[:, None]) * BLK + jnp.arange(3 * BLK)[None, :]
    inside = (spot >= SHARED) & (spot < length)
    allowed = inside[:, None, :] & (seg_window[:, None, :] == segments.reshape(blocks_here, BLK)[:, :, None])
    shut = jnp.pad(jnp.where(allowed, 0.0, masked_score), ((0, 0), (0, 0), (0, BLK)))

    weights = [
        fetch_layer(layer, w_qkv, w_out, w_up, w_down, seq_count, depth) for layer in range(L)
    ]
    resid = layer_input[0].astype(jnp.float32)
    low = layer_input[0]
    saved = []
    for layer in range(L):
        mat_qkv, mat_out, mat_up, mat_down = weights[layer]
        bias = vectors[layer]
        proj = dot32(low, mat_qkv)
        queries = (proj[:, :D] + bias[0]).astype(jnp.bfloat16)
        kv = jnp.concatenate([proj[:, D : 2 * D], proj[:, 2 * D :] + bias[1]], axis=1).astype(jnp.bfloat16)
        kv_all, part = gather_rows(kv, queries, seq_count, depth, 2 + layer)
        mixed, part_mixed = attend(picks, first, queries, kv_all, shut, part)
        mixed = collect(part_mixed, mixed, seq_count, 4 + layer)
        resid_one = resid + dot32(mixed, mat_out) + bias[2]
        middle, normed_one, inv_one = norm_rows(resid_one, bias[6], bias[3])
        middle_low = middle.astype(jnp.bfloat16)
        hidden = dot32(middle_low, mat_up) + hidden_shifts[layer]
        active = jax.nn.gelu(hidden, approximate=False).astype(jnp.bfloat16)
        resid_two = middle + dot32(active, mat_down) + bias[4]
        result, normed_two, inv_two = norm_rows(resid_two, bias[7], bias[5])
        saved.append(
            (low, queries, kv_all, part, mixed, normed_one, inv_one, middle_low, hidden, active, normed_two, inv_two)
        )
        resid = result
        low = resid.astype(jnp.bfloat16)

    grad = d_out[0].astype(jnp.float32)
    owned = [None] * L
    is_shared = (own_index == 0) & (jnp.arange(rows) < SHARED)[:, None]
    for layer in reversed(range(L)):
        (low_in, queries, kv_all, part, mixed, normed_one, inv_one, middle_low, hidden, active, normed_two, inv_two) = saved[layer]
        mat_qkv, mat_out, mat_up, mat_down = weights[layer]
        bias = vectors[layer]
        gain_two_grad = jnp.sum(grad * normed_two, axis=0)
        shift_two_grad = jnp.sum(grad, axis=0)
        grad_two = norm_back(grad, normed_two, inv_two, bias[7])
        grad_two_low = grad_two.astype(jnp.bfloat16)
        down_grad = product_tn(active, grad_two_low)
        active_grad = product_nt(grad_two_low, mat_down)
        hidden_grad = jax.vjp(partial(jax.nn.gelu, approximate=False), hidden)[1](active_grad)[0]
        hidden_grad_low = hidden_grad.astype(jnp.bfloat16)
        up_grad = product_tn(middle_low, hidden_grad_low)
        middle_grad = grad_two + product_nt(hidden_grad_low, mat_up)
        gain_one_grad = jnp.sum(middle_grad * normed_one, axis=0)
        shift_one_grad = jnp.sum(middle_grad, axis=0)
        grad_one = norm_back(middle_grad, normed_one, inv_one, bias[6])
        grad_one_low = grad_one.astype(jnp.bfloat16)
        out_grad = product_tn(mixed, grad_one_low)
        cot = product_nt(grad_one_low, mat_out).astype(jnp.bfloat16)
        part_cot = spread(cot, seq_count, depth, 6 + layer)
        part_cot = jnp.where(own_index < HELPERS, part_cot, 0)
        cot = jnp.where(is_shared, 0, cot)
        dq, dk, dv, part_dq = attend_back(picks, first, queries, kv_all, shut, cot, part, part_cot)
        dq = collect(part_dq, dq, seq_count, 8 + layer)
        dkv = reduce_rows(dk, dv, seq_count, depth, 10 + layer)
        proj_grad = jnp.concatenate([dq, dkv.astype(jnp.bfloat16)], axis=1)
        qkv_grad = product_tn(low_in, proj_grad)
        small_rows = jnp.stack(
            [
                jnp.sum(dq.astype(jnp.float32), axis=0),
                jnp.sum(dkv[:, D:], axis=0),
                jnp.sum(grad_one, axis=0),
                shift_one_grad,
                jnp.sum(grad_two, axis=0),
                shift_two_grad,
                gain_one_grad,
                gain_two_grad,
            ]
        )
        small_rows = jnp.moveaxis(small_rows.reshape(8, n_dev, piece), 1, 0)
        hidden_rows = jnp.sum(hidden_grad, axis=0).reshape(n_dev, 8, -1)
        small_rows = jnp.concatenate([small_rows, hidden_rows], axis=2)
        small_rows = jnp.pad(small_rows, ((0, 0), (0, 0), (0, 128 - small_rows.shape[2])))
        owned[layer] = own_layer(
            [qkv_grad, out_grad, up_grad, down_grad, small_rows], seq_count, depth, 12 + layer
        )
        grad = grad_one + product_nt(proj_grad, mat_qkv)
    stacked = [jnp.stack([owned[layer][i] for layer in range(L)]) for i in range(5)]
    narrow = stacked[4]
    return (
        low[None],
        grad[None],
        stacked[0],
        stacked[1],
        stacked[2],
        stacked[3],
        narrow[:, 6:8, :piece],
        narrow[:, 0:6, :piece],
        narrow[:, :, piece : piece + up_bias.shape[1] // 8].reshape(L, -1),
    )


def solution(mesh):
    placed = (
        P("batch", "seq", None),
        P("batch", "seq"),
        P("batch", "seq", None, None),
        P(None, ("seq", "batch"), None),
        P(None, ("seq", "batch"), None),
        P(None, ("seq", "batch"), None),
        P(None, ("seq", "batch"), None),
        P(None, None, ("seq", "batch")),
        P(None, None, ("seq", "batch")),
        P(None, ("seq", "batch")),
        P("batch", "seq", None),
    )
    return jax.shard_map(
        on_device,
        mesh=mesh,
        in_specs=placed,
        out_specs=(
            P("batch", "seq", None),
            P("batch", "seq", None),
            P(None, ("seq", "batch"), None),
            P(None, ("seq", "batch"), None),
            P(None, ("seq", "batch"), None),
            P(None, ("seq", "batch"), None),
            P(None, None, ("seq", "batch")),
            P(None, None, ("seq", "batch")),
            P(None, ("seq", "batch")),
        ),
        check_vma=False,
    )
```

```python
import functools
import itertools
from functools import partial

import jax
import jax.numpy as jnp
from jax import lax
from jax.experimental import pallas as pl
from jax.experimental.pallas import tpu as pltpu
from jax.sharding import PartitionSpec as P

MESH = pl.DeviceIdType.MESH


def place():
    s = lax.axis_index("seq")
    return {"y": s // 4, "x": (s // 2) % 2, "c": s % 2, "z": lax.axis_index("batch")}


def device_of(p):
    return ((p["y"] * 2 + p["x"]) * 2 + p["c"], p["z"])


def flipped(p, axis):
    return {**p, axis: 1 - p[axis]}


def at_depth(p, z):
    return {**p, "z": z}


def number_in(depth):
    return lambda p: device_of(p)[0] * depth + p["z"]


def number_in_sequence(p):
    return device_of(p)[0]


def when(cond, action):
    if cond is None:
        action()
    else:
        pl.when(cond)(action)


def ranked(z, rank, depth):
    near = [sorted(range(depth), key=lambda q: (abs(q - k), q))[rank] for k in range(depth)]
    return sum(jnp.where(z == k, near[k], 0) for k in range(depth))


def offsets(order, depth):
    return list(itertools.product(*[range(depth if a == "z" else 2) for a in order]))


def target_of(order, offset, depth, me):
    p = me
    for axis, d in zip(order, offset):
        if d:
            p = at_depth(p, ranked(me["z"], d, depth)) if axis == "z" else flipped(p, axis)
    return p


def last_move(offset):
    return max([-1] + [i for i, d in enumerate(offset) if d])


def greet(axes, depth, from_first=0):
    me = place()
    barrier = pltpu.get_barrier_semaphore()

    def signal(device):
        pl.semaphore_signal(barrier, inc=1, device_id=device, device_id_type=MESH)

    count = 0
    for axis in axes + ("c",):
        if axis == "z":
            for step in (1, -1):
                peer = at_depth(me, me["z"] + step)
                cond = (peer["z"] >= 0) & (peer["z"] < depth)
                when(cond, lambda peer=peer: signal(device_of(peer)))
                count = count + cond.astype(jnp.int32)
        else:
            signal(device_of(flipped(me, axis)))
            count = count + 1
    if from_first:
        seq = lax.axis_index("seq")
        when(seq != 0, lambda: signal((0, lax.axis_index("batch"))))
        count = count + jnp.where(seq == 0, from_first, 0)
    pl.semaphore_wait(barrier, count)


class Gather:
    def __init__(self, source, target, number, order, depth, send, recv, send_at):
        self.source, self.target, self.number = source, target, number
        self.order, self.depth, self.send, self.recv = order, depth, send, recv
        self.send_at = send_at
        self.me = place()
        self.sent = []

    @staticmethod
    def sends(order, depth):
        return sum(len(order) + 2 - last_move(t) for t in offsets(order, depth))

    def onward(self, offset):
        last = last_move(offset)
        z = self.me["z"]
        moves = []
        if last >= 0 and self.order[last] == "z":
            source = ranked(z, offset[last], self.depth)
            peer = jnp.where(source < z, z + 1, z - 1)
            moves.append((at_depth(self.me, peer), (peer >= 0) & (peer < self.depth)))
        for axis in self.order[last + 1 :]:
            if axis == "z":
                moves.append((at_depth(self.me, z + 1), z + 1 < self.depth))
                moves.append((at_depth(self.me, z - 1), z > 0))
            else:
                moves.append((flipped(self.me, axis), None))
        moves.append((flipped(self.me, "c"), None))
        return moves

    def arrival(self, p):
        ref = self.target(p)
        return pltpu.make_async_remote_copy(
            src_ref=ref, dst_ref=ref, send_sem=self.send.at[0], recv_sem=self.recv.at[self.number(p)],
            device_id=device_of(self.me), device_id_type=MESH,
        )

    def handle(self, offset):
        p = target_of(self.order, offset, self.depth, self.me)
        own = not any(offset)
        if not own:
            self.arrival(p).wait_recv()
        for peer, cond in self.onward(offset):
            copy = pltpu.make_async_remote_copy(
                src_ref=self.source if own else self.target(p), dst_ref=self.target(p),
                send_sem=self.send.at[self.send_at], recv_sem=self.recv.at[self.number(p)],
                device_id=device_of(peer), device_id_type=MESH,
            )
            when(cond, copy.start)
            self.sent.append((cond, self.send_at))
            self.send_at += 1

    def begin(self):
        self.handle((0,) * len(self.order))

    def events(self):
        return [
            (sum(t), partial(self.handle, t))
            for t in sorted(offsets(self.order, self.depth), key=lambda t: (sum(t), t))
            if any(t)
        ]

    def siblings(self):
        for t in offsets(self.order, self.depth):
            self.arrival(flipped(target_of(self.order, t, self.depth, self.me), "c")).wait_recv()

    def drain(self):
        for cond, slot in self.sent:
            copy = pltpu.make_async_remote_copy(
                src_ref=self.source, dst_ref=self.target(self.me), send_sem=self.send.at[slot],
                recv_sem=self.recv.at[self.number(self.me)], device_id=device_of(self.me), device_id_type=MESH,
            )
            when(cond, copy.wait_send)


def gather_events(jobs):
    todo = [
        (when_, i, k, act) for i, job in enumerate(jobs) for k, (when_, act) in enumerate(job.events())
    ]
    return [act for _, _, _, act in sorted(todo, key=lambda e: e[:3])]


def end_gathers(jobs):
    for job in jobs:
        job.siblings()
    for job in jobs:
        job.drain()


class Reduce:
    def __init__(self, partial_of, inbox, order, depth, send, recv):
        self.partial_of, self.inbox = partial_of, inbox
        self.order, self.depth, self.send, self.recv = order, depth, send, recv
        self.me = place()
        self.base, _ = self.slots(order, depth)
        self.marks = sorted(offsets(order, depth), key=lambda t: (-sum(t), t))
        self.sent = []

    @staticmethod
    def split(order, offset):
        if "z" not in order:
            return offset, 0
        i = order.index("z")
        return offset[:i] + (0,) + offset[i + 1 :], offset[i]

    @staticmethod
    def slots(order, depth):
        base, count = {}, 0
        deep = depth if "z" in order else 1
        for t in offsets(order, depth):
            key, rank = Reduce.split(order, t)
            if rank:
                continue
            last = last_move(key)
            for i, axis in enumerate(order):
                if i <= last:
                    continue
                base[(key, axis)] = count
                if axis == "z":
                    count += deep + 1
                elif "z" in order and i > order.index("z"):
                    count += deep
                else:
                    count += 1
            base[(key, "c")] = count
            count += deep
        return base, count

    def where_(self, key, axis, z):
        deep = "z" in self.order and (axis == "c" or self.order.index(axis) > self.order.index("z"))
        return self.base[(key, axis)] + (z if deep else 0)

    def copy(self, source, edge, slot, peer):
        return pltpu.make_async_remote_copy(
            src_ref=source, dst_ref=self.inbox.at[edge], send_sem=self.send.at[slot],
            recv_sem=self.recv.at[edge], device_id=device_of(peer), device_id_type=MESH,
        )

    def start(self, offset):
        p = target_of(self.order, offset, self.depth, self.me)
        key, _ = self.split(self.order, offset)
        slot = self.marks.index(offset)
        edge = self.where_(key, "c", p["z"])
        peer = flipped(self.me, "c")
        self.copy(self.partial_of(flipped(p, "c")), edge, slot, peer).start()
        self.sent.append(slot)

    def kids(self, offset, p):
        key, rank = self.split(self.order, offset)
        last, z = last_move(offset), self.me["z"]
        found = [(self.where_(key, "c", p["z"]), None)]
        for axis in self.order[last + 1 :]:
            if axis == "z":
                at = self.base[(key, "z")]
                found += [(at + z, z > 0), (at + self.depth, z + 1 < self.depth)]
            else:
                found.append((self.where_(key, axis, p["z"]), None))
        if last >= 0 and self.order[last] == "z":
            far = jnp.where(p["z"] < z, z + 1, z - 1)
            found.append((self.base[(key, "z")] + p["z"], (far >= 0) & (far < self.depth)))
        return found

    def upward(self, offset, p):
        key, rank = self.split(self.order, offset)
        k, z = last_move(offset), self.me["z"]
        axis = self.order[k]
        if axis == "z":
            edge = self.base[(key, "z")] + jnp.where(p["z"] == z - 1, self.depth, p["z"])
            return edge, at_depth(self.me, jnp.where(p["z"] < z, z - 1, z + 1))
        parent = key[:k] + (0,) + key[k + 1 :]
        return self.where_(parent, axis, p["z"]), flipped(self.me, axis)

    def handle(self, offset, add, finish):
        p = target_of(self.order, offset, self.depth, self.me)
        kids = self.kids(offset, p)
        slot = len(self.marks) + self.marks.index(offset)
        for edge, cond in kids:
            when(cond, self.copy(self.inbox.at[edge], edge, slot, self.me).wait_recv)
        parts = [(self.inbox.at[edge], cond) for edge, cond in kids]
        if any(offset):
            into = parts[0][0]
            add(self.partial_of(p), parts, into)
            edge, peer = self.upward(offset, p)
            self.copy(into, edge, slot, peer).start()
            self.sent.append(slot)
        else:
            finish(self.partial_of(p), parts)

    def drain(self):
        for slot in self.sent:
            self.copy(self.inbox.at[0], 0, slot, self.me).wait_send()


D = 768
H = 12
DH = 64
BLK = 64
R = 3
GLOB = 2
L = 2
PAIRS = H // 2
WIDE = 2 * DH
SHARED = GLOB * BLK
SHARE = 16
HELPERS = SHARED // SHARE
VMEM_LIMIT = 60 * 1024 * 1024

layer_eps = 1e-06
masked_score = -1e30

Z_Y_X, Z_X_Y, X_Y_Z, Y_X_Z = ("z", "y", "x"), ("z", "x", "y"), ("x", "y", "z"), ("y", "x", "z")
Y_X, X_Y = ("y", "x"), ("x", "y")
ANYWHERE = pl.BlockSpec(memory_space=pl.ANY)
IN_VMEM = pl.BlockSpec(memory_space=pltpu.VMEM)


def dma(*shape):
    return pltpu.SemaphoreType.DMA(shape)


def gather_pieces(pieces, sources, targets, depth, send, recv, at=0):
    jobs = []
    for i, (which, first, rows, order) in enumerate(pieces):
        rows = pl.ds(first, rows)
        number = number_in(depth) if "z" in order else number_in_sequence
        jobs.append(
            Gather(
                sources[which].at[rows],
                lambda p, which=which, rows=rows, number=number: targets[which].at[number(p), rows],
                number, order, depth, send, recv.at[i], at,
            )
        )
        at += Gather.sends(order, depth)
    return jobs


def own_copies(pieces, sources, targets, depth, local):
    me = place()
    numbers = {which: (number_in(depth) if "z" in order else number_in_sequence) for which, _, _, order in pieces}
    return [
        pltpu.make_async_copy(sources[which], targets[which].at[number(me)], local.at[which])
        for which, number in numbers.items()
    ]


def gather_weights_kernel(depth, pieces, n, *refs):
    sources, targets = refs[:n], refs[n : 2 * n]
    send, recv, local = refs[2 * n :]
    greet(("y", "x", "z"), depth)
    own = own_copies(pieces, sources, targets, depth, local)
    jobs = gather_pieces(pieces, sources, targets, depth, send, recv)
    for job in jobs:
        job.begin()
    for copy in own:
        copy.start()
    for act in gather_events(jobs):
        act()
    end_gathers(jobs)
    for copy in own:
        copy.wait()


def gather_weights(arrays, pieces, depth, n_dev, cid):
    n = len(arrays)
    seq_only = {which for which, _, _, order in pieces if "z" not in order}
    counts = [n_dev // depth if i in seq_only else n_dev for i in range(n)]
    total = sum(Gather.sends(order, depth) for _, _, _, order in pieces)
    return pl.pallas_call(
        partial(gather_weights_kernel, depth, pieces, n),
        out_shape=[jax.ShapeDtypeStruct((k,) + a.shape, a.dtype) for k, a in zip(counts, arrays)],
        in_specs=[ANYWHERE] * n,
        out_specs=[ANYWHERE] * n,
        scratch_shapes=[dma(total), dma(len(pieces), n_dev), dma(n)],
        compiler_params=pltpu.CompilerParams(collective_id=cid, has_side_effects=True),
        name="gather_weights",
    )(*arrays)


def weight_pieces(rows_in, rows_down):
    two_thirds = rows_down * 2 // 3
    return [
        (0, 0, rows_in, Z_Y_X),
        (1, 0, rows_in, Z_X_Y),
        (2, 0, rows_in, Z_X_Y),
        (3, 0, two_thirds, X_Y_Z),
        (3, two_thirds, rows_down - two_thirds, Z_Y_X),
    ]


def to_helpers(depth, source, target, send, recv):
    seq, z = lax.axis_index("seq"), lax.axis_index("batch")

    def copy(j):
        return pltpu.make_async_remote_copy(
            src_ref=source.at[pl.ds(j * SHARE, SHARE)], dst_ref=target, send_sem=send.at[j],
            recv_sem=recv, device_id=(j, z), device_id_type=MESH,
        )

    def begin():
        for j in range(1, HELPERS):
            copy(j).start()

    def own():
        pltpu.sync_copy(source.at[pl.ds(0, SHARE)], target)
        for j in range(1, HELPERS):
            copy(j).wait_send()

    def end():
        pl.when(seq == 0)(own)
        pl.when(seq != 0)(lambda: copy(1).wait_recv())

    pl.when(seq == 0)(begin)
    return end


def to_first(source, target, send, recv):
    seq, z = lax.axis_index("seq"), lax.axis_index("batch")

    def copy(j):
        return pltpu.make_async_remote_copy(
            src_ref=source, dst_ref=target.at[pl.ds(j * SHARE, SHARE)], send_sem=send,
            recv_sem=recv.at[j], device_id=(0, z), device_id_type=MESH,
        )

    for j in range(1, HELPERS):
        pl.when(seq == j)(copy(j).start)

    def end():
        def mine():
            pltpu.sync_copy(source, target.at[pl.ds(0, SHARE)])
            for j in range(1, HELPERS):
                copy(j).wait_recv()

        pl.when(seq == 0)(mine)
        pl.when(seq != 0)(lambda: copy(1).wait_send())

    return end


def greet_first():
    seq, z = lax.axis_index("seq"), lax.axis_index("batch")
    barrier = pltpu.get_barrier_semaphore()

    @pl.when(seq != 0)
    def _():
        pl.semaphore_signal(barrier, inc=1, device_id=(0, z), device_id_type=MESH)

    @pl.when(seq == 0)
    def _():
        pl.semaphore_wait(barrier, HELPERS - 1)


def greet_helpers():
    seq, z = lax.axis_index("seq"), lax.axis_index("batch")
    barrier = pltpu.get_barrier_semaphore()

    @pl.when(seq == 0)
    def _():
        for j in range(1, HELPERS):
            pl.semaphore_signal(barrier, inc=1, device_id=(j, z), device_id_type=MESH)

    @pl.when(seq != 0)
    def _():
        pl.semaphore_wait(barrier, 1)


def number_in_sequence(p):
    return device_of(p)[0]


def gather_rows_kernel(depth, kv_ref, q_ref, all_ref, part_ref, send, recv, local, give, take):
    greet(("y", "x"), depth, HELPERS - 1)
    me = place()
    end = to_helpers(depth, q_ref, part_ref, give, take)
    own = pltpu.make_async_copy(kv_ref, all_ref.at[number_in_sequence(me)], local)
    own.start()
    rows, half = kv_ref.shape[0] // 2, kv_ref.shape[1] // 2
    jobs, at = [], 0
    for i in range(4):
        window = (pl.ds(i // 2 * rows, rows), pl.ds(i % 2 * half, half))
        order = (X_Y, Y_X)[i % 2]
        jobs.append(
            Gather(
                kv_ref.at[window], lambda p, window=window: all_ref.at[(number_in_sequence(p),) + window],
                number_in_sequence, order, depth, send, recv.at[i], at,
            )
        )
        at += Gather.sends(order, depth)
    for job in jobs:
        job.begin()
    for act in gather_events(jobs):
        act()
    end_gathers(jobs)
    own.wait()
    end()


def gather_rows(kv, queries, seq_count, depth, cid):
    if seq_count != 8:
        every = lax.all_gather(kv, "seq", axis=0, tiled=True)
        first = lax.all_gather(queries[:SHARED], "seq", axis=0)[0]
        own = jnp.minimum(lax.axis_index("seq"), HELPERS - 1) * SHARE
        return every, lax.dynamic_slice_in_dim(first, own, SHARE, axis=0)
    every, share = pl.pallas_call(
        partial(gather_rows_kernel, depth),
        out_shape=[
            jax.ShapeDtypeStruct((seq_count,) + kv.shape, kv.dtype),
            jax.ShapeDtypeStruct((SHARE, D), queries.dtype),
        ],
        in_specs=[ANYWHERE] * 2,
        out_specs=[ANYWHERE] * 2,
        scratch_shapes=[
            dma(4 * Gather.sends(Y_X, depth)), dma(4, seq_count), dma(), dma(HELPERS), dma(),
        ],
        compiler_params=pltpu.CompilerParams(collective_id=cid, has_side_effects=True),
        name="gather_rows",
    )(kv, queries)
    return every.reshape(-1, kv.shape[1]), share


def spread_kernel(depth, source, target, give, take):
    greet_first()
    to_helpers(depth, source, target, give, take)()


def spread(rows, seq_count, depth, cid):
    if seq_count != 8:
        first = lax.all_gather(rows[:SHARED], "seq", axis=0)[0]
        own = jnp.minimum(lax.axis_index("seq"), HELPERS - 1) * SHARE
        return lax.dynamic_slice_in_dim(first, own, SHARE, axis=0)
    return pl.pallas_call(
        partial(spread_kernel, depth),
        out_shape=jax.ShapeDtypeStruct((SHARE, D), rows.dtype),
        in_specs=[ANYWHERE], out_specs=ANYWHERE,
        scratch_shapes=[dma(HELPERS), dma()],
        compiler_params=pltpu.CompilerParams(collective_id=cid, has_side_effects=True),
        name="spread",
    )(rows)


def collect_kernel(source, target, send, recv):
    greet_helpers()
    to_first(source, target, send, recv)()


def collect(part, rows, seq_count, cid):
    own_index = lax.axis_index("seq")
    if seq_count != 8:
        first = lax.all_gather(part, "seq", axis=0)[:HELPERS].reshape(SHARED, D)
    else:
        first = pl.pallas_call(
            collect_kernel,
            out_shape=jax.ShapeDtypeStruct((SHARED, D), part.dtype),
            in_specs=[ANYWHERE], out_specs=ANYWHERE,
            scratch_shapes=[dma(), dma(HELPERS)],
            compiler_params=pltpu.CompilerParams(collective_id=cid, has_side_effects=True),
            name="collect",
        )(part)
    head = jnp.where(own_index == 0, first.astype(rows.dtype), rows[:SHARED])
    return jnp.concatenate([head, rows[SHARED:]], axis=0)


def chunked(shape):
    rows, columns = shape
    width = columns
    while rows * width > 24 * 1024 and width % 256 == 0:
        width //= 2
    if rows * width > 24 * 1024 and width % 384 == 0:
        width //= 3
    return width, columns // width


def total_of(own, kids, window):
    total = own[window].astype(jnp.float32)
    for ref, cond in kids:
        if cond is None:
            total = total + ref[window].astype(jnp.float32)
        else:
            total = total + lax.cond(
                cond,
                lambda ref=ref: ref[window].astype(jnp.float32),
                lambda total=total: jnp.zeros_like(total),
            )
    return total


def over_chunks(shape, act):
    width, count = chunked(shape)

    def step(i, carry):
        act((slice(None), pl.ds(pl.multiple_of(i * width, width), width)))
        return carry

    lax.fori_loop(0, count, step, 0)


def add_up(own, kids, into):
    def act(window):
        into[window] = total_of(own, kids, window).astype(into.dtype)

    over_chunks(into.shape, act)


def write_total(target):
    def finish(own, kids):
        def act(window):
            target[window] = total_of(own, kids, window).astype(target.dtype)

        over_chunks(target.shape, act)

    return finish


def run_reduces(jobs):
    marks = [(k, i, t) for i, (job, _) in enumerate(jobs) for k, t in enumerate(job.marks)]
    marks.sort()
    for _, i, t in marks:
        jobs[i][0].start(t)
    for _, i, t in marks:
        jobs[i][0].handle(t, add_up, write_total(jobs[i][1]))
    for job, _ in jobs:
        job.drain()


def reduce_rows_kernel(depth, dk_ref, dv_ref, out_ref, *scratch):
    inboxes, (send, recv) = scratch[:4], scratch[4:]
    greet(("y", "x"), depth)
    rows, half = out_ref.shape[0] // 2, out_ref.shape[1] // 2
    jobs = []
    for i in range(4):
        source = (dk_ref, dv_ref)[i % 2]
        window = pl.ds(i // 2 * rows, rows)
        order = (X_Y, Y_X)[i % 2]
        jobs.append(
            (
                Reduce(
                    lambda p, source=source, window=window: source.at[number_in_sequence(p), window],
                    inboxes[i], order, depth, send.at[i], recv.at[i],
                ),
                out_ref.at[window, pl.ds(i % 2 * half, half)],
            )
        )
    run_reduces(jobs)


def reduce_rows(dk, dv, seq_count, depth, cid):
    if seq_count != 8:
        both_parts = jnp.concatenate([dk, dv], axis=1).astype(jnp.float32)
        return lax.psum_scatter(both_parts, "seq", scatter_dimension=0, tiled=True)
    rows = dk.shape[0] // seq_count
    _, edges = Reduce.slots(Y_X, depth)
    slots = 2 * len(offsets(Y_X, depth))
    return pl.pallas_call(
        partial(reduce_rows_kernel, depth),
        out_shape=jax.ShapeDtypeStruct((rows, 2 * D), jnp.float32),
        in_specs=[IN_VMEM] * 2,
        out_specs=IN_VMEM,
        scratch_shapes=[pltpu.VMEM((edges, rows // 2, D), dk.dtype) for _ in range(4)]
        + [dma(4, slots), dma(4, edges)],
        compiler_params=pltpu.CompilerParams(
            collective_id=cid, has_side_effects=True, vmem_limit_bytes=VMEM_LIMIT
        ),
        name="reduce_rows",
    )(dk.reshape(seq_count, rows, D), dv.reshape(seq_count, rows, D))


def reduce_weights_kernel(depth, pieces, n, *refs):
    m = len(pieces)
    sources, targets, inboxes = refs[:n], refs[n : 2 * n], refs[2 * n : 2 * n + m]
    send, recv = refs[2 * n + m : 2 * n + 2 * m], refs[2 * n + 2 * m :]
    greet(("y", "x", "z"), depth)
    number = number_in(depth)
    jobs = []
    for i, (which, first, rows, order) in enumerate(pieces):
        rows = pl.ds(first, rows)
        jobs.append(
            (
                Reduce(
                    lambda p, which=which, rows=rows: sources[which].at[number(p), rows],
                    inboxes[i], order, depth, send[i], recv[i],
                ),
                targets[which].at[rows],
            )
        )
    run_reduces(jobs)


def reduce_weights(parts, pieces, depth, cid):
    n = len(parts)
    edges = [Reduce.slots(order, depth)[1] for _, _, _, order in pieces]
    slots = [2 * len(offsets(order, depth)) for _, _, _, order in pieces]
    return pl.pallas_call(
        partial(reduce_weights_kernel, depth, pieces, n),
        out_shape=[jax.ShapeDtypeStruct(a.shape[1:], jnp.float32) for a in parts],
        in_specs=[IN_VMEM] * n,
        out_specs=[IN_VMEM] * n,
        scratch_shapes=[
            pltpu.VMEM((e, rows, parts[which].shape[2]), parts[which].dtype)
            for e, (which, _, rows, _) in zip(edges, pieces)
        ]
        + [dma(s) for s in slots]
        + [dma(e) for e in edges],
        compiler_params=pltpu.CompilerParams(
            collective_id=cid, has_side_effects=True, vmem_limit_bytes=VMEM_LIMIT
        ),
        name="reduce_weights",
    )(*parts)


def own_layer(parts, seq_count, depth, cid):
    n_dev = seq_count * depth
    if seq_count != 8:
        *matrices, small = parts
        return [
            lax.psum_scatter(a.astype(jnp.float32), ("seq", "batch"), scatter_dimension=0, tiled=True)
            for a in matrices
        ] + [lax.psum_scatter(small, ("seq", "batch"), scatter_dimension=0, tiled=True)[0]]
    cut = [a.astype(jnp.bfloat16).reshape(n_dev, -1, a.shape[-1]) for a in parts[:4]] + [parts[4]]
    pieces = weight_pieces(cut[0].shape[1], cut[3].shape[1]) + [(4, 0, 8, Z_Y_X)]
    return reduce_weights(cut, pieces, depth, cid)


def product(a, b):
    return lax.dot_general(a, b, (((1,), (0,)), ((), ())), preferred_element_type=jnp.float32)


def product_nt(a, b):
    return lax.dot_general(a, b, (((1,), (1,)), ((), ())), preferred_element_type=jnp.float32)


def product_tn(a, b):
    return lax.dot_general(a, b, (((0,), (0,)), ((), ())), preferred_element_type=jnp.float32)


def head_masks(dtype):
    lane = lax.broadcasted_iota(jnp.int32, (1, WIDE), 1)
    return [(lane < DH).astype(dtype), (lane >= DH).astype(dtype)]


def key_places(picks_ref, first, block, head, blocks_all):
    def row(index):
        return pl.multiple_of(index * BLK, BLK)

    drawn = [row(picks_ref[(block * H + head) * R + r]) for r in range(R)]
    window = [row(jnp.clip(first + block + j - 1, 0, blocks_all - 1)) for j in range(3)]
    return [drawn[0], drawn[1]] + window + [drawn[2]]


def bring(picks_ref, first_ref, pair, pairs, blocks_here):
    for block in range(blocks_here):
        for side in range(2):
            places = key_places(
                picks_ref, first_ref[0], block, 2 * pair + side, pairs[0][0].shape[0] // BLK
            )
            for source, target in pairs:
                for i, at in enumerate(places):
                    target[2 * block + side, i * BLK : (i + 1) * BLK] = source[pl.ds(at, BLK)]


def with_shared(ref, near):
    return jnp.concatenate([ref[0:SHARED], near], axis=0)


def soft(scores):
    top = jnp.max(scores, axis=1, keepdims=True)
    weight = jnp.exp(scores - top)
    return weight * (1.0 / jnp.sum(weight, axis=1, keepdims=True))


def local_scores(q_head, keys, shut):
    scores = product_nt(q_head, keys)
    half = scores.shape[1] // 2
    return jnp.concatenate([scores[:, :half], scores[:, half:] + shut], axis=1)


def attend_kernel(
    picks_ref, first_ref, q_ref, k_ref, v_ref, shut_ref, part_ref, o_ref, po_ref, near_k, near_v
):
    pair = pl.program_id(0)
    blocks_here = q_ref.shape[0] // BLK
    bring(picks_ref, first_ref, pair, [(k_ref, near_k), (v_ref, near_v)], blocks_here)
    masks = head_masks(jnp.bfloat16)
    low_lanes = lax.broadcasted_iota(jnp.int32, (1, WIDE), 1) < DH
    scale = jnp.bfloat16(DH ** (-0.5))
    part = part_ref[...] * scale
    both_heads = jnp.concatenate([part * masks[0], part * masks[1]], axis=0)
    weight = soft(product_nt(both_heads, k_ref[...])).astype(jnp.bfloat16)
    mixed = product(weight, v_ref[...])
    po_ref[...] = jnp.where(low_lanes, mixed[:SHARE], mixed[SHARE:]).astype(po_ref.dtype)
    for block in range(blocks_here):
        q = q_ref[block * BLK : (block + 1) * BLK] * scale
        mixed = []
        for side in range(2):
            at = 2 * block + side
            scores = local_scores(q * masks[side], with_shared(k_ref, near_k[at]), shut_ref[block])
            weight = soft(scores).astype(jnp.bfloat16)
            mixed.append(product(weight, with_shared(v_ref, near_v[at])))
        o_ref[block * BLK : (block + 1) * BLK] = jnp.where(low_lanes, mixed[0], mixed[1]).astype(o_ref.dtype)


def near_rows(rows, dtype):
    return pltpu.VMEM((2 * (rows // BLK), 6 * BLK, WIDE), dtype)


def columns(rows, shift=0):
    return pl.BlockSpec((rows, WIDE), lambda p, *_: (0, p + shift))


def attend(picks, first, queries, kv, shut, part):
    rows, length = queries.shape[0], kv.shape[0]
    return pl.pallas_call(
        attend_kernel,
        grid_spec=pltpu.PrefetchScalarGridSpec(
            num_scalar_prefetch=2,
            grid=(PAIRS,),
            in_specs=[
                columns(rows), columns(length), columns(length, PAIRS),
                pl.BlockSpec(shut.shape, lambda p, *_: (0, 0, 0)), columns(SHARE),
            ],
            out_specs=[columns(rows), columns(SHARE)],
            scratch_shapes=[near_rows(rows, jnp.bfloat16)] * 2,
        ),
        out_shape=[
            jax.ShapeDtypeStruct((rows, D), jnp.bfloat16),
            jax.ShapeDtypeStruct((SHARE, D), jnp.bfloat16),
        ],
        compiler_params=pltpu.CompilerParams(vmem_limit_bytes=VMEM_LIMIT),
        name="attend",
    )(picks, first, queries, kv, kv, shut, part)


def score_grads(weight, cot_head, values):
    grads = product_nt(cot_head, values)
    mean = jnp.sum(weight * grads, axis=1, keepdims=True)
    return (weight * (grads - mean)).astype(jnp.bfloat16)


def attend_back_kernel(
    picks_ref, first_ref, q_ref, k_ref, v_ref, shut_ref, do_ref, part_ref, pdo_ref,
    dq_ref, dk_ref, dv_ref, pdq_ref, sum_k, sum_v, near_k, near_v, grad_k, grad_v,
):
    pair = pl.program_id(0)
    blocks_here, blocks_all = q_ref.shape[0] // BLK, k_ref.shape[0] // BLK
    bring(picks_ref, first_ref, pair, [(k_ref, near_k), (v_ref, near_v)], blocks_here)
    masks = head_masks(jnp.bfloat16)
    low_lanes = lax.broadcasted_iota(jnp.int32, (1, WIDE), 1) < DH
    step = DH ** (-0.5)
    scale = jnp.bfloat16(step)
    part = part_ref[...] * scale
    part = jnp.concatenate([part * masks[0], part * masks[1]], axis=0)
    cot = pdo_ref[...]
    cot = jnp.concatenate([cot * masks[0], cot * masks[1]], axis=0)
    weight = soft(product_nt(part, k_ref[...]))
    grads = score_grads(weight, cot, v_ref[...])
    mixed = product(grads, k_ref[...]) * step
    pdq_ref[...] = jnp.where(low_lanes, mixed[:SHARE], mixed[SHARE:]).astype(pdq_ref.dtype)
    sum_k[...] = product_tn(grads, part)
    sum_v[...] = product_tn(weight.astype(jnp.bfloat16), cot)
    shared_k = jnp.zeros((SHARED, WIDE), jnp.float32)
    shared_v = jnp.zeros((SHARED, WIDE), jnp.float32)
    for block in range(blocks_here):
        here = slice(block * BLK, (block + 1) * BLK)
        q, do = q_ref[here] * scale, do_ref[here]
        mixed = []
        for side in range(2):
            near = 2 * block + side
            keys, values = with_shared(k_ref, near_k[near]), with_shared(v_ref, near_v[near])
            q_head, do_head = q * masks[side], do * masks[side]
            weight = soft(local_scores(q_head, keys, shut_ref[block]))
            grads = score_grads(weight, do_head, values)
            mixed.append(product(grads, keys))
            key_grad = product_tn(grads, q_head)
            value_grad = product_tn(weight.astype(jnp.bfloat16), do_head)
            shared_k = shared_k + key_grad[:SHARED]
            shared_v = shared_v + value_grad[:SHARED]
            grad_k[near] = key_grad[SHARED:]
            grad_v[near] = value_grad[SHARED:]
        dq_ref[here] = (jnp.where(low_lanes, mixed[0], mixed[1]) * step).astype(dq_ref.dtype)
    sum_k[0:SHARED] += shared_k
    sum_v[0:SHARED] += shared_v
    for block in range(blocks_here):
        for side in range(2):
            places = key_places(picks_ref, first_ref[0], block, 2 * pair + side, blocks_all)
            for i, at in enumerate(places):
                source = slice(i * BLK, (i + 1) * BLK)
                sum_k[pl.ds(at, BLK)] += grad_k[2 * block + side, source]
                sum_v[pl.ds(at, BLK)] += grad_v[2 * block + side, source]
    dk_ref[...] = sum_k[...].astype(dk_ref.dtype)
    dv_ref[...] = sum_v[...].astype(dv_ref.dtype)


def attend_back(picks, first, queries, kv, shut, cot, part, part_cot):
    rows, length = queries.shape[0], kv.shape[0]
    return pl.pallas_call(
        attend_back_kernel,
        grid_spec=pltpu.PrefetchScalarGridSpec(
            num_scalar_prefetch=2,
            grid=(PAIRS,),
            in_specs=[
                columns(rows), columns(length), columns(length, PAIRS),
                pl.BlockSpec(shut.shape, lambda p, *_: (0, 0, 0)), columns(rows), columns(SHARE), columns(SHARE),
            ],
            out_specs=[columns(rows), columns(length), columns(length), columns(SHARE)],
            scratch_shapes=[pltpu.VMEM((length, WIDE), jnp.float32)] * 2
            + [near_rows(rows, jnp.bfloat16)] * 2
            + [near_rows(rows, jnp.float32)] * 2,
        ),
        out_shape=[
            jax.ShapeDtypeStruct((rows, D), jnp.bfloat16),
            jax.ShapeDtypeStruct((length, D), jnp.bfloat16),
            jax.ShapeDtypeStruct((length, D), jnp.bfloat16),
            jax.ShapeDtypeStruct((SHARE, D), jnp.bfloat16),
        ],
        compiler_params=pltpu.CompilerParams(vmem_limit_bytes=VMEM_LIMIT),
        name="attend_back",
    )(picks, first, queries, kv, kv, shut, cot, part, part_cot)


def norm_rows(resid, gain, shift):
    center = resid - jnp.mean(resid, axis=-1, keepdims=True)
    inv_std = lax.rsqrt(jnp.mean(center * center, axis=-1, keepdims=True) + layer_eps)
    normed = center * inv_std
    return (normed * gain + shift, normed, inv_std)


def norm_back(grad_rows, normed, inv_std, gain):
    scaled = grad_rows * gain
    return (
        scaled
        - jnp.mean(scaled, axis=-1, keepdims=True)
        - normed * jnp.mean(scaled * normed, axis=-1, keepdims=True)
    ) * inv_std


def dot32(a, b):
    return jnp.dot(a, b, preferred_element_type=jnp.float32)


def on_device(
    layer_input, segments, rand_blocks, w_qkv, w_out, w_up, w_down, gains, biases, up_bias, d_out
):
    seq_count, depth = lax.axis_size("seq"), lax.axis_size("batch")
    n_dev = seq_count * depth
    own_index = lax.axis_index("seq")
    rows = layer_input.shape[1]
    blocks_here, length = rows // BLK, rows * seq_count
    picks = rand_blocks.reshape(-1)
    first = (own_index * blocks_here).reshape(1)

    piece = D // n_dev
    small = jnp.concatenate(
        [biases.reshape(-1, piece), gains.reshape(-1, piece), up_bias.reshape(-1, piece)], axis=0
    ).T
    pieces = weight_pieces(w_qkv.shape[1], w_down.shape[1])
    arrays = [[w[layer] for w in (w_qkv, w_out, w_up, w_down)] for layer in range(L)]
    if seq_count == 8:
        small = jnp.pad(small, ((0, 0), (0, 128 - small.shape[1])))
        segs = jnp.pad(segments.reshape(-1, 128), ((0, 8 - rows // 128), (0, 0)))
        more = [(4, 0, piece, Z_Y_X), (5, 0, 8, Y_X)]
        *first_layer, small, segs_all = gather_weights(
            arrays[0] + [small, segs], more + pieces, depth, n_dev, 0
        )
        weights = [first_layer, gather_weights(arrays[1], pieces, depth, n_dev, 1)]
        weights = [[w.reshape(-1, w.shape[-1]) for w in held] for held in weights]
        segs_all = segs_all[:, : rows // 128].reshape(-1)
        small = small.reshape(D, 128)
    else:
        small = lax.all_gather(small, ("seq", "batch"), axis=0, tiled=True)
        segs_all = lax.all_gather(segments[0], "seq", axis=0, tiled=True)
        weights = [
            [lax.all_gather(w, ("seq", "batch"), axis=0, tiled=True) for w in held] for held in arrays
        ]
    small = small.astype(jnp.float32).T
    vectors = jnp.concatenate(
        [small[: 6 * L].reshape(L, 6, D), small[6 * L : 8 * L].reshape(L, 2, D)], axis=1
    )
    hidden_shifts = small[8 * L : 12 * L].reshape(L, 4, n_dev, piece)
    hidden_shifts = jnp.swapaxes(hidden_shifts, 1, 2).reshape(L, -1)

    padding = jnp.full((BLK,), -1, jnp.int32)
    segs_all = jnp.concatenate([padding, segs_all, padding]).reshape(-1, BLK)
    segs_near = lax.dynamic_slice_in_dim(segs_all, first[0], blocks_here + 2, axis=0)
    seg_window = jnp.concatenate([segs_near[j : j + blocks_here] for j in range(3)], axis=1)
    spot = (first[0] - 1 + jnp.arange(blocks_here)[:, None]) * BLK + jnp.arange(3 * BLK)[None, :]
    inside = (spot >= SHARED) & (spot < length)
    allowed = inside[:, None, :] & (seg_window[:, None, :] == segments.reshape(blocks_here, BLK)[:, :, None])
    shut = jnp.pad(jnp.where(allowed, 0.0, masked_score), ((0, 0), (0, 0), (0, BLK)))

    resid = layer_input[0].astype(jnp.float32)
    low = layer_input[0]
    saved = []
    for layer in range(L):
        mat_qkv, mat_out, mat_up, mat_down = weights[layer]
        bias = vectors[layer]
        proj = dot32(low, mat_qkv)
        queries = (proj[:, :D] + bias[0]).astype(jnp.bfloat16)
        kv = jnp.concatenate([proj[:, D : 2 * D], proj[:, 2 * D :] + bias[1]], axis=1).astype(jnp.bfloat16)
        kv_all, part = gather_rows(kv, queries, seq_count, depth, 2 + layer)
        mixed, part_mixed = attend(picks, first, queries, kv_all, shut, part)
        mixed = collect(part_mixed, mixed, seq_count, 4 + layer)
        resid_one = resid + dot32(mixed, mat_out) + bias[2]
        middle, normed_one, inv_one = norm_rows(resid_one, bias[6], bias[3])
        middle_low = middle.astype(jnp.bfloat16)
        hidden = dot32(middle_low, mat_up) + hidden_shifts[layer]
        active = jax.nn.gelu(hidden, approximate=False).astype(jnp.bfloat16)
        resid_two = middle + dot32(active, mat_down) + bias[4]
        result, normed_two, inv_two = norm_rows(resid_two, bias[7], bias[5])
        saved.append(
            (low, queries, kv_all, part, mixed, normed_one, inv_one, middle_low, hidden, active, normed_two, inv_two)
        )
        resid = result
        low = resid.astype(jnp.bfloat16)

    grad = d_out[0].astype(jnp.float32)
    owned = [None] * L
    is_shared = (own_index == 0) & (jnp.arange(rows) < SHARED)[:, None]
    for layer in reversed(range(L)):
        (low_in, queries, kv_all, part, mixed, normed_one, inv_one, middle_low, hidden, active, normed_two, inv_two) = saved[layer]
        mat_qkv, mat_out, mat_up, mat_down = weights[layer]
        bias = vectors[layer]
        gain_two_grad = jnp.sum(grad * normed_two, axis=0)
        shift_two_grad = jnp.sum(grad, axis=0)
        grad_two = norm_back(grad, normed_two, inv_two, bias[7])
        grad_two_low = grad_two.astype(jnp.bfloat16)
        down_grad = product_tn(active, grad_two_low)
        active_grad = product_nt(grad_two_low, mat_down)
        hidden_grad = jax.vjp(partial(jax.nn.gelu, approximate=False), hidden)[1](active_grad)[0]
        hidden_grad_low = hidden_grad.astype(jnp.bfloat16)
        up_grad = product_tn(middle_low, hidden_grad_low)
        middle_grad = grad_two + product_nt(hidden_grad_low, mat_up)
        gain_one_grad = jnp.sum(middle_grad * normed_one, axis=0)
        shift_one_grad = jnp.sum(middle_grad, axis=0)
        grad_one = norm_back(middle_grad, normed_one, inv_one, bias[6])
        grad_one_low = grad_one.astype(jnp.bfloat16)
        out_grad = product_tn(mixed, grad_one_low)
        cot = product_nt(grad_one_low, mat_out).astype(jnp.bfloat16)
        part_cot = spread(cot, seq_count, depth, 6 + layer)
        part_cot = jnp.where(own_index < HELPERS, part_cot, 0)
        cot = jnp.where(is_shared, 0, cot)
        dq, dk, dv, part_dq = attend_back(picks, first, queries, kv_all, shut, cot, part, part_cot)
        dq = collect(part_dq, dq, seq_count, 8 + layer)
        dkv = reduce_rows(dk, dv, seq_count, depth, 10 + layer)
        proj_grad = jnp.concatenate([dq, dkv.astype(jnp.bfloat16)], axis=1)
        qkv_grad = product_tn(low_in, proj_grad)
        small_rows = jnp.stack(
            [
                jnp.sum(dq.astype(jnp.float32), axis=0),
                jnp.sum(dkv[:, D:], axis=0),
                jnp.sum(grad_one, axis=0),
                shift_one_grad,
                jnp.sum(grad_two, axis=0),
                shift_two_grad,
                gain_one_grad,
                gain_two_grad,
            ]
        )
        small_rows = jnp.moveaxis(small_rows.reshape(8, n_dev, piece), 1, 0)
        hidden_rows = jnp.sum(hidden_grad, axis=0).reshape(n_dev, 8, -1)
        small_rows = jnp.concatenate([small_rows, hidden_rows], axis=2)
        small_rows = jnp.pad(small_rows, ((0, 0), (0, 0), (0, 128 - small_rows.shape[2])))
        owned[layer] = own_layer(
            [qkv_grad, out_grad, up_grad, down_grad, small_rows], seq_count, depth, 12 + layer
        )
        grad = grad_one + product_nt(proj_grad, mat_qkv)
    stacked = [jnp.stack([owned[layer][i] for layer in range(L)]) for i in range(5)]
    narrow = stacked[4]
    return (
        low[None],
        grad[None],
        stacked[0],
        stacked[1],
        stacked[2],
        stacked[3],
        narrow[:, 6:8, :piece],
        narrow[:, 0:6, :piece],
        narrow[:, :, piece : piece + up_bias.shape[1] // 8].reshape(L, -1),
    )


def solution(mesh):
    placed = (
        P("batch", "seq", None),
        P("batch", "seq"),
        P("batch", "seq", None, None),
        P(None, ("seq", "batch"), None),
        P(None, ("seq", "batch"), None),
        P(None, ("seq", "batch"), None),
        P(None, ("seq", "batch"), None),
        P(None, None, ("seq", "batch")),
        P(None, None, ("seq", "batch")),
        P(None, ("seq", "batch")),
        P("batch", "seq", None),
    )
    return jax.shard_map(
        on_device,
        mesh=mesh,
        in_specs=placed,
        out_specs=(
            P("batch", "seq", None),
            P("batch", "seq", None),
            P(None, ("seq", "batch"), None),
            P(None, ("seq", "batch"), None),
            P(None, ("seq", "batch"), None),
            P(None, ("seq", "batch"), None),
            P(None, None, ("seq", "batch")),
            P(None, None, ("seq", "batch")),
            P(None, ("seq", "batch")),
        ),
        check_vma=False,
    )
```

```python
import itertools
from functools import partial
from types import SimpleNamespace

import jax
import jax.numpy as jnp
from jax import lax
from jax.experimental import pallas as pl
from jax.experimental.pallas import tpu as pltpu
from jax.sharding import PartitionSpec as P

MESH = pl.DeviceIdType.MESH
SEQ, BATCH = "seq", "batch"


HEAD_PLACES = SimpleNamespace(
    arrivals=(
        (13, 14, 32, 23, 53, 40, 88, 31, 59, 61, 74, 67, 81, 87, 107),
        (11, 12, 29),
        (21, 15, 41, 25, 42, 50, 90, 34, 58, 64, 79, 68, 101, 92, 105),
        (18, 33, 46, 17, 43, 66, 96, 45, 97, 65, 104, 71, 106, 89, 108),
        (30, 20, 49, 10, 62, 63, 115, 48, 77, 69, 111, 82, 120, 110, 125),
        (27, 24, 57, 22, 60, 52, 94, 39, 78, 80, 100, 76, 91, 103, 114),
        (38, 26, 51, 35, 70, 73, 95, 37, 84, 85, 117, 93, 123, 109, 128),
        (16, 28, 83, 19, 47, 99, 118, 4, 36, 75, 126, 72, 122, 134, 131),
        (55, 54, 127, 56, 86, 132, 142, 44, 98, 137, 140, 102, 135, 143, 145),
        (129, 124, 146),
        (133, 130, 141),
        (138, 136, 147),
        (144, 139, 148),
    ),
    project=112,
)
TAIL_PLACES = SimpleNamespace(
    arrivals=(
        (9, 8, 48, 19, 39, 31, 73, 26, 62, 57, 75, 65, 86, 83, 93),
        (36, 5, 32, 6, 17, 38, 68, 13, 67, 50, 72, 56, 69, 70, 87),
        (28, 10, 61, 11, 47, 46, 80, 20, 60, 64, 82, 74, 91, 89, 110),
        (34, 23, 44, 24, 49, 51, 78, 43, 81, 88, 107, 77, 92, 99, 104),
        (33, 29, 66, 30, 59, 71, 95, 45, 76, 79, 102, 84, 119, 98, 114),
        (53, 55, 90, 35, 52, 96, 103, 40, 58, 106, 115, 63, 112, 123, 122),
        (37, 105, 120, 42, 85, 117, 129, 54, 94, 121, 131, 97, 130, 133, 135),
        (116, 113, 132),
        (118, 126, 134),
        (125, 124, 136),
        (127, 128, 137),
    ),
    steps=(3, 4, 12, 15, 16, 21, 22, 27, 41),
    project=100,
)
ROWS_PLACES = SimpleNamespace(
    rows=(
        (0, 3, 4, 17, 53),
        (1, 7, 9, 25, 45),
        (11, 23, 21, 43, 52),
        (6, 13, 30, 38, 54),
    ),
    weights=(
        (5, 10, 16, 14, 15, 8, 19, 18, 12, 24, 20, 34, 31, 22, 32, 46, 55),
        (27, 28, 29, 37, 33, 39, 36, 41, 35, 47, 42, 44, 40, 49, 50, 48, 56),
    ),
    grads=(2, 26),
    collect=51,
)
BELOW_PLACES = SimpleNamespace(
    weights=(
        (9, 12, 11, 14, 47, 36, 45, 27, 66, 48, 20, 52, 70, 54, 61, 73, 77),
        (10, 37, 49, 24, 58, 26, 33, 69, 68, 30, 32, 64, 72, 40, 63, 75, 78),
        (6, 22, 18, 23, 31, 21, 39, 29, 42, 38, 43, 46, 60, 53, 62, 74, 76),
        (1, 4, 3, 2, 15, 13, 7, 19, 41, 17, 44, 28, 59, 16, 55, 67, 71),
    ),
    grads=(8, 5, 0),
    steps=(25, 34, 35, 50, 51, 56, 57, 65),
)
LAST_PLACES = SimpleNamespace(
    weights=(
        (22, 31, 32, 33, 61, 36, 57, 65, 74, 41, 63, 67, 79, 58, 72, 84, 88),
        (21, 43, 45, 47, 62, 46, 48, 75, 77, 51, 64, 78, 80, 56, 83, 81, 87),
        (11, 29, 34, 40, 49, 50, 44, 37, 52, 53, 55, 60, 68, 66, 70, 82, 86),
        (9, 13, 15, 18, 30, 35, 23, 42, 54, 25, 27, 59, 71, 39, 69, 76, 85),
        (1, 2, 5, 12, 14, 3, 4, 17, 24, 6, 7, 16, 28, 8, 19, 26, 38),
    ),
    grads=(20, 10, 0),
    steps=(73,),
)


def place():
    s = lax.axis_index(SEQ)
    return {"y": s // 4, "x": (s // 2) % 2, "c": s % 2, "z": lax.axis_index(BATCH)}


def device_of(p):
    return ((p["y"] * 2 + p["x"]) * 2 + p["c"], p["z"])


def flipped(p, axis):
    return {**p, axis: 1 - p[axis]}


def at_depth(p, z):
    return {**p, "z": z}


def number_in(depth):
    return lambda p: device_of(p)[0] * depth + p["z"]


def number_in_sequence(p):
    return device_of(p)[0]


def when(cond, action):
    if cond is None:
        action()
    else:
        pl.when(cond)(action)


def ranked(z, rank, depth):
    near = [sorted(range(depth), key=lambda q: (abs(q - k), q))[rank] for k in range(depth)]
    return sum(jnp.where(z == k, near[k], 0) for k in range(depth))


def offsets(order, depth):
    return list(itertools.product(*[range(depth if a == "z" else 2) for a in order]))


def target_of(order, offset, depth, me):
    p = me
    for axis, d in zip(order, offset):
        if d:
            p = at_depth(p, ranked(me["z"], d, depth)) if axis == "z" else flipped(p, axis)
    return p


def last_move(offset):
    return max([-1] + [i for i, d in enumerate(offset) if d])


def greet(axes, depth, spread=False, collect=False):
    me = place()
    barrier = pltpu.get_barrier_semaphore()

    def signal(device):
        pl.semaphore_signal(barrier, inc=1, device_id=device, device_id_type=MESH)

    count = 0
    for axis in axes + ("c",):
        if axis == "z":
            for step in (1, -1):
                peer = at_depth(me, me["z"] + step)
                cond = (peer["z"] >= 0) & (peer["z"] < depth)
                when(cond, lambda peer=peer: signal(device_of(peer)))
                count = count + cond.astype(jnp.int32)
        else:
            signal(device_of(flipped(me, axis)))
            count = count + 1
    if spread or collect:
        seq, z = lax.axis_index(SEQ), lax.axis_index(BATCH)
        if spread:
            when(seq != 0, lambda: signal((0, z)))
            count = count + jnp.where(seq == 0, HELPERS - 1, 0)
        if collect:

            @pl.when(seq == 0)
            def _():
                for j in range(1, HELPERS):
                    signal((j, z))

            count = count + jnp.where(seq == 0, 0, 1)
    pl.semaphore_wait(barrier, count)


class Gather:
    def __init__(self, source, target, number, order, depth, send, recv, send_at):
        self.source, self.target, self.number = source, target, number
        self.order, self.depth, self.send, self.recv = order, depth, send, recv
        self.send_at = send_at
        self.me = place()
        self.sent = []

    @staticmethod
    def sends(order, depth):
        return sum(len(order) + 2 - last_move(t) for t in offsets(order, depth))

    def onward(self, offset):
        last = last_move(offset)
        z = self.me["z"]
        moves = []
        if last >= 0 and self.order[last] == "z":
            source = ranked(z, offset[last], self.depth)
            peer = jnp.where(source < z, z + 1, z - 1)
            moves.append((at_depth(self.me, peer), (peer >= 0) & (peer < self.depth)))
        for axis in self.order[last + 1 :]:
            if axis == "z":
                moves.append((at_depth(self.me, z + 1), z + 1 < self.depth))
                moves.append((at_depth(self.me, z - 1), z > 0))
            else:
                moves.append((flipped(self.me, axis), None))
        moves.append((flipped(self.me, "c"), None))
        return moves

    def arrival(self, p):
        ref = self.target(p)
        return pltpu.make_async_remote_copy(
            src_ref=ref, dst_ref=ref, send_sem=self.send.at[0], recv_sem=self.recv.at[self.number(p)],
            device_id=device_of(self.me), device_id_type=MESH,
        )

    def handle(self, offset):
        p = target_of(self.order, offset, self.depth, self.me)
        own = not any(offset)
        if not own:
            self.arrival(p).wait_recv()
        for peer, cond in self.onward(offset):
            copy = pltpu.make_async_remote_copy(
                src_ref=self.source if own else self.target(p), dst_ref=self.target(p),
                send_sem=self.send.at[self.send_at], recv_sem=self.recv.at[self.number(p)],
                device_id=device_of(peer), device_id_type=MESH,
            )
            when(cond, copy.start)
            self.sent.append((cond, self.send_at))
            self.send_at += 1

    def begin(self):
        self.handle((0,) * len(self.order))

    def events(self, places):
        marks = [t for t in offsets(self.order, self.depth) if any(t)]
        return [(at, partial(self.handle, t)) for at, t in zip(places, marks, strict=True)]

    def siblings(self):
        for t in offsets(self.order, self.depth):
            self.arrival(flipped(target_of(self.order, t, self.depth, self.me), "c")).wait_recv()

    def drain(self):
        for cond, slot in self.sent:
            copy = pltpu.make_async_remote_copy(
                src_ref=self.source, dst_ref=self.target(self.me), send_sem=self.send.at[slot],
                recv_sem=self.recv.at[self.number(self.me)], device_id=device_of(self.me), device_id_type=MESH,
            )
            when(cond, copy.wait_send)


def end_gathers(jobs):
    for job in jobs:
        job.siblings()
    for job in jobs:
        job.drain()


class Reduce:
    def __init__(self, partial_of, inbox, order, depth, send, recv):
        self.partial_of, self.inbox = partial_of, inbox
        self.order, self.depth, self.send, self.recv = order, depth, send, recv
        self.me = place()
        self.base, _ = self.slots(order, depth)
        self.marks = sorted(offsets(order, depth), key=lambda t: (-sum(t), t))
        self.sent = []

    @staticmethod
    def split(order, offset):
        if "z" not in order:
            return offset, 0
        i = order.index("z")
        return offset[:i] + (0,) + offset[i + 1 :], offset[i]

    @staticmethod
    def slots(order, depth):
        base, count = {}, 0
        deep = depth if "z" in order else 1
        for t in offsets(order, depth):
            key, rank = Reduce.split(order, t)
            if rank:
                continue
            last = last_move(key)
            for i, axis in enumerate(order):
                if i <= last:
                    continue
                base[(key, axis)] = count
                if axis == "z":
                    count += deep + 1
                elif "z" in order and i > order.index("z"):
                    count += deep
                else:
                    count += 1
            base[(key, "c")] = count
            count += deep
        return base, count

    def where_(self, key, axis, z):
        deep = "z" in self.order and (axis == "c" or self.order.index(axis) > self.order.index("z"))
        return self.base[(key, axis)] + (z if deep else 0)

    def copy(self, source, edge, slot, peer):
        return pltpu.make_async_remote_copy(
            src_ref=source, dst_ref=self.inbox.at[edge], send_sem=self.send.at[slot],
            recv_sem=self.recv.at[edge], device_id=device_of(peer), device_id_type=MESH,
        )

    def start(self, offset):
        p = target_of(self.order, offset, self.depth, self.me)
        key, _ = self.split(self.order, offset)
        slot = self.marks.index(offset)
        edge = self.where_(key, "c", p["z"])
        peer = flipped(self.me, "c")
        self.copy(self.partial_of(flipped(p, "c")), edge, slot, peer).start()
        self.sent.append(slot)

    def kids(self, offset, p):
        key, rank = self.split(self.order, offset)
        last, z = last_move(offset), self.me["z"]
        found = [(self.where_(key, "c", p["z"]), None)]
        for axis in self.order[last + 1 :]:
            if axis == "z":
                at = self.base[(key, "z")]
                found += [(at + z, z > 0), (at + self.depth, z + 1 < self.depth)]
            else:
                found.append((self.where_(key, axis, p["z"]), None))
        if last >= 0 and self.order[last] == "z":
            far = jnp.where(p["z"] < z, z + 1, z - 1)
            found.append((self.base[(key, "z")] + p["z"], (far >= 0) & (far < self.depth)))
        return found

    def upward(self, offset, p):
        key, rank = self.split(self.order, offset)
        k, z = last_move(offset), self.me["z"]
        axis = self.order[k]
        if axis == "z":
            edge = self.base[(key, "z")] + jnp.where(p["z"] == z - 1, self.depth, p["z"])
            return edge, at_depth(self.me, jnp.where(p["z"] < z, z - 1, z + 1))
        parent = key[:k] + (0,) + key[k + 1 :]
        return self.where_(parent, axis, p["z"]), flipped(self.me, axis)

    def handle(self, offset, add, finish):
        p = target_of(self.order, offset, self.depth, self.me)
        kids = self.kids(offset, p)
        slot = len(self.marks) + self.marks.index(offset)
        for edge, cond in kids:
            when(cond, self.copy(self.inbox.at[edge], edge, slot, self.me).wait_recv)
        parts = [(self.inbox.at[edge], cond) for edge, cond in kids]
        if any(offset):
            into = parts[0][0]
            add(self.partial_of(p), parts, into)
            edge, peer = self.upward(offset, p)
            self.copy(into, edge, slot, peer).start()
            self.sent.append(slot)
        else:
            finish(self.partial_of(p), parts)

    def drain(self):
        for slot in self.sent:
            self.copy(self.inbox.at[0], 0, slot, self.me).wait_send()


D = 768
H = 12
DH = 64
BLK = 64
R = 3
GLOB = 2
L = 2
PAIRS = H // 2
WIDE = 2 * DH
SHARED = GLOB * BLK
SHARE = 16
HELPERS = SHARED // SHARE
VMEM_LIMIT = 60 * 1024 * 1024

layer_eps = 1e-06
masked_score = -1e30

Z_Y_X, Z_X_Y, X_Y_Z, Y_X_Z = ("z", "y", "x"), ("z", "x", "y"), ("x", "y", "z"), ("y", "x", "z")
Y_X, X_Y = ("y", "x"), ("x", "y")
ANYWHERE = pl.BlockSpec(memory_space=pl.ANY)
IN_VMEM = pl.BlockSpec(memory_space=pltpu.VMEM)


def dma(*shape):
    return pltpu.SemaphoreType.DMA(shape)


def product(a, b):
    return lax.dot_general(a, b, (((1,), (0,)), ((), ())), preferred_element_type=jnp.float32)


def product_nt(a, b):
    return lax.dot_general(a, b, (((1,), (1,)), ((), ())), preferred_element_type=jnp.float32)


def product_tn(a, b):
    return lax.dot_general(a, b, (((0,), (0,)), ((), ())), preferred_element_type=jnp.float32)


def split_heads(pair_rows):
    low_lanes = lax.broadcasted_iota(jnp.int32, (1, WIDE), 1) < DH
    zero = jnp.zeros_like(pair_rows)
    return jnp.concatenate([jnp.where(low_lanes, pair_rows, zero), jnp.where(low_lanes, zero, pair_rows)], axis=0)


def join_heads(stacked):
    low_lanes = lax.broadcasted_iota(jnp.int32, (1, WIDE), 1) < DH
    rows = stacked.shape[0] // 2
    return jnp.where(low_lanes, stacked[:rows], stacked[rows:])


def row_of(block):
    return pl.multiple_of(block * BLK, BLK)


def block_of(ref, block):
    held = ref.shape[2] // BLK
    return ref[block // held, 0, pl.ds(row_of(block % held), BLK)]


def whole(ref):
    return ref[...].reshape(-1, WIDE)


def window_blocks(first, block, blocks_all):
    return [(first + block + j - 1 + blocks_all) % blocks_all for j in range(3)]


def drawn_blocks(picks_ref, pair, block, r):
    return [picks_ref[(block * H + 2 * pair + side) * R + r] for side in range(2)]


def bring(picks_ref, first, pair, pairs, blocks_here):
    low_lanes = lax.broadcasted_iota(jnp.int32, (1, WIDE), 1) < DH
    for block in range(blocks_here):
        for source, target in pairs:
            blocks_all = source.shape[0] * source.shape[2] // BLK
            for j, one in enumerate(window_blocks(first, block, blocks_all)):
                target[block, j * BLK : (j + 1) * BLK] = block_of(source, one)
            for r in range(R):
                one, two = drawn_blocks(picks_ref, pair, block, r)
                target[block, (3 + r) * BLK : (4 + r) * BLK] = jnp.where(
                    low_lanes, block_of(source, one), block_of(source, two)
                )


def with_shared(ref, near):
    return jnp.concatenate([ref[0, 0, 0:SHARED], near], axis=0)


def key_scores(keys, q_heads, shut):
    scores = product_nt(keys, q_heads)
    end = SHARED + 3 * BLK
    return jnp.concatenate([scores[:SHARED], scores[SHARED:end] + shut, scores[end:]], axis=0)


def soft(scores):
    top = jnp.max(scores, axis=0, keepdims=True)
    weight = jnp.exp(scores - top)
    total = jnp.sum(weight, axis=0, keepdims=True)
    return weight * (1.0 / total), top + jnp.log(total)


def attend_kernel(
    picks_ref, first_ref, q_ref, k_ref, v_ref, shut_ref, part_ref, o_ref, po_ref, log_ref, plog_ref, near_k, near_v
):
    pair = pl.program_id(0)
    blocks_here = q_ref.shape[0] // BLK
    bring(picks_ref, first_ref[0], pair, [(k_ref, near_k), (v_ref, near_v)], blocks_here)
    scale = jnp.bfloat16(DH ** (-0.5))
    weight, logs = soft(product_nt(whole(k_ref), split_heads(part_ref[...] * scale)))
    mixed = product_tn(weight.astype(jnp.bfloat16), whole(v_ref))
    po_ref[...] = join_heads(mixed).astype(po_ref.dtype)
    plog_ref[0] = logs
    for block in range(blocks_here):
        here = slice(block * BLK, (block + 1) * BLK)
        q_heads = split_heads(q_ref[here] * scale)
        weight, logs = soft(key_scores(with_shared(k_ref, near_k[block]), q_heads, shut_ref[block]))
        mixed = product_tn(weight.astype(jnp.bfloat16), with_shared(v_ref, near_v[block]))
        o_ref[here] = join_heads(mixed).astype(o_ref.dtype)
        log_ref[0, block : block + 1] = logs


def near_rows(rows, dtype):
    return pltpu.VMEM((rows // BLK, 6 * BLK, WIDE), dtype)


def columns(rows, shift=0):
    return pl.BlockSpec((rows, WIDE), lambda p, *_: (0, p + shift))


def of_all(kv, shift=0):
    return pl.BlockSpec((kv.shape[0], 1, kv.shape[2], WIDE), lambda p, *_: (0, p + shift, 0, 0))


def by_pair(rows, lanes):
    return pl.BlockSpec((1, rows, lanes), lambda p, *_: (p, 0, 0))


def attend(picks, first, queries, kv, shut, part):
    rows = queries.shape[0]
    blocks = rows // BLK
    return pl.pallas_call(
        attend_kernel,
        grid_spec=pltpu.PrefetchScalarGridSpec(
            num_scalar_prefetch=2,
            grid=(PAIRS,),
            in_specs=[
                columns(rows), of_all(kv), of_all(kv, PAIRS),
                pl.BlockSpec(shut.shape, lambda p, *_: (0, 0, 0)), columns(SHARE),
            ],
            out_specs=[columns(rows), columns(SHARE), by_pair(blocks, WIDE), by_pair(1, 2 * SHARE)],
            scratch_shapes=[near_rows(rows, jnp.bfloat16)] * 2,
        ),
        out_shape=[
            jax.ShapeDtypeStruct((rows, D), jnp.bfloat16),
            jax.ShapeDtypeStruct((SHARE, D), jnp.bfloat16),
            jax.ShapeDtypeStruct((PAIRS, blocks, WIDE), jnp.float32),
            jax.ShapeDtypeStruct((PAIRS, 1, 2 * SHARE), jnp.float32),
        ],
        compiler_params=pltpu.CompilerParams(vmem_limit_bytes=VMEM_LIMIT),
        name="attend",
    )(picks, first, queries, kv, kv, shut, part)


def score_grads(weight, values, cot_heads):
    grads = product_nt(values, cot_heads)
    mean = jnp.sum(weight * grads, axis=0, keepdims=True)
    return (weight * (grads - mean)).astype(jnp.bfloat16)


def attend_back_kernel(
    picks_ref, first_ref, q_ref, k_ref, v_ref, shut_ref, do_ref, part_ref, pdo_ref, log_ref, plog_ref,
    dq_ref, dk_ref, dv_ref, pdq_ref, sum_k, sum_v, near_k, near_v, grad_k, grad_v,
):
    pair = pl.program_id(0)
    first = first_ref[0]
    blocks_here, blocks_all = q_ref.shape[0] // BLK, sum_k.shape[0] // BLK
    bring(picks_ref, first, pair, [(k_ref, near_k), (v_ref, near_v)], blocks_here)
    low_lanes = lax.broadcasted_iota(jnp.int32, (1, WIDE), 1) < DH
    step = DH ** (-0.5)
    scale = jnp.bfloat16(step)
    part, cot = split_heads(part_ref[...] * scale), split_heads(pdo_ref[...])
    weight = jnp.exp(product_nt(whole(k_ref), part) - plog_ref[0])
    grads = score_grads(weight, whole(v_ref), cot)
    pdq_ref[...] = (join_heads(product_tn(grads, whole(k_ref))) * step).astype(pdq_ref.dtype)
    sum_k[...] = product(grads, part)
    sum_v[...] = product(weight.astype(jnp.bfloat16), cot)
    shared_k = jnp.zeros((SHARED, WIDE), jnp.float32)
    shared_v = jnp.zeros((SHARED, WIDE), jnp.float32)
    for block in range(blocks_here):
        here = slice(block * BLK, (block + 1) * BLK)
        do = jnp.where(first + block < GLOB, jnp.bfloat16(0), do_ref[here])
        q_heads, do_heads = split_heads(q_ref[here] * scale), split_heads(do)
        keys, values = with_shared(k_ref, near_k[block]), with_shared(v_ref, near_v[block])
        weight = jnp.exp(key_scores(keys, q_heads, shut_ref[block]) - log_ref[0, block : block + 1])
        grads = score_grads(weight, values, do_heads)
        dq_ref[here] = (join_heads(product_tn(grads, keys)) * step).astype(dq_ref.dtype)
        key_grad = product(grads, q_heads)
        value_grad = product(weight.astype(jnp.bfloat16), do_heads)
        shared_k = shared_k + key_grad[:SHARED]
        shared_v = shared_v + value_grad[:SHARED]
        grad_k[block] = key_grad[SHARED:]
        grad_v[block] = value_grad[SHARED:]
    sum_k[0:SHARED] += shared_k
    sum_v[0:SHARED] += shared_v
    for block in range(blocks_here):
        for grad, total in ((grad_k, sum_k), (grad_v, sum_v)):
            for j, one in enumerate(window_blocks(first, block, blocks_all)):
                total[pl.ds(row_of(one), BLK)] += grad[block, j * BLK : (j + 1) * BLK]
            for r in range(R):
                tile = grad[block, (3 + r) * BLK : (4 + r) * BLK]
                one, two = drawn_blocks(picks_ref, pair, block, r)
                total[pl.ds(row_of(one), BLK)] += jnp.where(low_lanes, tile, 0.0)
                total[pl.ds(row_of(two), BLK)] += jnp.where(low_lanes, 0.0, tile)
    dk_ref[...] = sum_k[...].astype(dk_ref.dtype).reshape(dk_ref.shape)
    dv_ref[...] = sum_v[...].astype(dv_ref.dtype).reshape(dv_ref.shape)


def attend_back(picks, first, queries, kv, shut, cot, part, part_cot, logs, part_logs):
    rows, grads = queries.shape[0], (kv.shape[0], PAIRS) + kv.shape[2:]
    length = kv.shape[0] * kv.shape[2]
    return pl.pallas_call(
        attend_back_kernel,
        grid_spec=pltpu.PrefetchScalarGridSpec(
            num_scalar_prefetch=2,
            grid=(PAIRS,),
            in_specs=[
                columns(rows), of_all(kv), of_all(kv, PAIRS),
                pl.BlockSpec(shut.shape, lambda p, *_: (0, 0, 0)), columns(rows), columns(SHARE), columns(SHARE),
                by_pair(rows // BLK, WIDE), by_pair(1, 2 * SHARE),
            ],
            out_specs=[columns(rows), of_all(kv), of_all(kv), columns(SHARE)],
            scratch_shapes=[pltpu.VMEM((length, WIDE), jnp.float32)] * 2
            + [near_rows(rows, jnp.bfloat16)] * 2
            + [near_rows(rows, jnp.float32)] * 2,
        ),
        out_shape=[
            jax.ShapeDtypeStruct((rows, D), jnp.bfloat16),
            jax.ShapeDtypeStruct(grads, jnp.bfloat16),
            jax.ShapeDtypeStruct(grads, jnp.bfloat16),
            jax.ShapeDtypeStruct((SHARE, D), jnp.bfloat16),
        ],
        compiler_params=pltpu.CompilerParams(vmem_limit_bytes=VMEM_LIMIT),
        name="attend_back",
    )(picks, first, queries, kv, kv, shut, cot, part, part_cot, logs, part_logs)


def call(body, name, cid, ins, outs, scratch):
    names = list(ins) + list(outs) + list(scratch)
    got = pl.pallas_call(
        lambda *refs: body(SimpleNamespace(**dict(zip(names, refs)))),
        out_shape=[jax.ShapeDtypeStruct(shape, dtype) for shape, dtype, _ in outs.values()],
        in_specs=[where for _, where in ins.values()],
        out_specs=[where for _, _, where in outs.values()],
        scratch_shapes=list(scratch.values()),
        compiler_params=pltpu.CompilerParams(
            collective_id=cid, has_side_effects=cid is not None, vmem_limit_bytes=VMEM_LIMIT
        ),
        name=name,
    )(*[array for array, _ in ins.values()])
    return SimpleNamespace(**dict(zip(outs, got)))


def over(count, act):
    def step(i, carry):
        act(i)
        return carry

    lax.fori_loop(0, count, step, 0)


def span(i, size, first=0):
    return pl.ds(pl.multiple_of(first + i * size, size), size)


def run_in_order(timed):
    for _, act in sorted(timed, key=lambda pair: pair[0]):
        act()


def layer_pieces(rows_in, rows_down, first):
    half, wide = rows_down // 2, 3 * D // 2
    return [
        (first, 0, rows_in, 0, wide, Z_Y_X),
        (first, 0, rows_in, wide, wide, Z_X_Y),
        (first + 1, 0, rows_in, 0, D, Z_X_Y),
        (first + 2, 0, rows_in, 0, 2 * D, Z_Y_X),
        (first + 2, 0, rows_in, 2 * D, 2 * D, Z_X_Y),
        (first + 3, 0, half, 0, D, X_Y_Z),
        (first + 3, half, half, 0, D, Y_X_Z),
    ]


class Gathering:
    def __init__(self, arrays, pieces, seq_count, depth, near):
        self.near = near
        self.arrays, self.pieces, self.depth, self.n_dev = arrays, pieces, depth, seq_count * depth
        flat_only = {which for which, *_, order in pieces if "z" not in order}
        self.counts = [seq_count if i in flat_only else self.n_dev for i in range(len(arrays))]

    def ins(self):
        return {"slab%d" % i: (a, ANYWHERE) for i, a in enumerate(self.arrays)}

    def outs(self):
        return {
            "every%d" % i: ((n,) + a.shape, a.dtype, IN_VMEM if i in self.near else ANYWHERE)
            for i, (n, a) in enumerate(zip(self.counts, self.arrays))
        }

    def scratch(self):
        total = sum(Gather.sends(order, self.depth) for *_, order in self.pieces)
        return {
            "g_send": dma(total),
            "g_recv": dma(len(self.pieces), self.n_dev),
            "g_local": dma(len(self.arrays)),
        }

    def number(self, i):
        return number_in(self.depth) if self.counts[i] == self.n_dev else number_in_sequence

    def begin(self, refs):
        slabs = [getattr(refs, "slab%d" % i) for i in range(len(self.arrays))]
        every = [getattr(refs, "every%d" % i) for i in range(len(self.arrays))]
        self.jobs, at = [], 0
        for k, (which, row, rows, column, columns_, order) in enumerate(self.pieces):
            window = (pl.ds(row, rows), pl.ds(column, columns_))
            number = self.number(which)
            self.jobs.append(
                Gather(
                    slabs[which].at[window],
                    lambda p, which=which, window=window, number=number: every[which].at[(number(p),) + window],
                    number, order, self.depth, refs.g_send, refs.g_recv.at[k], at,
                )
            )
            at += Gather.sends(order, self.depth)
        for job in self.jobs:
            job.begin()
        me = place()
        self.own = [
            pltpu.make_async_copy(slab, all_.at[self.number(i)(me)], refs.g_local.at[i])
            for i, (slab, all_) in enumerate(zip(slabs, every))
        ]
        for copy in self.own:
            copy.start()

    def hurry(self, refs, arrays):
        for (which, *_), job in zip(self.pieces, self.jobs):
            if which in arrays:
                job.siblings()
        for i in arrays:
            self.own[i].wait()
        self.early = arrays

    def end(self):
        for (which, *_), job in zip(self.pieces, self.jobs):
            if which not in self.early:
                job.siblings()
        for job in self.jobs:
            job.drain()
        for i, copy in enumerate(self.own):
            if i not in self.early:
                copy.wait()

    def results(self, got):
        return [getattr(got, "every%d" % i) for i in range(len(self.arrays))]


def to_helpers(source, target, send, recv):
    seq, z = lax.axis_index(SEQ), lax.axis_index(BATCH)

    def copy(j):
        return pltpu.make_async_remote_copy(
            src_ref=source.at[pl.ds(j * SHARE, SHARE)], dst_ref=target, send_sem=send.at[j],
            recv_sem=recv, device_id=(j, z), device_id_type=MESH,
        )

    def begin():
        for j in range(1, HELPERS):
            copy(j).start()

    def own():
        pltpu.sync_copy(source.at[pl.ds(0, SHARE)], target)
        for j in range(1, HELPERS):
            copy(j).wait_send()

    def end():
        pl.when(seq == 0)(own)
        pl.when(seq != 0)(lambda: copy(1).wait_recv())

    pl.when(seq == 0)(begin)
    return end


def to_first(source, target, send, recv):
    seq, z = lax.axis_index(SEQ), lax.axis_index(BATCH)

    def copy(j):
        return pltpu.make_async_remote_copy(
            src_ref=source, dst_ref=target.at[pl.ds(j * SHARE, SHARE)], send_sem=send,
            recv_sem=recv.at[j], device_id=(0, z), device_id_type=MESH,
        )

    for j in range(1, HELPERS):
        pl.when(seq == j)(copy(j).start)

    def end():
        def mine():
            pltpu.sync_copy(source, target.at[pl.ds(0, SHARE)])
            for j in range(1, HELPERS):
                copy(j).wait_recv()

        pl.when(seq == 0)(mine)
        pl.when(seq != 0)(lambda: copy(1).wait_send())

    return end


def from_slabs(ref):
    def get(at):
        slabs = ref[:, :, at]
        return slabs.astype(jnp.float32).reshape(-1, slabs.shape[2]).astype(ref.dtype)

    return get


def project(low, w, bias, q, kv):
    def queries(i):
        at = span(i, 256)
        q[:, at] = (product(low[...], w(at)) + bias[0:1, at]).astype(q.dtype)

    def keys(i):
        keep(2 * i, product(low[...], w(span(i, 256, D))))

    def values(i):
        keep(PAIRS + 2 * i, product(low[...], w(span(i, 256, 2 * D))) + bias[1:2, span(i, 256)])

    def keep(pair, acc):
        kv[pair] = acc[:, :WIDE].astype(kv.dtype)
        kv[pair + 1] = acc[:, WIDE:].astype(kv.dtype)

    for act in (keys, values, queries):
        over(D // 256, act)


class Sequence:
    def __init__(self, rows, seq_count, depth, dtype):
        self.rows, self.seq_count, self.depth, self.dtype = rows, seq_count, depth, dtype

    def outs(self):
        return dict(
            q=((self.rows, D), self.dtype, IN_VMEM),
            every=((self.seq_count, 2 * PAIRS, self.rows, WIDE), self.dtype, ANYWHERE),
            part=((SHARE, D), self.dtype, ANYWHERE),
        )

    def scratch(self):
        return dict(
            kv=pltpu.VMEM((2 * PAIRS, self.rows, WIDE), self.dtype), send=dma(4 * Gather.sends(Y_X, self.depth)),
            recv=dma(4, self.seq_count), local=dma(), give=dma(HELPERS), take=dma(),
        )

    def prepare(self, refs):
        count, at = PAIRS // 2, 0
        self.jobs = []
        for i in range(4):
            window = pl.ds(i * count, count)
            self.jobs.append(
                Gather(
                    refs.kv.at[window],
                    lambda p, window=window: refs.every.at[number_in_sequence(p), window],
                    number_in_sequence, (X_Y, Y_X)[i % 2], self.depth, refs.send, refs.recv.at[i], at,
                )
            )
            at += Gather.sends(Y_X, self.depth)

    def begin(self, refs):
        for job in self.jobs:
            job.begin()
        self.finish = to_helpers(refs.q, refs.part, refs.give, refs.take)
        self.own = pltpu.make_async_copy(refs.kv, refs.every.at[number_in_sequence(place())], refs.local)
        self.own.start()

    def end(self):
        end_gathers(self.jobs)
        self.own.wait()
        self.finish()


def project_and_send(refs, gathering, sequence, low, which):
    def act():
        gathering.hurry(refs, [which])
        w = from_slabs(getattr(refs, "every%d" % which))
        project(low, w, refs.bias, refs.q, refs.kv)
        sequence.begin(refs)

    return act


def timed_events(jobs, places):
    return [pair for job, at in zip(jobs, places, strict=True) for pair in job.events(at)]


def first_head(low, small, segs, weights, seq_count, depth, cid):
    rows = low.shape[0]
    pieces = [(0, 0, small.shape[0], 0, 128, Z_Y_X), (1, 0, 8, 0, 128, Y_X)]
    pieces += layer_pieces(small.shape[0], weights[3].shape[0], 2)
    gathering = Gathering([small, segs] + weights, pieces, seq_count, depth, (0, 2))
    sequence = Sequence(rows, seq_count, depth, low.dtype)

    def body(refs):
        greet(("y", "x", "z"), depth, spread=True)
        gathering.begin(refs)
        sequence.prepare(refs)
        refs.bias = refs.vectors.at[0]

        def vectors():
            gathering.hurry(refs, [0])
            table = refs.every0[...].astype(jnp.float32).reshape(D, 128).T
            for layer in range(L):
                refs.vectors[layer, 0:6] = table[6 * layer : 6 * layer + 6]
                refs.vectors[layer, 6:8] = table[6 * L + 2 * layer : 6 * L + 2 * layer + 2]
            refs.table[...] = table[8 * L : 12 * L]

        def project_now():
            project_and_send(refs, gathering, sequence, refs.low, 2)()
            gathering.early = [0, 2]

        at = HEAD_PLACES
        run_in_order(
            timed_events(gathering.jobs + sequence.jobs, at.arrivals) + [(at.project, vectors), (at.project + 0.1, project_now)]
        )
        sequence.end()
        gathering.end()

    got = call(
        body, "first_head", cid,
        {"low": (low, IN_VMEM), **gathering.ins()},
        {
            **dict(vectors=((L, 8, D), jnp.float32, IN_VMEM), table=((4 * L, D), jnp.float32, IN_VMEM)),
            **sequence.outs(), **gathering.outs(),
        },
        {**sequence.scratch(), **gathering.scratch()},
    )
    results = gathering.results(got)
    return got, results[1], results[2:]


def norm_block(resid, gain, shift):
    center = resid - jnp.mean(resid, axis=1, keepdims=True)
    inv_std = lax.rsqrt(jnp.mean(center * center, axis=1, keepdims=True) + layer_eps)
    normed = center * inv_std
    return normed * gain + shift, normed, inv_std


ROW_BLOCK = 64


def tail_steps(refs, w_out, w_up, w_down, waits):
    rows, hidden = refs.resid.shape[0], refs.shifts.shape[1]

    def out():
        waits[0]()

        def act(i):
            at = span(i, 256)
            refs.sum[:, at] = refs.resid[:, at].astype(jnp.float32) + product(refs.mixed[...], w_out[:, at]) + refs.bias[2:3, at]

        over(D // 256, act)

    def norm_one():
        def act(i):
            at = span(i, ROW_BLOCK)
            y, normed, inv = norm_block(refs.sum[at], refs.bias[6:7], refs.bias[3:4])
            refs.n1[at], refs.inv1[at], refs.sum[at] = normed, inv, y
            refs.y_low[at] = y.astype(jnp.bfloat16)

        over(rows // ROW_BLOCK, act)
        waits[1]()

    def up(first, count):
        def act(i):
            at = span(first + i, 256)
            u = product(refs.y_low[...], w_up[:, at]) + refs.shifts[0:1, at]
            share = 0.5 + 0.5 * lax.erf(u * (0.5 ** 0.5))
            refs.a_low[:, at] = (u * share).astype(jnp.bfloat16)
            slope = share + u * jnp.exp(-0.5 * u * u) * ((2.0 * jnp.pi) ** -0.5)
            refs.slope[:, at] = slope.astype(jnp.bfloat16)

        over(count, act)

    def down():
        waits[2]()

        def act(i):
            at = span(i, 256)
            refs.sum[:, at] = refs.sum[:, at] + product(refs.a_low[...], w_down[:, at]) + refs.bias[4:5, at]

        over(D // 256, act)

    def norm_two():
        def act(i):
            at = span(i, ROW_BLOCK)
            z, normed, inv = norm_block(refs.sum[at], refs.bias[7:8], refs.bias[5:6])
            refs.n2[at], refs.inv2[at] = normed, inv
            if hasattr(refs, "z"):
                refs.z[at] = z
            refs.z_low[at] = z.astype(jnp.bfloat16)

        over(rows // ROW_BLOCK, act)

    quarter = hidden // 256 // 4
    return [out, norm_one] + [partial(up, k * quarter, quarter) for k in range(4)] + [down, norm_two]


def tail_ins(mixed, part, resid, vectors, shifts, weights):
    return {
        "generic": (mixed, IN_VMEM), "own_part": (part, ANYWHERE), "resid": (resid, IN_VMEM), "vectors": (vectors, IN_VMEM),
        "shifts": (shifts, IN_VMEM), "w_out": (weights[1], ANYWHERE), "w_up": (weights[2], ANYWHERE), "w_down": (weights[3], ANYWHERE),
    }


def tail_outs(rows, hidden):
    f32, low = jnp.float32, jnp.bfloat16
    return {
        "mixed": ((rows, D), low, IN_VMEM), "n1": ((rows, D), f32, IN_VMEM), "inv1": ((rows, 1), f32, IN_VMEM),
        "y_low": ((rows, D), low, IN_VMEM), "a_low": ((rows, hidden), low, IN_VMEM), "slope": ((rows, hidden), low, IN_VMEM),
        "n2": ((rows, D), f32, IN_VMEM), "inv2": ((rows, 1), f32, IN_VMEM), "z_low": ((rows, D), low, IN_VMEM),
    }


def tail_scratch(rows, hidden):
    low = jnp.bfloat16
    return {
        "sum": pltpu.VMEM((rows, D), jnp.float32), "v_out": pltpu.VMEM((D, D), low),
        "v_up": pltpu.VMEM((D, hidden), low), "v_down": pltpu.VMEM((hidden, D), low),
        "load": dma(3), "t_send": dma(), "t_recv": dma(HELPERS),
    }


def start_loads(refs):
    loads = [
        pltpu.make_async_copy(refs.w_out, refs.v_out, refs.load.at[0]),
        pltpu.make_async_copy(refs.w_up, refs.v_up, refs.load.at[1]),
        pltpu.make_async_copy(refs.w_down, refs.v_down, refs.load.at[2]),
    ]
    for copy in loads:
        copy.start()
    return [copy.wait for copy in loads]


def tail(mixed, part, resid, vectors, shifts, weights, next_weights, seq_count, depth, cid):
    rows, hidden = resid.shape[0], shifts.shape[1]
    pieces = layer_pieces(next_weights[0].shape[0], next_weights[3].shape[0], 0)
    gathering = Gathering(next_weights, pieces, seq_count, depth, (0,))
    sequence = Sequence(rows, seq_count, depth, mixed.dtype)

    def body(refs):
        waits = start_loads(refs)
        refs.mixed[...] = refs.generic[...]
        greet(("y", "x", "z"), depth, spread=True, collect=True)
        finish = to_first(refs.own_part, refs.mixed, refs.t_send, refs.t_recv)
        gathering.begin(refs)
        sequence.prepare(refs)
        refs.bias = refs.vectors.at[0]
        steps = [finish] + tail_steps(refs, refs.v_out, refs.v_up, refs.v_down, waits)

        def project_now():
            refs.bias = refs.vectors.at[1]
            project_and_send(refs, gathering, sequence, refs.z_low, 0)()

        at = TAIL_PLACES
        run_in_order(
            timed_events(gathering.jobs + sequence.jobs, at.arrivals)
            + list(zip(at.steps, steps, strict=True)) + [(at.project, project_now)]
        )
        sequence.end()
        gathering.end()

    outs = tail_outs(rows, hidden)
    outs.update(z=((rows, D), jnp.float32, IN_VMEM))
    got = call(
        body, "tail", cid,
        {**tail_ins(mixed, part, resid, vectors, shifts, weights), **gathering.ins()},
        {**outs, **sequence.outs(), **gathering.outs()},
        {**tail_scratch(rows, hidden), **sequence.scratch(), **gathering.scratch()},
    )
    return got, gathering.results(got)


def folded(block):
    return jnp.sum(block.reshape(-1, 8, block.shape[1]), axis=0)


def norm_block_back(grad, normed, inv_std, gain):
    scaled = grad * gain
    return (
        scaled
        - jnp.mean(scaled, axis=1, keepdims=True)
        - normed * jnp.mean(scaled * normed, axis=1, keepdims=True)
    ) * inv_std


def back_steps(refs, dz, w_down, w_up, w_out, waits):
    rows, hidden = refs.n2.shape[0], refs.slope.shape[1]
    zero = jnp.zeros((8, D), jnp.float32)

    def row(k, total):
        refs.totals[k : k + 1] = jnp.sum(total, axis=0, keepdims=True)

    def norm_two():
        def act(i, sums):
            at = span(i, ROW_BLOCK)
            grad, normed = dz(at), refs.n2[at]
            back = norm_block_back(grad, normed, refs.inv2[at], refs.bias[7:8])
            refs.work[at] = back
            refs.dr2_low[at] = back.astype(jnp.bfloat16)
            return sums[0] + folded(back), sums[1] + folded(grad), sums[2] + folded(grad * normed)

        sums = lax.fori_loop(0, rows // ROW_BLOCK, act, (zero,) * 3)
        row(4, sums[0]), row(5, sums[1]), row(7, sums[2])
        waits[0]()

    def down(first, count):
        def act(i):
            at = span(first + i, 256)
            du = product_nt(refs.dr2_low[...], w_down[at]) * refs.slope[:, at].astype(jnp.float32)
            refs.du_low[:, at] = du.astype(jnp.bfloat16)
            refs.hidden_totals[0:1, at] = jnp.sum(du, axis=0, keepdims=True)

        over(count, act)

    def up():
        waits[1]()

        def act(i):
            at = span(i, 256)
            refs.work[:, at] = refs.work[:, at] + product_nt(refs.du_low[...], w_up[at])

        over(D // 256, act)

    def norm_one():
        def act(i, sums):
            at = span(i, ROW_BLOCK)
            grad, normed = refs.work[at], refs.n1[at]
            back = norm_block_back(grad, normed, refs.inv1[at], refs.bias[6:7])
            refs.dr1[at] = back
            refs.dr1_low[at] = back.astype(jnp.bfloat16)
            return sums[0] + folded(back), sums[1] + folded(grad), sums[2] + folded(grad * normed)

        sums = lax.fori_loop(0, rows // ROW_BLOCK, act, (zero,) * 3)
        row(2, sums[0]), row(3, sums[1]), row(6, sums[2])

    def out():
        waits[2]()

        def act(i):
            at = span(i, 256)
            refs.cot[:, at] = product_nt(refs.dr1_low[...], w_out[at]).astype(jnp.bfloat16)

        over(D // 256, act)

    half = hidden // 256 // 2
    return [norm_two, partial(down, 0, half), partial(down, half, half), up, norm_one, out]


def back_outs(rows, hidden):
    f32, low = jnp.float32, jnp.bfloat16
    return {
        "dr2_low": ((rows, D), low, IN_VMEM), "du_low": ((rows, hidden), low, IN_VMEM), "dr1": ((rows, D), f32, IN_VMEM),
        "dr1_low": ((rows, D), low, IN_VMEM), "cot": ((rows, D), low, IN_VMEM), "totals": ((8, D), f32, IN_VMEM),
        "hidden_totals": ((1, hidden), f32, IN_VMEM), "part_cot": ((SHARE, D), low, ANYWHERE),
    }


def turn(mixed, part, resid, vectors, shifts, weights, d_out, depth, cid):
    rows, hidden = resid.shape[0], shifts.shape[1]

    def body(refs):
        waits = start_loads(refs)
        refs.mixed[...] = refs.generic[...]
        refs.bias = refs.vectors.at[1]
        greet((), depth, spread=True, collect=True)
        to_first(refs.own_part, refs.mixed, refs.t_send, refs.t_recv)()
        for step in tail_steps(refs, refs.v_out, refs.v_up, refs.v_down, waits):
            step()
        done = [lambda: None] * 3
        refs.totals[...] = jnp.zeros_like(refs.totals)
        for step in back_steps(
            refs, lambda at: refs.d_out[at].astype(jnp.float32), refs.v_down, refs.v_up, refs.v_out, done
        ):
            step()
        to_helpers(refs.cot, refs.part_cot, refs.give, refs.take)()

    return call(
        body, "turn", cid,
        {**tail_ins(mixed, part, resid, vectors, shifts, weights), "d_out": (d_out, IN_VMEM)},
        {**tail_outs(rows, hidden), **back_outs(rows, hidden)},
        {
            **tail_scratch(rows, hidden), "work": pltpu.VMEM((rows, D), jnp.float32), "give": dma(HELPERS), "take": dma(),
        },
    )


def chunked(shape):
    rows, columns = shape
    width = columns
    while rows * width > 24 * 1024 and width % 256 == 0:
        width //= 2
    if rows * width > 24 * 1024 and width % 384 == 0:
        width //= 3
    return width, columns // width


def total_of(own, kids, window):
    total = own[window].astype(jnp.float32)
    for ref, cond in kids:
        if cond is None:
            total = total + ref[window].astype(jnp.float32)
        else:
            total = total + lax.cond(
                cond,
                lambda ref=ref: ref[window].astype(jnp.float32),
                lambda total=total: jnp.zeros_like(total),
            )
    return total


def over_chunks(shape, act):
    if len(shape) == 3:
        size = shape[1] // 2

        def part(i, carry):
            act((i // 2, span(i % 2, size)))
            return carry

        lax.fori_loop(0, 2 * shape[0], part, 0)
        return
    width, count = chunked(shape)

    def step(i, carry):
        act((slice(None), pl.ds(pl.multiple_of(i * width, width), width)))
        return carry

    lax.fori_loop(0, count, step, 0)


def add_up(own, kids, into):
    def act(window):
        into[window] = total_of(own, kids, window).astype(into.dtype)

    over_chunks(into.shape, act)


def write_total(target):
    def finish(own, kids):
        def act(window):
            target[window] = total_of(own, kids, window).astype(target.dtype)

        over_chunks(target.shape, act)

    return finish


def weight_grad(left, right, into, first=0):
    share = into.shape[1]
    count = 384 // share

    def act(i):
        across = into.shape[2] // 256
        rows, at = i // across, span(i % across, 256)
        acc = product_tn(left[:, span(rows, 384)], right[:, span(i % across, 256, first)])
        for k in range(count):
            into[rows * count + k, :, at] = acc[k * share : (k + 1) * share].astype(into.dtype)

    over(left.shape[1] // 384 * (into.shape[2] // 256), act)


class Sums:
    def __init__(self, tag, pieces, depth):
        self.tag, self.pieces, self.depth = tag, pieces, depth

    def name(self, what, k):
        return "%s_%s%d" % (self.tag, what, k)

    def scratch(self):
        made = {}
        for k, (_, shape, _, order, dtype) in enumerate(self.pieces):
            edges = Reduce.slots(order, self.depth)[1]
            made[self.name("box", k)] = pltpu.VMEM((edges,) + shape, dtype)
            made[self.name("send", k)] = dma(2 * len(offsets(order, self.depth)))
            made[self.name("recv", k)] = dma(edges)
        return made

    def prepare(self, refs):
        self.jobs = []
        for k, (source, _, target, order, _) in enumerate(self.pieces):
            box, send, recv = (getattr(refs, self.name(what, k)) for what in ("box", "send", "recv"))
            job = Reduce(partial(source, refs), box, order, self.depth, send, recv)
            self.jobs.append((job, target(refs)))

    def start(self, k):
        job, _ = self.jobs[k]
        for t in job.marks:
            job.start(t)

    def timed(self, places):
        timed = []
        for k, ((job, finish), at) in enumerate(zip(self.jobs, places, strict=True)):
            timed.append((at[0], partial(self.start, k)))
            acts = [partial(job.handle, t, add_up, finish) for t in job.marks]
            timed += zip(at[1:], acts, strict=True)
        return timed

    def end(self):
        for job, _ in self.jobs:
            job.drain()


def weight_sums(windows, depth, n_dev, dtypes):
    number = number_in(depth)

    def piece(which, row, rows, column, columns_, order):
        window = (pl.ds(row, rows), pl.ds(column, columns_))
        return (
            lambda refs, p: getattr(refs, "grad%d" % which).at[(number(p),) + window],
            (rows, columns_),
            lambda refs: write_total(getattr(refs, "owned%d" % which).at[window]),
            order,
            dtypes[which],
        )

    return Sums("w", [piece(*w) for w in windows], depth)


def sum_rows(dk, dv, dq, part_dq, held, grads, seq_count, depth, cid):
    rows, hidden, n_dev = dq.shape[0], grads.du_low.shape[1], seq_count * depth
    low, f32 = dk.dtype, jnp.float32
    share, count = D // n_dev, PAIRS // 2

    def piece(i):
        window = pl.ds(i % 2 * count, count)

        def target(refs):
            def finish(own, kids):
                def act(at):
                    lanes = pl.ds(pl.multiple_of((PAIRS + i * count + at[0]) * WIDE, WIDE), WIDE)
                    refs.proj[at[1], lanes] = total_of(own, kids, at).astype(low)

                over_chunks((count, rows, WIDE), act)

            return finish

        return (
            lambda refs, p: (refs.dk, refs.dv)[i // 2].at[number_in_sequence(p), window],
            (count, rows, WIDE),
            target,
            (X_Y, Y_X)[i % 2],
            low,
        )

    by_rows = Sums("r", [piece(i) for i in range(4)], depth)
    windows = [(1, 0, share, 0, D, X_Y_Z), (2, 0, share, 0, hidden // 2, Y_X_Z)]
    by_weights = weight_sums(windows, depth, n_dev, {1: low, 2: low})

    def body(refs):
        refs.proj[:, 0:D] = refs.dq[...]
        greet(("y", "x", "z"), depth, collect=True)
        by_rows.prepare(refs)
        by_weights.prepare(refs)
        ends = [to_first(refs.part, refs.proj.at[:, pl.ds(0, D)], refs.t_send, refs.t_recv)]
        at = ROWS_PLACES
        run_in_order(
            by_rows.timed(at.rows) + by_weights.timed(at.weights)
            + [
                (at.grads[0], lambda: weight_grad(refs.mixed, refs.dr1_low, refs.grad1)),
                (at.grads[1], lambda: weight_grad(refs.y_low, refs.du_low, refs.grad2)),
                (at.collect, ends[0]),
            ]
        )
        by_rows.end()
        by_weights.end()

        def act(i, sums):
            at = span(i, ROW_BLOCK)
            return tuple(
                total + folded(refs.proj[at, pl.ds(first, D)].astype(f32)) for total, first in zip(sums, (0, 2 * D))
            )

        zero = jnp.zeros((8, D), f32)
        sums = lax.fori_loop(0, rows // ROW_BLOCK, act, (zero, zero))
        refs.totals[...] = jnp.zeros_like(refs.totals)
        for k in range(2):
            refs.totals[k : k + 1] = jnp.sum(sums[k], axis=0, keepdims=True)

    return call(
        body, "sum_rows", cid,
        dict(
            dk=(dk, IN_VMEM), dv=(dv, IN_VMEM), dq=(dq, IN_VMEM), part=(part_dq, ANYWHERE),
            mixed=(held.mixed, IN_VMEM), y_low=(held.y_low, IN_VMEM), dr1_low=(grads.dr1_low, IN_VMEM),
            du_low=(grads.du_low, IN_VMEM),
        ),
        dict(
            proj=((rows, 3 * D), low, IN_VMEM), totals=((8, D), f32, IN_VMEM), owned1=((share, D), f32, IN_VMEM),
            owned2=((share, hidden // 2), f32, IN_VMEM),
        ),
        {
            **dict(
                grad1=pltpu.VMEM((n_dev, share, D), low), grad2=pltpu.VMEM((n_dev, share, hidden // 2), low),
                t_send=dma(), t_recv=dma(HELPERS),
            ),
            **by_rows.scratch(), **by_weights.scratch(),
        },
    )


def sum_weights(held, low_in, proj, vectors, w_qkv, small, below, n_dev, depth, cid):
    rows, hidden = proj.shape[0], held.du_low.shape[1]
    low, f32 = jnp.bfloat16, jnp.float32
    share, tall = D // n_dev, hidden // n_dev
    shapes = {0: (share, 3 * D), 2: (share, hidden // 2), 3: (tall, D)}
    cut = tall * 2 // 3
    windows = [
        (3, 0, cut, 0, D, Z_X_Y),
        (3, cut, tall - cut, 0, D, Z_Y_X),
        (2, 0, share, 0, hidden // 2, Y_X_Z),
        (0, 0, share, 0, 3 * D, Z_Y_X),
    ]
    ins = {k: (getattr(held, k), IN_VMEM) for k in ("y_low", "du_low", "a_low", "dr2_low", "dr1")}
    ins = {"up_" + k: v for k, v in ins.items()}
    ins.update(low_in=(low_in, IN_VMEM), proj=(proj, IN_VMEM), w_qkv=(w_qkv, ANYWHERE))
    outs = {"owned%d" % i: (s, f32, IN_VMEM) for i, s in shapes.items()}
    scratch = {"grad%d" % i: pltpu.VMEM((n_dev,) + s, low) for i, s in shapes.items()}
    if small is not None:
        windows.append((4, 0, small.shape[1], 0, small.shape[2], Z_Y_X))
        ins.update(grad4=(small, IN_VMEM))
        outs.update(owned4=(small.shape[1:], f32, IN_VMEM))
    by_weights = weight_sums(windows, depth, n_dev, {0: low, 2: low, 3: low, 4: f32})
    scratch.update(by_weights.scratch())
    scratch.update(load=dma(4), wide=pltpu.VMEM((D, hidden), low))
    if below is not None:
        below_weights, below_held = below
        ins.update({k: (getattr(below_held, k), IN_VMEM) for k in ("n1", "inv1", "n2", "inv2", "slope")})
        ins.update(
            vectors=(vectors, IN_VMEM), w_out=(below_weights[1], ANYWHERE), w_up=(below_weights[2], ANYWHERE),
            w_down=(below_weights[3], ANYWHERE),
        )
        outs.update(back_outs(rows, hidden))
        scratch.update(
            tall=pltpu.VMEM((hidden, D), low), work=pltpu.VMEM((rows, D), f32), give=dma(HELPERS), take=dma()
        )
    outs.update(dx=((rows, D), f32, IN_VMEM))

    def body(refs):
        v_qkv = refs.wide.at[:, pl.ds(0, 3 * D)]
        load_qkv = pltpu.make_async_copy(refs.w_qkv, v_qkv, refs.load.at[0])
        load_qkv.start()
        if below is not None:
            refs.bias = refs.vectors.at[0]
            refs.totals[...] = jnp.zeros_like(refs.totals)
            load_down = pltpu.make_async_copy(refs.w_down, refs.tall, refs.load.at[1])
            load_down.start()
            load_up = pltpu.make_async_copy(refs.w_up, refs.wide, refs.load.at[2])
            load_out = pltpu.make_async_copy(refs.w_out, refs.tall.at[pl.ds(0, D)], refs.load.at[3])
        greet(("y", "x", "z"), depth, spread=below is not None)
        by_weights.prepare(refs)
        def dx():
            load_qkv.wait()

            def act(i):
                at = span(i, 256)
                refs.dx[:, at] = refs.up_dr1[:, at] + product_nt(refs.proj[...], v_qkv[at])

            over(D // 256, act)
            if below is not None:
                load_up.start()

        steps = [dx]
        if below is not None:

            def up_ready():
                load_out.start()
                load_up.wait()

            steps += back_steps(
                refs, lambda at: refs.dx[at], refs.tall, refs.wide, refs.tall, [load_down.wait, up_ready, load_out.wait]
            )
            ends = []
            steps.append(lambda: ends.append(to_helpers(refs.cot, refs.part_cot, refs.give, refs.take)))
        at = LAST_PLACES if below is None else BELOW_PLACES
        run_in_order(
            by_weights.timed(at.weights)
            + [
                (at.grads[0], lambda: weight_grad(refs.up_a_low, refs.up_dr2_low, refs.grad3)),
                (at.grads[1], lambda: weight_grad(refs.up_y_low, refs.up_du_low, refs.grad2, hidden // 2)),
                (at.grads[2], lambda: weight_grad(refs.low_in, refs.proj, refs.grad0)),
            ]
            + list(zip(at.steps, steps, strict=True))
        )
        by_weights.end()
        if below is not None:
            ends[0]()

    return call(body, "sum_weights", cid, ins, outs, scratch)


def norm_rows(resid, gain, shift):
    center = resid - jnp.mean(resid, axis=-1, keepdims=True)
    inv_std = lax.rsqrt(jnp.mean(center * center, axis=-1, keepdims=True) + layer_eps)
    normed = center * inv_std
    return (normed * gain + shift, normed, inv_std)


def norm_back(grad_rows, normed, inv_std, gain):
    scaled = grad_rows * gain
    return (
        scaled
        - jnp.mean(scaled, axis=-1, keepdims=True)
        - normed * jnp.mean(scaled * normed, axis=-1, keepdims=True)
    ) * inv_std


def dot32(a, b):
    return jnp.dot(a, b, preferred_element_type=jnp.float32)


def small_vectors(small, n_dev):
    small = small.astype(jnp.float32).T
    vectors = jnp.concatenate(
        [small[: 6 * L].reshape(L, 6, D), small[6 * L : 8 * L].reshape(L, 2, D)], axis=1
    )
    hidden_shifts = small[8 * L : 12 * L].reshape(L, 4, n_dev, D // n_dev)
    return vectors, jnp.swapaxes(hidden_shifts, 1, 2).reshape(L, -1)


def shut_keys(segs_all, segments, first, blocks_here):
    length = segs_all.shape[0]
    padding = jnp.full((BLK,), -1, jnp.int32)
    segs_all = jnp.concatenate([padding, segs_all, padding]).reshape(-1, BLK)
    segs_near = lax.dynamic_slice_in_dim(segs_all, first, blocks_here + 2, axis=0)
    seg_window = jnp.concatenate([segs_near[j : j + blocks_here] for j in range(3)], axis=1)
    spot = (first - 1 + jnp.arange(blocks_here)[:, None]) * BLK + jnp.arange(3 * BLK)[None, :]
    inside = (spot >= SHARED) & (spot < length)
    own = segments.reshape(blocks_here, 1, BLK)
    allowed = inside[:, :, None] & (seg_window[:, :, None] == jnp.concatenate([own, own], axis=2))
    return jnp.where(allowed, 0.0, masked_score)


def small_by_owner(vectors, hidden, n_dev):
    rows = jnp.moveaxis(vectors.reshape(8, n_dev, -1), 1, 0)
    rows = jnp.concatenate([rows, hidden.reshape(n_dev, 8, -1)], axis=2)
    return jnp.pad(rows, ((0, 0), (0, 0), (0, 128 - rows.shape[2])))


def small_outputs(narrow, piece, hidden):
    return (
        narrow[:, 6:8, :piece],
        narrow[:, 0:6, :piece],
        narrow[:, :, piece : piece + hidden // 8].reshape(L, -1),
    )


def share_of(rows):
    first = lax.all_gather(rows[:SHARED], SEQ, axis=0)[0]
    own = jnp.minimum(lax.axis_index(SEQ), HELPERS - 1) * SHARE
    return lax.dynamic_slice_in_dim(first, own, SHARE, axis=0)


def rows_of_all(kv, queries):
    kv = jnp.moveaxis(kv.reshape(-1, 2 * PAIRS, WIDE), 1, 0)
    return lax.all_gather(kv, SEQ, axis=0), share_of(queries)


def with_shared_rows(part, rows):
    first = lax.all_gather(part, SEQ, axis=0)[:HELPERS].reshape(SHARED, D)
    head_rows = jnp.where(lax.axis_index(SEQ) == 0, first.astype(rows.dtype), rows[:SHARED])
    return jnp.concatenate([head_rows, rows[SHARED:]], axis=0)


def on_any_slice(
    layer_input, segments, rand_blocks, w_qkv, w_out, w_up, w_down, gains, biases, up_bias, d_out
):
    seq_count, depth = lax.axis_size(SEQ), lax.axis_size(BATCH)
    n_dev = seq_count * depth
    own_index = lax.axis_index(SEQ)
    rows = layer_input.shape[1]
    blocks_here, length = rows // BLK, rows * seq_count
    picks = rand_blocks.reshape(-1)
    first = (own_index * blocks_here).reshape(1)

    piece = D // n_dev
    small = jnp.concatenate(
        [biases.reshape(-1, piece), gains.reshape(-1, piece), up_bias.reshape(-1, piece)], axis=0
    ).T
    small = lax.all_gather(small, (SEQ, BATCH), axis=0, tiled=True)
    segs_all = lax.all_gather(segments[0], SEQ, axis=0, tiled=True)
    weights = [
        [lax.all_gather(w[layer], (SEQ, BATCH), axis=0, tiled=True) for w in (w_qkv, w_out, w_up, w_down)]
        for layer in range(L)
    ]
    vectors, hidden_shifts = small_vectors(small, n_dev)
    shut = shut_keys(segs_all, segments, first[0], blocks_here)

    resid = layer_input[0].astype(jnp.float32)
    low = layer_input[0]
    saved = []
    for layer in range(L):
        mat_qkv, mat_out, mat_up, mat_down = weights[layer]
        bias = vectors[layer]
        proj = dot32(low, mat_qkv)
        queries = (proj[:, :D] + bias[0]).astype(jnp.bfloat16)
        kv = jnp.concatenate([proj[:, D : 2 * D], proj[:, 2 * D :] + bias[1]], axis=1).astype(jnp.bfloat16)
        kv_all, part = rows_of_all(kv, queries)
        mixed, part_mixed, *logs = attend(picks, first, queries, kv_all, shut, part)
        mixed = with_shared_rows(part_mixed, mixed)
        resid_one = resid + dot32(mixed, mat_out) + bias[2]
        middle, normed_one, inv_one = norm_rows(resid_one, bias[6], bias[3])
        middle_low = middle.astype(jnp.bfloat16)
        hidden = dot32(middle_low, mat_up) + hidden_shifts[layer]
        active = jax.nn.gelu(hidden, approximate=False).astype(jnp.bfloat16)
        resid_two = middle + dot32(active, mat_down) + bias[4]
        result, normed_two, inv_two = norm_rows(resid_two, bias[7], bias[5])
        saved.append(
            (low, queries, kv_all, part, logs, mixed, normed_one, inv_one, middle_low, hidden, active, normed_two, inv_two)
        )
        resid = result
        low = resid.astype(jnp.bfloat16)

    grad = d_out[0].astype(jnp.float32)
    owned = [None] * L
    for layer in reversed(range(L)):
        (low_in, queries, kv_all, part, logs, mixed, normed_one, inv_one, middle_low, hidden, active, normed_two, inv_two) = saved[layer]
        mat_qkv, mat_out, mat_up, mat_down = weights[layer]
        bias = vectors[layer]
        gain_two_grad = jnp.sum(grad * normed_two, axis=0)
        shift_two_grad = jnp.sum(grad, axis=0)
        grad_two = norm_back(grad, normed_two, inv_two, bias[7])
        grad_two_low = grad_two.astype(jnp.bfloat16)
        down_grad = product_tn(active, grad_two_low)
        active_grad = product_nt(grad_two_low, mat_down)
        hidden_grad = jax.vjp(partial(jax.nn.gelu, approximate=False), hidden)[1](active_grad)[0]
        hidden_grad_low = hidden_grad.astype(jnp.bfloat16)
        up_grad = product_tn(middle_low, hidden_grad_low)
        middle_grad = grad_two + product_nt(hidden_grad_low, mat_up)
        gain_one_grad = jnp.sum(middle_grad * normed_one, axis=0)
        shift_one_grad = jnp.sum(middle_grad, axis=0)
        grad_one = norm_back(middle_grad, normed_one, inv_one, bias[6])
        grad_one_low = grad_one.astype(jnp.bfloat16)
        out_grad = product_tn(mixed, grad_one_low)
        cot = product_nt(grad_one_low, mat_out).astype(jnp.bfloat16)
        part_cot = share_of(cot)
        part_cot = jnp.where(own_index < HELPERS, part_cot, 0)
        dq, dk, dv, part_dq = attend_back(picks, first, queries, kv_all, shut, cot, part, part_cot, *logs)
        dq = with_shared_rows(part_dq, dq)
        dkv = jnp.concatenate([dk, dv], axis=1).astype(jnp.float32)
        dkv = lax.psum_scatter(dkv, SEQ, scatter_dimension=0)
        dkv = jnp.moveaxis(dkv, 0, 1).reshape(rows, 2 * D)
        proj_grad = jnp.concatenate([dq, dkv.astype(jnp.bfloat16)], axis=1)
        qkv_grad = product_tn(low_in, proj_grad)
        small_rows = jnp.stack(
            [
                jnp.sum(dq.astype(jnp.float32), axis=0),
                jnp.sum(dkv[:, D:], axis=0),
                jnp.sum(grad_one, axis=0),
                shift_one_grad,
                jnp.sum(grad_two, axis=0),
                shift_two_grad,
                gain_one_grad,
                gain_two_grad,
            ]
        )
        small_rows = small_by_owner(small_rows, jnp.sum(hidden_grad, axis=0), n_dev)
        owned[layer] = [
            lax.psum_scatter(a, (SEQ, BATCH), scatter_dimension=0, tiled=True)
            for a in (qkv_grad, out_grad, up_grad, down_grad, small_rows)
        ]
        owned[layer][4] = owned[layer][4][0]
        grad = grad_one + product_nt(proj_grad, mat_qkv)
    stacked = [jnp.stack([owned[layer][i] for layer in range(L)]) for i in range(5)]
    return (low[None], grad[None], *stacked[:4], *small_outputs(stacked[4], piece, up_bias.shape[1]))


def on_pairs(
    layer_input, segments, rand_blocks, w_qkv, w_out, w_up, w_down, gains, biases, up_bias, d_out
):
    seq_count, depth = lax.axis_size(SEQ), lax.axis_size(BATCH)
    n_dev = seq_count * depth
    rows, hidden = layer_input.shape[1], up_bias.shape[1] * n_dev
    blocks_here = rows // BLK
    picks = rand_blocks.reshape(-1)
    first = (lax.axis_index(SEQ) * blocks_here).reshape(1)
    piece = D // n_dev

    small = jnp.concatenate(
        [biases.reshape(-1, piece), gains.reshape(-1, piece), up_bias.reshape(-1, piece)], axis=0
    ).T
    small = jnp.pad(small, ((0, 0), (0, 128 - small.shape[1])))
    segs = jnp.pad(segments.reshape(-1, 128), ((0, 8 - rows // 128), (0, 0)))

    def flat(slabs):
        return [w.reshape(-1, w.shape[2]) for w in slabs]

    def attention(got):
        return attend(picks, first, got.q, got.every, shut, got.part)

    def attention_back(got, back, logs):
        return attend_back(
            picks, first, got.q, got.every, shut, back.cot, got.part, back.part_cot, *logs
        )

    x = layer_input[0]
    layers = [[w[layer] for w in (w_qkv, w_out, w_up, w_down)] for layer in range(L)]
    head_one, segs_all, weights_one = first_head(x, small, segs, layers[0], seq_count, depth, 0)
    weights_one = flat(weights_one)
    vectors = head_one.vectors
    shifts = head_one.table.reshape(L, 4, n_dev, piece)
    shifts = jnp.swapaxes(shifts, 1, 2).reshape(L, 1, hidden)
    shut = shut_keys(segs_all[:, : rows // 128].reshape(-1), segments, first[0], blocks_here)
    mixed, part, *logs_one = attention(head_one)
    rows_one, weights_two = tail(
        mixed, part, x, vectors, shifts[0], weights_one, layers[1], seq_count, depth, 1
    )
    weights_two = flat(weights_two)
    middle = rows_one.z_low
    mixed, part, *logs_two = attention(rows_one)
    rows_two = turn(mixed, part, rows_one.z, vectors, shifts[1], weights_two, d_out[0], depth, 2)
    dq, dk, dv, part = attention_back(rows_one, rows_two, logs_two)
    sums_two = sum_rows(dk, dv, dq, part, rows_two, rows_two, seq_count, depth, 3)
    back_one = sum_weights(
        rows_two, middle, sums_two.proj, vectors, weights_two[0], None, (weights_one, rows_one), n_dev, depth, 4
    )
    dq, dk, dv, part = attention_back(head_one, back_one, logs_one)
    sums_one = sum_rows(dk, dv, dq, part, rows_one, back_one, seq_count, depth, 5)
    small = jnp.concatenate(
        [
            small_by_owner(back.totals + sums.totals, back.hidden_totals[0], n_dev)
            for back, sums in ((back_one, sums_one), (rows_two, sums_two))
        ],
        axis=1,
    )
    last = sum_weights(
        SimpleNamespace(**{**vars(rows_one), **vars(back_one)}),
        x, sums_one.proj, None, weights_one[0], small, None, n_dev, depth, 6,
    )
    by_layer = [(sums_one, last), (sums_two, back_one)]
    stacked = [
        jnp.stack([one.owned0 for _, one in by_layer]),
        jnp.stack([one.owned1 for one, _ in by_layer]),
        jnp.stack([jnp.concatenate([one.owned2, two.owned2], axis=1) for one, two in by_layer]),
        jnp.stack([one.owned3 for _, one in by_layer]),
    ]
    return (
        rows_two.z_low[None],
        last.dx[None],
        *stacked,
        *small_outputs(last.owned4.reshape(L, 8, 128), piece, up_bias.shape[1]),
    )


def solution(mesh):
    placed = (
        P(BATCH, SEQ, None),
        P(BATCH, SEQ),
        P(BATCH, SEQ, None, None),
        P(None, (SEQ, BATCH), None),
        P(None, (SEQ, BATCH), None),
        P(None, (SEQ, BATCH), None),
        P(None, (SEQ, BATCH), None),
        P(None, None, (SEQ, BATCH)),
        P(None, None, (SEQ, BATCH)),
        P(None, (SEQ, BATCH)),
        P(BATCH, SEQ, None),
    )
    return jax.shard_map(
        on_pairs if mesh.shape[SEQ] == 8 and mesh.shape[BATCH] == 4 else on_any_slice,
        mesh=mesh,
        in_specs=placed,
        out_specs=(
            P(BATCH, SEQ, None),
            P(BATCH, SEQ, None),
            P(None, (SEQ, BATCH), None),
            P(None, (SEQ, BATCH), None),
            P(None, (SEQ, BATCH), None),
            P(None, (SEQ, BATCH), None),
            P(None, None, (SEQ, BATCH)),
            P(None, None, (SEQ, BATCH)),
            P(None, (SEQ, BATCH)),
        ),
        check_vma=False,
    )
```

```python
import itertools
from functools import partial
from types import SimpleNamespace

import jax
import jax.numpy as jnp
from jax import lax
from jax.experimental import pallas as pl
from jax.experimental.pallas import tpu as pltpu
from jax.sharding import PartitionSpec as P

MESH = pl.DeviceIdType.MESH
SEQ, BATCH = "seq", "batch"


HEAD_PLACES = SimpleNamespace(
    begins=(0, 3, 1, 2, 16, 28, 46, 15, 31),
    arrivals=(
        (5, 4, 17, 6, 18, 19, 32, 20, 33, 30, 54, 34, 55, 56, 77),
        (12, 13, 29),
        (7, 14, 21, 8, 22, 23, 35, 24, 36, 37, 57, 38, 58, 59, 78),
        (9, 10, 50, 11, 25, 26, 39, 27, 40, 41, 60, 42, 62, 61, 79),
        (47, 48, 72, 49, 73, 74, 102, 75, 103, 104, 125, 105, 126, 127, 143),
        (51, 52, 80, 53, 83, 81, 106, 82, 93, 107, 128, 108, 129, 130, 142),
        (76, 70, 98, 71, 99, 100, 119, 101, 120, 121, 140, 122, 144, 141, 150),
        (43, 66, 94, 44, 67, 95, 117, 45, 68, 91, 118, 69, 96, 133, 139),
        (64, 87, 115, 65, 88, 109, 136, 63, 89, 114, 137, 90, 116, 138, 147),
        (112, 113, 134),
        (123, 124, 145),
        (131, 132, 146),
        (110, 111, 135),
    ),
    project=84,
    attention=(148, 149, 151),
)
TAIL_PLACES = SimpleNamespace(
    begins=(0, 2, 5, 11, 29, 22, 3),
    arrivals=(
        (6, 7, 17, 8, 18, 19, 31, 20, 32, 33, 44, 34, 45, 46, 65),
        (15, 10, 23, 14, 26, 24, 37, 28, 38, 39, 52, 40, 53, 54, 64),
        (27, 36, 59, 16, 60, 61, 86, 62, 113, 88, 115, 85, 123, 112, 133),
        (51, 48, 74, 47, 68, 73, 90, 63, 95, 93, 120, 96, 129, 121, 134),
        (57, 55, 81, 56, 82, 83, 107, 87, 108, 104, 124, 92, 126, 131, 137),
        (49, 76, 102, 50, 105, 110, 119, 58, 77, 103, 118, 70, 99, 125, 138),
        (41, 71, 98, 42, 78, 91, 114, 43, 79, 94, 128, 69, 97, 117, 135),
        (100, 101, 127),
        (122, 109, 130),
        (116, 111, 132),
        (80, 75, 106),
    ),
    steps=(1, 4, 9, 12, 13, 21, 25, 30, 35),
    project=66,
    attention=(136, 139, 140),
)
ROWS_PLACES = SimpleNamespace(
    rows=(
        (0, 3, 4, 17, 53),
        (1, 7, 9, 25, 45),
        (11, 23, 21, 43, 52),
        (6, 13, 30, 38, 54),
    ),
    weights=(
        (5, 10, 16, 14, 15, 8, 19, 18, 12, 24, 20, 34, 31, 22, 32, 46, 55),
        (27, 28, 29, 37, 33, 39, 36, 41, 35, 47, 42, 44, 40, 49, 50, 48, 56),
    ),
    grads=(2, 26),
    collect=51,
)
BELOW_PLACES = SimpleNamespace(
    weights=(
        (9, 12, 11, 14, 47, 36, 45, 27, 66, 48, 20, 52, 70, 54, 61, 73, 77),
        (10, 37, 49, 24, 58, 26, 33, 69, 68, 30, 32, 64, 72, 40, 63, 75, 78),
        (6, 22, 18, 23, 31, 21, 39, 29, 42, 38, 43, 46, 60, 53, 62, 74, 76),
        (1, 4, 3, 2, 15, 13, 7, 19, 41, 17, 44, 28, 59, 16, 55, 67, 71),
    ),
    grads=(8, 5, 0),
    steps=(25, 34, 35, 50, 51, 56, 57, 65),
)
LAST_PLACES = SimpleNamespace(
    weights=(
        (22, 31, 32, 33, 61, 36, 57, 65, 74, 41, 63, 67, 79, 58, 72, 84, 88),
        (21, 43, 45, 47, 62, 46, 48, 75, 77, 51, 64, 78, 80, 56, 83, 81, 87),
        (11, 29, 34, 40, 49, 50, 44, 37, 52, 53, 55, 60, 68, 66, 70, 82, 86),
        (9, 13, 15, 18, 30, 35, 23, 42, 54, 25, 27, 59, 71, 39, 69, 76, 85),
        (1, 2, 5, 12, 14, 3, 4, 17, 24, 6, 7, 16, 28, 8, 19, 26, 38),
    ),
    grads=(20, 10, 0),
    steps=(73,),
)


def place():
    s = lax.axis_index(SEQ)
    return {"y": s // 4, "x": (s // 2) % 2, "c": s % 2, "z": lax.axis_index(BATCH)}


def device_of(p):
    return ((p["y"] * 2 + p["x"]) * 2 + p["c"], p["z"])


def flipped(p, axis):
    return {**p, axis: 1 - p[axis]}


def at_depth(p, z):
    return {**p, "z": z}


def number_in(depth):
    return lambda p: device_of(p)[0] * depth + p["z"]


def number_in_sequence(p):
    return device_of(p)[0]


def when(cond, action):
    if cond is None:
        action()
    else:
        pl.when(cond)(action)


def ranked(z, rank, depth):
    near = [sorted(range(depth), key=lambda q: (abs(q - k), q))[rank] for k in range(depth)]
    return sum(jnp.where(z == k, near[k], 0) for k in range(depth))


def offsets(order, depth):
    return list(itertools.product(*[range(depth if a == "z" else 2) for a in order]))


def target_of(order, offset, depth, me):
    p = me
    for axis, d in zip(order, offset):
        if d:
            p = at_depth(p, ranked(me["z"], d, depth)) if axis == "z" else flipped(p, axis)
    return p


def last_move(offset):
    return max([-1] + [i for i, d in enumerate(offset) if d])


def greet(axes, depth, spread=False, collect=False):
    me = place()
    barrier = pltpu.get_barrier_semaphore()

    def signal(device):
        pl.semaphore_signal(barrier, inc=1, device_id=device, device_id_type=MESH)

    count = 0
    for axis in axes + ("c",):
        if axis == "z":
            for step in (1, -1):
                peer = at_depth(me, me["z"] + step)
                cond = (peer["z"] >= 0) & (peer["z"] < depth)
                when(cond, lambda peer=peer: signal(device_of(peer)))
                count = count + cond.astype(jnp.int32)
        else:
            signal(device_of(flipped(me, axis)))
            count = count + 1
    if spread or collect:
        seq, z = lax.axis_index(SEQ), lax.axis_index(BATCH)
        if spread:
            when(seq != 0, lambda: signal((0, z)))
            count = count + jnp.where(seq == 0, HELPERS - 1, 0)
        if collect:

            @pl.when(seq == 0)
            def _():
                for j in range(1, HELPERS):
                    signal((j, z))

            count = count + jnp.where(seq == 0, 0, 1)
    pl.semaphore_wait(barrier, count)


class Gather:
    def __init__(self, source, target, number, order, depth, send, recv, send_at):
        self.source, self.target, self.number = source, target, number
        self.order, self.depth, self.send, self.recv = order, depth, send, recv
        self.send_at = send_at
        self.me = place()
        self.sent = []

    @staticmethod
    def sends(order, depth):
        return sum(len(order) + 2 - last_move(t) for t in offsets(order, depth))

    def onward(self, offset):
        last = last_move(offset)
        z = self.me["z"]
        moves = []
        if last >= 0 and self.order[last] == "z":
            source = ranked(z, offset[last], self.depth)
            peer = jnp.where(source < z, z + 1, z - 1)
            moves.append((at_depth(self.me, peer), (peer >= 0) & (peer < self.depth)))
        for axis in self.order[last + 1 :]:
            if axis == "z":
                moves.append((at_depth(self.me, z + 1), z + 1 < self.depth))
                moves.append((at_depth(self.me, z - 1), z > 0))
            else:
                moves.append((flipped(self.me, axis), None))
        moves.append((flipped(self.me, "c"), None))
        return moves

    def arrival(self, p):
        ref = self.target(p)
        return pltpu.make_async_remote_copy(
            src_ref=ref, dst_ref=ref, send_sem=self.send.at[0], recv_sem=self.recv.at[self.number(p)],
            device_id=device_of(self.me), device_id_type=MESH,
        )

    def handle(self, offset):
        p = target_of(self.order, offset, self.depth, self.me)
        own = not any(offset)
        if not own:
            self.arrival(p).wait_recv()
        for peer, cond in self.onward(offset):
            copy = pltpu.make_async_remote_copy(
                src_ref=self.source if own else self.target(p), dst_ref=self.target(p),
                send_sem=self.send.at[self.send_at], recv_sem=self.recv.at[self.number(p)],
                device_id=device_of(peer), device_id_type=MESH,
            )
            when(cond, copy.start)
            self.sent.append((cond, self.send_at))
            self.send_at += 1

    def begin(self):
        self.handle((0,) * len(self.order))

    def events(self, places):
        marks = [t for t in offsets(self.order, self.depth) if any(t)]
        return [(at, partial(self.handle, t)) for at, t in zip(places, marks, strict=True)]

    def siblings(self):
        for t in offsets(self.order, self.depth):
            self.arrival(flipped(target_of(self.order, t, self.depth, self.me), "c")).wait_recv()

    def drain(self):
        for cond, slot in self.sent:
            copy = pltpu.make_async_remote_copy(
                src_ref=self.source, dst_ref=self.target(self.me), send_sem=self.send.at[slot],
                recv_sem=self.recv.at[self.number(self.me)], device_id=device_of(self.me), device_id_type=MESH,
            )
            when(cond, copy.wait_send)


class Reduce:
    def __init__(self, partial_of, far_partial_of, inbox, order, depth, send, recv):
        self.partial_of, self.far_partial_of, self.inbox = partial_of, far_partial_of, inbox
        self.order, self.depth, self.send, self.recv = order, depth, send, recv
        self.me = place()
        self.base, _ = self.slots(order, depth)
        self.marks = sorted(offsets(order, depth), key=lambda t: (-sum(t), t))
        self.sent = []

    @staticmethod
    def split(order, offset):
        if "z" not in order:
            return offset, 0
        i = order.index("z")
        return offset[:i] + (0,) + offset[i + 1 :], offset[i]

    @staticmethod
    def slots(order, depth):
        base, count = {}, 0
        deep = depth if "z" in order else 1
        for t in offsets(order, depth):
            key, rank = Reduce.split(order, t)
            if rank:
                continue
            last = last_move(key)
            for i, axis in enumerate(order):
                if i <= last:
                    continue
                base[(key, axis)] = count
                if axis == "z":
                    count += deep + 1
                elif "z" in order and i > order.index("z"):
                    count += deep
                else:
                    count += 1
            base[(key, "c")] = count
            count += deep
        return base, count

    def where_(self, key, axis, z):
        deep = "z" in self.order and (axis == "c" or self.order.index(axis) > self.order.index("z"))
        return self.base[(key, axis)] + (z if deep else 0)

    def copy(self, source, edge, slot, peer):
        return pltpu.make_async_remote_copy(
            src_ref=source, dst_ref=self.inbox.at[edge], send_sem=self.send.at[slot],
            recv_sem=self.recv.at[edge], device_id=device_of(peer), device_id_type=MESH,
        )

    def start(self, offset):
        p = target_of(self.order, offset, self.depth, self.me)
        key, _ = self.split(self.order, offset)
        slot = self.marks.index(offset)
        edge = self.where_(key, "c", p["z"])
        peer = flipped(self.me, "c")
        self.copy(self.far_partial_of(flipped(p, "c")), edge, slot, peer).start()
        self.sent.append(slot)

    def kids(self, offset, p):
        key, rank = self.split(self.order, offset)
        last, z = last_move(offset), self.me["z"]
        found = [(self.where_(key, "c", p["z"]), None)]
        for axis in self.order[last + 1 :]:
            if axis == "z":
                at = self.base[(key, "z")]
                found += [(at + z, z > 0), (at + self.depth, z + 1 < self.depth)]
            else:
                found.append((self.where_(key, axis, p["z"]), None))
        if last >= 0 and self.order[last] == "z":
            far = jnp.where(p["z"] < z, z + 1, z - 1)
            found.append((self.base[(key, "z")] + p["z"], (far >= 0) & (far < self.depth)))
        return found

    def upward(self, offset, p):
        key, rank = self.split(self.order, offset)
        k, z = last_move(offset), self.me["z"]
        axis = self.order[k]
        if axis == "z":
            edge = self.base[(key, "z")] + jnp.where(p["z"] == z - 1, self.depth, p["z"])
            return edge, at_depth(self.me, jnp.where(p["z"] < z, z - 1, z + 1))
        parent = key[:k] + (0,) + key[k + 1 :]
        return self.where_(parent, axis, p["z"]), flipped(self.me, axis)

    def handle(self, offset, add, finish):
        p = target_of(self.order, offset, self.depth, self.me)
        kids = self.kids(offset, p)
        slot = len(self.marks) + self.marks.index(offset)
        for edge, cond in kids:
            when(cond, self.copy(self.inbox.at[edge], edge, slot, self.me).wait_recv)
        parts = [(self.inbox.at[edge], cond) for edge, cond in kids]
        if any(offset):
            into = parts[0][0]
            add(self.partial_of(p), parts, into)
            edge, peer = self.upward(offset, p)
            self.copy(into, edge, slot, peer).start()
            self.sent.append(slot)
        else:
            finish(self.partial_of(p), parts)

    def drain(self):
        for slot in self.sent:
            self.copy(self.inbox.at[0], 0, slot, self.me).wait_send()


D = 768
H = 12
DH = 64
BLK = 64
R = 3
GLOB = 2
L = 2
PAIRS = H // 2
WIDE = 2 * DH
SHARED = GLOB * BLK
SHARE = 16
HELPERS = SHARED // SHARE
VMEM_LIMIT = 60 * 1024 * 1024

layer_eps = 1e-06
masked_score = -1e30

Z_Y_X, Z_X_Y, X_Y_Z, Y_X_Z = ("z", "y", "x"), ("z", "x", "y"), ("x", "y", "z"), ("y", "x", "z")
Y_X, X_Y = ("y", "x"), ("x", "y")
ANYWHERE = pl.BlockSpec(memory_space=pl.ANY)
IN_SMEM = pl.BlockSpec(memory_space=pltpu.SMEM)
IN_VMEM = pl.BlockSpec(memory_space=pltpu.VMEM)
LOAD, SAVE = pl.BlockSpec(memory_space=pl.ANY), pl.BlockSpec(memory_space=pl.ANY)


def dma(*shape):
    return pltpu.SemaphoreType.DMA(shape)


def product(a, b):
    return lax.dot_general(a, b, (((1,), (0,)), ((), ())), preferred_element_type=jnp.float32)


def product_nt(a, b):
    return lax.dot_general(a, b, (((1,), (1,)), ((), ())), preferred_element_type=jnp.float32)


def product_tn(a, b):
    return lax.dot_general(a, b, (((0,), (0,)), ((), ())), preferred_element_type=jnp.float32)


def split_heads(pair_rows):
    low_lanes = lax.broadcasted_iota(jnp.int32, (1, WIDE), 1) < DH
    zero = jnp.zeros_like(pair_rows)
    return jnp.concatenate([jnp.where(low_lanes, pair_rows, zero), jnp.where(low_lanes, zero, pair_rows)], axis=0)


def join_heads(stacked):
    low_lanes = lax.broadcasted_iota(jnp.int32, (1, WIDE), 1) < DH
    rows = stacked.shape[0] // 2
    return jnp.where(low_lanes, stacked[:rows], stacked[rows:])


def row_of(block):
    return pl.multiple_of(block * BLK, BLK)


class Keys:
    def __init__(self, ref, pair=None):
        self.ref, self.pair = ref, pair
        self.held = ref.shape[2] // (BLK if pair is None else 1)
        self.blocks_all = ref.shape[0] * self.held

    def block(self, device, inner):
        if self.pair is None:
            return self.ref[device, 0, pl.ds(row_of(inner), BLK)]
        return self.ref[device, self.pair, inner]

    def whole(self):
        held = self.ref[...] if self.pair is None else self.ref[:, self.pair]
        return held.reshape(-1, WIDE)

    def with_shared(self, near):
        if self.pair is None:
            shared = self.ref[0, 0, 0:SHARED]
        else:
            shared = self.ref[0, self.pair, 0:GLOB].reshape(SHARED, WIDE)
        return jnp.concatenate([shared, near], axis=0)


def window_blocks(first, block, blocks_all):
    return [(first + block + j - 1 + blocks_all) % blocks_all for j in range(3)]


def drawn_blocks(picks_ref, pair, block, r):
    return [picks_ref[(block * H + 2 * pair + side) * R + r] for side in range(2)]


def bring(drawn, first, pairs, blocks_here):
    low_lanes = lax.broadcasted_iota(jnp.int32, (1, WIDE), 1) < DH
    for block in range(blocks_here):
        for source, target in pairs:
            for j, one in enumerate(window_blocks(first, block, source.blocks_all)):
                rows = source.block(one // source.held, one % source.held)
                target[block, j * BLK : (j + 1) * BLK] = rows
            for r in range(R):
                one, two = drawn(block, r)
                target[block, (3 + r) * BLK : (4 + r) * BLK] = jnp.where(
                    low_lanes, source.block(*one), source.block(*two)
                )


def key_scores(keys, q_heads, shut):
    scores = product_nt(keys, q_heads)
    end = SHARED + 3 * BLK
    return jnp.concatenate([scores[:SHARED], scores[SHARED:end] + shut, scores[end:]], axis=0)


def soft(scores):
    top = jnp.max(scores, axis=0, keepdims=True)
    weight = jnp.exp(scores - top)
    total = jnp.sum(weight, axis=0, keepdims=True)
    return weight * (1.0 / total), top + jnp.log(total)


def attend_pair(
    drawn, first, q_ref, keys, values, shut_ref, part_ref, o_ref, po_ref, log_ref, plog_ref, near_k, near_v
):
    blocks_here = q_ref.shape[0] // BLK
    bring(drawn, first, [(keys, near_k), (values, near_v)], blocks_here)
    scale = jnp.bfloat16(DH ** (-0.5))
    weight, logs = soft(product_nt(keys.whole(), split_heads(part_ref[...] * scale)))
    mixed = product_tn(weight.astype(jnp.bfloat16), values.whole())
    po_ref[...] = join_heads(mixed).astype(po_ref.dtype)
    plog_ref[0] = logs
    for block in range(blocks_here):
        here = slice(block * BLK, (block + 1) * BLK)
        q_heads = split_heads(q_ref[here] * scale)
        weight, logs = soft(key_scores(keys.with_shared(near_k[block]), q_heads, shut_ref[block]))
        mixed = product_tn(weight.astype(jnp.bfloat16), values.with_shared(near_v[block]))
        o_ref[here] = join_heads(mixed).astype(o_ref.dtype)
        log_ref[0, block : block + 1] = logs


def drawn_places(picks_ref, pair, held):
    def drawn(block, r):
        return [(one // held, one % held) for one in drawn_blocks(picks_ref, pair, block, r)]

    return drawn


def attend_kernel(picks_ref, first_ref, q_ref, k_ref, v_ref, *refs):
    keys, values = Keys(k_ref), Keys(v_ref)
    drawn = drawn_places(picks_ref, pl.program_id(0), keys.held)
    attend_pair(drawn, first_ref[0], q_ref, keys, values, *refs)


def near_rows(rows, dtype):
    return pltpu.VMEM((rows // BLK, 6 * BLK, WIDE), dtype)


def columns(rows, shift=0):
    return pl.BlockSpec((rows, WIDE), lambda p, *_: (0, p + shift))


def of_all(kv, shift=0):
    return pl.BlockSpec((kv.shape[0], 1, kv.shape[2], WIDE), lambda p, *_: (0, p + shift, 0, 0))


def by_pair(rows, lanes):
    return pl.BlockSpec((1, rows, lanes), lambda p, *_: (p, 0, 0))


def attend(picks, first, queries, kv, shut, part):
    rows = queries.shape[0]
    blocks = rows // BLK
    return pl.pallas_call(
        attend_kernel,
        grid_spec=pltpu.PrefetchScalarGridSpec(
            num_scalar_prefetch=2,
            grid=(PAIRS,),
            in_specs=[
                columns(rows), of_all(kv), of_all(kv, PAIRS),
                pl.BlockSpec(shut.shape, lambda p, *_: (0, 0, 0)), columns(SHARE),
            ],
            out_specs=[columns(rows), columns(SHARE), by_pair(blocks, WIDE), by_pair(1, 2 * SHARE)],
            scratch_shapes=[near_rows(rows, jnp.bfloat16)] * 2,
        ),
        out_shape=[
            jax.ShapeDtypeStruct((rows, D), jnp.bfloat16),
            jax.ShapeDtypeStruct((SHARE, D), jnp.bfloat16),
            jax.ShapeDtypeStruct((PAIRS, blocks, WIDE), jnp.float32),
            jax.ShapeDtypeStruct((PAIRS, 1, 2 * SHARE), jnp.float32),
        ],
        compiler_params=pltpu.CompilerParams(vmem_limit_bytes=VMEM_LIMIT),
        name="attend",
    )(picks, first, queries, kv, kv, shut, part)


def score_grads(weight, values, cot_heads):
    grads = product_nt(values, cot_heads)
    mean = jnp.sum(weight * grads, axis=0, keepdims=True)
    return (weight * (grads - mean)).astype(jnp.bfloat16)


def attend_back_kernel(
    picks_ref, first_ref, q_ref, k_ref, v_ref, shut_ref, do_ref, part_ref, pdo_ref, log_ref, plog_ref,
    dq_ref, dk_ref, dv_ref, pdq_ref, sum_k, sum_v, near_k, near_v, grad_k, grad_v,
):
    pair = pl.program_id(0)
    first = first_ref[0]
    blocks_here, blocks_all = q_ref.shape[0] // BLK, sum_k.shape[0] // BLK
    all_keys, all_values = Keys(k_ref), Keys(v_ref)
    drawn = drawn_places(picks_ref, pair, all_keys.held)
    bring(drawn, first, [(all_keys, near_k), (all_values, near_v)], blocks_here)
    low_lanes = lax.broadcasted_iota(jnp.int32, (1, WIDE), 1) < DH
    step = DH ** (-0.5)
    scale = jnp.bfloat16(step)
    part, cot = split_heads(part_ref[...] * scale), split_heads(pdo_ref[...])
    weight = jnp.exp(product_nt(all_keys.whole(), part) - plog_ref[0])
    grads = score_grads(weight, all_values.whole(), cot)
    pdq_ref[...] = (join_heads(product_tn(grads, all_keys.whole())) * step).astype(pdq_ref.dtype)
    sum_k[...] = product(grads, part)
    sum_v[...] = product(weight.astype(jnp.bfloat16), cot)
    shared_k = jnp.zeros((SHARED, WIDE), jnp.float32)
    shared_v = jnp.zeros((SHARED, WIDE), jnp.float32)
    for block in range(blocks_here):
        here = slice(block * BLK, (block + 1) * BLK)
        do = jnp.where(first + block < GLOB, jnp.bfloat16(0), do_ref[here])
        q_heads, do_heads = split_heads(q_ref[here] * scale), split_heads(do)
        keys, values = all_keys.with_shared(near_k[block]), all_values.with_shared(near_v[block])
        weight = jnp.exp(key_scores(keys, q_heads, shut_ref[block]) - log_ref[0, block : block + 1])
        grads = score_grads(weight, values, do_heads)
        dq_ref[here] = (join_heads(product_tn(grads, keys)) * step).astype(dq_ref.dtype)
        key_grad = product(grads, q_heads)
        value_grad = product(weight.astype(jnp.bfloat16), do_heads)
        shared_k = shared_k + key_grad[:SHARED]
        shared_v = shared_v + value_grad[:SHARED]
        grad_k[block] = key_grad[SHARED:]
        grad_v[block] = value_grad[SHARED:]
    sum_k[0:SHARED] += shared_k
    sum_v[0:SHARED] += shared_v
    for block in range(blocks_here):
        for grad, total in ((grad_k, sum_k), (grad_v, sum_v)):
            for j, one in enumerate(window_blocks(first, block, blocks_all)):
                total[pl.ds(row_of(one), BLK)] += grad[block, j * BLK : (j + 1) * BLK]
            for r in range(R):
                tile = grad[block, (3 + r) * BLK : (4 + r) * BLK]
                one, two = drawn_blocks(picks_ref, pair, block, r)
                total[pl.ds(row_of(one), BLK)] += jnp.where(low_lanes, tile, 0.0)
                total[pl.ds(row_of(two), BLK)] += jnp.where(low_lanes, 0.0, tile)
    dk_ref[...] = sum_k[...].astype(dk_ref.dtype).reshape(dk_ref.shape)
    dv_ref[...] = sum_v[...].astype(dv_ref.dtype).reshape(dv_ref.shape)


def attend_back(picks, first, queries, kv, shut, cot, part, part_cot, logs, part_logs):
    rows, grads = queries.shape[0], (kv.shape[0], PAIRS) + kv.shape[2:]
    length = kv.shape[0] * kv.shape[2]
    return pl.pallas_call(
        attend_back_kernel,
        grid_spec=pltpu.PrefetchScalarGridSpec(
            num_scalar_prefetch=2,
            grid=(PAIRS,),
            in_specs=[
                columns(rows), of_all(kv), of_all(kv, PAIRS),
                pl.BlockSpec(shut.shape, lambda p, *_: (0, 0, 0)), columns(rows), columns(SHARE), columns(SHARE),
                by_pair(rows // BLK, WIDE), by_pair(1, 2 * SHARE),
            ],
            out_specs=[columns(rows), of_all(kv), of_all(kv), columns(SHARE)],
            scratch_shapes=[pltpu.VMEM((length, WIDE), jnp.float32)] * 2
            + [near_rows(rows, jnp.bfloat16)] * 2
            + [near_rows(rows, jnp.float32)] * 2,
        ),
        out_shape=[
            jax.ShapeDtypeStruct((rows, D), jnp.bfloat16),
            jax.ShapeDtypeStruct(grads, jnp.bfloat16),
            jax.ShapeDtypeStruct(grads, jnp.bfloat16),
            jax.ShapeDtypeStruct((SHARE, D), jnp.bfloat16),
        ],
        compiler_params=pltpu.CompilerParams(vmem_limit_bytes=VMEM_LIMIT),
        name="attend_back",
    )(picks, first, queries, kv, kv, shut, cot, part, part_cot, logs, part_logs)


def call(body, name, cid, ins, outs, scratch):
    loads = [k for k, (_, where) in ins.items() if where is LOAD]
    saves = [k for k, (_, _, where) in outs.items() if where is SAVE]
    names = ["far_" + k if k in loads or k in saves else k for k in (*ins, *outs)]
    scratch = {
        **scratch,
        **{k: pltpu.VMEM(ins[k][0].shape, ins[k][0].dtype) for k in loads},
        **{k: pltpu.VMEM(outs[k][0], outs[k][1]) for k in saves},
        **dict(moves=dma(len(loads) + len(saves) + 1)),
    }

    def run(*given):
        refs = SimpleNamespace(**dict(zip(names + list(scratch), given)))
        copies = {}
        for i, k in enumerate(loads + saves):
            pair = (getattr(refs, "far_" + k), getattr(refs, k))
            copies[k] = pltpu.make_async_copy(*(pair if k in loads else pair[::-1]), refs.moves.at[i])
        coming, going = list(loads), []
        for k in loads:
            copies[k].start()

        def ready(*wanted):
            for k in wanted:
                if k in coming:
                    coming.remove(k)
                    copies[k].wait()

        def save(*given):
            for k in given:
                if k in saves:
                    going.append(k)
                    copies[k].start()

        refs.ready, refs.save = ready, save
        body(refs)
        ready(*loads)
        save(*[k for k in saves if k not in going])
        for k in saves:
            copies[k].wait()

    got = pl.pallas_call(
        run,
        out_shape=[jax.ShapeDtypeStruct(shape, dtype) for shape, dtype, _ in outs.values()],
        in_specs=[where for _, where in ins.values()],
        out_specs=[where for _, _, where in outs.values()],
        scratch_shapes=list(scratch.values()),
        compiler_params=pltpu.CompilerParams(
            collective_id=cid, has_side_effects=True, vmem_limit_bytes=VMEM_LIMIT
        ),
        name=name,
    )(*[array for array, _ in ins.values()])
    return SimpleNamespace(**dict(zip(outs, got)))


def over(count, act):
    def step(i, carry):
        act(i)
        return carry

    lax.fori_loop(0, count, step, 0)


def span(i, size, first=0):
    return pl.ds(pl.multiple_of(first + i * size, size), size)


def run_in_order(timed):
    for _, act in sorted(timed, key=lambda pair: pair[0]):
        act()


def layer_pieces(rows_in, rows_down, first):
    half, wide = rows_down // 2, 3 * D // 2
    return [
        (first, 0, rows_in, 0, wide, Z_Y_X),
        (first, 0, rows_in, wide, wide, Z_X_Y),
        (first + 1, 0, rows_in, 0, D, Z_X_Y),
        (first + 2, 0, rows_in, 0, 2 * D, Z_Y_X),
        (first + 2, 0, rows_in, 2 * D, 2 * D, Z_X_Y),
        (first + 3, 0, half, 0, D, X_Y_Z),
        (first + 3, half, half, 0, D, Y_X_Z),
    ]


class Gathering:
    def __init__(self, arrays, pieces, seq_count, depth, near):
        self.near, self.layers = near, [layer for _, layer in arrays]
        shapes = [a.shape if layer is None else a.shape[1:] for a, layer in arrays]
        self.shapes = [jax.ShapeDtypeStruct(shape, a.dtype) for shape, (a, _) in zip(shapes, arrays)]
        arrays = [a for a, _ in arrays]
        self.arrays, self.pieces, self.depth, self.n_dev = arrays, pieces, depth, seq_count * depth
        flat_only = {which for which, *_, order in pieces if "z" not in order}
        self.counts = [seq_count if i in flat_only else self.n_dev for i in range(len(arrays))]

    def ins(self):
        return {"slab%d" % i: (a, ANYWHERE) for i, a in enumerate(self.arrays)}

    def outs(self):
        return {
            "every%d" % i: ((n,) + a.shape, a.dtype, SAVE if i in self.near else ANYWHERE)
            for i, (n, a) in enumerate(zip(self.counts, self.shapes))
        }

    def scratch(self):
        total = sum(Gather.sends(order, self.depth) for *_, order in self.pieces)
        return {
            "g_send": dma(total),
            "g_recv": dma(len(self.pieces), self.n_dev),
            "g_local": dma(len(self.arrays)),
        }

    def number(self, i):
        return number_in(self.depth) if self.counts[i] == self.n_dev else number_in_sequence

    def begin(self, refs):
        slabs = [getattr(refs, "slab%d" % i) for i in range(len(self.arrays))]
        slabs = [ref if layer is None else ref.at[layer] for ref, layer in zip(slabs, self.layers)]
        every = [getattr(refs, "every%d" % i) for i in range(len(self.arrays))]
        self.jobs, at = [], 0
        for k, (which, row, rows, column, columns_, order) in enumerate(self.pieces):
            window = (pl.ds(row, rows), pl.ds(column, columns_))
            number = self.number(which)
            self.jobs.append(
                Gather(
                    slabs[which].at[window],
                    lambda p, which=which, window=window, number=number: every[which].at[(number(p),) + window],
                    number, order, self.depth, refs.g_send, refs.g_recv.at[k], at,
                )
            )
            at += Gather.sends(order, self.depth)
        me = place()
        self.own = [
            pltpu.make_async_copy(slab, all_.at[self.number(i)(me)], refs.g_local.at[i])
            for i, (slab, all_) in enumerate(zip(slabs, every))
        ]
        for copy in self.own:
            copy.start()

    def hurry(self, refs, arrays):
        for (which, *_), job in zip(self.pieces, self.jobs):
            if which in arrays:
                job.siblings()
        for i in arrays:
            self.own[i].wait()
            refs.save("every%d" % i)
        self.early = arrays

    def end(self):
        for (which, *_), job in zip(self.pieces, self.jobs):
            if which not in self.early:
                job.siblings()
        for job in self.jobs:
            job.drain()
        for i, copy in enumerate(self.own):
            if i not in self.early:
                copy.wait()

    def results(self, got):
        return [getattr(got, "every%d" % i) for i in range(len(self.arrays))]


def to_helpers(source, target, send, recv):
    seq, z = lax.axis_index(SEQ), lax.axis_index(BATCH)

    def copy(j):
        return pltpu.make_async_remote_copy(
            src_ref=source.at[pl.ds(j * SHARE, SHARE)], dst_ref=target, send_sem=send.at[j],
            recv_sem=recv, device_id=(j, z), device_id_type=MESH,
        )

    def begin():
        for j in range(1, HELPERS):
            copy(j).start()

    def own():
        pltpu.sync_copy(source.at[pl.ds(0, SHARE)], target)
        for j in range(1, HELPERS):
            copy(j).wait_send()

    def end():
        pl.when(seq == 0)(own)
        pl.when(seq != 0)(lambda: copy(1).wait_recv())

    pl.when(seq == 0)(begin)
    return end


def to_first(source, target, send, recv):
    seq, z = lax.axis_index(SEQ), lax.axis_index(BATCH)

    def copy(j):
        return pltpu.make_async_remote_copy(
            src_ref=source, dst_ref=target.at[pl.ds(j * SHARE, SHARE)], send_sem=send,
            recv_sem=recv.at[j], device_id=(0, z), device_id_type=MESH,
        )

    for j in range(1, HELPERS):
        pl.when(seq == j)(copy(j).start)

    def end():
        def mine():
            pltpu.sync_copy(source, target.at[pl.ds(0, SHARE)])
            for j in range(1, HELPERS):
                copy(j).wait_recv()

        pl.when(seq == 0)(mine)
        pl.when(seq != 0)(lambda: copy(1).wait_send())

    return end


def from_slabs(ref):
    def get(at):
        slabs = ref[:, :, at]
        return slabs.astype(jnp.float32).reshape(-1, slabs.shape[2]).astype(ref.dtype)

    return get


def project(low, w, bias, q, kv):
    def queries(i):
        at = span(i, 256)
        q[:, at] = (product(low[...], w(at)) + bias[0:1, at]).astype(q.dtype)

    def keys(i):
        keep(2 * i, product(low[...], w(span(i, 256, D))))

    def values(i):
        keep(PAIRS + 2 * i, product(low[...], w(span(i, 256, 2 * D))) + bias[1:2, span(i, 256)])

    def keep(pair, acc):
        for half in range(2):
            lanes = acc[:, half * WIDE : (half + 1) * WIDE].astype(kv.dtype)
            kv[pair + half] = lanes.reshape(kv.shape[1:])

    for act in (keys, values, queries):
        over(D // 256, act)


class Sequence:
    def __init__(self, rows, seq_count, depth, dtype):
        self.rows, self.seq_count, self.depth, self.dtype = rows, seq_count, depth, dtype

    def outs(self):
        blocks, f32 = self.rows // BLK, jnp.float32
        return dict(
            q=((self.rows, D), self.dtype, SAVE),
            every=((self.seq_count, 2 * PAIRS, blocks, BLK, WIDE), self.dtype, SAVE),
            part=((SHARE, D), self.dtype, SAVE),
            o=((self.rows, D), self.dtype, SAVE), po=((SHARE, D), self.dtype, SAVE),
            log=((PAIRS, blocks, WIDE), f32, SAVE), plog=((PAIRS, 1, 2 * SHARE), f32, SAVE),
        )

    def scratch(self):
        return dict(
            kv=pltpu.VMEM((2 * PAIRS, self.rows // BLK, BLK, WIDE), self.dtype), send=dma(4 * Gather.sends(Y_X, self.depth)),
            recv=dma(4, self.seq_count), local=dma(), give=dma(HELPERS), take=dma(),
            near_k=near_rows(self.rows, self.dtype), near_v=near_rows(self.rows, self.dtype),
        )

    def prepare(self, refs):
        count, at = PAIRS // 2, 0
        self.jobs = []
        for i in range(4):
            window = pl.ds(i * count, count)
            self.jobs.append(
                Gather(
                    refs.kv.at[window],
                    lambda p, window=window: refs.every.at[number_in_sequence(p), window],
                    number_in_sequence, (X_Y, Y_X)[i % 2], self.depth, refs.send, refs.recv.at[i], at,
                )
            )
            at += Gather.sends(Y_X, self.depth)

    def begin(self, refs):
        for job in self.jobs:
            job.begin()
        self.finish = to_helpers(refs.q, refs.part, refs.give, refs.take)
        self.own = pltpu.make_async_copy(refs.kv, refs.every.at[number_in_sequence(place())], refs.local)
        self.own.start()

    def arrived(self, refs):
        for job in self.jobs:
            job.siblings()
        self.own.wait()
        self.finish()
        refs.save("every", "part")

    def attention(self, refs, steps):
        first = lax.axis_index(SEQ) * (self.rows // BLK)
        count = PAIRS // steps

        def pair_of(pair):
            at, one = span(pair, WIDE), pl.ds(pair, 1)

            def drawn(block, r):
                first_one = (block * H + 2 * pair) * R + r
                return [(refs.picks[0, i], refs.picks[1, i]) for i in (first_one, first_one + R)]

            attend_pair(
                drawn, first, refs.q.at[:, at], Keys(refs.every, pair), Keys(refs.every, PAIRS + pair), refs.shut,
                refs.part.at[:, at], refs.o.at[:, at], refs.po.at[:, at], refs.log.at[one], refs.plog.at[one],
                refs.near_k, refs.near_v,
            )

        def step(k):
            if k == 0:
                self.arrived(refs)
                refs.ready("shut")
            over(count, lambda i: pair_of(k * count + i))
            if k == steps - 1:
                refs.save("o", "po", "log", "plog")

        return [partial(step, k) for k in range(steps)]

    def end(self):
        for job in self.jobs:
            job.drain()


def project_and_send(refs, gathering, sequence, low, which):
    def act():
        gathering.hurry(refs, [which])
        w = from_slabs(getattr(refs, "every%d" % which))
        refs.ready("low")
        project(low, w, refs.bias, refs.q, refs.kv)
        sequence.begin(refs)
        refs.save("q")

    return act


def timed_events(jobs, places):
    return [pair for job, at in zip(jobs, places, strict=True) for pair in job.events(at)]


def shut_keys_here(segs, own_segs, shut):
    me, count = lax.axis_index(SEQ), segs.shape[0]
    blocks = shut.shape[0]
    rows = blocks * BLK

    def column(device):
        held = segs[device].astype(jnp.float32).T
        return [held[:, r : r + 1] for r in range(rows // WIDE)]

    before, here, after = column((me + count - 1) % count), column(me), column((me + 1) % count)
    near = jnp.concatenate([before[-1][WIDE - BLK :]] + here + [after[0][:BLK]], axis=0)
    for block in range(blocks):
        spot = (me * blocks + block - 1) * BLK + lax.broadcasted_iota(jnp.int32, (3 * BLK, WIDE), 0)
        same = near[block * BLK : (block + 3) * BLK] == own_segs[block : block + 1]
        shut[block] = jnp.where(same & (spot >= SHARED) & (spot < count * rows), 0.0, masked_score)


def first_head(low, small, segs, own_segs, picks, weights, seq_count, depth, cid):
    rows = low.shape[0]
    pieces = [(0, 0, small.shape[0], 0, 128, Z_Y_X), (1, 0, 8, 0, 128, Y_X)]
    pieces += layer_pieces(small.shape[0], weights[3][0].shape[1], 2)
    gathering = Gathering([(small, None), (segs, None)] + weights, pieces, seq_count, depth, (0, 1, 2))
    sequence = Sequence(rows, seq_count, depth, low.dtype)

    def body(refs):
        greet(("y", "x", "z"), depth, spread=True)
        gathering.begin(refs)
        sequence.prepare(refs)
        refs.bias = refs.vectors.at[0]

        def vectors():
            gathering.hurry(refs, [0, 1])
            shut_keys_here(refs.every1, refs.own_segs, refs.shut)
            refs.save("shut")
            table = refs.every0[...].astype(jnp.float32).reshape(D, 128).T
            for layer in range(L):
                refs.vectors[layer, 0:6] = table[6 * layer : 6 * layer + 6]
                refs.vectors[layer, 6:8] = table[6 * L + 2 * layer : 6 * L + 2 * layer + 2]
            refs.table[...] = table[8 * L : 12 * L]

        def project_now():
            project_and_send(refs, gathering, sequence, refs.low, 2)()
            gathering.early = [0, 1, 2]

        at = HEAD_PLACES
        run_in_order(
            [(place_, job.begin) for place_, job in zip(at.begins, gathering.jobs, strict=True)]
            + timed_events(gathering.jobs + sequence.jobs, at.arrivals)
            + [(at.project, vectors), (at.project + 0.1, project_now)]
            + list(zip(at.attention, sequence.attention(refs, len(at.attention)), strict=True))
        )
        sequence.end()
        gathering.end()

    got = call(
        body, "first_head", cid,
        {
            **dict(low=(low, LOAD), own_segs=(own_segs, IN_VMEM), picks=(picks, IN_SMEM)), **gathering.ins(),
        },
        {
            **dict(
                vectors=((L, 8, D), jnp.float32, IN_VMEM), table=((4 * L, D), jnp.float32, IN_VMEM),
                shut=((rows // BLK, 3 * BLK, WIDE), jnp.float32, SAVE),
            ),
            **sequence.outs(), **gathering.outs(),
        },
        {**sequence.scratch(), **gathering.scratch()},
    )
    return got, gathering.results(got)[2:]


def norm_block(resid, gain, shift):
    center = resid - jnp.mean(resid, axis=1, keepdims=True)
    inv_std = lax.rsqrt(jnp.mean(center * center, axis=1, keepdims=True) + layer_eps)
    normed = center * inv_std
    return normed * gain + shift, normed, inv_std


ROW_BLOCK = 64


def tail_steps(refs):
    rows, hidden = refs.resid.shape[0], refs.shifts.shape[1]

    def out():
        refs.ready("resid", "w_out")

        def act(i):
            at = span(i, 256)
            own = refs.resid[:, at].astype(jnp.float32)
            refs.sum[:, at] = own + product(refs.mixed[...], refs.w_out[:, at]) + refs.bias[2:3, at]

        over(D // 256, act)
        refs.save("mixed")

    def norm_one():
        def act(i):
            at = span(i, ROW_BLOCK)
            y, normed, inv = norm_block(refs.sum[at], refs.bias[6:7], refs.bias[3:4])
            refs.n1[at], refs.inv1[at], refs.sum[at] = normed, inv, y
            refs.y_low[at] = y.astype(jnp.bfloat16)

        over(rows // ROW_BLOCK, act)
        refs.save("n1", "inv1", "y_low")
        refs.ready("w_up")

    def up(first, count):
        def act(i):
            at = span(first + i, 256)
            u = product(refs.y_low[...], refs.w_up[:, at]) + refs.shifts[0:1, at]
            share = 0.5 + 0.5 * lax.erf(u * (0.5 ** 0.5))
            refs.a_low[:, at] = (u * share).astype(jnp.bfloat16)
            slope = share + u * jnp.exp(-0.5 * u * u) * ((2.0 * jnp.pi) ** -0.5)
            refs.slope[:, at] = slope.astype(jnp.bfloat16)

        over(count, act)

    def down():
        refs.ready("w_down")
        refs.save("a_low", "slope")

        def act(i):
            at = span(i, 256)
            refs.sum[:, at] = refs.sum[:, at] + product(refs.a_low[...], refs.w_down[:, at]) + refs.bias[4:5, at]

        over(D // 256, act)

    def norm_two():
        def act(i):
            at = span(i, ROW_BLOCK)
            z, normed, inv = norm_block(refs.sum[at], refs.bias[7:8], refs.bias[5:6])
            refs.n2[at], refs.inv2[at] = normed, inv
            if hasattr(refs, "z"):
                refs.z[at] = z
            refs.z_low[at] = z.astype(jnp.bfloat16)

        over(rows // ROW_BLOCK, act)
        refs.save("n2", "inv2", "z", "z_low")

    quarter = hidden // 256 // 4
    return [out, norm_one] + [partial(up, k * quarter, quarter) for k in range(4)] + [down, norm_two]


def tail_ins(mixed, part, resid, vectors, shifts, weights):
    return dict(
        generic=(mixed, LOAD), own_part=(part, ANYWHERE), resid=(resid, LOAD), vectors=(vectors, IN_VMEM),
        shifts=(shifts, IN_VMEM), w_out=(weights[1], LOAD), w_up=(weights[2], LOAD), w_down=(weights[3], LOAD),
    )


def tail_results(rows, hidden):
    f32, low = jnp.float32, jnp.bfloat16
    kept = dict(mixed=((rows, D), low), y_low=((rows, D), low), a_low=((rows, hidden), low), z_low=((rows, D), low))
    norms = dict(
        n1=((rows, D), f32), inv1=((rows, 1), f32), slope=((rows, hidden), low), n2=((rows, D), f32), inv2=((rows, 1), f32)
    )
    return kept, norms


def saved(shapes):
    return {k: (*v, SAVE) for k, v in shapes.items()}


def tail_scratch(rows):
    return dict(sum=pltpu.VMEM((rows, D), jnp.float32), t_send=dma(), t_recv=dma(HELPERS))


def tail(mixed, part, resid, vectors, shifts, weights, next_weights, shut, picks, seq_count, depth, cid):
    rows, hidden = resid.shape[0], shifts.shape[1]
    pieces = layer_pieces(next_weights[0][0].shape[1], next_weights[3][0].shape[1], 0)
    gathering = Gathering(next_weights, pieces, seq_count, depth, (0,))
    sequence = Sequence(rows, seq_count, depth, mixed.dtype)

    def body(refs):
        refs.ready("generic")
        refs.mixed[...] = refs.generic[...]
        greet(("y", "x", "z"), depth, spread=True, collect=True)
        finish = to_first(refs.own_part, refs.mixed, refs.t_send, refs.t_recv)
        gathering.begin(refs)
        sequence.prepare(refs)
        refs.bias = refs.vectors.at[0]
        steps = [finish] + tail_steps(refs)

        def project_now():
            refs.bias = refs.vectors.at[1]
            project_and_send(refs, gathering, sequence, refs.z_low, 0)()

        at = TAIL_PLACES
        run_in_order(
            [(place_, job.begin) for place_, job in zip(at.begins, gathering.jobs, strict=True)]
            + timed_events(gathering.jobs + sequence.jobs, at.arrivals)
            + list(zip(at.steps, steps, strict=True)) + [(at.project, project_now)]
            + list(zip(at.attention, sequence.attention(refs, len(at.attention)), strict=True))
        )
        sequence.end()
        gathering.end()

    kept, norms = tail_results(rows, hidden)
    got = call(
        body, "tail", cid,
        {
            **tail_ins(mixed, part, resid, vectors, shifts, weights),
            **dict(shut=(shut, LOAD), picks=(picks, IN_SMEM)), **gathering.ins(),
        },
        {
            **saved(kept), **saved(norms), **dict(z=((rows, D), jnp.float32, SAVE)), **sequence.outs(),
            **gathering.outs(),
        },
        {**tail_scratch(rows), **sequence.scratch(), **gathering.scratch()},
    )
    return got, gathering.results(got)


def folded(block):
    return jnp.sum(block.reshape(-1, 8, block.shape[1]), axis=0)


def norm_block_back(grad, normed, inv_std, gain):
    scaled = grad * gain
    return (
        scaled
        - jnp.mean(scaled, axis=1, keepdims=True)
        - normed * jnp.mean(scaled * normed, axis=1, keepdims=True)
    ) * inv_std


def back_steps(refs, dz, w_down, w_up, w_out, waits=(lambda: None,) * 3):
    rows, hidden = refs.n2.shape[0], refs.slope.shape[1]
    zero = jnp.zeros((8, D), jnp.float32)

    def row(k, total):
        refs.totals[k : k + 1] = jnp.sum(total, axis=0, keepdims=True)

    def norm_two():
        refs.ready("n2", "inv2", "d_out")

        def act(i, sums):
            at = span(i, ROW_BLOCK)
            grad, normed = dz(at), refs.n2[at]
            back = norm_block_back(grad, normed, refs.inv2[at], refs.bias[7:8])
            refs.work[at] = back
            refs.dr2_low[at] = back.astype(jnp.bfloat16)
            return sums[0] + folded(back), sums[1] + folded(grad), sums[2] + folded(grad * normed)

        sums = lax.fori_loop(0, rows // ROW_BLOCK, act, (zero,) * 3)
        row(4, sums[0]), row(5, sums[1]), row(7, sums[2])
        refs.save("dr2_low")
        refs.ready("slope")
        waits[0]()

    def down(first, count):
        def act(i):
            at = span(first + i, 256)
            du = product_nt(refs.dr2_low[...], w_down[at]) * refs.slope[:, at].astype(jnp.float32)
            refs.du_low[:, at] = du.astype(jnp.bfloat16)
            refs.hidden_totals[0:1, at] = jnp.sum(du, axis=0, keepdims=True)

        over(count, act)

    def up():
        refs.save("du_low")
        waits[1]()

        def act(i):
            at = span(i, 256)
            refs.work[:, at] = refs.work[:, at] + product_nt(refs.du_low[...], w_up[at])

        over(D // 256, act)

    def norm_one():
        refs.ready("n1", "inv1")

        def act(i, sums):
            at = span(i, ROW_BLOCK)
            grad, normed = refs.work[at], refs.n1[at]
            back = norm_block_back(grad, normed, refs.inv1[at], refs.bias[6:7])
            refs.dr1[at] = back
            refs.dr1_low[at] = back.astype(jnp.bfloat16)
            return sums[0] + folded(back), sums[1] + folded(grad), sums[2] + folded(grad * normed)

        sums = lax.fori_loop(0, rows // ROW_BLOCK, act, (zero,) * 3)
        row(2, sums[0]), row(3, sums[1]), row(6, sums[2])
        refs.save("dr1", "dr1_low")

    def out():
        waits[2]()

        def act(i):
            at = span(i, 256)
            refs.cot[:, at] = product_nt(refs.dr1_low[...], w_out[at]).astype(jnp.bfloat16)

        over(D // 256, act)
        refs.save("cot")

    half = hidden // 256 // 2
    return [norm_two, partial(down, 0, half), partial(down, half, half), up, norm_one, out]


def back_outs(rows, hidden):
    f32, low = jnp.float32, jnp.bfloat16
    return dict(
        dr2_low=((rows, D), low, SAVE), du_low=((rows, hidden), low, SAVE), dr1=((rows, D), f32, SAVE),
        dr1_low=((rows, D), low, SAVE), cot=((rows, D), low, SAVE), totals=((8, D), f32, IN_VMEM),
        hidden_totals=((1, hidden), f32, IN_VMEM), part_cot=((SHARE, D), low, ANYWHERE),
    )


def turn(mixed, part, resid, vectors, shifts, weights, d_out, depth, cid):
    rows, hidden = resid.shape[0], shifts.shape[1]

    def body(refs):
        refs.ready("generic")
        refs.mixed[...] = refs.generic[...]
        refs.bias = refs.vectors.at[1]
        greet((), depth, spread=True, collect=True)
        to_first(refs.own_part, refs.mixed, refs.t_send, refs.t_recv)()
        for step in tail_steps(refs):
            step()
        refs.totals[...] = jnp.zeros_like(refs.totals)
        for step in back_steps(refs, lambda at: refs.d_out[at].astype(jnp.float32), refs.w_down, refs.w_up, refs.w_out):
            step()
        to_helpers(refs.cot, refs.part_cot, refs.give, refs.take)()

    kept, norms = tail_results(rows, hidden)
    return call(
        body, "turn", cid,
        {**tail_ins(mixed, part, resid, vectors, shifts, weights), **dict(d_out=(d_out, LOAD))},
        {**saved(kept), **back_outs(rows, hidden)},
        {
            **tail_scratch(rows), **{k: pltpu.VMEM(*v) for k, v in norms.items()},
            **dict(work=pltpu.VMEM((rows, D), jnp.float32), give=dma(HELPERS), take=dma()),
        },
    )


def chunked(shape):
    rows, columns = shape
    width = columns
    while rows * width > 24 * 1024 and width % 256 == 0:
        width //= 2
    if rows * width > 24 * 1024 and width % 384 == 0:
        width //= 3
    return width, columns // width


def total_of(own, kids, window):
    total = own[window].astype(jnp.float32)
    for ref, cond in kids:
        if cond is None:
            total = total + ref[window].astype(jnp.float32)
        else:
            total = total + lax.cond(
                cond,
                lambda ref=ref: ref[window].astype(jnp.float32),
                lambda total=total: jnp.zeros_like(total),
            )
    return total


def over_chunks(shape, act):
    if len(shape) == 3:
        size = shape[1] // 2

        def part(i, carry):
            act((i // 2, span(i % 2, size)))
            return carry

        lax.fori_loop(0, 2 * shape[0], part, 0)
        return
    width, count = chunked(shape)

    def step(i, carry):
        act((slice(None), pl.ds(pl.multiple_of(i * width, width), width)))
        return carry

    lax.fori_loop(0, count, step, 0)


def add_up(own, kids, into):
    def act(window):
        into[window] = total_of(own, kids, window).astype(into.dtype)

    over_chunks(into.shape, act)


def write_total(target):
    def finish(own, kids):
        def act(window):
            target[window] = total_of(own, kids, window).astype(target.dtype)

        over_chunks(target.shape, act)

    return finish


def weight_grad(left, right, into, first=0):
    share = into.shape[1]
    count = 384 // share

    def act(i):
        across = into.shape[2] // 256
        rows, at = i // across, span(i % across, 256)
        acc = product_tn(left[:, span(rows, 384)], right[:, span(i % across, 256, first)])
        for k in range(count):
            into[rows * count + k, :, at] = acc[k * share : (k + 1) * share].astype(into.dtype)

    over(left.shape[1] // 384 * (into.shape[2] // 256), act)


class Sums:
    def __init__(self, tag, pieces, depth):
        self.tag, self.pieces, self.depth = tag, pieces, depth

    def name(self, what, k):
        return "%s_%s%d" % (self.tag, what, k)

    def scratch(self):
        made = {}
        for k, (_, _, shape, _, order, dtype) in enumerate(self.pieces):
            edges = Reduce.slots(order, self.depth)[1]
            made[self.name("box", k)] = pltpu.VMEM((edges,) + shape, dtype)
            made[self.name("send", k)] = dma(2 * len(offsets(order, self.depth)))
            made[self.name("recv", k)] = dma(edges)
        return made

    def prepare(self, refs):
        self.jobs = []
        for k, (source, far, _, target, order, _) in enumerate(self.pieces):
            box, send, recv = (getattr(refs, self.name(what, k)) for what in ("box", "send", "recv"))
            job = Reduce(partial(source, refs), partial(far, refs), box, order, self.depth, send, recv)
            self.jobs.append((job, target(refs)))

    def start(self, k):
        job, _ = self.jobs[k]
        for t in job.marks:
            job.start(t)

    def timed(self, places):
        timed = []
        for k, ((job, finish), at) in enumerate(zip(self.jobs, places, strict=True)):
            timed.append((at[0], partial(self.start, k)))
            acts = [partial(job.handle, t, add_up, finish) for t in job.marks]
            timed += zip(at[1:], acts, strict=True)
        return timed

    def end(self):
        for job, _ in self.jobs:
            job.drain()


def weight_sums(windows, depth, n_dev, dtypes):
    number = number_in(depth)

    def piece(which, row, rows, column, columns_, order):
        window = (pl.ds(row, rows), pl.ds(column, columns_))

        def source(refs, p):
            return getattr(refs, "grad%d" % which).at[(number(p),) + window]

        return (
            source,
            source,
            (rows, columns_),
            lambda refs: write_total(getattr(refs, "owned%d" % which).at[window]),
            order,
            dtypes[which],
        )

    return Sums("w", [piece(*w) for w in windows], depth)


def sum_rows(dk, dv, dq, part_dq, held, grads, seq_count, depth, cid):
    rows, hidden, n_dev = dq.shape[0], grads.du_low.shape[1], seq_count * depth
    low, f32 = dk.dtype, jnp.float32
    share, count = D // n_dev, PAIRS // 2

    def piece(i):
        window = pl.ds(i % 2 * count, count)

        def target(refs):
            def finish(own, kids):
                def act(at):
                    lanes = pl.ds(pl.multiple_of((PAIRS + i * count + at[0]) * WIDE, WIDE), WIDE)
                    refs.proj[at[1], lanes] = total_of(own, kids, at).astype(low)

                over_chunks((count, rows, WIDE), act)

            return finish

        return (
            lambda refs, p: (refs.dk, refs.dv)[i // 2].at[number_in_sequence(p), window],
            lambda refs, p: (refs.far_dk, refs.far_dv)[i // 2].at[number_in_sequence(p), window],
            (count, rows, WIDE),
            target,
            (X_Y, Y_X)[i % 2],
            low,
        )

    by_rows = Sums("r", [piece(i) for i in range(4)], depth)
    windows = [(1, 0, share, 0, D, X_Y_Z), (2, 0, share, 0, hidden // 2, Y_X_Z)]
    by_weights = weight_sums(windows, depth, n_dev, {1: low, 2: low})

    def body(refs):
        refs.ready("dq")
        refs.proj[:, 0:D] = refs.dq[...]
        greet(("y", "x", "z"), depth, collect=True)
        by_rows.prepare(refs)
        by_weights.prepare(refs)
        ends = [to_first(refs.part, refs.proj.at[:, pl.ds(0, D)], refs.t_send, refs.t_recv)]
        at = ROWS_PLACES

        def grad(left, right, into):
            refs.ready(left, right)
            weight_grad(getattr(refs, left), getattr(refs, right), into)

        first_block = min(place for places in at.rows for place in places[1:])
        run_in_order(
            by_rows.timed(at.rows) + by_weights.timed(at.weights)
            + [
                (at.grads[0], partial(grad, "mixed", "dr1_low", refs.grad1)),
                (at.grads[1], partial(grad, "y_low", "du_low", refs.grad2)),
                (first_block - 0.5, partial(refs.ready, "dk", "dv")),
                (at.collect, ends[0]),
            ]
        )
        by_rows.end()
        by_weights.end()

        def act(i, sums):
            at = span(i, ROW_BLOCK)
            return tuple(
                total + folded(refs.proj[at, pl.ds(first, D)].astype(f32)) for total, first in zip(sums, (0, 2 * D))
            )

        zero = jnp.zeros((8, D), f32)
        sums = lax.fori_loop(0, rows // ROW_BLOCK, act, (zero, zero))
        refs.totals[...] = jnp.zeros_like(refs.totals)
        for k in range(2):
            refs.totals[k : k + 1] = jnp.sum(sums[k], axis=0, keepdims=True)

    return call(
        body, "sum_rows", cid,
        dict(
            dq=(dq, LOAD), part=(part_dq, ANYWHERE), mixed=(held.mixed, LOAD), dr1_low=(grads.dr1_low, LOAD),
            dk=(dk, LOAD), dv=(dv, LOAD), y_low=(held.y_low, LOAD), du_low=(grads.du_low, LOAD),
        ),
        dict(
            proj=((rows, 3 * D), low, IN_VMEM), totals=((8, D), f32, IN_VMEM), owned1=((share, D), f32, IN_VMEM),
            owned2=((share, hidden // 2), f32, IN_VMEM),
        ),
        {
            **dict(
                grad1=pltpu.VMEM((n_dev, share, D), low), grad2=pltpu.VMEM((n_dev, share, hidden // 2), low),
                t_send=dma(), t_recv=dma(HELPERS),
            ),
            **by_rows.scratch(), **by_weights.scratch(),
        },
    )


def sum_weights(held, low_in, proj, vectors, w_qkv, small, below, n_dev, depth, cid):
    rows, hidden = proj.shape[0], held.du_low.shape[1]
    low, f32 = jnp.bfloat16, jnp.float32
    share, tall = D // n_dev, hidden // n_dev
    shapes = {0: (share, 3 * D), 2: (share, hidden // 2), 3: (tall, D)}
    cut = tall * 2 // 3
    windows = [
        (3, 0, cut, 0, D, Z_X_Y),
        (3, cut, tall - cut, 0, D, Z_Y_X),
        (2, 0, share, 0, hidden // 2, Y_X_Z),
        (0, 0, share, 0, 3 * D, Z_Y_X),
    ]
    ins = dict(low_in=(low_in, LOAD), proj=(proj, LOAD))
    ins.update({"up_" + k: (getattr(held, k), LOAD) for k in ("y_low", "du_low", "a_low", "dr2_low")})
    ins.update(up_dr1=(held.dr1, LOAD), w_qkv=(w_qkv, ANYWHERE))
    outs = {"owned%d" % i: (s, f32, IN_VMEM) for i, s in shapes.items()}
    scratch = {"grad%d" % i: pltpu.VMEM((n_dev,) + s, low) for i, s in shapes.items()}
    if small is not None:
        windows.append((4, 0, small.shape[1], 0, small.shape[2], Z_Y_X))
        ins.update(grad4=(small, IN_VMEM))
        outs.update(owned4=(small.shape[1:], f32, IN_VMEM))
    by_weights = weight_sums(windows, depth, n_dev, {0: low, 2: low, 3: low, 4: f32})
    scratch.update(by_weights.scratch())
    scratch.update(load=dma(4), wide=pltpu.VMEM((D, hidden), low))
    if below is not None:
        below_weights, below_held = below
        ins.update({k: (getattr(below_held, k), LOAD) for k in ("n2", "inv2", "slope", "n1", "inv1")})
        ins.update(
            vectors=(vectors, IN_VMEM), w_out=(below_weights[1], ANYWHERE), w_up=(below_weights[2], ANYWHERE),
            w_down=(below_weights[3], ANYWHERE),
        )
        outs.update(back_outs(rows, hidden))
        scratch.update(
            tall=pltpu.VMEM((hidden, D), low), work=pltpu.VMEM((rows, D), f32), give=dma(HELPERS), take=dma()
        )
    if below is None:
        outs.update(dx=((rows, D), f32, SAVE))
    else:
        scratch.update(dx=pltpu.VMEM((rows, D), f32))

    def body(refs):
        v_qkv = refs.wide.at[:, pl.ds(0, 3 * D)]
        load_qkv = pltpu.make_async_copy(refs.w_qkv, v_qkv, refs.load.at[0])
        load_qkv.start()
        if below is not None:
            refs.bias = refs.vectors.at[0]
            refs.totals[...] = jnp.zeros_like(refs.totals)
            load_down = pltpu.make_async_copy(refs.w_down, refs.tall, refs.load.at[1])
            load_down.start()
            load_up = pltpu.make_async_copy(refs.w_up, refs.wide, refs.load.at[2])
            load_out = pltpu.make_async_copy(refs.w_out, refs.tall.at[pl.ds(0, D)], refs.load.at[3])
        greet(("y", "x", "z"), depth, spread=below is not None)
        by_weights.prepare(refs)
        def dx():
            load_qkv.wait()
            refs.ready("proj", "up_dr1")

            def act(i):
                at = span(i, 256)
                refs.dx[:, at] = refs.up_dr1[:, at] + product_nt(refs.proj[...], v_qkv[at])

            over(D // 256, act)
            refs.save("dx")
            if below is not None:
                load_up.start()

        steps = [dx]
        if below is not None:

            def up_ready():
                load_out.start()
                load_up.wait()

            steps += back_steps(
                refs, lambda at: refs.dx[at], refs.tall, refs.wide, refs.tall, [load_down.wait, up_ready, load_out.wait]
            )
            ends = []
            steps.append(lambda: ends.append(to_helpers(refs.cot, refs.part_cot, refs.give, refs.take)))
        at = LAST_PLACES if below is None else BELOW_PLACES

        def grad(left, right, into, column=0):
            refs.ready(left, right)
            weight_grad(getattr(refs, left), getattr(refs, right), into, column)

        run_in_order(
            by_weights.timed(at.weights)
            + [
                (at.grads[0], partial(grad, "up_a_low", "up_dr2_low", refs.grad3)),
                (at.grads[1], partial(grad, "up_y_low", "up_du_low", refs.grad2, hidden // 2)),
                (at.grads[2], partial(grad, "low_in", "proj", refs.grad0)),
            ]
            + list(zip(at.steps, steps, strict=True))
        )
        by_weights.end()
        if below is not None:
            ends[0]()

    return call(body, "sum_weights", cid, ins, outs, scratch)


def norm_rows(resid, gain, shift):
    center = resid - jnp.mean(resid, axis=-1, keepdims=True)
    inv_std = lax.rsqrt(jnp.mean(center * center, axis=-1, keepdims=True) + layer_eps)
    normed = center * inv_std
    return (normed * gain + shift, normed, inv_std)


def norm_back(grad_rows, normed, inv_std, gain):
    scaled = grad_rows * gain
    return (
        scaled
        - jnp.mean(scaled, axis=-1, keepdims=True)
        - normed * jnp.mean(scaled * normed, axis=-1, keepdims=True)
    ) * inv_std


def dot32(a, b):
    return jnp.dot(a, b, preferred_element_type=jnp.float32)


def small_vectors(small, n_dev):
    small = small.astype(jnp.float32).T
    vectors = jnp.concatenate(
        [small[: 6 * L].reshape(L, 6, D), small[6 * L : 8 * L].reshape(L, 2, D)], axis=1
    )
    hidden_shifts = small[8 * L : 12 * L].reshape(L, 4, n_dev, D // n_dev)
    return vectors, jnp.swapaxes(hidden_shifts, 1, 2).reshape(L, -1)


def shut_keys(segs_all, segments, first, blocks_here):
    length = segs_all.shape[0]
    padding = jnp.full((BLK,), -1, jnp.int32)
    segs_all = jnp.concatenate([padding, segs_all, padding]).reshape(-1, BLK)
    segs_near = lax.dynamic_slice_in_dim(segs_all, first, blocks_here + 2, axis=0)
    seg_window = jnp.concatenate([segs_near[j : j + blocks_here] for j in range(3)], axis=1)
    spot = (first - 1 + jnp.arange(blocks_here)[:, None]) * BLK + jnp.arange(3 * BLK)[None, :]
    inside = (spot >= SHARED) & (spot < length)
    own = segments.reshape(blocks_here, 1, BLK)
    allowed = inside[:, :, None] & (seg_window[:, :, None] == jnp.concatenate([own, own], axis=2))
    return jnp.where(allowed, 0.0, masked_score)


def small_by_owner(vectors, hidden, n_dev):
    rows = jnp.moveaxis(vectors.reshape(8, n_dev, -1), 1, 0)
    rows = jnp.concatenate([rows, hidden.reshape(n_dev, 8, -1)], axis=2)
    return jnp.pad(rows, ((0, 0), (0, 0), (0, 128 - rows.shape[2])))


def small_outputs(narrow, piece, hidden):
    return (
        narrow[:, 6:8, :piece],
        narrow[:, 0:6, :piece],
        narrow[:, :, piece : piece + hidden // 8].reshape(L, -1),
    )


def share_of(rows):
    first = lax.all_gather(rows[:SHARED], SEQ, axis=0)[0]
    own = jnp.minimum(lax.axis_index(SEQ), HELPERS - 1) * SHARE
    return lax.dynamic_slice_in_dim(first, own, SHARE, axis=0)


def rows_of_all(kv, queries):
    kv = jnp.moveaxis(kv.reshape(-1, 2 * PAIRS, WIDE), 1, 0)
    return lax.all_gather(kv, SEQ, axis=0), share_of(queries)


def with_shared_rows(part, rows):
    first = lax.all_gather(part, SEQ, axis=0)[:HELPERS].reshape(SHARED, D)
    head_rows = jnp.where(lax.axis_index(SEQ) == 0, first.astype(rows.dtype), rows[:SHARED])
    return jnp.concatenate([head_rows, rows[SHARED:]], axis=0)


def on_any_slice(
    layer_input, segments, rand_blocks, w_qkv, w_out, w_up, w_down, gains, biases, up_bias, d_out
):
    seq_count, depth = lax.axis_size(SEQ), lax.axis_size(BATCH)
    n_dev = seq_count * depth
    own_index = lax.axis_index(SEQ)
    rows = layer_input.shape[1]
    blocks_here, length = rows // BLK, rows * seq_count
    picks = rand_blocks.reshape(-1)
    first = (own_index * blocks_here).reshape(1)

    piece = D // n_dev
    small = jnp.concatenate(
        [biases.reshape(-1, piece), gains.reshape(-1, piece), up_bias.reshape(-1, piece)], axis=0
    ).T
    small = lax.all_gather(small, (SEQ, BATCH), axis=0, tiled=True)
    segs_all = lax.all_gather(segments[0], SEQ, axis=0, tiled=True)
    weights = [
        [lax.all_gather(w[layer], (SEQ, BATCH), axis=0, tiled=True) for w in (w_qkv, w_out, w_up, w_down)]
        for layer in range(L)
    ]
    vectors, hidden_shifts = small_vectors(small, n_dev)
    shut = shut_keys(segs_all, segments, first[0], blocks_here)

    resid = layer_input[0].astype(jnp.float32)
    low = layer_input[0]
    saved = []
    for layer in range(L):
        mat_qkv, mat_out, mat_up, mat_down = weights[layer]
        bias = vectors[layer]
        proj = dot32(low, mat_qkv)
        queries = (proj[:, :D] + bias[0]).astype(jnp.bfloat16)
        kv = jnp.concatenate([proj[:, D : 2 * D], proj[:, 2 * D :] + bias[1]], axis=1).astype(jnp.bfloat16)
        kv_all, part = rows_of_all(kv, queries)
        mixed, part_mixed, *logs = attend(picks, first, queries, kv_all, shut, part)
        mixed = with_shared_rows(part_mixed, mixed)
        resid_one = resid + dot32(mixed, mat_out) + bias[2]
        middle, normed_one, inv_one = norm_rows(resid_one, bias[6], bias[3])
        middle_low = middle.astype(jnp.bfloat16)
        hidden = dot32(middle_low, mat_up) + hidden_shifts[layer]
        active = jax.nn.gelu(hidden, approximate=False).astype(jnp.bfloat16)
        resid_two = middle + dot32(active, mat_down) + bias[4]
        result, normed_two, inv_two = norm_rows(resid_two, bias[7], bias[5])
        saved.append(
            (low, queries, kv_all, part, logs, mixed, normed_one, inv_one, middle_low, hidden, active, normed_two, inv_two)
        )
        resid = result
        low = resid.astype(jnp.bfloat16)

    grad = d_out[0].astype(jnp.float32)
    owned = [None] * L
    for layer in reversed(range(L)):
        (low_in, queries, kv_all, part, logs, mixed, normed_one, inv_one, middle_low, hidden, active, normed_two, inv_two) = saved[layer]
        mat_qkv, mat_out, mat_up, mat_down = weights[layer]
        bias = vectors[layer]
        gain_two_grad = jnp.sum(grad * normed_two, axis=0)
        shift_two_grad = jnp.sum(grad, axis=0)
        grad_two = norm_back(grad, normed_two, inv_two, bias[7])
        grad_two_low = grad_two.astype(jnp.bfloat16)
        down_grad = product_tn(active, grad_two_low)
        active_grad = product_nt(grad_two_low, mat_down)
        hidden_grad = jax.vjp(partial(jax.nn.gelu, approximate=False), hidden)[1](active_grad)[0]
        hidden_grad_low = hidden_grad.astype(jnp.bfloat16)
        up_grad = product_tn(middle_low, hidden_grad_low)
        middle_grad = grad_two + product_nt(hidden_grad_low, mat_up)
        gain_one_grad = jnp.sum(middle_grad * normed_one, axis=0)
        shift_one_grad = jnp.sum(middle_grad, axis=0)
        grad_one = norm_back(middle_grad, normed_one, inv_one, bias[6])
        grad_one_low = grad_one.astype(jnp.bfloat16)
        out_grad = product_tn(mixed, grad_one_low)
        cot = product_nt(grad_one_low, mat_out).astype(jnp.bfloat16)
        part_cot = share_of(cot)
        part_cot = jnp.where(own_index < HELPERS, part_cot, 0)
        dq, dk, dv, part_dq = attend_back(picks, first, queries, kv_all, shut, cot, part, part_cot, *logs)
        dq = with_shared_rows(part_dq, dq)
        dkv = jnp.concatenate([dk, dv], axis=1).astype(jnp.float32)
        dkv = lax.psum_scatter(dkv, SEQ, scatter_dimension=0)
        dkv = jnp.moveaxis(dkv, 0, 1).reshape(rows, 2 * D)
        proj_grad = jnp.concatenate([dq, dkv.astype(jnp.bfloat16)], axis=1)
        qkv_grad = product_tn(low_in, proj_grad)
        small_rows = jnp.stack(
            [
                jnp.sum(dq.astype(jnp.float32), axis=0),
                jnp.sum(dkv[:, D:], axis=0),
                jnp.sum(grad_one, axis=0),
                shift_one_grad,
                jnp.sum(grad_two, axis=0),
                shift_two_grad,
                gain_one_grad,
                gain_two_grad,
            ]
        )
        small_rows = small_by_owner(small_rows, jnp.sum(hidden_grad, axis=0), n_dev)
        owned[layer] = [
            lax.psum_scatter(a, (SEQ, BATCH), scatter_dimension=0, tiled=True)
            for a in (qkv_grad, out_grad, up_grad, down_grad, small_rows)
        ]
        owned[layer][4] = owned[layer][4][0]
        grad = grad_one + product_nt(proj_grad, mat_qkv)
    stacked = [jnp.stack([owned[layer][i] for layer in range(L)]) for i in range(5)]
    return (low[None], grad[None], *stacked[:4], *small_outputs(stacked[4], piece, up_bias.shape[1]))


def assemble(wanted):
    parts = [part for _, parts in wanted for part in parts]

    def body(*refs):
        sources, targets = list(refs[: len(parts)]), refs[len(parts) :]
        for target, (_, held) in zip(targets, wanted):
            for array, layer, column in held:
                target[layer, :, column : column + array.shape[1]] = sources.pop(0)[...]

    return pl.pallas_call(
        body,
        out_shape=[jax.ShapeDtypeStruct(shape, jnp.float32) for shape, _ in wanted],
        in_specs=[IN_VMEM] * len(parts),
        out_specs=[IN_VMEM] * len(wanted),
        compiler_params=pltpu.CompilerParams(vmem_limit_bytes=VMEM_LIMIT),
        name="assemble",
    )(*[array for array, _, _ in parts])


def on_pairs(
    layer_input, segments, rand_blocks, w_qkv, w_out, w_up, w_down, gains, biases, up_bias, d_out
):
    seq_count, depth = lax.axis_size(SEQ), lax.axis_size(BATCH)
    n_dev = seq_count * depth
    rows, hidden = layer_input.shape[1], up_bias.shape[1] * n_dev
    blocks_here = rows // BLK
    picks = rand_blocks.reshape(-1)
    first = (lax.axis_index(SEQ) * blocks_here).reshape(1)
    piece = D // n_dev

    small = jnp.concatenate(
        [biases.reshape(-1, piece), gains.reshape(-1, piece), up_bias.reshape(-1, piece)], axis=0
    ).T
    small = jnp.pad(small, ((0, 0), (0, 128 - small.shape[1])))
    segs = jnp.pad(segments.reshape(-1, 128), ((0, 8 - rows // 128), (0, 0)))

    def flat(slabs):
        return [w.reshape(-1, w.shape[2]) for w in slabs]

    places = jnp.stack([picks // blocks_here, picks % blocks_here])

    def attention_back(got, back):
        return attend_back(
            picks, first, got.q, got.every.reshape(seq_count, 2 * PAIRS, rows, WIDE), shut, back.cot, got.part, back.part_cot, got.log, got.plog
        )

    x = layer_input[0]
    layers = [[(w, layer) for w in (w_qkv, w_out, w_up, w_down)] for layer in range(L)]
    own_segs = segments.reshape(blocks_here, BLK).astype(jnp.float32)
    own_segs = jnp.concatenate([own_segs, own_segs], axis=1)
    head_one, weights_one = first_head(x, small, segs, own_segs, places, layers[0], seq_count, depth, 0)
    weights_one = flat(weights_one)
    vectors = head_one.vectors
    shifts = head_one.table.reshape(L, 4, n_dev, piece)
    shifts = jnp.swapaxes(shifts, 1, 2).reshape(L, 1, hidden)
    shut = head_one.shut
    rows_one, weights_two = tail(
        head_one.o, head_one.po, x, vectors, shifts[0], weights_one, layers[1], shut, places, seq_count, depth, 1
    )
    weights_two = flat(weights_two)
    middle = rows_one.z_low
    rows_two = turn(rows_one.o, rows_one.po, rows_one.z, vectors, shifts[1], weights_two, d_out[0], depth, 2)
    dq, dk, dv, part = attention_back(rows_one, rows_two)
    sums_two = sum_rows(dk, dv, dq, part, rows_two, rows_two, seq_count, depth, 3)
    back_one = sum_weights(
        rows_two, middle, sums_two.proj, vectors, weights_two[0], None, (weights_one, rows_one), n_dev, depth, 4
    )
    dq, dk, dv, part = attention_back(head_one, back_one)
    sums_one = sum_rows(dk, dv, dq, part, rows_one, back_one, seq_count, depth, 5)
    small = jnp.concatenate(
        [
            small_by_owner(back.totals + sums.totals, back.hidden_totals[0], n_dev)
            for back, sums in ((back_one, sums_one), (rows_two, sums_two))
        ],
        axis=1,
    )
    last = sum_weights(
        SimpleNamespace(**{**vars(rows_one), **vars(back_one)}),
        x, sums_one.proj, None, weights_one[0], small, None, n_dev, depth, 6,
    )
    whole_outputs = assemble(
        [
            ((L, piece, 3 * D), [(last.owned0, 0, 0), (back_one.owned0, 1, 0)]),
            ((L, piece, D), [(sums_one.owned1, 0, 0), (sums_two.owned1, 1, 0)]),
            (
                (L, piece, hidden),
                [
                    (sums_one.owned2, 0, 0), (last.owned2, 0, hidden // 2),
                    (sums_two.owned2, 1, 0), (back_one.owned2, 1, hidden // 2),
                ],
            ),
            ((L, hidden // n_dev, D), [(last.owned3, 0, 0), (back_one.owned3, 1, 0)]),
            ((1, rows, D), [(last.dx, 0, 0)]),
        ]
    )
    return (
        rows_two.z_low[None],
        whole_outputs[4],
        *whole_outputs[:4],
        *small_outputs(last.owned4.reshape(L, 8, 128), piece, up_bias.shape[1]),
    )


def solution(mesh):
    placed = (
        P(BATCH, SEQ, None),
        P(BATCH, SEQ),
        P(BATCH, SEQ, None, None),
        P(None, (SEQ, BATCH), None),
        P(None, (SEQ, BATCH), None),
        P(None, (SEQ, BATCH), None),
        P(None, (SEQ, BATCH), None),
        P(None, None, (SEQ, BATCH)),
        P(None, None, (SEQ, BATCH)),
        P(None, (SEQ, BATCH)),
        P(BATCH, SEQ, None),
    )
    return jax.shard_map(
        on_pairs if mesh.shape[SEQ] == 8 and mesh.shape[BATCH] == 4 else on_any_slice,
        mesh=mesh,
        in_specs=placed,
        out_specs=(
            P(BATCH, SEQ, None),
            P(BATCH, SEQ, None),
            P(None, (SEQ, BATCH), None),
            P(None, (SEQ, BATCH), None),
            P(None, (SEQ, BATCH), None),
            P(None, (SEQ, BATCH), None),
            P(None, None, (SEQ, BATCH)),
            P(None, None, (SEQ, BATCH)),
            P(None, (SEQ, BATCH)),
        ),
        check_vma=False,
    )
```

```python
import itertools
from functools import partial
from types import SimpleNamespace

import jax
import jax.numpy as jnp
from jax import lax
from jax.experimental import pallas as pl
from jax.experimental.pallas import tpu as pltpu
from jax.sharding import PartitionSpec as P

MESH = pl.DeviceIdType.MESH
SEQ, BATCH = "seq", "batch"


HEAD_PLACES = SimpleNamespace(
    begins=(1, 4, 3, 2, 0, 64, 61, 56, 14),
    arrivals=(
        (8, 9, 21, 10, 22, 20, 36, 23, 37, 38, 55, 39, 51, 52, 62),
        (15, 16, 27),
        (19, 17, 29, 18, 30, 31, 45, 32, 57, 46, 58, 47, 59, 60, 69),
        (11, 12, 44, 13, 24, 25, 40, 26, 41, 42, 53, 43, 75, 54, 63),
        (5, 6, 28, 7, 33, 34, 65, 35, 66, 67, 86, 68, 87, 88, 106),
        (81, 82, 136, 83, 107, 108, 131, 100, 130, 132, 143, 118, 144, 142, 150),
        (78, 79, 103, 80, 104, 105, 127, 102, 128, 129, 145, 125, 140, 141, 149),
        (76, 99, 119, 74, 96, 117, 135, 77, 97, 122, 126, 98, 120, 138, 146),
        (48, 70, 111, 50, 71, 91, 121, 49, 72, 92, 114, 73, 90, 115, 133),
        (113, 109, 134),
        (123, 124, 139),
        (94, 95, 116),
        (110, 112, 137),
    ),
    project=84,
    attention=(147, 148, 151),
)
TAIL_PLACES = SimpleNamespace(
    begins=(1, 2, 0, 14, 38, 43, 4),
    arrivals=(
        (10, 11, 19, 12, 20, 21, 61, 22, 42, 33, 47, 34, 49, 48, 70),
        (32, 13, 23, 17, 26, 24, 46, 25, 35, 36, 52, 37, 53, 54, 71),
        (6, 7, 27, 8, 28, 29, 62, 31, 50, 56, 74, 51, 72, 75, 92),
        (39, 40, 63, 41, 64, 65, 93, 66, 86, 87, 108, 88, 129, 110, 128),
        (55, 59, 80, 60, 111, 89, 105, 79, 118, 98, 122, 101, 123, 124, 137),
        (67, 81, 95, 68, 82, 106, 125, 69, 83, 112, 126, 84, 107, 127, 136),
        (57, 78, 100, 73, 96, 102, 120, 58, 99, 113, 121, 91, 103, 119, 132),
        (97, 104, 130),
        (114, 115, 135),
        (133, 117, 134),
        (116, 109, 131),
    ),
    steps=(3, 5, 9, 15, 16, 18, 30, 44, 45),
    project=76,
    attention=(138, 139, 140),
)
ROWS_PLACES = SimpleNamespace(
    rows=(
        (0, 3, 4, 17, 53),
        (1, 7, 9, 25, 45),
        (11, 23, 21, 43, 52),
        (6, 13, 30, 38, 54),
    ),
    weights=(
        (5, 10, 16, 14, 15, 8, 19, 18, 12, 24, 20, 34, 31, 22, 32, 46, 55),
        (27, 28, 29, 37, 33, 39, 36, 41, 35, 47, 42, 44, 40, 49, 50, 48, 56),
    ),
    grads=(2, 26),
    collect=51,
)
BELOW_PLACES = SimpleNamespace(
    weights=(
        (9, 12, 11, 14, 47, 36, 45, 27, 66, 48, 20, 52, 70, 54, 61, 73, 77),
        (10, 37, 49, 24, 58, 26, 33, 69, 68, 30, 32, 64, 72, 40, 63, 75, 78),
        (6, 22, 18, 23, 31, 21, 39, 29, 42, 38, 43, 46, 60, 53, 62, 74, 76),
        (1, 4, 3, 2, 15, 13, 7, 19, 41, 17, 44, 28, 59, 16, 55, 67, 71),
    ),
    grads=(8, 5, 0),
    steps=(25, 34, 35, 50, 51, 56, 57, 65),
)
LAST_PLACES = SimpleNamespace(
    weights=(
        (22, 31, 32, 33, 61, 36, 57, 65, 74, 41, 63, 67, 79, 58, 72, 84, 88),
        (21, 43, 45, 47, 62, 46, 48, 75, 77, 51, 64, 78, 80, 56, 83, 81, 87),
        (11, 29, 34, 40, 49, 50, 44, 37, 52, 53, 55, 60, 68, 66, 70, 82, 86),
        (9, 13, 15, 18, 30, 35, 23, 42, 54, 25, 27, 59, 71, 39, 69, 76, 85),
        (1, 2, 5, 12, 14, 3, 4, 17, 24, 6, 7, 16, 28, 8, 19, 26, 38),
    ),
    grads=(20, 10, 0),
    steps=(73,),
)


def place():
    s = lax.axis_index(SEQ)
    return {"y": s // 4, "x": (s // 2) % 2, "c": s % 2, "z": lax.axis_index(BATCH)}


def device_of(p):
    return ((p["y"] * 2 + p["x"]) * 2 + p["c"], p["z"])


def flipped(p, axis):
    return {**p, axis: 1 - p[axis]}


def at_depth(p, z):
    return {**p, "z": z}


def number_in(depth):
    return lambda p: device_of(p)[0] * depth + p["z"]


def number_in_sequence(p):
    return device_of(p)[0]


def when(cond, action):
    if cond is None:
        action()
    else:
        pl.when(cond)(action)


def ranked(z, rank, depth):
    near = [sorted(range(depth), key=lambda q: (abs(q - k), q))[rank] for k in range(depth)]
    return sum(jnp.where(z == k, near[k], 0) for k in range(depth))


def offsets(order, depth):
    return list(itertools.product(*[range(depth if a == "z" else 2) for a in order]))


def target_of(order, offset, depth, me):
    p = me
    for axis, d in zip(order, offset):
        if d:
            p = at_depth(p, ranked(me["z"], d, depth)) if axis == "z" else flipped(p, axis)
    return p


def last_move(offset):
    return max([-1] + [i for i, d in enumerate(offset) if d])


def greet(axes, depth, spread=False, collect=False):
    me = place()
    barrier = pltpu.get_barrier_semaphore()

    def signal(device):
        pl.semaphore_signal(barrier, inc=1, device_id=device, device_id_type=MESH)

    count = 0
    for axis in axes + ("c",):
        if axis == "z":
            for step in (1, -1):
                peer = at_depth(me, me["z"] + step)
                cond = (peer["z"] >= 0) & (peer["z"] < depth)
                when(cond, lambda peer=peer: signal(device_of(peer)))
                count = count + cond.astype(jnp.int32)
        else:
            signal(device_of(flipped(me, axis)))
            count = count + 1
    if spread or collect:
        seq, z = lax.axis_index(SEQ), lax.axis_index(BATCH)
        if spread:
            when(seq != 0, lambda: signal((0, z)))
            count = count + jnp.where(seq == 0, HELPERS - 1, 0)
        if collect:

            @pl.when(seq == 0)
            def _():
                for j in range(1, HELPERS):
                    signal((j, z))

            count = count + jnp.where(seq == 0, 0, 1)
    pl.semaphore_wait(barrier, count)


class Gather:
    def __init__(self, source, target, number, order, depth, send, recv, send_at):
        self.source, self.target, self.number = source, target, number
        self.order, self.depth, self.send, self.recv = order, depth, send, recv
        self.send_at = send_at
        self.me = place()
        self.sent = []

    @staticmethod
    def sends(order, depth):
        return sum(len(order) + 2 - last_move(t) for t in offsets(order, depth))

    def onward(self, offset):
        last = last_move(offset)
        z = self.me["z"]
        moves = []
        if last >= 0 and self.order[last] == "z":
            source = ranked(z, offset[last], self.depth)
            peer = jnp.where(source < z, z + 1, z - 1)
            moves.append((at_depth(self.me, peer), (peer >= 0) & (peer < self.depth)))
        for axis in self.order[last + 1 :]:
            if axis == "z":
                moves.append((at_depth(self.me, z + 1), z + 1 < self.depth))
                moves.append((at_depth(self.me, z - 1), z > 0))
            else:
                moves.append((flipped(self.me, axis), None))
        moves.append((flipped(self.me, "c"), None))
        return moves

    def arrival(self, p):
        ref = self.target(p)
        return pltpu.make_async_remote_copy(
            src_ref=ref, dst_ref=ref, send_sem=self.send.at[0], recv_sem=self.recv.at[self.number(p)],
            device_id=device_of(self.me), device_id_type=MESH,
        )

    def handle(self, offset):
        p = target_of(self.order, offset, self.depth, self.me)
        own = not any(offset)
        if not own:
            self.arrival(p).wait_recv()
        for peer, cond in self.onward(offset):
            copy = pltpu.make_async_remote_copy(
                src_ref=self.source if own else self.target(p), dst_ref=self.target(p),
                send_sem=self.send.at[self.send_at], recv_sem=self.recv.at[self.number(p)],
                device_id=device_of(peer), device_id_type=MESH,
            )
            when(cond, copy.start)
            self.sent.append((cond, self.send_at))
            self.send_at += 1

    def begin(self):
        self.handle((0,) * len(self.order))

    def events(self, places):
        marks = [t for t in offsets(self.order, self.depth) if any(t)]
        return [(at, partial(self.handle, t)) for at, t in zip(places, marks, strict=True)]

    def siblings(self):
        for t in offsets(self.order, self.depth):
            self.arrival(flipped(target_of(self.order, t, self.depth, self.me), "c")).wait_recv()

    def drain(self):
        for cond, slot in self.sent:
            copy = pltpu.make_async_remote_copy(
                src_ref=self.source, dst_ref=self.target(self.me), send_sem=self.send.at[slot],
                recv_sem=self.recv.at[self.number(self.me)], device_id=device_of(self.me), device_id_type=MESH,
            )
            when(cond, copy.wait_send)


class Reduce:
    def __init__(self, partial_of, far_partial_of, inbox, order, depth, send, recv):
        self.partial_of, self.far_partial_of, self.inbox = partial_of, far_partial_of, inbox
        self.order, self.depth, self.send, self.recv = order, depth, send, recv
        self.me = place()
        self.base, _ = self.slots(order, depth)
        self.marks = sorted(offsets(order, depth), key=lambda t: (-sum(t), t))
        self.sent = []

    @staticmethod
    def split(order, offset):
        if "z" not in order:
            return offset, 0
        i = order.index("z")
        return offset[:i] + (0,) + offset[i + 1 :], offset[i]

    @staticmethod
    def slots(order, depth):
        base, count = {}, 0
        deep = depth if "z" in order else 1
        for t in offsets(order, depth):
            key, rank = Reduce.split(order, t)
            if rank:
                continue
            last = last_move(key)
            for i, axis in enumerate(order):
                if i <= last:
                    continue
                base[(key, axis)] = count
                if axis == "z":
                    count += deep + 1
                elif "z" in order and i > order.index("z"):
                    count += deep
                else:
                    count += 1
            base[(key, "c")] = count
            count += deep
        return base, count

    def where_(self, key, axis, z):
        deep = "z" in self.order and (axis == "c" or self.order.index(axis) > self.order.index("z"))
        return self.base[(key, axis)] + (z if deep else 0)

    def copy(self, source, edge, slot, peer):
        return pltpu.make_async_remote_copy(
            src_ref=source, dst_ref=self.inbox.at[edge], send_sem=self.send.at[slot],
            recv_sem=self.recv.at[edge], device_id=device_of(peer), device_id_type=MESH,
        )

    def start(self, offset):
        p = target_of(self.order, offset, self.depth, self.me)
        key, _ = self.split(self.order, offset)
        slot = self.marks.index(offset)
        edge = self.where_(key, "c", p["z"])
        peer = flipped(self.me, "c")
        self.copy(self.far_partial_of(flipped(p, "c")), edge, slot, peer).start()
        self.sent.append(slot)

    def kids(self, offset, p):
        key, rank = self.split(self.order, offset)
        last, z = last_move(offset), self.me["z"]
        found = [(self.where_(key, "c", p["z"]), None)]
        for axis in self.order[last + 1 :]:
            if axis == "z":
                at = self.base[(key, "z")]
                found += [(at + z, z > 0), (at + self.depth, z + 1 < self.depth)]
            else:
                found.append((self.where_(key, axis, p["z"]), None))
        if last >= 0 and self.order[last] == "z":
            far = jnp.where(p["z"] < z, z + 1, z - 1)
            found.append((self.base[(key, "z")] + p["z"], (far >= 0) & (far < self.depth)))
        return found

    def upward(self, offset, p):
        key, rank = self.split(self.order, offset)
        k, z = last_move(offset), self.me["z"]
        axis = self.order[k]
        if axis == "z":
            edge = self.base[(key, "z")] + jnp.where(p["z"] == z - 1, self.depth, p["z"])
            return edge, at_depth(self.me, jnp.where(p["z"] < z, z - 1, z + 1))
        parent = key[:k] + (0,) + key[k + 1 :]
        return self.where_(parent, axis, p["z"]), flipped(self.me, axis)

    def handle(self, offset, add, finish):
        p = target_of(self.order, offset, self.depth, self.me)
        kids = self.kids(offset, p)
        slot = len(self.marks) + self.marks.index(offset)
        for edge, cond in kids:
            when(cond, self.copy(self.inbox.at[edge], edge, slot, self.me).wait_recv)
        parts = [(self.inbox.at[edge], cond) for edge, cond in kids]
        if any(offset):
            into = parts[0][0]
            add(self.partial_of(p), parts, into)
            edge, peer = self.upward(offset, p)
            self.copy(into, edge, slot, peer).start()
            self.sent.append(slot)
        else:
            finish(self.partial_of(p), parts)

    def drain(self):
        for slot in self.sent:
            self.copy(self.inbox.at[0], 0, slot, self.me).wait_send()


D = 768
H = 12
DH = 64
BLK = 64
R = 3
GLOB = 2
L = 2
PAIRS = H // 2
WIDE = 2 * DH
SHARED = GLOB * BLK
SHARE = 16
HELPERS = SHARED // SHARE
VMEM_LIMIT = 60 * 1024 * 1024

layer_eps = 1e-06
masked_score = -1e30

Z_Y_X, Z_X_Y, X_Y_Z, Y_X_Z = ("z", "y", "x"), ("z", "x", "y"), ("x", "y", "z"), ("y", "x", "z")
Y_X, X_Y = ("y", "x"), ("x", "y")
ANYWHERE = pl.BlockSpec(memory_space=pl.ANY)
IN_SMEM = pl.BlockSpec(memory_space=pltpu.SMEM)
IN_VMEM = pl.BlockSpec(memory_space=pltpu.VMEM)
LOAD, SAVE = pl.BlockSpec(memory_space=pl.ANY), pl.BlockSpec(memory_space=pl.ANY)


def dma(*shape):
    return pltpu.SemaphoreType.DMA(shape)


def product(a, b):
    return lax.dot_general(a, b, (((1,), (0,)), ((), ())), preferred_element_type=jnp.float32)


def product_nt(a, b):
    return lax.dot_general(a, b, (((1,), (1,)), ((), ())), preferred_element_type=jnp.float32)


def product_tn(a, b):
    return lax.dot_general(a, b, (((0,), (0,)), ((), ())), preferred_element_type=jnp.float32)


def split_heads(pair_rows):
    low_lanes = lax.broadcasted_iota(jnp.int32, (1, WIDE), 1) < DH
    zero = jnp.zeros_like(pair_rows)
    return jnp.concatenate([jnp.where(low_lanes, pair_rows, zero), jnp.where(low_lanes, zero, pair_rows)], axis=0)


def join_heads(stacked):
    low_lanes = lax.broadcasted_iota(jnp.int32, (1, WIDE), 1) < DH
    rows = stacked.shape[0] // 2
    return jnp.where(low_lanes, stacked[:rows], stacked[rows:])


def row_of(block):
    return pl.multiple_of(block * BLK, BLK)


class Keys:
    def __init__(self, ref, pair=None):
        self.ref, self.pair = ref, pair
        self.held = ref.shape[2] // (BLK if pair is None else 1)
        self.blocks_all = ref.shape[0] * self.held

    def block(self, device, inner):
        if self.pair is None:
            return self.ref[device, 0, pl.ds(row_of(inner), BLK)]
        return self.ref[device, self.pair, inner]

    def whole(self):
        held = self.ref[...] if self.pair is None else self.ref[:, self.pair]
        return held.reshape(-1, WIDE)

    def with_shared(self, near):
        if self.pair is None:
            shared = self.ref[0, 0, 0:SHARED]
        else:
            shared = self.ref[0, self.pair, 0:GLOB].reshape(SHARED, WIDE)
        return jnp.concatenate([shared, near], axis=0)


def window_blocks(first, block, blocks_all):
    return [(first + block + j - 1 + blocks_all) % blocks_all for j in range(3)]


def drawn_blocks(picks_ref, pair, block, r):
    return [picks_ref[(block * H + 2 * pair + side) * R + r] for side in range(2)]


def bring(drawn, first, pairs, blocks_here):
    low_lanes = lax.broadcasted_iota(jnp.int32, (1, WIDE), 1) < DH
    for block in range(blocks_here):
        for source, target in pairs:
            for j, one in enumerate(window_blocks(first, block, source.blocks_all)):
                rows = source.block(one // source.held, one % source.held)
                target[block, j * BLK : (j + 1) * BLK] = rows
            for r in range(R):
                one, two = drawn(block, r)
                target[block, (3 + r) * BLK : (4 + r) * BLK] = jnp.where(
                    low_lanes, source.block(*one), source.block(*two)
                )


def key_scores(keys, q_heads, shut):
    scores = product_nt(keys, q_heads)
    end = SHARED + 3 * BLK
    return jnp.concatenate([scores[:SHARED], scores[SHARED:end] + shut, scores[end:]], axis=0)


def soft(scores):
    top = jnp.max(scores, axis=0, keepdims=True)
    weight = jnp.exp(scores - top)
    total = jnp.sum(weight, axis=0, keepdims=True)
    return weight * (1.0 / total), top + jnp.log(total)


def attend_pair(
    drawn, first, q_ref, keys, values, shut_ref, part_ref, o_ref, po_ref, log_ref, plog_ref, near_k, near_v
):
    blocks_here = q_ref.shape[0] // BLK
    bring(drawn, first, [(keys, near_k), (values, near_v)], blocks_here)
    scale = jnp.bfloat16(DH ** (-0.5))
    weight, logs = soft(product_nt(keys.whole(), split_heads(part_ref[...] * scale)))
    mixed = product_tn(weight.astype(jnp.bfloat16), values.whole())
    po_ref[...] = join_heads(mixed).astype(po_ref.dtype)
    plog_ref[0] = logs
    for block in range(blocks_here):
        here = slice(block * BLK, (block + 1) * BLK)
        q_heads = split_heads(q_ref[here] * scale)
        weight, logs = soft(key_scores(keys.with_shared(near_k[block]), q_heads, shut_ref[block]))
        mixed = product_tn(weight.astype(jnp.bfloat16), values.with_shared(near_v[block]))
        o_ref[here] = join_heads(mixed).astype(o_ref.dtype)
        log_ref[0, block : block + 1] = logs


def drawn_places(picks_ref, pair, held):
    def drawn(block, r):
        return [(one // held, one % held) for one in drawn_blocks(picks_ref, pair, block, r)]

    return drawn


def attend_kernel(picks_ref, first_ref, q_ref, k_ref, v_ref, *refs):
    keys, values = Keys(k_ref), Keys(v_ref)
    drawn = drawn_places(picks_ref, pl.program_id(0), keys.held)
    attend_pair(drawn, first_ref[0], q_ref, keys, values, *refs)


def near_rows(rows, dtype):
    return pltpu.VMEM((rows // BLK, 6 * BLK, WIDE), dtype)


def columns(rows, shift=0):
    return pl.BlockSpec((rows, WIDE), lambda p, *_: (0, p + shift))


def of_all(kv, shift=0):
    return pl.BlockSpec((kv.shape[0], 1, kv.shape[2], WIDE), lambda p, *_: (0, p + shift, 0, 0))


def by_pair(rows, lanes):
    return pl.BlockSpec((1, rows, lanes), lambda p, *_: (p, 0, 0))


def attend(picks, first, queries, kv, shut, part):
    rows = queries.shape[0]
    blocks = rows // BLK
    return pl.pallas_call(
        attend_kernel,
        grid_spec=pltpu.PrefetchScalarGridSpec(
            num_scalar_prefetch=2,
            grid=(PAIRS,),
            in_specs=[
                columns(rows), of_all(kv), of_all(kv, PAIRS),
                pl.BlockSpec(shut.shape, lambda p, *_: (0, 0, 0)), columns(SHARE),
            ],
            out_specs=[columns(rows), columns(SHARE), by_pair(blocks, WIDE), by_pair(1, 2 * SHARE)],
            scratch_shapes=[near_rows(rows, jnp.bfloat16)] * 2,
        ),
        out_shape=[
            jax.ShapeDtypeStruct((rows, D), jnp.bfloat16),
            jax.ShapeDtypeStruct((SHARE, D), jnp.bfloat16),
            jax.ShapeDtypeStruct((PAIRS, blocks, WIDE), jnp.float32),
            jax.ShapeDtypeStruct((PAIRS, 1, 2 * SHARE), jnp.float32),
        ],
        compiler_params=pltpu.CompilerParams(vmem_limit_bytes=VMEM_LIMIT),
        name="attend",
    )(picks, first, queries, kv, kv, shut, part)


def score_grads(weight, values, cot_heads):
    grads = product_nt(values, cot_heads)
    mean = jnp.sum(weight * grads, axis=0, keepdims=True)
    return (weight * (grads - mean)).astype(jnp.bfloat16)


def attend_back_kernel(
    picks_ref, first_ref, q_ref, k_ref, v_ref, shut_ref, do_ref, part_ref, pdo_ref, log_ref, plog_ref,
    dq_ref, dk_ref, dv_ref, pdq_ref, sum_k, sum_v, near_k, near_v, grad_k, grad_v,
):
    pair = pl.program_id(0)
    first = first_ref[0]
    blocks_here, blocks_all = q_ref.shape[0] // BLK, sum_k.shape[0] // BLK
    all_keys, all_values = Keys(k_ref), Keys(v_ref)
    drawn = drawn_places(picks_ref, pair, all_keys.held)
    bring(drawn, first, [(all_keys, near_k), (all_values, near_v)], blocks_here)
    low_lanes = lax.broadcasted_iota(jnp.int32, (1, WIDE), 1) < DH
    step = DH ** (-0.5)
    scale = jnp.bfloat16(step)
    part, cot = split_heads(part_ref[...] * scale), split_heads(pdo_ref[...])
    weight = jnp.exp(product_nt(all_keys.whole(), part) - plog_ref[0])
    grads = score_grads(weight, all_values.whole(), cot)
    pdq_ref[...] = (join_heads(product_tn(grads, all_keys.whole())) * step).astype(pdq_ref.dtype)
    sum_k[...] = product(grads, part)
    sum_v[...] = product(weight.astype(jnp.bfloat16), cot)
    shared_k = jnp.zeros((SHARED, WIDE), jnp.float32)
    shared_v = jnp.zeros((SHARED, WIDE), jnp.float32)
    for block in range(blocks_here):
        here = slice(block * BLK, (block + 1) * BLK)
        do = jnp.where(first + block < GLOB, jnp.bfloat16(0), do_ref[here])
        q_heads, do_heads = split_heads(q_ref[here] * scale), split_heads(do)
        keys, values = all_keys.with_shared(near_k[block]), all_values.with_shared(near_v[block])
        weight = jnp.exp(key_scores(keys, q_heads, shut_ref[block]) - log_ref[0, block : block + 1])
        grads = score_grads(weight, values, do_heads)
        dq_ref[here] = (join_heads(product_tn(grads, keys)) * step).astype(dq_ref.dtype)
        key_grad = product(grads, q_heads)
        value_grad = product(weight.astype(jnp.bfloat16), do_heads)
        shared_k = shared_k + key_grad[:SHARED]
        shared_v = shared_v + value_grad[:SHARED]
        grad_k[block] = key_grad[SHARED:]
        grad_v[block] = value_grad[SHARED:]
    sum_k[0:SHARED] += shared_k
    sum_v[0:SHARED] += shared_v
    for block in range(blocks_here):
        for grad, total in ((grad_k, sum_k), (grad_v, sum_v)):
            for j, one in enumerate(window_blocks(first, block, blocks_all)):
                total[pl.ds(row_of(one), BLK)] += grad[block, j * BLK : (j + 1) * BLK]
            for r in range(R):
                tile = grad[block, (3 + r) * BLK : (4 + r) * BLK]
                one, two = drawn_blocks(picks_ref, pair, block, r)
                total[pl.ds(row_of(one), BLK)] += jnp.where(low_lanes, tile, 0.0)
                total[pl.ds(row_of(two), BLK)] += jnp.where(low_lanes, 0.0, tile)
    dk_ref[...] = sum_k[...].astype(dk_ref.dtype).reshape(dk_ref.shape)
    dv_ref[...] = sum_v[...].astype(dv_ref.dtype).reshape(dv_ref.shape)


def attend_back(picks, first, queries, kv, shut, cot, part, part_cot, logs, part_logs):
    rows, grads = queries.shape[0], (kv.shape[0], PAIRS) + kv.shape[2:]
    length = kv.shape[0] * kv.shape[2]
    return pl.pallas_call(
        attend_back_kernel,
        grid_spec=pltpu.PrefetchScalarGridSpec(
            num_scalar_prefetch=2,
            grid=(PAIRS,),
            in_specs=[
                columns(rows), of_all(kv), of_all(kv, PAIRS),
                pl.BlockSpec(shut.shape, lambda p, *_: (0, 0, 0)), columns(rows), columns(SHARE), columns(SHARE),
                by_pair(rows // BLK, WIDE), by_pair(1, 2 * SHARE),
            ],
            out_specs=[columns(rows), of_all(kv), of_all(kv), columns(SHARE)],
            scratch_shapes=[pltpu.VMEM((length, WIDE), jnp.float32)] * 2
            + [near_rows(rows, jnp.bfloat16)] * 2
            + [near_rows(rows, jnp.float32)] * 2,
        ),
        out_shape=[
            jax.ShapeDtypeStruct((rows, D), jnp.bfloat16),
            jax.ShapeDtypeStruct(grads, jnp.bfloat16),
            jax.ShapeDtypeStruct(grads, jnp.bfloat16),
            jax.ShapeDtypeStruct((SHARE, D), jnp.bfloat16),
        ],
        compiler_params=pltpu.CompilerParams(vmem_limit_bytes=VMEM_LIMIT),
        name="attend_back",
    )(picks, first, queries, kv, kv, shut, cot, part, part_cot, logs, part_logs)


def call(body, name, cid, ins, outs, scratch):
    loads = [k for k, (_, where) in ins.items() if where is LOAD]
    saves = [k for k, (_, _, where) in outs.items() if where is SAVE]
    names = ["far_" + k if k in loads or k in saves else k for k in (*ins, *outs)]
    scratch = {
        **scratch,
        **{k: pltpu.VMEM(ins[k][0].shape, ins[k][0].dtype) for k in loads},
        **{k: pltpu.VMEM(outs[k][0], outs[k][1]) for k in saves},
        **dict(moves=dma(len(loads) + len(saves) + 1)),
    }

    def run(*given):
        refs = SimpleNamespace(**dict(zip(names + list(scratch), given)))
        copies = {}
        for i, k in enumerate(loads + saves):
            pair = (getattr(refs, "far_" + k), getattr(refs, k))
            copies[k] = pltpu.make_async_copy(*(pair if k in loads else pair[::-1]), refs.moves.at[i])
        coming, going = list(loads), []
        for k in loads:
            copies[k].start()

        def ready(*wanted):
            for k in wanted:
                if k in coming:
                    coming.remove(k)
                    copies[k].wait()

        def save(*given):
            for k in given:
                if k in saves:
                    going.append(k)
                    copies[k].start()

        refs.ready, refs.save = ready, save
        body(refs)
        ready(*loads)
        save(*[k for k in saves if k not in going])
        for k in saves:
            copies[k].wait()

    got = pl.pallas_call(
        run,
        out_shape=[jax.ShapeDtypeStruct(shape, dtype) for shape, dtype, _ in outs.values()],
        in_specs=[where for _, where in ins.values()],
        out_specs=[where for _, _, where in outs.values()],
        scratch_shapes=list(scratch.values()),
        compiler_params=pltpu.CompilerParams(
            collective_id=cid, has_side_effects=True, vmem_limit_bytes=VMEM_LIMIT
        ),
        name=name,
    )(*[array for array, _ in ins.values()])
    return SimpleNamespace(**dict(zip(outs, got)))


def over(count, act):
    def step(i, carry):
        act(i)
        return carry

    lax.fori_loop(0, count, step, 0)


def span(i, size, first=0):
    return pl.ds(pl.multiple_of(first + i * size, size), size)


def run_in_order(timed):
    for _, act in sorted(timed, key=lambda pair: pair[0]):
        act()


def layer_pieces(rows_in, rows_down, first):
    half, wide = rows_down // 2, 3 * D // 2
    return [
        (first, 0, rows_in, 0, wide, Z_Y_X),
        (first, 0, rows_in, wide, wide, Z_X_Y),
        (first + 1, 0, rows_in, 0, D, Z_X_Y),
        (first + 2, 0, rows_in, 0, 2 * D, Z_Y_X),
        (first + 2, 0, rows_in, 2 * D, 2 * D, Z_X_Y),
        (first + 3, 0, half, 0, D, X_Y_Z),
        (first + 3, half, half, 0, D, Y_X_Z),
    ]


class Gathering:
    def __init__(self, arrays, pieces, seq_count, depth, near):
        self.near, self.layers = near, [layer for _, layer in arrays]
        shapes = [a.shape if layer is None else a.shape[1:] for a, layer in arrays]
        self.shapes = [jax.ShapeDtypeStruct(shape, a.dtype) for shape, (a, _) in zip(shapes, arrays)]
        arrays = [a for a, _ in arrays]
        self.arrays, self.pieces, self.depth, self.n_dev = arrays, pieces, depth, seq_count * depth
        flat_only = {which for which, *_, order in pieces if "z" not in order}
        self.counts = [seq_count if i in flat_only else self.n_dev for i in range(len(arrays))]

    def ins(self):
        return {"slab%d" % i: (a, ANYWHERE) for i, a in enumerate(self.arrays)}

    def outs(self):
        return {
            "every%d" % i: ((n,) + a.shape, a.dtype, SAVE if i in self.near else ANYWHERE)
            for i, (n, a) in enumerate(zip(self.counts, self.shapes))
        }

    def scratch(self):
        total = sum(Gather.sends(order, self.depth) for *_, order in self.pieces)
        return {
            "g_send": dma(total),
            "g_recv": dma(len(self.pieces), self.n_dev),
            "g_local": dma(len(self.arrays)),
        }

    def number(self, i):
        return number_in(self.depth) if self.counts[i] == self.n_dev else number_in_sequence

    def begin(self, refs):
        slabs = [getattr(refs, "slab%d" % i) for i in range(len(self.arrays))]
        slabs = [ref if layer is None else ref.at[layer] for ref, layer in zip(slabs, self.layers)]
        every = [getattr(refs, "every%d" % i) for i in range(len(self.arrays))]
        self.jobs, at = [], 0
        for k, (which, row, rows, column, columns_, order) in enumerate(self.pieces):
            window = (pl.ds(row, rows), pl.ds(column, columns_))
            number = self.number(which)
            self.jobs.append(
                Gather(
                    slabs[which].at[window],
                    lambda p, which=which, window=window, number=number: every[which].at[(number(p),) + window],
                    number, order, self.depth, refs.g_send, refs.g_recv.at[k], at,
                )
            )
            at += Gather.sends(order, self.depth)
        me = place()
        self.own = [
            pltpu.make_async_copy(slab, all_.at[self.number(i)(me)], refs.g_local.at[i])
            for i, (slab, all_) in enumerate(zip(slabs, every))
        ]
        for copy in self.own:
            copy.start()

    def hurry(self, refs, arrays):
        for (which, *_), job in zip(self.pieces, self.jobs):
            if which in arrays:
                job.siblings()
        for i in arrays:
            self.own[i].wait()
            refs.save("every%d" % i)
        self.early = arrays

    def end(self):
        for (which, *_), job in zip(self.pieces, self.jobs):
            if which not in self.early:
                job.siblings()
        for job in self.jobs:
            job.drain()
        for i, copy in enumerate(self.own):
            if i not in self.early:
                copy.wait()

    def results(self, got):
        return [getattr(got, "every%d" % i) for i in range(len(self.arrays))]


def to_helpers(source, target, send, recv):
    seq, z = lax.axis_index(SEQ), lax.axis_index(BATCH)

    def copy(j):
        return pltpu.make_async_remote_copy(
            src_ref=source.at[pl.ds(j * SHARE, SHARE)], dst_ref=target, send_sem=send.at[j],
            recv_sem=recv, device_id=(j, z), device_id_type=MESH,
        )

    def begin():
        for j in range(1, HELPERS):
            copy(j).start()

    def own():
        pltpu.sync_copy(source.at[pl.ds(0, SHARE)], target)
        for j in range(1, HELPERS):
            copy(j).wait_send()

    def end():
        pl.when(seq == 0)(own)
        pl.when(seq != 0)(lambda: copy(1).wait_recv())

    pl.when(seq == 0)(begin)
    return end


def to_first(source, target, send, recv):
    seq, z = lax.axis_index(SEQ), lax.axis_index(BATCH)

    def copy(j):
        return pltpu.make_async_remote_copy(
            src_ref=source, dst_ref=target.at[pl.ds(j * SHARE, SHARE)], send_sem=send,
            recv_sem=recv.at[j], device_id=(0, z), device_id_type=MESH,
        )

    for j in range(1, HELPERS):
        pl.when(seq == j)(copy(j).start)

    def end():
        def mine():
            pltpu.sync_copy(source, target.at[pl.ds(0, SHARE)])
            for j in range(1, HELPERS):
                copy(j).wait_recv()

        pl.when(seq == 0)(mine)
        pl.when(seq != 0)(lambda: copy(1).wait_send())

    return end


def from_slabs(ref):
    def get(at):
        slabs = ref[:, :, at]
        return slabs.astype(jnp.float32).reshape(-1, slabs.shape[2]).astype(ref.dtype)

    return get


def project(low, w, bias, q, kv):
    def queries(i):
        at = span(i, 256)
        q[:, at] = (product(low[...], w(at)) + bias[0:1, at]).astype(q.dtype)

    def keys(i):
        keep(2 * i, product(low[...], w(span(i, 256, D))))

    def values(i):
        keep(PAIRS + 2 * i, product(low[...], w(span(i, 256, 2 * D))) + bias[1:2, span(i, 256)])

    def keep(pair, acc):
        for half in range(2):
            lanes = acc[:, half * WIDE : (half + 1) * WIDE].astype(kv.dtype)
            kv[pair + half] = lanes.reshape(kv.shape[1:])

    for act in (keys, values, queries):
        over(D // 256, act)


class Sequence:
    def __init__(self, rows, seq_count, depth, dtype):
        self.rows, self.seq_count, self.depth, self.dtype = rows, seq_count, depth, dtype

    def outs(self):
        blocks, f32 = self.rows // BLK, jnp.float32
        return dict(
            q=((self.rows, D), self.dtype, SAVE),
            every=((self.seq_count, 2 * PAIRS, blocks, BLK, WIDE), self.dtype, SAVE),
            part=((SHARE, D), self.dtype, SAVE),
            o=((self.rows, D), self.dtype, SAVE), po=((SHARE, D), self.dtype, SAVE),
            log=((PAIRS, blocks, WIDE), f32, SAVE), plog=((PAIRS, 1, 2 * SHARE), f32, SAVE),
        )

    def scratch(self):
        return dict(
            kv=pltpu.VMEM((2 * PAIRS, self.rows // BLK, BLK, WIDE), self.dtype), send=dma(4 * Gather.sends(Y_X, self.depth)),
            recv=dma(4, self.seq_count), local=dma(), give=dma(HELPERS), take=dma(),
            near_k=near_rows(self.rows, self.dtype), near_v=near_rows(self.rows, self.dtype),
        )

    def prepare(self, refs):
        count, at = PAIRS // 2, 0
        self.jobs = []
        for i in range(4):
            window = pl.ds(i * count, count)
            self.jobs.append(
                Gather(
                    refs.kv.at[window],
                    lambda p, window=window: refs.every.at[number_in_sequence(p), window],
                    number_in_sequence, (X_Y, Y_X)[i % 2], self.depth, refs.send, refs.recv.at[i], at,
                )
            )
            at += Gather.sends(Y_X, self.depth)

    def begin(self, refs):
        for job in self.jobs:
            job.begin()
        self.finish = to_helpers(refs.q, refs.part, refs.give, refs.take)
        self.own = pltpu.make_async_copy(refs.kv, refs.every.at[number_in_sequence(place())], refs.local)
        self.own.start()

    def arrived(self, refs):
        for job in self.jobs:
            job.siblings()
        self.own.wait()
        self.finish()
        refs.save("every", "part")

    def attention(self, refs, steps):
        first = lax.axis_index(SEQ) * (self.rows // BLK)
        count = PAIRS // steps

        def pair_of(pair):
            at, one = span(pair, WIDE), pl.ds(pair, 1)

            def drawn(block, r):
                first_one = (block * H + 2 * pair) * R + r
                return [(refs.picks[0, i], refs.picks[1, i]) for i in (first_one, first_one + R)]

            attend_pair(
                drawn, first, refs.q.at[:, at], Keys(refs.every, pair), Keys(refs.every, PAIRS + pair), refs.shut,
                refs.part.at[:, at], refs.o.at[:, at], refs.po.at[:, at], refs.log.at[one], refs.plog.at[one],
                refs.near_k, refs.near_v,
            )

        def step(k):
            if k == 0:
                self.arrived(refs)
                refs.ready("shut")
            over(count, lambda i: pair_of(k * count + i))
            if k == steps - 1:
                refs.save("o", "po", "log", "plog")

        return [partial(step, k) for k in range(steps)]

    def end(self):
        for job in self.jobs:
            job.drain()


def project_and_send(refs, gathering, sequence, low, which):
    def act():
        gathering.hurry(refs, [which])
        w = from_slabs(getattr(refs, "every%d" % which))
        refs.ready("low")
        project(low, w, refs.bias, refs.q, refs.kv)
        sequence.begin(refs)
        refs.save("q")

    return act


def timed_events(jobs, places):
    return [pair for job, at in zip(jobs, places, strict=True) for pair in job.events(at)]


def shut_keys_here(segs, own_segs, shut):
    me, count = lax.axis_index(SEQ), segs.shape[0]
    blocks = shut.shape[0]
    rows = blocks * BLK

    def column(device):
        held = segs[device].astype(jnp.float32).T
        return [held[:, r : r + 1] for r in range(rows // WIDE)]

    before, here, after = column((me + count - 1) % count), column(me), column((me + 1) % count)
    near = jnp.concatenate([before[-1][WIDE - BLK :]] + here + [after[0][:BLK]], axis=0)
    for block in range(blocks):
        spot = (me * blocks + block - 1) * BLK + lax.broadcasted_iota(jnp.int32, (3 * BLK, WIDE), 0)
        same = near[block * BLK : (block + 3) * BLK] == own_segs[block : block + 1]
        shut[block] = jnp.where(same & (spot >= SHARED) & (spot < count * rows), 0.0, masked_score)


def first_head(low, small, segs, own_segs, picks, weights, seq_count, depth, cid):
    rows = low.shape[0]
    pieces = [(0, 0, small.shape[0], 0, 128, Z_Y_X), (1, 0, 8, 0, 128, Y_X)]
    pieces += layer_pieces(small.shape[0], weights[3][0].shape[1], 2)
    gathering = Gathering([(small, None), (segs, None)] + weights, pieces, seq_count, depth, (0, 1, 2))
    sequence = Sequence(rows, seq_count, depth, low.dtype)

    def body(refs):
        greet(("y", "x", "z"), depth, spread=True)
        gathering.begin(refs)
        sequence.prepare(refs)
        refs.bias = refs.vectors.at[0]

        def vectors():
            gathering.hurry(refs, [0, 1])
            shut_keys_here(refs.every1, refs.own_segs, refs.shut)
            refs.save("shut")
            table = refs.every0[...].astype(jnp.float32).reshape(D, 128).T
            for layer in range(L):
                refs.vectors[layer, 0:6] = table[6 * layer : 6 * layer + 6]
                refs.vectors[layer, 6:8] = table[6 * L + 2 * layer : 6 * L + 2 * layer + 2]
            refs.table[...] = table[8 * L : 12 * L]

        def project_now():
            project_and_send(refs, gathering, sequence, refs.low, 2)()
            gathering.early = [0, 1, 2]

        at = HEAD_PLACES
        run_in_order(
            [(place_, job.begin) for place_, job in zip(at.begins, gathering.jobs, strict=True)]
            + timed_events(gathering.jobs + sequence.jobs, at.arrivals)
            + [(at.project, vectors), (at.project + 0.1, project_now)]
            + list(zip(at.attention, sequence.attention(refs, len(at.attention)), strict=True))
        )
        sequence.end()
        gathering.end()

    got = call(
        body, "first_head", cid,
        {
            **dict(low=(low, LOAD), own_segs=(own_segs, IN_VMEM), picks=(picks, IN_SMEM)), **gathering.ins(),
        },
        {
            **dict(
                vectors=((L, 8, D), jnp.float32, IN_VMEM), table=((4 * L, D), jnp.float32, IN_VMEM),
                shut=((rows // BLK, 3 * BLK, WIDE), jnp.float32, SAVE),
            ),
            **sequence.outs(), **gathering.outs(),
        },
        {**sequence.scratch(), **gathering.scratch()},
    )
    return got, gathering.results(got)[2:]


def norm_block(resid, gain, shift):
    center = resid - jnp.mean(resid, axis=1, keepdims=True)
    inv_std = lax.rsqrt(jnp.mean(center * center, axis=1, keepdims=True) + layer_eps)
    normed = center * inv_std
    return normed * gain + shift, normed, inv_std


ROW_BLOCK = 64


WIDE_D, WIDE_FF = 384, 512


def tail_steps(refs):
    rows, hidden = refs.resid.shape[0], refs.shifts.shape[1]

    def out():
        refs.ready("resid", "w_out")

        def act(i):
            at = span(i, WIDE_D)
            own = refs.resid[:, at].astype(jnp.float32)
            refs.sum[:, at] = own + product(refs.mixed[...], refs.w_out[:, at]) + refs.bias[2:3, at]

        over(D // WIDE_D, act)
        refs.save("mixed")

    def norm_one():
        def act(i):
            at = span(i, ROW_BLOCK)
            y, normed, inv = norm_block(refs.sum[at], refs.bias[6:7], refs.bias[3:4])
            refs.n1[at], refs.inv1[at], refs.sum[at] = normed, inv, y
            refs.y_low[at] = y.astype(jnp.bfloat16)

        over(rows // ROW_BLOCK, act)
        refs.save("n1", "inv1", "y_low")
        refs.ready("w_up")

    def up(first, count):
        def act(i):
            at = span(first + i, WIDE_FF)
            u = product(refs.y_low[...], refs.w_up[:, at]) + refs.shifts[0:1, at]
            share = 0.5 + 0.5 * lax.erf(u * (0.5 ** 0.5))
            refs.a_low[:, at] = (u * share).astype(jnp.bfloat16)
            slope = share + u * jnp.exp(-0.5 * u * u) * ((2.0 * jnp.pi) ** -0.5)
            refs.slope[:, at] = slope.astype(jnp.bfloat16)

        over(count, act)

    def down():
        refs.ready("w_down")
        refs.save("a_low", "slope")

        def act(i):
            at = span(i, WIDE_D)
            refs.sum[:, at] = refs.sum[:, at] + product(refs.a_low[...], refs.w_down[:, at]) + refs.bias[4:5, at]

        over(D // WIDE_D, act)

    def norm_two():
        def act(i):
            at = span(i, ROW_BLOCK)
            z, normed, inv = norm_block(refs.sum[at], refs.bias[7:8], refs.bias[5:6])
            refs.n2[at], refs.inv2[at] = normed, inv
            if hasattr(refs, "z"):
                refs.z[at] = z
            refs.z_low[at] = z.astype(jnp.bfloat16)

        over(rows // ROW_BLOCK, act)
        refs.save("n2", "inv2", "z", "z_low")

    ends = [hidden // WIDE_FF * k // 4 for k in range(5)]
    ups = [partial(up, a, b - a) for a, b in zip(ends, ends[1:])]
    return [out, norm_one] + ups + [down, norm_two]


def tail_ins(mixed, part, resid, vectors, shifts, weights):
    return dict(
        generic=(mixed, LOAD), own_part=(part, ANYWHERE), resid=(resid, LOAD), vectors=(vectors, IN_VMEM),
        shifts=(shifts, IN_VMEM), w_out=(weights[1], LOAD), w_up=(weights[2], LOAD), w_down=(weights[3], LOAD),
    )


def tail_results(rows, hidden):
    f32, low = jnp.float32, jnp.bfloat16
    kept = dict(mixed=((rows, D), low), y_low=((rows, D), low), a_low=((rows, hidden), low), z_low=((rows, D), low))
    norms = dict(
        n1=((rows, D), f32), inv1=((rows, 1), f32), slope=((rows, hidden), low), n2=((rows, D), f32), inv2=((rows, 1), f32)
    )
    return kept, norms


def saved(shapes):
    return {k: (*v, SAVE) for k, v in shapes.items()}


def tail_scratch(rows):
    return dict(sum=pltpu.VMEM((rows, D), jnp.float32), t_send=dma(), t_recv=dma(HELPERS))


def tail(mixed, part, resid, vectors, shifts, weights, next_weights, shut, picks, seq_count, depth, cid):
    rows, hidden = resid.shape[0], shifts.shape[1]
    pieces = layer_pieces(next_weights[0][0].shape[1], next_weights[3][0].shape[1], 0)
    gathering = Gathering(next_weights, pieces, seq_count, depth, (0,))
    sequence = Sequence(rows, seq_count, depth, mixed.dtype)

    def body(refs):
        refs.ready("generic")
        refs.mixed[...] = refs.generic[...]
        greet(("y", "x", "z"), depth, spread=True, collect=True)
        finish = to_first(refs.own_part, refs.mixed, refs.t_send, refs.t_recv)
        gathering.begin(refs)
        sequence.prepare(refs)
        refs.bias = refs.vectors.at[0]
        steps = [finish] + tail_steps(refs)

        def project_now():
            refs.bias = refs.vectors.at[1]
            project_and_send(refs, gathering, sequence, refs.z_low, 0)()

        at = TAIL_PLACES
        run_in_order(
            [(place_, job.begin) for place_, job in zip(at.begins, gathering.jobs, strict=True)]
            + timed_events(gathering.jobs + sequence.jobs, at.arrivals)
            + list(zip(at.steps, steps, strict=True)) + [(at.project, project_now)]
            + list(zip(at.attention, sequence.attention(refs, len(at.attention)), strict=True))
        )
        sequence.end()
        gathering.end()

    kept, norms = tail_results(rows, hidden)
    got = call(
        body, "tail", cid,
        {
            **tail_ins(mixed, part, resid, vectors, shifts, weights),
            **dict(shut=(shut, LOAD), picks=(picks, IN_SMEM)), **gathering.ins(),
        },
        {
            **saved(kept), **saved(norms), **dict(z=((rows, D), jnp.float32, SAVE)), **sequence.outs(),
            **gathering.outs(),
        },
        {**tail_scratch(rows), **sequence.scratch(), **gathering.scratch()},
    )
    return got, gathering.results(got)


def folded(block):
    return jnp.sum(block.reshape(-1, 8, block.shape[1]), axis=0)


def norm_block_back(grad, normed, inv_std, gain):
    scaled = grad * gain
    return (
        scaled
        - jnp.mean(scaled, axis=1, keepdims=True)
        - normed * jnp.mean(scaled * normed, axis=1, keepdims=True)
    ) * inv_std


def back_steps(refs, dz, w_down, w_up, w_out, waits=(lambda: None,) * 3):
    rows, hidden = refs.n2.shape[0], refs.slope.shape[1]
    zero = jnp.zeros((8, D), jnp.float32)

    def row(k, total):
        refs.totals[k : k + 1] = jnp.sum(total, axis=0, keepdims=True)

    def norm_two():
        refs.ready("n2", "inv2", "d_out")

        def act(i, sums):
            at = span(i, ROW_BLOCK)
            grad, normed = dz(at), refs.n2[at]
            back = norm_block_back(grad, normed, refs.inv2[at], refs.bias[7:8])
            refs.work[at] = back
            refs.dr2_low[at] = back.astype(jnp.bfloat16)
            return sums[0] + folded(back), sums[1] + folded(grad), sums[2] + folded(grad * normed)

        sums = lax.fori_loop(0, rows // ROW_BLOCK, act, (zero,) * 3)
        row(4, sums[0]), row(5, sums[1]), row(7, sums[2])
        refs.save("dr2_low")
        refs.ready("slope")
        waits[0]()

    def down(first, count):
        def act(i):
            at = span(first + i, WIDE_FF)
            du = product_nt(refs.dr2_low[...], w_down[at]) * refs.slope[:, at].astype(jnp.float32)
            refs.du_low[:, at] = du.astype(jnp.bfloat16)
            refs.hidden_totals[0:1, at] = jnp.sum(du, axis=0, keepdims=True)

        over(count, act)

    def up():
        refs.save("du_low")
        waits[1]()

        def act(i):
            at = span(i, WIDE_D)
            refs.work[:, at] = refs.work[:, at] + product_nt(refs.du_low[...], w_up[at])

        over(D // WIDE_D, act)

    def norm_one():
        refs.ready("n1", "inv1")

        def act(i, sums):
            at = span(i, ROW_BLOCK)
            grad, normed = refs.work[at], refs.n1[at]
            back = norm_block_back(grad, normed, refs.inv1[at], refs.bias[6:7])
            refs.dr1[at] = back
            refs.dr1_low[at] = back.astype(jnp.bfloat16)
            return sums[0] + folded(back), sums[1] + folded(grad), sums[2] + folded(grad * normed)

        sums = lax.fori_loop(0, rows // ROW_BLOCK, act, (zero,) * 3)
        row(2, sums[0]), row(3, sums[1]), row(6, sums[2])
        refs.save("dr1", "dr1_low")

    def out():
        waits[2]()

        def act(i):
            at = span(i, WIDE_D)
            refs.cot[:, at] = product_nt(refs.dr1_low[...], w_out[at]).astype(jnp.bfloat16)

        over(D // WIDE_D, act)
        refs.save("cot")

    half = hidden // WIDE_FF // 2
    return [norm_two, partial(down, 0, half), partial(down, half, half), up, norm_one, out]


def back_outs(rows, hidden):
    f32, low = jnp.float32, jnp.bfloat16
    return dict(
        dr2_low=((rows, D), low, SAVE), du_low=((rows, hidden), low, SAVE), dr1=((rows, D), f32, SAVE),
        dr1_low=((rows, D), low, SAVE), cot=((rows, D), low, SAVE), totals=((8, D), f32, IN_VMEM),
        hidden_totals=((1, hidden), f32, IN_VMEM), part_cot=((SHARE, D), low, ANYWHERE),
    )


def turn(mixed, part, resid, vectors, shifts, weights, d_out, depth, cid):
    rows, hidden = resid.shape[0], shifts.shape[1]

    def body(refs):
        refs.ready("generic")
        refs.mixed[...] = refs.generic[...]
        refs.bias = refs.vectors.at[1]
        greet((), depth, spread=True, collect=True)
        to_first(refs.own_part, refs.mixed, refs.t_send, refs.t_recv)()
        for step in tail_steps(refs):
            step()
        refs.totals[...] = jnp.zeros_like(refs.totals)
        for step in back_steps(refs, lambda at: refs.d_out[at].astype(jnp.float32), refs.w_down, refs.w_up, refs.w_out):
            step()
        to_helpers(refs.cot, refs.part_cot, refs.give, refs.take)()

    kept, norms = tail_results(rows, hidden)
    return call(
        body, "turn", cid,
        {**tail_ins(mixed, part, resid, vectors, shifts, weights), **dict(d_out=(d_out, LOAD))},
        {**saved(kept), **back_outs(rows, hidden)},
        {
            **tail_scratch(rows), **{k: pltpu.VMEM(*v) for k, v in norms.items()},
            **dict(work=pltpu.VMEM((rows, D), jnp.float32), give=dma(HELPERS), take=dma()),
        },
    )


def chunked(shape):
    rows, columns = shape
    width = columns
    while rows * width > 24 * 1024 and width % 256 == 0:
        width //= 2
    if rows * width > 24 * 1024 and width % 384 == 0:
        width //= 3
    return width, columns // width


def total_of(own, kids, window):
    total = own[window].astype(jnp.float32)
    for ref, cond in kids:
        if cond is None:
            total = total + ref[window].astype(jnp.float32)
        else:
            total = total + lax.cond(
                cond,
                lambda ref=ref: ref[window].astype(jnp.float32),
                lambda total=total: jnp.zeros_like(total),
            )
    return total


def over_chunks(shape, act):
    if len(shape) == 3:
        size = shape[1] // 2

        def part(i, carry):
            act((i // 2, span(i % 2, size)))
            return carry

        lax.fori_loop(0, 2 * shape[0], part, 0)
        return
    width, count = chunked(shape)

    def step(i, carry):
        act((slice(None), pl.ds(pl.multiple_of(i * width, width), width)))
        return carry

    lax.fori_loop(0, count, step, 0)


def add_up(own, kids, into):
    def act(window):
        into[window] = total_of(own, kids, window).astype(into.dtype)

    over_chunks(into.shape, act)


def write_total(target):
    def finish(own, kids):
        def act(window):
            target[window] = total_of(own, kids, window).astype(target.dtype)

        over_chunks(target.shape, act)

    return finish


def weight_grad(left, right, into, first=0):
    share = into.shape[1]
    width = WIDE_FF if into.shape[2] % WIDE_FF == 0 else WIDE_D
    count = 384 // share

    def act(i):
        across = into.shape[2] // width
        rows, at = i // across, span(i % across, width)
        acc = product_tn(left[:, span(rows, 384)], right[:, pl.ds(pl.multiple_of(first + i % across * width, WIDE), width)])
        for k in range(count):
            into[rows * count + k, :, at] = acc[k * share : (k + 1) * share].astype(into.dtype)

    over(left.shape[1] // 384 * (into.shape[2] // width), act)


class Sums:
    def __init__(self, tag, pieces, depth):
        self.tag, self.pieces, self.depth = tag, pieces, depth

    def name(self, what, k):
        return "%s_%s%d" % (self.tag, what, k)

    def scratch(self):
        made = {}
        for k, (_, _, shape, _, order, dtype) in enumerate(self.pieces):
            edges = Reduce.slots(order, self.depth)[1]
            made[self.name("box", k)] = pltpu.VMEM((edges,) + shape, dtype)
            made[self.name("send", k)] = dma(2 * len(offsets(order, self.depth)))
            made[self.name("recv", k)] = dma(edges)
        return made

    def prepare(self, refs):
        self.jobs = []
        for k, (source, far, _, target, order, _) in enumerate(self.pieces):
            box, send, recv = (getattr(refs, self.name(what, k)) for what in ("box", "send", "recv"))
            job = Reduce(partial(source, refs), partial(far, refs), box, order, self.depth, send, recv)
            self.jobs.append((job, target(refs)))

    def start(self, k):
        job, _ = self.jobs[k]
        for t in job.marks:
            job.start(t)

    def timed(self, places):
        timed = []
        for k, ((job, finish), at) in enumerate(zip(self.jobs, places, strict=True)):
            timed.append((at[0], partial(self.start, k)))
            acts = [partial(job.handle, t, add_up, finish) for t in job.marks]
            timed += zip(at[1:], acts, strict=True)
        return timed

    def end(self):
        for job, _ in self.jobs:
            job.drain()


def weight_sums(windows, depth, n_dev, dtypes):
    number = number_in(depth)

    def piece(which, row, rows, column, columns_, order):
        window = (pl.ds(row, rows), pl.ds(column, columns_))

        def source(refs, p):
            return getattr(refs, "grad%d" % which).at[(number(p),) + window]

        return (
            source,
            source,
            (rows, columns_),
            lambda refs: write_total(getattr(refs, "owned%d" % which).at[window]),
            order,
            dtypes[which],
        )

    return Sums("w", [piece(*w) for w in windows], depth)


def sum_rows(dk, dv, dq, part_dq, held, grads, seq_count, depth, cid):
    rows, hidden, n_dev = dq.shape[0], grads.du_low.shape[1], seq_count * depth
    low, f32 = dk.dtype, jnp.float32
    share, count = D // n_dev, PAIRS // 2

    def piece(i):
        window = pl.ds(i % 2 * count, count)

        def target(refs):
            def finish(own, kids):
                def act(at):
                    lanes = pl.ds(pl.multiple_of((PAIRS + i * count + at[0]) * WIDE, WIDE), WIDE)
                    refs.proj[at[1], lanes] = total_of(own, kids, at).astype(low)

                over_chunks((count, rows, WIDE), act)

            return finish

        return (
            lambda refs, p: (refs.dk, refs.dv)[i // 2].at[number_in_sequence(p), window],
            lambda refs, p: (refs.far_dk, refs.far_dv)[i // 2].at[number_in_sequence(p), window],
            (count, rows, WIDE),
            target,
            (X_Y, Y_X)[i % 2],
            low,
        )

    by_rows = Sums("r", [piece(i) for i in range(4)], depth)
    windows = [(1, 0, share, 0, D, X_Y_Z), (2, 0, share, 0, hidden // 2, Y_X_Z)]
    by_weights = weight_sums(windows, depth, n_dev, {1: low, 2: low})

    def body(refs):
        refs.ready("dq")
        refs.proj[:, 0:D] = refs.dq[...]
        greet(("y", "x", "z"), depth, collect=True)
        by_rows.prepare(refs)
        by_weights.prepare(refs)
        ends = [to_first(refs.part, refs.proj.at[:, pl.ds(0, D)], refs.t_send, refs.t_recv)]
        at = ROWS_PLACES

        def grad(left, right, into):
            refs.ready(left, right)
            weight_grad(getattr(refs, left), getattr(refs, right), into)

        first_block = min(place for places in at.rows for place in places[1:])
        run_in_order(
            by_rows.timed(at.rows) + by_weights.timed(at.weights)
            + [
                (at.grads[0], partial(grad, "mixed", "dr1_low", refs.grad1)),
                (at.grads[1], partial(grad, "y_low", "du_low", refs.grad2)),
                (first_block - 0.5, partial(refs.ready, "dk", "dv")),
                (at.collect, ends[0]),
            ]
        )
        by_rows.end()
        by_weights.end()

        def act(i, sums):
            at = span(i, ROW_BLOCK)
            return tuple(
                total + folded(refs.proj[at, pl.ds(first, D)].astype(f32)) for total, first in zip(sums, (0, 2 * D))
            )

        zero = jnp.zeros((8, D), f32)
        sums = lax.fori_loop(0, rows // ROW_BLOCK, act, (zero, zero))
        refs.totals[...] = jnp.zeros_like(refs.totals)
        for k in range(2):
            refs.totals[k : k + 1] = jnp.sum(sums[k], axis=0, keepdims=True)

    return call(
        body, "sum_rows", cid,
        dict(
            dq=(dq, LOAD), part=(part_dq, ANYWHERE), mixed=(held.mixed, LOAD), dr1_low=(grads.dr1_low, LOAD),
            dk=(dk, LOAD), dv=(dv, LOAD), y_low=(held.y_low, LOAD), du_low=(grads.du_low, LOAD),
        ),
        dict(
            proj=((rows, 3 * D), low, IN_VMEM), totals=((8, D), f32, IN_VMEM), owned1=((share, D), f32, IN_VMEM),
            owned2=((share, hidden // 2), f32, IN_VMEM),
        ),
        {
            **dict(
                grad1=pltpu.VMEM((n_dev, share, D), low), grad2=pltpu.VMEM((n_dev, share, hidden // 2), low),
                t_send=dma(), t_recv=dma(HELPERS),
            ),
            **by_rows.scratch(), **by_weights.scratch(),
        },
    )


def sum_weights(held, low_in, proj, vectors, w_qkv, small, below, n_dev, depth, cid):
    rows, hidden = proj.shape[0], held.du_low.shape[1]
    low, f32 = jnp.bfloat16, jnp.float32
    share, tall = D // n_dev, hidden // n_dev
    shapes = {0: (share, 3 * D), 2: (share, hidden // 2), 3: (tall, D)}
    cut = tall * 2 // 3
    windows = [
        (3, 0, cut, 0, D, Z_X_Y),
        (3, cut, tall - cut, 0, D, Z_Y_X),
        (2, 0, share, 0, hidden // 2, Y_X_Z),
        (0, 0, share, 0, 3 * D, Z_Y_X),
    ]
    ins = dict(low_in=(low_in, LOAD), proj=(proj, LOAD))
    ins.update({"up_" + k: (getattr(held, k), LOAD) for k in ("y_low", "du_low", "a_low", "dr2_low")})
    ins.update(up_dr1=(held.dr1, LOAD), w_qkv=(w_qkv, ANYWHERE))
    outs = {"owned%d" % i: (s, f32, IN_VMEM) for i, s in shapes.items()}
    scratch = {"grad%d" % i: pltpu.VMEM((n_dev,) + s, low) for i, s in shapes.items()}
    if small is not None:
        windows.append((4, 0, small.shape[1], 0, small.shape[2], Z_Y_X))
        ins.update(grad4=(small, IN_VMEM))
        outs.update(owned4=(small.shape[1:], f32, IN_VMEM))
    by_weights = weight_sums(windows, depth, n_dev, {0: low, 2: low, 3: low, 4: f32})
    scratch.update(by_weights.scratch())
    scratch.update(load=dma(4), wide=pltpu.VMEM((D, hidden), low))
    if below is not None:
        below_weights, below_held = below
        ins.update({k: (getattr(below_held, k), LOAD) for k in ("n2", "inv2", "slope", "n1", "inv1")})
        ins.update(
            vectors=(vectors, IN_VMEM), w_out=(below_weights[1], ANYWHERE), w_up=(below_weights[2], ANYWHERE),
            w_down=(below_weights[3], ANYWHERE),
        )
        outs.update(back_outs(rows, hidden))
        scratch.update(
            tall=pltpu.VMEM((hidden, D), low), work=pltpu.VMEM((rows, D), f32), give=dma(HELPERS), take=dma()
        )
    if below is None:
        outs.update(dx=((rows, D), f32, SAVE))
    else:
        scratch.update(dx=pltpu.VMEM((rows, D), f32))

    def body(refs):
        v_qkv = refs.wide.at[:, pl.ds(0, 3 * D)]
        load_qkv = pltpu.make_async_copy(refs.w_qkv, v_qkv, refs.load.at[0])
        load_qkv.start()
        if below is not None:
            refs.bias = refs.vectors.at[0]
            refs.totals[...] = jnp.zeros_like(refs.totals)
            load_down = pltpu.make_async_copy(refs.w_down, refs.tall, refs.load.at[1])
            load_down.start()
            load_up = pltpu.make_async_copy(refs.w_up, refs.wide, refs.load.at[2])
            load_out = pltpu.make_async_copy(refs.w_out, refs.tall.at[pl.ds(0, D)], refs.load.at[3])
        greet(("y", "x", "z"), depth, spread=below is not None)
        by_weights.prepare(refs)
        def dx():
            load_qkv.wait()
            refs.ready("proj", "up_dr1")

            def act(i):
                at = span(i, WIDE_D)
                refs.dx[:, at] = refs.up_dr1[:, at] + product_nt(refs.proj[...], v_qkv[at])

            over(D // WIDE_D, act)
            refs.save("dx")
            if below is not None:
                load_up.start()

        steps = [dx]
        if below is not None:

            def up_ready():
                load_out.start()
                load_up.wait()

            steps += back_steps(
                refs, lambda at: refs.dx[at], refs.tall, refs.wide, refs.tall, [load_down.wait, up_ready, load_out.wait]
            )
            ends = []
            steps.append(lambda: ends.append(to_helpers(refs.cot, refs.part_cot, refs.give, refs.take)))
        at = LAST_PLACES if below is None else BELOW_PLACES

        def grad(left, right, into, column=0):
            refs.ready(left, right)
            weight_grad(getattr(refs, left), getattr(refs, right), into, column)

        run_in_order(
            by_weights.timed(at.weights)
            + [
                (at.grads[0], partial(grad, "up_a_low", "up_dr2_low", refs.grad3)),
                (at.grads[1], partial(grad, "up_y_low", "up_du_low", refs.grad2, hidden // 2)),
                (at.grads[2], partial(grad, "low_in", "proj", refs.grad0)),
            ]
            + list(zip(at.steps, steps, strict=True))
        )
        by_weights.end()
        if below is not None:
            ends[0]()

    return call(body, "sum_weights", cid, ins, outs, scratch)


def norm_rows(resid, gain, shift):
    center = resid - jnp.mean(resid, axis=-1, keepdims=True)
    inv_std = lax.rsqrt(jnp.mean(center * center, axis=-1, keepdims=True) + layer_eps)
    normed = center * inv_std
    return (normed * gain + shift, normed, inv_std)


def norm_back(grad_rows, normed, inv_std, gain):
    scaled = grad_rows * gain
    return (
        scaled
        - jnp.mean(scaled, axis=-1, keepdims=True)
        - normed * jnp.mean(scaled * normed, axis=-1, keepdims=True)
    ) * inv_std


def dot32(a, b):
    return jnp.dot(a, b, preferred_element_type=jnp.float32)


def small_vectors(small, n_dev):
    small = small.astype(jnp.float32).T
    vectors = jnp.concatenate(
        [small[: 6 * L].reshape(L, 6, D), small[6 * L : 8 * L].reshape(L, 2, D)], axis=1
    )
    hidden_shifts = small[8 * L : 12 * L].reshape(L, 4, n_dev, D // n_dev)
    return vectors, jnp.swapaxes(hidden_shifts, 1, 2).reshape(L, -1)


def shut_keys(segs_all, segments, first, blocks_here):
    length = segs_all.shape[0]
    padding = jnp.full((BLK,), -1, jnp.int32)
    segs_all = jnp.concatenate([padding, segs_all, padding]).reshape(-1, BLK)
    segs_near = lax.dynamic_slice_in_dim(segs_all, first, blocks_here + 2, axis=0)
    seg_window = jnp.concatenate([segs_near[j : j + blocks_here] for j in range(3)], axis=1)
    spot = (first - 1 + jnp.arange(blocks_here)[:, None]) * BLK + jnp.arange(3 * BLK)[None, :]
    inside = (spot >= SHARED) & (spot < length)
    own = segments.reshape(blocks_here, 1, BLK)
    allowed = inside[:, :, None] & (seg_window[:, :, None] == jnp.concatenate([own, own], axis=2))
    return jnp.where(allowed, 0.0, masked_score)


def small_by_owner(vectors, hidden, n_dev):
    rows = jnp.moveaxis(vectors.reshape(8, n_dev, -1), 1, 0)
    rows = jnp.concatenate([rows, hidden.reshape(n_dev, 8, -1)], axis=2)
    return jnp.pad(rows, ((0, 0), (0, 0), (0, 128 - rows.shape[2])))


def small_outputs(narrow, piece, hidden):
    return (
        narrow[:, 6:8, :piece],
        narrow[:, 0:6, :piece],
        narrow[:, :, piece : piece + hidden // 8].reshape(L, -1),
    )


def share_of(rows):
    first = lax.all_gather(rows[:SHARED], SEQ, axis=0)[0]
    own = jnp.minimum(lax.axis_index(SEQ), HELPERS - 1) * SHARE
    return lax.dynamic_slice_in_dim(first, own, SHARE, axis=0)


def rows_of_all(kv, queries):
    kv = jnp.moveaxis(kv.reshape(-1, 2 * PAIRS, WIDE), 1, 0)
    return lax.all_gather(kv, SEQ, axis=0), share_of(queries)


def with_shared_rows(part, rows):
    first = lax.all_gather(part, SEQ, axis=0)[:HELPERS].reshape(SHARED, D)
    head_rows = jnp.where(lax.axis_index(SEQ) == 0, first.astype(rows.dtype), rows[:SHARED])
    return jnp.concatenate([head_rows, rows[SHARED:]], axis=0)


def on_any_slice(
    layer_input, segments, rand_blocks, w_qkv, w_out, w_up, w_down, gains, biases, up_bias, d_out
):
    seq_count, depth = lax.axis_size(SEQ), lax.axis_size(BATCH)
    n_dev = seq_count * depth
    own_index = lax.axis_index(SEQ)
    rows = layer_input.shape[1]
    blocks_here, length = rows // BLK, rows * seq_count
    picks = rand_blocks.reshape(-1)
    first = (own_index * blocks_here).reshape(1)

    piece = D // n_dev
    small = jnp.concatenate(
        [biases.reshape(-1, piece), gains.reshape(-1, piece), up_bias.reshape(-1, piece)], axis=0
    ).T
    small = lax.all_gather(small, (SEQ, BATCH), axis=0, tiled=True)
    segs_all = lax.all_gather(segments[0], SEQ, axis=0, tiled=True)
    weights = [
        [lax.all_gather(w[layer], (SEQ, BATCH), axis=0, tiled=True) for w in (w_qkv, w_out, w_up, w_down)]
        for layer in range(L)
    ]
    vectors, hidden_shifts = small_vectors(small, n_dev)
    shut = shut_keys(segs_all, segments, first[0], blocks_here)

    resid = layer_input[0].astype(jnp.float32)
    low = layer_input[0]
    saved = []
    for layer in range(L):
        mat_qkv, mat_out, mat_up, mat_down = weights[layer]
        bias = vectors[layer]
        proj = dot32(low, mat_qkv)
        queries = (proj[:, :D] + bias[0]).astype(jnp.bfloat16)
        kv = jnp.concatenate([proj[:, D : 2 * D], proj[:, 2 * D :] + bias[1]], axis=1).astype(jnp.bfloat16)
        kv_all, part = rows_of_all(kv, queries)
        mixed, part_mixed, *logs = attend(picks, first, queries, kv_all, shut, part)
        mixed = with_shared_rows(part_mixed, mixed)
        resid_one = resid + dot32(mixed, mat_out) + bias[2]
        middle, normed_one, inv_one = norm_rows(resid_one, bias[6], bias[3])
        middle_low = middle.astype(jnp.bfloat16)
        hidden = dot32(middle_low, mat_up) + hidden_shifts[layer]
        active = jax.nn.gelu(hidden, approximate=False).astype(jnp.bfloat16)
        resid_two = middle + dot32(active, mat_down) + bias[4]
        result, normed_two, inv_two = norm_rows(resid_two, bias[7], bias[5])
        saved.append(
            (low, queries, kv_all, part, logs, mixed, normed_one, inv_one, middle_low, hidden, active, normed_two, inv_two)
        )
        resid = result
        low = resid.astype(jnp.bfloat16)

    grad = d_out[0].astype(jnp.float32)
    owned = [None] * L
    for layer in reversed(range(L)):
        (low_in, queries, kv_all, part, logs, mixed, normed_one, inv_one, middle_low, hidden, active, normed_two, inv_two) = saved[layer]
        mat_qkv, mat_out, mat_up, mat_down = weights[layer]
        bias = vectors[layer]
        gain_two_grad = jnp.sum(grad * normed_two, axis=0)
        shift_two_grad = jnp.sum(grad, axis=0)
        grad_two = norm_back(grad, normed_two, inv_two, bias[7])
        grad_two_low = grad_two.astype(jnp.bfloat16)
        down_grad = product_tn(active, grad_two_low)
        active_grad = product_nt(grad_two_low, mat_down)
        hidden_grad = jax.vjp(partial(jax.nn.gelu, approximate=False), hidden)[1](active_grad)[0]
        hidden_grad_low = hidden_grad.astype(jnp.bfloat16)
        up_grad = product_tn(middle_low, hidden_grad_low)
        middle_grad = grad_two + product_nt(hidden_grad_low, mat_up)
        gain_one_grad = jnp.sum(middle_grad * normed_one, axis=0)
        shift_one_grad = jnp.sum(middle_grad, axis=0)
        grad_one = norm_back(middle_grad, normed_one, inv_one, bias[6])
        grad_one_low = grad_one.astype(jnp.bfloat16)
        out_grad = product_tn(mixed, grad_one_low)
        cot = product_nt(grad_one_low, mat_out).astype(jnp.bfloat16)
        part_cot = share_of(cot)
        part_cot = jnp.where(own_index < HELPERS, part_cot, 0)
        dq, dk, dv, part_dq = attend_back(picks, first, queries, kv_all, shut, cot, part, part_cot, *logs)
        dq = with_shared_rows(part_dq, dq)
        dkv = jnp.concatenate([dk, dv], axis=1).astype(jnp.float32)
        dkv = lax.psum_scatter(dkv, SEQ, scatter_dimension=0)
        dkv = jnp.moveaxis(dkv, 0, 1).reshape(rows, 2 * D)
        proj_grad = jnp.concatenate([dq, dkv.astype(jnp.bfloat16)], axis=1)
        qkv_grad = product_tn(low_in, proj_grad)
        small_rows = jnp.stack(
            [
                jnp.sum(dq.astype(jnp.float32), axis=0),
                jnp.sum(dkv[:, D:], axis=0),
                jnp.sum(grad_one, axis=0),
                shift_one_grad,
                jnp.sum(grad_two, axis=0),
                shift_two_grad,
                gain_one_grad,
                gain_two_grad,
            ]
        )
        small_rows = small_by_owner(small_rows, jnp.sum(hidden_grad, axis=0), n_dev)
        owned[layer] = [
            lax.psum_scatter(a, (SEQ, BATCH), scatter_dimension=0, tiled=True)
            for a in (qkv_grad, out_grad, up_grad, down_grad, small_rows)
        ]
        owned[layer][4] = owned[layer][4][0]
        grad = grad_one + product_nt(proj_grad, mat_qkv)
    stacked = [jnp.stack([owned[layer][i] for layer in range(L)]) for i in range(5)]
    return (low[None], grad[None], *stacked[:4], *small_outputs(stacked[4], piece, up_bias.shape[1]))


def assemble(wanted):
    parts = [part for _, parts in wanted for part in parts]

    def body(*refs):
        sources, targets = list(refs[: len(parts)]), refs[len(parts) :]
        for target, (_, held) in zip(targets, wanted):
            for array, layer, column in held:
                target[layer, :, column : column + array.shape[1]] = sources.pop(0)[...]

    return pl.pallas_call(
        body,
        out_shape=[jax.ShapeDtypeStruct(shape, jnp.float32) for shape, _ in wanted],
        in_specs=[IN_VMEM] * len(parts),
        out_specs=[IN_VMEM] * len(wanted),
        compiler_params=pltpu.CompilerParams(vmem_limit_bytes=VMEM_LIMIT),
        name="assemble",
    )(*[array for array, _, _ in parts])


def on_pairs(
    layer_input, segments, rand_blocks, w_qkv, w_out, w_up, w_down, gains, biases, up_bias, d_out
):
    seq_count, depth = lax.axis_size(SEQ), lax.axis_size(BATCH)
    n_dev = seq_count * depth
    rows, hidden = layer_input.shape[1], up_bias.shape[1] * n_dev
    blocks_here = rows // BLK
    picks = rand_blocks.reshape(-1)
    first = (lax.axis_index(SEQ) * blocks_here).reshape(1)
    piece = D // n_dev

    small = jnp.concatenate(
        [biases.reshape(-1, piece), gains.reshape(-1, piece), up_bias.reshape(-1, piece)], axis=0
    ).T
    small = jnp.pad(small, ((0, 0), (0, 128 - small.shape[1])))
    segs = jnp.pad(segments.reshape(-1, 128), ((0, 8 - rows // 128), (0, 0)))

    def flat(slabs):
        return [w.reshape(-1, w.shape[2]) for w in slabs]

    places = jnp.stack([picks // blocks_here, picks % blocks_here])

    def attention_back(got, back):
        return attend_back(
            picks, first, got.q, got.every.reshape(seq_count, 2 * PAIRS, rows, WIDE), shut, back.cot, got.part, back.part_cot, got.log, got.plog
        )

    x = layer_input[0]
    layers = [[(w, layer) for w in (w_qkv, w_out, w_up, w_down)] for layer in range(L)]
    own_segs = segments.reshape(blocks_here, BLK).astype(jnp.float32)
    own_segs = jnp.concatenate([own_segs, own_segs], axis=1)
    head_one, weights_one = first_head(x, small, segs, own_segs, places, layers[0], seq_count, depth, 0)
    weights_one = flat(weights_one)
    vectors = head_one.vectors
    shifts = head_one.table.reshape(L, 4, n_dev, piece)
    shifts = jnp.swapaxes(shifts, 1, 2).reshape(L, 1, hidden)
    shut = head_one.shut
    rows_one, weights_two = tail(
        head_one.o, head_one.po, x, vectors, shifts[0], weights_one, layers[1], shut, places, seq_count, depth, 1
    )
    weights_two = flat(weights_two)
    middle = rows_one.z_low
    rows_two = turn(rows_one.o, rows_one.po, rows_one.z, vectors, shifts[1], weights_two, d_out[0], depth, 2)
    dq, dk, dv, part = attention_back(rows_one, rows_two)
    sums_two = sum_rows(dk, dv, dq, part, rows_two, rows_two, seq_count, depth, 3)
    back_one = sum_weights(
        rows_two, middle, sums_two.proj, vectors, weights_two[0], None, (weights_one, rows_one), n_dev, depth, 4
    )
    dq, dk, dv, part = attention_back(head_one, back_one)
    sums_one = sum_rows(dk, dv, dq, part, rows_one, back_one, seq_count, depth, 5)
    small = jnp.concatenate(
        [
            small_by_owner(back.totals + sums.totals, back.hidden_totals[0], n_dev)
            for back, sums in ((back_one, sums_one), (rows_two, sums_two))
        ],
        axis=1,
    )
    last = sum_weights(
        SimpleNamespace(**{**vars(rows_one), **vars(back_one)}),
        x, sums_one.proj, None, weights_one[0], small, None, n_dev, depth, 6,
    )
    whole_outputs = assemble(
        [
            ((L, piece, 3 * D), [(last.owned0, 0, 0), (back_one.owned0, 1, 0)]),
            ((L, piece, D), [(sums_one.owned1, 0, 0), (sums_two.owned1, 1, 0)]),
            (
                (L, piece, hidden),
                [
                    (sums_one.owned2, 0, 0), (last.owned2, 0, hidden // 2),
                    (sums_two.owned2, 1, 0), (back_one.owned2, 1, hidden // 2),
                ],
            ),
            ((L, hidden // n_dev, D), [(last.owned3, 0, 0), (back_one.owned3, 1, 0)]),
            ((1, rows, D), [(last.dx, 0, 0)]),
        ]
    )
    return (
        rows_two.z_low[None],
        whole_outputs[4],
        *whole_outputs[:4],
        *small_outputs(last.owned4.reshape(L, 8, 128), piece, up_bias.shape[1]),
    )


def solution(mesh):
    placed = (
        P(BATCH, SEQ, None),
        P(BATCH, SEQ),
        P(BATCH, SEQ, None, None),
        P(None, (SEQ, BATCH), None),
        P(None, (SEQ, BATCH), None),
        P(None, (SEQ, BATCH), None),
        P(None, (SEQ, BATCH), None),
        P(None, None, (SEQ, BATCH)),
        P(None, None, (SEQ, BATCH)),
        P(None, (SEQ, BATCH)),
        P(BATCH, SEQ, None),
    )
    return jax.shard_map(
        on_pairs if mesh.shape[SEQ] == 8 and mesh.shape[BATCH] == 4 else on_any_slice,
        mesh=mesh,
        in_specs=placed,
        out_specs=(
            P(BATCH, SEQ, None),
            P(BATCH, SEQ, None),
            P(None, (SEQ, BATCH), None),
            P(None, (SEQ, BATCH), None),
            P(None, (SEQ, BATCH), None),
            P(None, (SEQ, BATCH), None),
            P(None, None, (SEQ, BATCH)),
            P(None, None, (SEQ, BATCH)),
            P(None, (SEQ, BATCH)),
        ),
        check_vma=False,
    )
```

```python
import itertools
from functools import partial
from types import SimpleNamespace

import jax
import jax.numpy as jnp
from jax import lax
from jax.experimental import pallas as pl
from jax.experimental.pallas import tpu as pltpu
from jax.sharding import PartitionSpec as P

MESH = pl.DeviceIdType.MESH
SEQ, BATCH = "seq", "batch"


HEAD_PLACES = SimpleNamespace(
    begins=(1, 4, 3, 2, 0, 64, 61, 56, 14),
    arrivals=(
        (8, 9, 21, 10, 22, 20, 36, 23, 37, 38, 55, 39, 51, 52, 62),
        (15, 16, 27),
        (19, 17, 29, 18, 30, 31, 45, 32, 57, 46, 58, 47, 59, 60, 69),
        (11, 12, 44, 13, 24, 25, 40, 26, 41, 42, 53, 43, 75, 54, 63),
        (5, 6, 28, 7, 33, 34, 65, 35, 66, 67, 86, 68, 87, 88, 106),
        (81, 82, 136, 83, 107, 108, 131, 100, 130, 132, 143, 118, 144, 142, 150),
        (78, 79, 103, 80, 104, 105, 127, 102, 128, 129, 145, 125, 140, 141, 149),
        (76, 99, 119, 74, 96, 117, 135, 77, 97, 122, 126, 98, 120, 138, 146),
        (48, 70, 111, 50, 71, 91, 121, 49, 72, 92, 114, 73, 90, 115, 133),
        (113, 109, 134),
        (123, 124, 139),
        (94, 95, 116),
        (110, 112, 137),
    ),
    project=84,
    attention=(147, 148, 151),
)
TAIL_PLACES = SimpleNamespace(
    begins=(1, 2, 0, 14, 38, 43, 4),
    arrivals=(
        (10, 11, 19, 12, 20, 21, 61, 22, 42, 33, 47, 34, 49, 48, 70),
        (32, 13, 23, 17, 26, 24, 46, 25, 35, 36, 52, 37, 53, 54, 71),
        (6, 7, 27, 8, 28, 29, 62, 31, 50, 56, 74, 51, 72, 75, 92),
        (39, 40, 63, 41, 64, 65, 93, 66, 86, 87, 108, 88, 129, 110, 128),
        (55, 59, 80, 60, 111, 89, 105, 79, 118, 98, 122, 101, 123, 124, 137),
        (67, 81, 95, 68, 82, 106, 125, 69, 83, 112, 126, 84, 107, 127, 136),
        (57, 78, 100, 73, 96, 102, 120, 58, 99, 113, 121, 91, 103, 119, 132),
        (97, 104, 130),
        (114, 115, 135),
        (133, 117, 134),
        (116, 109, 131),
    ),
    steps=(3, 5, 9, 15, 16, 18, 30, 44, 45),
    project=76,
    attention=(138, 139, 140),
)
ROWS_PLACES = SimpleNamespace(
    rows=(
        (0, 3, 4, 17, 53),
        (1, 7, 9, 25, 45),
        (11, 23, 21, 43, 52),
        (6, 13, 30, 38, 54),
    ),
    weights=(
        (5, 10, 16, 14, 15, 8, 19, 18, 12, 24, 20, 34, 31, 22, 32, 46, 55),
        (27, 28, 29, 37, 33, 39, 36, 41, 35, 47, 42, 44, 40, 49, 50, 48, 56),
    ),
    grads=(2, 26),
    collect=51,
)
BELOW_PLACES = SimpleNamespace(
    weights=(
        (9, 12, 11, 14, 47, 36, 45, 27, 66, 48, 20, 52, 70, 54, 61, 73, 77),
        (10, 37, 49, 24, 58, 26, 33, 69, 68, 30, 32, 64, 72, 40, 63, 75, 78),
        (6, 22, 18, 23, 31, 21, 39, 29, 42, 38, 43, 46, 60, 53, 62, 74, 76),
        (1, 4, 3, 2, 15, 13, 7, 19, 41, 17, 44, 28, 59, 16, 55, 67, 71),
    ),
    grads=(8, 5, 0),
    steps=(25, 34, 35, 50, 51, 56, 57, 65),
)
LAST_PLACES = SimpleNamespace(
    weights=(
        (22, 31, 32, 33, 61, 36, 57, 65, 74, 41, 63, 67, 79, 58, 72, 84, 88),
        (21, 43, 45, 47, 62, 46, 48, 75, 77, 51, 64, 78, 80, 56, 83, 81, 87),
        (11, 29, 34, 40, 49, 50, 44, 37, 52, 53, 55, 60, 68, 66, 70, 82, 86),
        (9, 13, 15, 18, 30, 35, 23, 42, 54, 25, 27, 59, 71, 39, 69, 76, 85),
        (1, 2, 5, 12, 14, 3, 4, 17, 24, 6, 7, 16, 28, 8, 19, 26, 38),
    ),
    grads=(20, 10, 0),
    steps=(73,),
)


def place():
    s = lax.axis_index(SEQ)
    return {"y": s // 4, "x": (s // 2) % 2, "c": s % 2, "z": lax.axis_index(BATCH)}


def device_of(p):
    return ((p["y"] * 2 + p["x"]) * 2 + p["c"], p["z"])


def flipped(p, axis):
    return {**p, axis: 1 - p[axis]}


def at_depth(p, z):
    return {**p, "z": z}


def number_in(depth):
    return lambda p: device_of(p)[0] * depth + p["z"]


def number_in_sequence(p):
    return device_of(p)[0]


def when(cond, action):
    if cond is None:
        action()
    else:
        pl.when(cond)(action)


def ranked(z, rank, depth):
    near = [sorted(range(depth), key=lambda q: (abs(q - k), q))[rank] for k in range(depth)]
    return sum(jnp.where(z == k, near[k], 0) for k in range(depth))


def offsets(order, depth):
    return list(itertools.product(*[range(depth if a == "z" else 2) for a in order]))


def target_of(order, offset, depth, me):
    p = me
    for axis, d in zip(order, offset):
        if d:
            p = at_depth(p, ranked(me["z"], d, depth)) if axis == "z" else flipped(p, axis)
    return p


def last_move(offset):
    return max([-1] + [i for i, d in enumerate(offset) if d])


def greet(axes, depth, spread=False, collect=False):
    me = place()
    barrier = pltpu.get_barrier_semaphore()

    def signal(device):
        pl.semaphore_signal(barrier, inc=1, device_id=device, device_id_type=MESH)

    count = 0
    for axis in axes + ("c",):
        if axis == "z":
            for step in (1, -1):
                peer = at_depth(me, me["z"] + step)
                cond = (peer["z"] >= 0) & (peer["z"] < depth)
                when(cond, lambda peer=peer: signal(device_of(peer)))
                count = count + cond.astype(jnp.int32)
        else:
            signal(device_of(flipped(me, axis)))
            count = count + 1
    if spread or collect:
        seq, z = lax.axis_index(SEQ), lax.axis_index(BATCH)
        if spread:
            when(seq != 0, lambda: signal((0, z)))
            count = count + jnp.where(seq == 0, HELPERS - 1, 0)
        if collect:

            @pl.when(seq == 0)
            def _():
                for j in range(1, HELPERS):
                    signal((j, z))

            count = count + jnp.where(seq == 0, 0, 1)
    pl.semaphore_wait(barrier, count)


class Gather:
    def __init__(self, source, target, number, order, depth, send, recv, send_at):
        self.source, self.target, self.number = source, target, number
        self.order, self.depth, self.send, self.recv = order, depth, send, recv
        self.send_at = send_at
        self.me = place()
        self.sent = []

    @staticmethod
    def sends(order, depth):
        return sum(len(order) + 2 - last_move(t) for t in offsets(order, depth))

    def onward(self, offset):
        last = last_move(offset)
        z = self.me["z"]
        moves = []
        if last >= 0 and self.order[last] == "z":
            source = ranked(z, offset[last], self.depth)
            peer = jnp.where(source < z, z + 1, z - 1)
            moves.append((at_depth(self.me, peer), (peer >= 0) & (peer < self.depth)))
        for axis in self.order[last + 1 :]:
            if axis == "z":
                moves.append((at_depth(self.me, z + 1), z + 1 < self.depth))
                moves.append((at_depth(self.me, z - 1), z > 0))
            else:
                moves.append((flipped(self.me, axis), None))
        moves.append((flipped(self.me, "c"), None))
        return moves

    def arrival(self, p):
        ref = self.target(p)
        return pltpu.make_async_remote_copy(
            src_ref=ref, dst_ref=ref, send_sem=self.send.at[0], recv_sem=self.recv.at[self.number(p)],
            device_id=device_of(self.me), device_id_type=MESH,
        )

    def handle(self, offset):
        p = target_of(self.order, offset, self.depth, self.me)
        own = not any(offset)
        if not own:
            self.arrival(p).wait_recv()
        for peer, cond in self.onward(offset):
            copy = pltpu.make_async_remote_copy(
                src_ref=self.source if own else self.target(p), dst_ref=self.target(p),
                send_sem=self.send.at[self.send_at], recv_sem=self.recv.at[self.number(p)],
                device_id=device_of(peer), device_id_type=MESH,
            )
            when(cond, copy.start)
            self.sent.append((cond, self.send_at))
            self.send_at += 1

    def begin(self):
        self.handle((0,) * len(self.order))

    def events(self, places):
        marks = [t for t in offsets(self.order, self.depth) if any(t)]
        return [(at, partial(self.handle, t)) for at, t in zip(places, marks, strict=True)]

    def siblings(self):
        for t in offsets(self.order, self.depth):
            self.arrival(flipped(target_of(self.order, t, self.depth, self.me), "c")).wait_recv()

    def drain(self):
        for cond, slot in self.sent:
            copy = pltpu.make_async_remote_copy(
                src_ref=self.source, dst_ref=self.target(self.me), send_sem=self.send.at[slot],
                recv_sem=self.recv.at[self.number(self.me)], device_id=device_of(self.me), device_id_type=MESH,
            )
            when(cond, copy.wait_send)


class Reduce:
    def __init__(self, partial_of, far_partial_of, inbox, order, depth, send, recv):
        self.partial_of, self.far_partial_of, self.inbox = partial_of, far_partial_of, inbox
        self.order, self.depth, self.send, self.recv = order, depth, send, recv
        self.me = place()
        self.base, _ = self.slots(order, depth)
        self.marks = sorted(offsets(order, depth), key=lambda t: (-sum(t), t))
        self.sent = []

    @staticmethod
    def split(order, offset):
        if "z" not in order:
            return offset, 0
        i = order.index("z")
        return offset[:i] + (0,) + offset[i + 1 :], offset[i]

    @staticmethod
    def slots(order, depth):
        base, count = {}, 0
        deep = depth if "z" in order else 1
        for t in offsets(order, depth):
            key, rank = Reduce.split(order, t)
            if rank:
                continue
            last = last_move(key)
            for i, axis in enumerate(order):
                if i <= last:
                    continue
                base[(key, axis)] = count
                if axis == "z":
                    count += deep + 1
                elif "z" in order and i > order.index("z"):
                    count += deep
                else:
                    count += 1
            base[(key, "c")] = count
            count += deep
        return base, count

    def where_(self, key, axis, z):
        deep = "z" in self.order and (axis == "c" or self.order.index(axis) > self.order.index("z"))
        return self.base[(key, axis)] + (z if deep else 0)

    def copy(self, source, edge, slot, peer):
        return pltpu.make_async_remote_copy(
            src_ref=source, dst_ref=self.inbox.at[edge], send_sem=self.send.at[slot],
            recv_sem=self.recv.at[edge], device_id=device_of(peer), device_id_type=MESH,
        )

    def start(self, offset):
        p = target_of(self.order, offset, self.depth, self.me)
        key, _ = self.split(self.order, offset)
        slot = self.marks.index(offset)
        edge = self.where_(key, "c", p["z"])
        peer = flipped(self.me, "c")
        self.copy(self.far_partial_of(flipped(p, "c")), edge, slot, peer).start()
        self.sent.append(slot)

    def kids(self, offset, p):
        key, rank = self.split(self.order, offset)
        last, z = last_move(offset), self.me["z"]
        found = [(self.where_(key, "c", p["z"]), None)]
        for axis in self.order[last + 1 :]:
            if axis == "z":
                at = self.base[(key, "z")]
                found += [(at + z, z > 0), (at + self.depth, z + 1 < self.depth)]
            else:
                found.append((self.where_(key, axis, p["z"]), None))
        if last >= 0 and self.order[last] == "z":
            far = jnp.where(p["z"] < z, z + 1, z - 1)
            found.append((self.base[(key, "z")] + p["z"], (far >= 0) & (far < self.depth)))
        return found

    def upward(self, offset, p):
        key, rank = self.split(self.order, offset)
        k, z = last_move(offset), self.me["z"]
        axis = self.order[k]
        if axis == "z":
            edge = self.base[(key, "z")] + jnp.where(p["z"] == z - 1, self.depth, p["z"])
            return edge, at_depth(self.me, jnp.where(p["z"] < z, z - 1, z + 1))
        parent = key[:k] + (0,) + key[k + 1 :]
        return self.where_(parent, axis, p["z"]), flipped(self.me, axis)

    def handle(self, offset, add, finish):
        p = target_of(self.order, offset, self.depth, self.me)
        kids = self.kids(offset, p)
        slot = len(self.marks) + self.marks.index(offset)
        for edge, cond in kids:
            when(cond, self.copy(self.inbox.at[edge], edge, slot, self.me).wait_recv)
        parts = [(self.inbox.at[edge], cond) for edge, cond in kids]
        if any(offset):
            into = parts[0][0]
            add(self.partial_of(p), parts, into)
            edge, peer = self.upward(offset, p)
            self.copy(into, edge, slot, peer).start()
            self.sent.append(slot)
        else:
            finish(self.partial_of(p), parts)

    def drain(self):
        for slot in self.sent:
            self.copy(self.inbox.at[0], 0, slot, self.me).wait_send()


D = 768
H = 12
DH = 64
BLK = 64
R = 3
GLOB = 2
L = 2
PAIRS = H // 2
WIDE = 2 * DH
SHARED = GLOB * BLK
SHARE = 16
HELPERS = SHARED // SHARE
VMEM_LIMIT = 60 * 1024 * 1024

layer_eps = 1e-06
masked_score = -1e30

Z_Y_X, Z_X_Y, X_Y_Z, Y_X_Z = ("z", "y", "x"), ("z", "x", "y"), ("x", "y", "z"), ("y", "x", "z")
Y_X, X_Y = ("y", "x"), ("x", "y")
ANYWHERE = pl.BlockSpec(memory_space=pl.ANY)
IN_SMEM = pl.BlockSpec(memory_space=pltpu.SMEM)
IN_VMEM = pl.BlockSpec(memory_space=pltpu.VMEM)
LOAD, SAVE = pl.BlockSpec(memory_space=pl.ANY), pl.BlockSpec(memory_space=pl.ANY)


def dma(*shape):
    return pltpu.SemaphoreType.DMA(shape)


def product(a, b):
    return lax.dot_general(a, b, (((1,), (0,)), ((), ())), preferred_element_type=jnp.float32)


def product_nt(a, b):
    return lax.dot_general(a, b, (((1,), (1,)), ((), ())), preferred_element_type=jnp.float32)


def product_tn(a, b):
    return lax.dot_general(a, b, (((0,), (0,)), ((), ())), preferred_element_type=jnp.float32)


def split_heads(pair_rows):
    low_lanes = lax.broadcasted_iota(jnp.int32, (1, WIDE), 1) < DH
    zero = jnp.zeros_like(pair_rows)
    return jnp.concatenate([jnp.where(low_lanes, pair_rows, zero), jnp.where(low_lanes, zero, pair_rows)], axis=0)


def join_heads(stacked):
    low_lanes = lax.broadcasted_iota(jnp.int32, (1, WIDE), 1) < DH
    rows = stacked.shape[0] // 2
    return jnp.where(low_lanes, stacked[:rows], stacked[rows:])


def row_of(block):
    return pl.multiple_of(block * BLK, BLK)


class Keys:
    def __init__(self, ref, pair=None):
        self.ref, self.pair = ref, pair
        self.held = ref.shape[2] // (BLK if pair is None else 1)
        self.blocks_all = ref.shape[0] * self.held

    def block(self, device, inner):
        if self.pair is None:
            return self.ref[device, 0, pl.ds(row_of(inner), BLK)]
        return self.ref[device, self.pair, inner]

    def whole(self):
        held = self.ref[...] if self.pair is None else self.ref[:, self.pair]
        return held.reshape(-1, WIDE)

    def with_shared(self, near):
        if self.pair is None:
            shared = self.ref[0, 0, 0:SHARED]
        else:
            shared = self.ref[0, self.pair, 0:GLOB].reshape(SHARED, WIDE)
        return jnp.concatenate([shared, near], axis=0)


def window_blocks(first, block, blocks_all):
    return [(first + block + j - 1 + blocks_all) % blocks_all for j in range(3)]


def drawn_blocks(picks_ref, pair, block, r):
    return [picks_ref[(block * H + 2 * pair + side) * R + r] for side in range(2)]


def bring(drawn, first, pairs, blocks_here):
    low_lanes = lax.broadcasted_iota(jnp.int32, (1, WIDE), 1) < DH
    for block in range(blocks_here):
        for source, target in pairs:
            for j, one in enumerate(window_blocks(first, block, source.blocks_all)):
                rows = source.block(one // source.held, one % source.held)
                target[block, j * BLK : (j + 1) * BLK] = rows
            for r in range(R):
                one, two = drawn(block, r)
                target[block, (3 + r) * BLK : (4 + r) * BLK] = jnp.where(
                    low_lanes, source.block(*one), source.block(*two)
                )


def key_scores(keys, q_heads, shut):
    scores = product_nt(keys, q_heads)
    end = SHARED + 3 * BLK
    return jnp.concatenate([scores[:SHARED], scores[SHARED:end] + shut, scores[end:]], axis=0)


def soft(scores):
    top = jnp.max(scores, axis=0, keepdims=True)
    weight = jnp.exp(scores - top)
    total = jnp.sum(weight, axis=0, keepdims=True)
    return weight * (1.0 / total), top + jnp.log(total)


def attend_pair(
    drawn, first, q_ref, keys, values, shut_ref, part_ref, o_ref, po_ref, log_ref, plog_ref, near_k, near_v
):
    blocks_here = q_ref.shape[0] // BLK
    bring(drawn, first, [(keys, near_k), (values, near_v)], blocks_here)
    scale = jnp.bfloat16(DH ** (-0.5))
    weight, logs = soft(product_nt(keys.whole(), split_heads(part_ref[...] * scale)))
    mixed = product_tn(weight.astype(jnp.bfloat16), values.whole())
    po_ref[...] = join_heads(mixed).astype(po_ref.dtype)
    plog_ref[0] = logs
    for block in range(blocks_here):
        here = slice(block * BLK, (block + 1) * BLK)
        q_heads = split_heads(q_ref[here] * scale)
        weight, logs = soft(key_scores(keys.with_shared(near_k[block]), q_heads, shut_ref[block]))
        mixed = product_tn(weight.astype(jnp.bfloat16), values.with_shared(near_v[block]))
        o_ref[here] = join_heads(mixed).astype(o_ref.dtype)
        log_ref[0, block : block + 1] = logs


def drawn_places(picks_ref, pair, held):
    def drawn(block, r):
        return [(one // held, one % held) for one in drawn_blocks(picks_ref, pair, block, r)]

    return drawn


def attend_kernel(picks_ref, first_ref, q_ref, k_ref, v_ref, *refs):
    keys, values = Keys(k_ref), Keys(v_ref)
    drawn = drawn_places(picks_ref, pl.program_id(0), keys.held)
    attend_pair(drawn, first_ref[0], q_ref, keys, values, *refs)


def near_rows(rows, dtype):
    return pltpu.VMEM((rows // BLK, 6 * BLK, WIDE), dtype)


def columns(rows, shift=0):
    return pl.BlockSpec((rows, WIDE), lambda p, *_: (0, p + shift))


def of_all(kv, shift=0):
    return pl.BlockSpec((kv.shape[0], 1, kv.shape[2], WIDE), lambda p, *_: (0, p + shift, 0, 0))


def by_pair(rows, lanes):
    return pl.BlockSpec((1, rows, lanes), lambda p, *_: (p, 0, 0))


def attend(picks, first, queries, kv, shut, part):
    rows = queries.shape[0]
    blocks = rows // BLK
    return pl.pallas_call(
        attend_kernel,
        grid_spec=pltpu.PrefetchScalarGridSpec(
            num_scalar_prefetch=2,
            grid=(PAIRS,),
            in_specs=[
                columns(rows), of_all(kv), of_all(kv, PAIRS),
                pl.BlockSpec(shut.shape, lambda p, *_: (0, 0, 0)), columns(SHARE),
            ],
            out_specs=[columns(rows), columns(SHARE), by_pair(blocks, WIDE), by_pair(1, 2 * SHARE)],
            scratch_shapes=[near_rows(rows, jnp.bfloat16)] * 2,
        ),
        out_shape=[
            jax.ShapeDtypeStruct((rows, D), jnp.bfloat16),
            jax.ShapeDtypeStruct((SHARE, D), jnp.bfloat16),
            jax.ShapeDtypeStruct((PAIRS, blocks, WIDE), jnp.float32),
            jax.ShapeDtypeStruct((PAIRS, 1, 2 * SHARE), jnp.float32),
        ],
        compiler_params=pltpu.CompilerParams(vmem_limit_bytes=VMEM_LIMIT),
        name="attend",
    )(picks, first, queries, kv, kv, shut, part)


def score_grads(weight, values, cot_heads):
    grads = product_nt(values, cot_heads)
    mean = jnp.sum(weight * grads, axis=0, keepdims=True)
    return (weight * (grads - mean)).astype(jnp.bfloat16)


def attend_back_kernel(
    picks_ref, first_ref, q_ref, k_ref, v_ref, shut_ref, do_ref, part_ref, pdo_ref, log_ref, plog_ref,
    dq_ref, dk_ref, dv_ref, pdq_ref, sum_k, sum_v, near_k, near_v, grad_k, grad_v,
):
    pair = pl.program_id(0)
    first = first_ref[0]
    blocks_here, blocks_all = q_ref.shape[0] // BLK, sum_k.shape[0] // BLK
    all_keys, all_values = Keys(k_ref), Keys(v_ref)
    drawn = drawn_places(picks_ref, pair, all_keys.held)
    bring(drawn, first, [(all_keys, near_k), (all_values, near_v)], blocks_here)
    low_lanes = lax.broadcasted_iota(jnp.int32, (1, WIDE), 1) < DH
    step = DH ** (-0.5)
    scale = jnp.bfloat16(step)
    part, cot = split_heads(part_ref[...] * scale), split_heads(pdo_ref[...])
    weight = jnp.exp(product_nt(all_keys.whole(), part) - plog_ref[0])
    grads = score_grads(weight, all_values.whole(), cot)
    pdq_ref[...] = (join_heads(product_tn(grads, all_keys.whole())) * step).astype(pdq_ref.dtype)
    sum_k[...] = product(grads, part)
    sum_v[...] = product(weight.astype(jnp.bfloat16), cot)
    shared_k = jnp.zeros((SHARED, WIDE), jnp.float32)
    shared_v = jnp.zeros((SHARED, WIDE), jnp.float32)
    for block in range(blocks_here):
        here = slice(block * BLK, (block + 1) * BLK)
        do = jnp.where(first + block < GLOB, jnp.bfloat16(0), do_ref[here])
        q_heads, do_heads = split_heads(q_ref[here] * scale), split_heads(do)
        keys, values = all_keys.with_shared(near_k[block]), all_values.with_shared(near_v[block])
        weight = jnp.exp(key_scores(keys, q_heads, shut_ref[block]) - log_ref[0, block : block + 1])
        grads = score_grads(weight, values, do_heads)
        dq_ref[here] = (join_heads(product_tn(grads, keys)) * step).astype(dq_ref.dtype)
        key_grad = product(grads, q_heads)
        value_grad = product(weight.astype(jnp.bfloat16), do_heads)
        shared_k = shared_k + key_grad[:SHARED]
        shared_v = shared_v + value_grad[:SHARED]
        grad_k[block] = key_grad[SHARED:]
        grad_v[block] = value_grad[SHARED:]
    sum_k[0:SHARED] += shared_k
    sum_v[0:SHARED] += shared_v
    for block in range(blocks_here):
        for grad, total in ((grad_k, sum_k), (grad_v, sum_v)):
            for j, one in enumerate(window_blocks(first, block, blocks_all)):
                total[pl.ds(row_of(one), BLK)] += grad[block, j * BLK : (j + 1) * BLK]
            for r in range(R):
                tile = grad[block, (3 + r) * BLK : (4 + r) * BLK]
                one, two = drawn_blocks(picks_ref, pair, block, r)
                total[pl.ds(row_of(one), BLK)] += jnp.where(low_lanes, tile, 0.0)
                total[pl.ds(row_of(two), BLK)] += jnp.where(low_lanes, 0.0, tile)
    dk_ref[...] = sum_k[...].astype(dk_ref.dtype).reshape(dk_ref.shape)
    dv_ref[...] = sum_v[...].astype(dv_ref.dtype).reshape(dv_ref.shape)


def attend_back(picks, first, queries, kv, shut, cot, part, part_cot, logs, part_logs):
    rows, grads = queries.shape[0], (kv.shape[0], PAIRS) + kv.shape[2:]
    length = kv.shape[0] * kv.shape[2]
    return pl.pallas_call(
        attend_back_kernel,
        grid_spec=pltpu.PrefetchScalarGridSpec(
            num_scalar_prefetch=2,
            grid=(PAIRS,),
            in_specs=[
                columns(rows), of_all(kv), of_all(kv, PAIRS),
                pl.BlockSpec(shut.shape, lambda p, *_: (0, 0, 0)), columns(rows), columns(SHARE), columns(SHARE),
                by_pair(rows // BLK, WIDE), by_pair(1, 2 * SHARE),
            ],
            out_specs=[columns(rows), of_all(kv), of_all(kv), columns(SHARE)],
            scratch_shapes=[pltpu.VMEM((length, WIDE), jnp.float32)] * 2
            + [near_rows(rows, jnp.bfloat16)] * 2
            + [near_rows(rows, jnp.float32)] * 2,
        ),
        out_shape=[
            jax.ShapeDtypeStruct((rows, D), jnp.bfloat16),
            jax.ShapeDtypeStruct(grads, jnp.bfloat16),
            jax.ShapeDtypeStruct(grads, jnp.bfloat16),
            jax.ShapeDtypeStruct((SHARE, D), jnp.bfloat16),
        ],
        compiler_params=pltpu.CompilerParams(vmem_limit_bytes=VMEM_LIMIT),
        name="attend_back",
    )(picks, first, queries, kv, kv, shut, cot, part, part_cot, logs, part_logs)


def call(body, name, cid, ins, outs, scratch):
    loads = [k for k, (_, where) in ins.items() if where is LOAD]
    saves = [k for k, (_, _, where) in outs.items() if where is SAVE]
    names = ["far_" + k if k in loads or k in saves else k for k in (*ins, *outs)]
    scratch = {
        **scratch,
        **{k: pltpu.VMEM(ins[k][0].shape, ins[k][0].dtype) for k in loads},
        **{k: pltpu.VMEM(outs[k][0], outs[k][1]) for k in saves},
        **dict(moves=dma(len(loads) + len(saves) + 1)),
    }

    def run(*given):
        refs = SimpleNamespace(**dict(zip(names + list(scratch), given)))
        copies = {}
        for i, k in enumerate(loads + saves):
            pair = (getattr(refs, "far_" + k), getattr(refs, k))
            copies[k] = pltpu.make_async_copy(*(pair if k in loads else pair[::-1]), refs.moves.at[i])
        coming, going = list(loads), []
        for k in loads:
            copies[k].start()

        def ready(*wanted):
            for k in wanted:
                if k in coming:
                    coming.remove(k)
                    copies[k].wait()

        def save(*given):
            for k in given:
                if k in saves:
                    going.append(k)
                    copies[k].start()

        refs.ready, refs.save = ready, save
        body(refs)
        ready(*loads)
        save(*[k for k in saves if k not in going])
        for k in saves:
            copies[k].wait()

    got = pl.pallas_call(
        run,
        out_shape=[jax.ShapeDtypeStruct(shape, dtype) for shape, dtype, _ in outs.values()],
        in_specs=[where for _, where in ins.values()],
        out_specs=[where for _, _, where in outs.values()],
        scratch_shapes=list(scratch.values()),
        compiler_params=pltpu.CompilerParams(
            collective_id=cid, has_side_effects=True, vmem_limit_bytes=VMEM_LIMIT
        ),
        name=name,
    )(*[array for array, _ in ins.values()])
    return SimpleNamespace(**dict(zip(outs, got)))


def over(count, act):
    def step(i, carry):
        act(i)
        return carry

    lax.fori_loop(0, count, step, 0)


def span(i, size, first=0):
    return pl.ds(pl.multiple_of(first + i * size, size), size)


def run_in_order(timed):
    for _, act in sorted(timed, key=lambda pair: pair[0]):
        act()


def layer_pieces(rows_in, rows_down, first):
    half, wide = rows_down // 2, 3 * D // 2
    return [
        (first, 0, rows_in, 0, wide, Z_Y_X),
        (first, 0, rows_in, wide, wide, Z_X_Y),
        (first + 1, 0, rows_in, 0, D, Z_X_Y),
        (first + 2, 0, rows_in, 0, 2 * D, Z_Y_X),
        (first + 2, 0, rows_in, 2 * D, 2 * D, Z_X_Y),
        (first + 3, 0, half, 0, D, X_Y_Z),
        (first + 3, half, half, 0, D, Y_X_Z),
    ]


class Gathering:
    def __init__(self, arrays, pieces, seq_count, depth, near):
        self.near, self.layers = near, [layer for _, layer in arrays]
        shapes = [a.shape if layer is None else a.shape[1:] for a, layer in arrays]
        self.shapes = [jax.ShapeDtypeStruct(shape, a.dtype) for shape, (a, _) in zip(shapes, arrays)]
        arrays = [a for a, _ in arrays]
        self.arrays, self.pieces, self.depth, self.n_dev = arrays, pieces, depth, seq_count * depth
        flat_only = {which for which, *_, order in pieces if "z" not in order}
        self.counts = [seq_count if i in flat_only else self.n_dev for i in range(len(arrays))]

    def ins(self):
        return {"slab%d" % i: (a, ANYWHERE) for i, a in enumerate(self.arrays)}

    def outs(self):
        return {
            "every%d" % i: ((n,) + a.shape, a.dtype, SAVE if i in self.near else ANYWHERE)
            for i, (n, a) in enumerate(zip(self.counts, self.shapes))
        }

    def scratch(self):
        total = sum(Gather.sends(order, self.depth) for *_, order in self.pieces)
        return {
            "g_send": dma(total),
            "g_recv": dma(len(self.pieces), self.n_dev),
            "g_local": dma(len(self.arrays)),
        }

    def number(self, i):
        return number_in(self.depth) if self.counts[i] == self.n_dev else number_in_sequence

    def begin(self, refs):
        slabs = [getattr(refs, "slab%d" % i) for i in range(len(self.arrays))]
        slabs = [ref if layer is None else ref.at[layer] for ref, layer in zip(slabs, self.layers)]
        every = [getattr(refs, "every%d" % i) for i in range(len(self.arrays))]
        self.jobs, at = [], 0
        for k, (which, row, rows, column, columns_, order) in enumerate(self.pieces):
            window = (pl.ds(row, rows), pl.ds(column, columns_))
            number = self.number(which)
            self.jobs.append(
                Gather(
                    slabs[which].at[window],
                    lambda p, which=which, window=window, number=number: every[which].at[(number(p),) + window],
                    number, order, self.depth, refs.g_send, refs.g_recv.at[k], at,
                )
            )
            at += Gather.sends(order, self.depth)
        me = place()
        self.own = [
            pltpu.make_async_copy(slab, all_.at[self.number(i)(me)], refs.g_local.at[i])
            for i, (slab, all_) in enumerate(zip(slabs, every))
        ]
        for copy in self.own:
            copy.start()

    def hurry(self, refs, arrays):
        for (which, *_), job in zip(self.pieces, self.jobs):
            if which in arrays:
                job.siblings()
        for i in arrays:
            self.own[i].wait()
            refs.save("every%d" % i)
        self.early = arrays

    def end(self):
        for (which, *_), job in zip(self.pieces, self.jobs):
            if which not in self.early:
                job.siblings()
        for job in self.jobs:
            job.drain()
        for i, copy in enumerate(self.own):
            if i not in self.early:
                copy.wait()

    def results(self, got):
        return [getattr(got, "every%d" % i) for i in range(len(self.arrays))]


def to_helpers(source, target, send, recv):
    seq, z = lax.axis_index(SEQ), lax.axis_index(BATCH)

    def copy(j):
        return pltpu.make_async_remote_copy(
            src_ref=source.at[pl.ds(j * SHARE, SHARE)], dst_ref=target, send_sem=send.at[j],
            recv_sem=recv, device_id=(j, z), device_id_type=MESH,
        )

    def begin():
        for j in range(1, HELPERS):
            copy(j).start()

    def own():
        pltpu.sync_copy(source.at[pl.ds(0, SHARE)], target)
        for j in range(1, HELPERS):
            copy(j).wait_send()

    def end():
        pl.when(seq == 0)(own)
        pl.when(seq != 0)(lambda: copy(1).wait_recv())

    pl.when(seq == 0)(begin)
    return end


def to_first(source, target, send, recv):
    seq, z = lax.axis_index(SEQ), lax.axis_index(BATCH)

    def copy(j):
        return pltpu.make_async_remote_copy(
            src_ref=source, dst_ref=target.at[pl.ds(j * SHARE, SHARE)], send_sem=send,
            recv_sem=recv.at[j], device_id=(0, z), device_id_type=MESH,
        )

    for j in range(1, HELPERS):
        pl.when(seq == j)(copy(j).start)

    def end():
        def mine():
            pltpu.sync_copy(source, target.at[pl.ds(0, SHARE)])
            for j in range(1, HELPERS):
                copy(j).wait_recv()

        pl.when(seq == 0)(mine)
        pl.when(seq != 0)(lambda: copy(1).wait_send())

    return end


def from_slabs(ref):
    def get(at):
        slabs = ref[:, :, at]
        return slabs.astype(jnp.float32).reshape(-1, slabs.shape[2]).astype(ref.dtype)

    return get


def project(low, w, bias, q, kv):
    def queries(i):
        at = span(i, 256)
        q[:, at] = (product(low[...], w(at)) + bias[0:1, at]).astype(q.dtype)

    def keys(i):
        keep(2 * i, product(low[...], w(span(i, 256, D))))

    def values(i):
        keep(PAIRS + 2 * i, product(low[...], w(span(i, 256, 2 * D))) + bias[1:2, span(i, 256)])

    def keep(pair, acc):
        for half in range(2):
            lanes = acc[:, half * WIDE : (half + 1) * WIDE].astype(kv.dtype)
            kv[pair + half] = lanes.reshape(kv.shape[1:])

    for act in (keys, values, queries):
        over(D // 256, act)


class Sequence:
    def __init__(self, rows, seq_count, depth, dtype):
        self.rows, self.seq_count, self.depth, self.dtype = rows, seq_count, depth, dtype

    def outs(self):
        blocks, f32 = self.rows // BLK, jnp.float32
        return dict(
            q=((self.rows, D), self.dtype, SAVE),
            every=((self.seq_count, 2 * PAIRS, blocks, BLK, WIDE), self.dtype, SAVE),
            part=((SHARE, D), self.dtype, SAVE),
            o=((self.rows, D), self.dtype, SAVE), po=((SHARE, D), self.dtype, SAVE),
            log=((PAIRS, blocks, WIDE), f32, SAVE), plog=((PAIRS, 1, 2 * SHARE), f32, SAVE),
        )

    def scratch(self):
        return dict(
            kv=pltpu.VMEM((2 * PAIRS, self.rows // BLK, BLK, WIDE), self.dtype), send=dma(4 * Gather.sends(Y_X, self.depth)),
            recv=dma(4, self.seq_count), local=dma(), give=dma(HELPERS), take=dma(),
            near_k=near_rows(self.rows, self.dtype), near_v=near_rows(self.rows, self.dtype),
        )

    def prepare(self, refs):
        count, at = PAIRS // 2, 0
        self.jobs = []
        for i in range(4):
            window = pl.ds(i * count, count)
            self.jobs.append(
                Gather(
                    refs.kv.at[window],
                    lambda p, window=window: refs.every.at[number_in_sequence(p), window],
                    number_in_sequence, (X_Y, Y_X)[i % 2], self.depth, refs.send, refs.recv.at[i], at,
                )
            )
            at += Gather.sends(Y_X, self.depth)

    def begin(self, refs):
        for job in self.jobs:
            job.begin()
        self.finish = to_helpers(refs.q, refs.part, refs.give, refs.take)
        self.own = pltpu.make_async_copy(refs.kv, refs.every.at[number_in_sequence(place())], refs.local)
        self.own.start()

    def arrived(self, refs):
        for job in self.jobs:
            job.siblings()
        self.own.wait()
        self.finish()
        refs.save("every", "part")

    def attention(self, refs, steps):
        first = lax.axis_index(SEQ) * (self.rows // BLK)
        count = PAIRS // steps

        def pair_of(pair):
            at, one = span(pair, WIDE), pl.ds(pair, 1)

            def drawn(block, r):
                first_one = (block * H + 2 * pair) * R + r
                return [(refs.picks[0, i], refs.picks[1, i]) for i in (first_one, first_one + R)]

            attend_pair(
                drawn, first, refs.q.at[:, at], Keys(refs.every, pair), Keys(refs.every, PAIRS + pair), refs.shut,
                refs.part.at[:, at], refs.o.at[:, at], refs.po.at[:, at], refs.log.at[one], refs.plog.at[one],
                refs.near_k, refs.near_v,
            )

        def step(k):
            if k == 0:
                self.arrived(refs)
                refs.ready("shut")
            over(count, lambda i: pair_of(k * count + i))
            if k == steps - 1:
                refs.save("o", "po", "log", "plog")

        return [partial(step, k) for k in range(steps)]

    def end(self):
        for job in self.jobs:
            job.drain()


def project_and_send(refs, gathering, sequence, low, which):
    def act():
        gathering.hurry(refs, [which])
        w = from_slabs(getattr(refs, "every%d" % which))
        refs.ready("low")
        project(low, w, refs.bias, refs.q, refs.kv)
        sequence.begin(refs)
        refs.save("q")

    return act


def timed_events(jobs, places):
    return [pair for job, at in zip(jobs, places, strict=True) for pair in job.events(at)]


def shut_keys_here(segs, own_segs, shut):
    me, count = lax.axis_index(SEQ), segs.shape[0]
    blocks = shut.shape[0]
    rows = blocks * BLK

    def column(device):
        held = segs[device].astype(jnp.float32).T
        return [held[:, r : r + 1] for r in range(rows // WIDE)]

    before, here, after = column((me + count - 1) % count), column(me), column((me + 1) % count)
    near = jnp.concatenate([before[-1][WIDE - BLK :]] + here + [after[0][:BLK]], axis=0)
    for block in range(blocks):
        spot = (me * blocks + block - 1) * BLK + lax.broadcasted_iota(jnp.int32, (3 * BLK, WIDE), 0)
        same = near[block * BLK : (block + 3) * BLK] == own_segs[block : block + 1]
        shut[block] = jnp.where(same & (spot >= SHARED) & (spot < count * rows), 0.0, masked_score)


def first_head(low, small, segs, own_segs, picks, weights, seq_count, depth, cid):
    rows = low.shape[0]
    pieces = [(0, 0, small.shape[0], 0, 128, Z_Y_X), (1, 0, 8, 0, 128, Y_X)]
    pieces += layer_pieces(small.shape[0], weights[3][0].shape[1], 2)
    gathering = Gathering([(small, None), (segs, None)] + weights, pieces, seq_count, depth, (0, 1, 2))
    sequence = Sequence(rows, seq_count, depth, low.dtype)

    def body(refs):
        greet(("y", "x", "z"), depth, spread=True)
        gathering.begin(refs)
        sequence.prepare(refs)
        refs.bias = refs.vectors.at[0]

        def vectors():
            gathering.hurry(refs, [0, 1])
            shut_keys_here(refs.every1, refs.own_segs, refs.shut)
            refs.save("shut")
            table = refs.every0[...].astype(jnp.float32).reshape(D, 128).T
            for layer in range(L):
                refs.vectors[layer, 0:6] = table[6 * layer : 6 * layer + 6]
                refs.vectors[layer, 6:8] = table[6 * L + 2 * layer : 6 * L + 2 * layer + 2]
            refs.table[...] = table[8 * L : 12 * L]

        def project_now():
            project_and_send(refs, gathering, sequence, refs.low, 2)()
            gathering.early = [0, 1, 2]

        at = HEAD_PLACES
        run_in_order(
            [(place_, job.begin) for place_, job in zip(at.begins, gathering.jobs, strict=True)]
            + timed_events(gathering.jobs + sequence.jobs, at.arrivals)
            + [(at.project, vectors), (at.project + 0.1, project_now)]
            + list(zip(at.attention, sequence.attention(refs, len(at.attention)), strict=True))
        )
        sequence.end()
        gathering.end()

    got = call(
        body, "first_head", cid,
        {
            **dict(low=(low, LOAD), own_segs=(own_segs, IN_VMEM), picks=(picks, IN_SMEM)), **gathering.ins(),
        },
        {
            **dict(
                vectors=((L, 8, D), jnp.float32, IN_VMEM), table=((4 * L, D), jnp.float32, IN_VMEM),
                shut=((rows // BLK, 3 * BLK, WIDE), jnp.float32, SAVE),
            ),
            **sequence.outs(), **gathering.outs(),
        },
        {**sequence.scratch(), **gathering.scratch()},
    )
    return got, gathering.results(got)[2:]


def norm_block(resid, gain, shift):
    center = resid - jnp.mean(resid, axis=1, keepdims=True)
    inv_std = lax.rsqrt(jnp.mean(center * center, axis=1, keepdims=True) + layer_eps)
    normed = center * inv_std
    return normed * gain + shift, normed, inv_std


ROW_BLOCK = 64


WIDE_D, WIDE_FF = 384, 512


def tail_steps(refs, wide_d, wide_ff):
    rows, hidden = refs.resid.shape[0], refs.shifts.shape[1]

    def out():
        refs.ready("resid", "w_out")

        def act(i):
            at = span(i, wide_d)
            own = refs.resid[:, at].astype(jnp.float32)
            refs.sum[:, at] = own + product(refs.mixed[...], refs.w_out[:, at]) + refs.bias[2:3, at]

        over(D // wide_d, act)
        refs.save("mixed")

    def norm_one():
        def act(i):
            at = span(i, ROW_BLOCK)
            y, normed, inv = norm_block(refs.sum[at], refs.bias[6:7], refs.bias[3:4])
            refs.n1[at], refs.inv1[at], refs.sum[at] = normed, inv, y
            refs.y_low[at] = y.astype(jnp.bfloat16)

        over(rows // ROW_BLOCK, act)
        refs.save("n1", "inv1", "y_low")
        refs.ready("w_up")

    def up(first, count):
        def act(i):
            at = span(first + i, wide_ff)
            u = product(refs.y_low[...], refs.w_up[:, at]) + refs.shifts[0:1, at]
            share = 0.5 + 0.5 * lax.erf(u * (0.5 ** 0.5))
            refs.a_low[:, at] = (u * share).astype(jnp.bfloat16)
            slope = share + u * jnp.exp(-0.5 * u * u) * ((2.0 * jnp.pi) ** -0.5)
            refs.slope[:, at] = slope.astype(jnp.bfloat16)

        over(count, act)

    def down():
        refs.ready("w_down")
        refs.save("a_low", "slope")

        def act(i):
            at = span(i, wide_d)
            refs.sum[:, at] = refs.sum[:, at] + product(refs.a_low[...], refs.w_down[:, at]) + refs.bias[4:5, at]

        over(D // wide_d, act)

    def norm_two():
        def act(i):
            at = span(i, ROW_BLOCK)
            z, normed, inv = norm_block(refs.sum[at], refs.bias[7:8], refs.bias[5:6])
            refs.n2[at], refs.inv2[at] = normed, inv
            if hasattr(refs, "z"):
                refs.z[at] = z
            refs.z_low[at] = z.astype(jnp.bfloat16)

        over(rows // ROW_BLOCK, act)
        refs.save("n2", "inv2", "z", "z_low")

    ends = [hidden // wide_ff * k // 4 for k in range(5)]
    ups = [partial(up, a, b - a) for a, b in zip(ends, ends[1:])]
    return [out, norm_one] + ups + [down, norm_two]


def tail_ins(mixed, part, resid, vectors, shifts, weights):
    return dict(
        generic=(mixed, LOAD), own_part=(part, ANYWHERE), resid=(resid, LOAD), vectors=(vectors, IN_VMEM),
        shifts=(shifts, IN_VMEM), w_out=(weights[1], LOAD), w_up=(weights[2], LOAD), w_down=(weights[3], LOAD),
    )


def tail_results(rows, hidden):
    f32, low = jnp.float32, jnp.bfloat16
    kept = dict(mixed=((rows, D), low), y_low=((rows, D), low), a_low=((rows, hidden), low), z_low=((rows, D), low))
    norms = dict(
        n1=((rows, D), f32), inv1=((rows, 1), f32), slope=((rows, hidden), low), n2=((rows, D), f32), inv2=((rows, 1), f32)
    )
    return kept, norms


def saved(shapes):
    return {k: (*v, SAVE) for k, v in shapes.items()}


def tail_scratch(rows):
    return dict(sum=pltpu.VMEM((rows, D), jnp.float32), t_send=dma(), t_recv=dma(HELPERS))


def tail(mixed, part, resid, vectors, shifts, weights, next_weights, shut, picks, seq_count, depth, cid):
    rows, hidden = resid.shape[0], shifts.shape[1]
    pieces = layer_pieces(next_weights[0][0].shape[1], next_weights[3][0].shape[1], 0)
    gathering = Gathering(next_weights, pieces, seq_count, depth, (0,))
    sequence = Sequence(rows, seq_count, depth, mixed.dtype)

    def body(refs):
        refs.ready("generic")
        refs.mixed[...] = refs.generic[...]
        greet(("y", "x", "z"), depth, spread=True, collect=True)
        finish = to_first(refs.own_part, refs.mixed, refs.t_send, refs.t_recv)
        gathering.begin(refs)
        sequence.prepare(refs)
        refs.bias = refs.vectors.at[0]
        steps = [finish] + tail_steps(refs, 256, 256)

        def project_now():
            refs.bias = refs.vectors.at[1]
            project_and_send(refs, gathering, sequence, refs.z_low, 0)()

        at = TAIL_PLACES
        run_in_order(
            [(place_, job.begin) for place_, job in zip(at.begins, gathering.jobs, strict=True)]
            + timed_events(gathering.jobs + sequence.jobs, at.arrivals)
            + list(zip(at.steps, steps, strict=True)) + [(at.project, project_now)]
            + list(zip(at.attention, sequence.attention(refs, len(at.attention)), strict=True))
        )
        sequence.end()
        gathering.end()

    kept, norms = tail_results(rows, hidden)
    got = call(
        body, "tail", cid,
        {
            **tail_ins(mixed, part, resid, vectors, shifts, weights),
            **dict(shut=(shut, LOAD), picks=(picks, IN_SMEM)), **gathering.ins(),
        },
        {
            **saved(kept), **saved(norms), **dict(z=((rows, D), jnp.float32, SAVE)), **sequence.outs(),
            **gathering.outs(),
        },
        {**tail_scratch(rows), **sequence.scratch(), **gathering.scratch()},
    )
    return got, gathering.results(got)


def folded(block):
    return jnp.sum(block.reshape(-1, 8, block.shape[1]), axis=0)


def norm_block_back(grad, normed, inv_std, gain):
    scaled = grad * gain
    return (
        scaled
        - jnp.mean(scaled, axis=1, keepdims=True)
        - normed * jnp.mean(scaled * normed, axis=1, keepdims=True)
    ) * inv_std


def back_steps(refs, dz, w_down, w_up, w_out, waits=(lambda: None,) * 3):
    rows, hidden = refs.n2.shape[0], refs.slope.shape[1]
    zero = jnp.zeros((8, D), jnp.float32)

    def row(k, total):
        refs.totals[k : k + 1] = jnp.sum(total, axis=0, keepdims=True)

    def norm_two():
        refs.ready("n2", "inv2", "d_out")

        def act(i, sums):
            at = span(i, ROW_BLOCK)
            grad, normed = dz(at), refs.n2[at]
            back = norm_block_back(grad, normed, refs.inv2[at], refs.bias[7:8])
            refs.work[at] = back
            refs.dr2_low[at] = back.astype(jnp.bfloat16)
            return sums[0] + folded(back), sums[1] + folded(grad), sums[2] + folded(grad * normed)

        sums = lax.fori_loop(0, rows // ROW_BLOCK, act, (zero,) * 3)
        row(4, sums[0]), row(5, sums[1]), row(7, sums[2])
        refs.save("dr2_low")
        refs.ready("slope")
        waits[0]()

    def down(first, count):
        def act(i):
            at = span(first + i, WIDE_FF)
            du = product_nt(refs.dr2_low[...], w_down[at]) * refs.slope[:, at].astype(jnp.float32)
            refs.du_low[:, at] = du.astype(jnp.bfloat16)
            refs.hidden_totals[0:1, at] = jnp.sum(du, axis=0, keepdims=True)

        over(count, act)

    def up():
        refs.save("du_low")
        waits[1]()

        def act(i):
            at = span(i, WIDE_D)
            refs.work[:, at] = refs.work[:, at] + product_nt(refs.du_low[...], w_up[at])

        over(D // WIDE_D, act)

    def norm_one():
        refs.ready("n1", "inv1")

        def act(i, sums):
            at = span(i, ROW_BLOCK)
            grad, normed = refs.work[at], refs.n1[at]
            back = norm_block_back(grad, normed, refs.inv1[at], refs.bias[6:7])
            refs.dr1[at] = back
            refs.dr1_low[at] = back.astype(jnp.bfloat16)
            return sums[0] + folded(back), sums[1] + folded(grad), sums[2] + folded(grad * normed)

        sums = lax.fori_loop(0, rows // ROW_BLOCK, act, (zero,) * 3)
        row(2, sums[0]), row(3, sums[1]), row(6, sums[2])
        refs.save("dr1", "dr1_low")

    def out():
        waits[2]()

        def act(i):
            at = span(i, WIDE_D)
            refs.cot[:, at] = product_nt(refs.dr1_low[...], w_out[at]).astype(jnp.bfloat16)

        over(D // WIDE_D, act)
        refs.save("cot")

    half = hidden // WIDE_FF // 2
    return [norm_two, partial(down, 0, half), partial(down, half, half), up, norm_one, out]


def back_outs(rows, hidden):
    f32, low = jnp.float32, jnp.bfloat16
    return dict(
        dr2_low=((rows, D), low, SAVE), du_low=((rows, hidden), low, SAVE), dr1=((rows, D), f32, SAVE),
        dr1_low=((rows, D), low, SAVE), cot=((rows, D), low, SAVE), totals=((8, D), f32, IN_VMEM),
        hidden_totals=((1, hidden), f32, IN_VMEM), part_cot=((SHARE, D), low, ANYWHERE),
    )


def turn(mixed, part, resid, vectors, shifts, weights, d_out, depth, cid):
    rows, hidden = resid.shape[0], shifts.shape[1]

    def body(refs):
        refs.ready("generic")
        refs.mixed[...] = refs.generic[...]
        refs.bias = refs.vectors.at[1]
        greet((), depth, spread=True, collect=True)
        to_first(refs.own_part, refs.mixed, refs.t_send, refs.t_recv)()
        for step in tail_steps(refs, WIDE_D, WIDE_FF):
            step()
        refs.totals[...] = jnp.zeros_like(refs.totals)
        for step in back_steps(refs, lambda at: refs.d_out[at].astype(jnp.float32), refs.w_down, refs.w_up, refs.w_out):
            step()
        to_helpers(refs.cot, refs.part_cot, refs.give, refs.take)()

    kept, norms = tail_results(rows, hidden)
    return call(
        body, "turn", cid,
        {**tail_ins(mixed, part, resid, vectors, shifts, weights), **dict(d_out=(d_out, LOAD))},
        {**saved(kept), **back_outs(rows, hidden)},
        {
            **tail_scratch(rows), **{k: pltpu.VMEM(*v) for k, v in norms.items()},
            **dict(work=pltpu.VMEM((rows, D), jnp.float32), give=dma(HELPERS), take=dma()),
        },
    )


def chunked(shape):
    rows, columns = shape
    width = columns
    while rows * width > 24 * 1024 and width % 256 == 0:
        width //= 2
    if rows * width > 24 * 1024 and width % 384 == 0:
        width //= 3
    return width, columns // width


def total_of(own, kids, window):
    total = own[window].astype(jnp.float32)
    for ref, cond in kids:
        if cond is None:
            total = total + ref[window].astype(jnp.float32)
        else:
            total = total + lax.cond(
                cond,
                lambda ref=ref: ref[window].astype(jnp.float32),
                lambda total=total: jnp.zeros_like(total),
            )
    return total


def over_chunks(shape, act):
    if len(shape) == 3:
        size = shape[1] // 2

        def part(i, carry):
            act((i // 2, span(i % 2, size)))
            return carry

        lax.fori_loop(0, 2 * shape[0], part, 0)
        return
    width, count = chunked(shape)

    def step(i, carry):
        act((slice(None), pl.ds(pl.multiple_of(i * width, width), width)))
        return carry

    lax.fori_loop(0, count, step, 0)


def add_up(own, kids, into):
    def act(window):
        into[window] = total_of(own, kids, window).astype(into.dtype)

    over_chunks(into.shape, act)


def write_total(target):
    def finish(own, kids):
        def act(window):
            target[window] = total_of(own, kids, window).astype(target.dtype)

        over_chunks(target.shape, act)

    return finish


def weight_grad(left, right, into, first=0):
    share = into.shape[1]
    width = WIDE_FF if into.shape[2] % WIDE_FF == 0 else WIDE_D
    count = 384 // share

    def act(i):
        across = into.shape[2] // width
        rows, at = i // across, span(i % across, width)
        acc = product_tn(left[:, span(rows, 384)], right[:, pl.ds(pl.multiple_of(first + i % across * width, WIDE), width)])
        for k in range(count):
            into[rows * count + k, :, at] = acc[k * share : (k + 1) * share].astype(into.dtype)

    over(left.shape[1] // 384 * (into.shape[2] // width), act)


class Sums:
    def __init__(self, tag, pieces, depth):
        self.tag, self.pieces, self.depth = tag, pieces, depth

    def name(self, what, k):
        return "%s_%s%d" % (self.tag, what, k)

    def scratch(self):
        made = {}
        for k, (_, _, shape, _, order, dtype) in enumerate(self.pieces):
            edges = Reduce.slots(order, self.depth)[1]
            made[self.name("box", k)] = pltpu.VMEM((edges,) + shape, dtype)
            made[self.name("send", k)] = dma(2 * len(offsets(order, self.depth)))
            made[self.name("recv", k)] = dma(edges)
        return made

    def prepare(self, refs):
        self.jobs = []
        for k, (source, far, _, target, order, _) in enumerate(self.pieces):
            box, send, recv = (getattr(refs, self.name(what, k)) for what in ("box", "send", "recv"))
            job = Reduce(partial(source, refs), partial(far, refs), box, order, self.depth, send, recv)
            self.jobs.append((job, target(refs)))

    def start(self, k):
        job, _ = self.jobs[k]
        for t in job.marks:
            job.start(t)

    def timed(self, places):
        timed = []
        for k, ((job, finish), at) in enumerate(zip(self.jobs, places, strict=True)):
            timed.append((at[0], partial(self.start, k)))
            acts = [partial(job.handle, t, add_up, finish) for t in job.marks]
            timed += zip(at[1:], acts, strict=True)
        return timed

    def end(self):
        for job, _ in self.jobs:
            job.drain()


def weight_sums(windows, depth, n_dev, dtypes):
    number = number_in(depth)

    def piece(which, row, rows, column, columns_, order):
        window = (pl.ds(row, rows), pl.ds(column, columns_))

        def source(refs, p):
            return getattr(refs, "grad%d" % which).at[(number(p),) + window]

        return (
            source,
            source,
            (rows, columns_),
            lambda refs: write_total(getattr(refs, "owned%d" % which).at[window]),
            order,
            dtypes[which],
        )

    return Sums("w", [piece(*w) for w in windows], depth)


def sum_rows(dk, dv, dq, part_dq, held, grads, seq_count, depth, cid):
    rows, hidden, n_dev = dq.shape[0], grads.du_low.shape[1], seq_count * depth
    low, f32 = dk.dtype, jnp.float32
    share, count = D // n_dev, PAIRS // 2

    def piece(i):
        window = pl.ds(i % 2 * count, count)

        def target(refs):
            def finish(own, kids):
                def act(at):
                    lanes = pl.ds(pl.multiple_of((PAIRS + i * count + at[0]) * WIDE, WIDE), WIDE)
                    refs.proj[at[1], lanes] = total_of(own, kids, at).astype(low)

                over_chunks((count, rows, WIDE), act)

            return finish

        return (
            lambda refs, p: (refs.dk, refs.dv)[i // 2].at[number_in_sequence(p), window],
            lambda refs, p: (refs.far_dk, refs.far_dv)[i // 2].at[number_in_sequence(p), window],
            (count, rows, WIDE),
            target,
            (X_Y, Y_X)[i % 2],
            low,
        )

    by_rows = Sums("r", [piece(i) for i in range(4)], depth)
    windows = [(1, 0, share, 0, D, X_Y_Z), (2, 0, share, 0, hidden // 2, Y_X_Z)]
    by_weights = weight_sums(windows, depth, n_dev, {1: low, 2: low})

    def body(refs):
        refs.ready("dq")
        refs.proj[:, 0:D] = refs.dq[...]
        greet(("y", "x", "z"), depth, collect=True)
        by_rows.prepare(refs)
        by_weights.prepare(refs)
        ends = [to_first(refs.part, refs.proj.at[:, pl.ds(0, D)], refs.t_send, refs.t_recv)]
        at = ROWS_PLACES

        def grad(left, right, into):
            refs.ready(left, right)
            weight_grad(getattr(refs, left), getattr(refs, right), into)

        first_block = min(place for places in at.rows for place in places[1:])
        run_in_order(
            by_rows.timed(at.rows) + by_weights.timed(at.weights)
            + [
                (at.grads[0], partial(grad, "mixed", "dr1_low", refs.grad1)),
                (at.grads[1], partial(grad, "y_low", "du_low", refs.grad2)),
                (first_block - 0.5, partial(refs.ready, "dk", "dv")),
                (at.collect, ends[0]),
            ]
        )
        by_rows.end()
        by_weights.end()

        def act(i, sums):
            at = span(i, ROW_BLOCK)
            return tuple(
                total + folded(refs.proj[at, pl.ds(first, D)].astype(f32)) for total, first in zip(sums, (0, 2 * D))
            )

        zero = jnp.zeros((8, D), f32)
        sums = lax.fori_loop(0, rows // ROW_BLOCK, act, (zero, zero))
        refs.totals[...] = jnp.zeros_like(refs.totals)
        for k in range(2):
            refs.totals[k : k + 1] = jnp.sum(sums[k], axis=0, keepdims=True)

    return call(
        body, "sum_rows", cid,
        dict(
            dq=(dq, LOAD), part=(part_dq, ANYWHERE), mixed=(held.mixed, LOAD), dr1_low=(grads.dr1_low, LOAD),
            dk=(dk, LOAD), dv=(dv, LOAD), y_low=(held.y_low, LOAD), du_low=(grads.du_low, LOAD),
        ),
        dict(
            proj=((rows, 3 * D), low, IN_VMEM), totals=((8, D), f32, IN_VMEM), owned1=((share, D), f32, IN_VMEM),
            owned2=((share, hidden // 2), f32, IN_VMEM),
        ),
        {
            **dict(
                grad1=pltpu.VMEM((n_dev, share, D), low), grad2=pltpu.VMEM((n_dev, share, hidden // 2), low),
                t_send=dma(), t_recv=dma(HELPERS),
            ),
            **by_rows.scratch(), **by_weights.scratch(),
        },
    )


def sum_weights(held, low_in, proj, vectors, w_qkv, small, below, n_dev, depth, cid):
    rows, hidden = proj.shape[0], held.du_low.shape[1]
    low, f32 = jnp.bfloat16, jnp.float32
    share, tall = D // n_dev, hidden // n_dev
    shapes = {0: (share, 3 * D), 2: (share, hidden // 2), 3: (tall, D)}
    cut = tall * 2 // 3
    windows = [
        (3, 0, cut, 0, D, Z_X_Y),
        (3, cut, tall - cut, 0, D, Z_Y_X),
        (2, 0, share, 0, hidden // 2, Y_X_Z),
        (0, 0, share, 0, 3 * D, Z_Y_X),
    ]
    ins = dict(low_in=(low_in, LOAD), proj=(proj, LOAD))
    ins.update({"up_" + k: (getattr(held, k), LOAD) for k in ("y_low", "du_low", "a_low", "dr2_low")})
    ins.update(up_dr1=(held.dr1, LOAD), w_qkv=(w_qkv, ANYWHERE))
    outs = {"owned%d" % i: (s, f32, IN_VMEM) for i, s in shapes.items()}
    scratch = {"grad%d" % i: pltpu.VMEM((n_dev,) + s, low) for i, s in shapes.items()}
    if small is not None:
        windows.append((4, 0, small.shape[1], 0, small.shape[2], Z_Y_X))
        ins.update(grad4=(small, IN_VMEM))
        outs.update(owned4=(small.shape[1:], f32, IN_VMEM))
    by_weights = weight_sums(windows, depth, n_dev, {0: low, 2: low, 3: low, 4: f32})
    scratch.update(by_weights.scratch())
    scratch.update(load=dma(4), wide=pltpu.VMEM((D, hidden), low))
    if below is not None:
        below_weights, below_held = below
        ins.update({k: (getattr(below_held, k), LOAD) for k in ("n2", "inv2", "slope", "n1", "inv1")})
        ins.update(
            vectors=(vectors, IN_VMEM), w_out=(below_weights[1], ANYWHERE), w_up=(below_weights[2], ANYWHERE),
            w_down=(below_weights[3], ANYWHERE),
        )
        outs.update(back_outs(rows, hidden))
        scratch.update(
            tall=pltpu.VMEM((hidden, D), low), work=pltpu.VMEM((rows, D), f32), give=dma(HELPERS), take=dma()
        )
    if below is None:
        outs.update(dx=((rows, D), f32, SAVE))
    else:
        scratch.update(dx=pltpu.VMEM((rows, D), f32))

    def body(refs):
        v_qkv = refs.wide.at[:, pl.ds(0, 3 * D)]
        load_qkv = pltpu.make_async_copy(refs.w_qkv, v_qkv, refs.load.at[0])
        load_qkv.start()
        if below is not None:
            refs.bias = refs.vectors.at[0]
            refs.totals[...] = jnp.zeros_like(refs.totals)
            load_down = pltpu.make_async_copy(refs.w_down, refs.tall, refs.load.at[1])
            load_down.start()
            load_up = pltpu.make_async_copy(refs.w_up, refs.wide, refs.load.at[2])
            load_out = pltpu.make_async_copy(refs.w_out, refs.tall.at[pl.ds(0, D)], refs.load.at[3])
        greet(("y", "x", "z"), depth, spread=below is not None)
        by_weights.prepare(refs)
        def dx():
            load_qkv.wait()
            refs.ready("proj", "up_dr1")

            def act(i):
                at = span(i, WIDE_D)
                refs.dx[:, at] = refs.up_dr1[:, at] + product_nt(refs.proj[...], v_qkv[at])

            over(D // WIDE_D, act)
            refs.save("dx")
            if below is not None:
                load_up.start()

        steps = [dx]
        if below is not None:

            def up_ready():
                load_out.start()
                load_up.wait()

            steps += back_steps(
                refs, lambda at: refs.dx[at], refs.tall, refs.wide, refs.tall, [load_down.wait, up_ready, load_out.wait]
            )
            ends = []
            steps.append(lambda: ends.append(to_helpers(refs.cot, refs.part_cot, refs.give, refs.take)))
        at = LAST_PLACES if below is None else BELOW_PLACES

        def grad(left, right, into, column=0):
            refs.ready(left, right)
            weight_grad(getattr(refs, left), getattr(refs, right), into, column)

        run_in_order(
            by_weights.timed(at.weights)
            + [
                (at.grads[0], partial(grad, "up_a_low", "up_dr2_low", refs.grad3)),
                (at.grads[1], partial(grad, "up_y_low", "up_du_low", refs.grad2, hidden // 2)),
                (at.grads[2], partial(grad, "low_in", "proj", refs.grad0)),
            ]
            + list(zip(at.steps, steps, strict=True))
        )
        by_weights.end()
        if below is not None:
            ends[0]()

    return call(body, "sum_weights", cid, ins, outs, scratch)


def norm_rows(resid, gain, shift):
    center = resid - jnp.mean(resid, axis=-1, keepdims=True)
    inv_std = lax.rsqrt(jnp.mean(center * center, axis=-1, keepdims=True) + layer_eps)
    normed = center * inv_std
    return (normed * gain + shift, normed, inv_std)


def norm_back(grad_rows, normed, inv_std, gain):
    scaled = grad_rows * gain
    return (
        scaled
        - jnp.mean(scaled, axis=-1, keepdims=True)
        - normed * jnp.mean(scaled * normed, axis=-1, keepdims=True)
    ) * inv_std


def dot32(a, b):
    return jnp.dot(a, b, preferred_element_type=jnp.float32)


def small_vectors(small, n_dev):
    small = small.astype(jnp.float32).T
    vectors = jnp.concatenate(
        [small[: 6 * L].reshape(L, 6, D), small[6 * L : 8 * L].reshape(L, 2, D)], axis=1
    )
    hidden_shifts = small[8 * L : 12 * L].reshape(L, 4, n_dev, D // n_dev)
    return vectors, jnp.swapaxes(hidden_shifts, 1, 2).reshape(L, -1)


def shut_keys(segs_all, segments, first, blocks_here):
    length = segs_all.shape[0]
    padding = jnp.full((BLK,), -1, jnp.int32)
    segs_all = jnp.concatenate([padding, segs_all, padding]).reshape(-1, BLK)
    segs_near = lax.dynamic_slice_in_dim(segs_all, first, blocks_here + 2, axis=0)
    seg_window = jnp.concatenate([segs_near[j : j + blocks_here] for j in range(3)], axis=1)
    spot = (first - 1 + jnp.arange(blocks_here)[:, None]) * BLK + jnp.arange(3 * BLK)[None, :]
    inside = (spot >= SHARED) & (spot < length)
    own = segments.reshape(blocks_here, 1, BLK)
    allowed = inside[:, :, None] & (seg_window[:, :, None] == jnp.concatenate([own, own], axis=2))
    return jnp.where(allowed, 0.0, masked_score)


def small_by_owner(vectors, hidden, n_dev):
    rows = jnp.moveaxis(vectors.reshape(8, n_dev, -1), 1, 0)
    rows = jnp.concatenate([rows, hidden.reshape(n_dev, 8, -1)], axis=2)
    return jnp.pad(rows, ((0, 0), (0, 0), (0, 128 - rows.shape[2])))


def small_outputs(narrow, piece, hidden):
    return (
        narrow[:, 6:8, :piece],
        narrow[:, 0:6, :piece],
        narrow[:, :, piece : piece + hidden // 8].reshape(L, -1),
    )


def share_of(rows):
    first = lax.all_gather(rows[:SHARED], SEQ, axis=0)[0]
    own = jnp.minimum(lax.axis_index(SEQ), HELPERS - 1) * SHARE
    return lax.dynamic_slice_in_dim(first, own, SHARE, axis=0)


def rows_of_all(kv, queries):
    kv = jnp.moveaxis(kv.reshape(-1, 2 * PAIRS, WIDE), 1, 0)
    return lax.all_gather(kv, SEQ, axis=0), share_of(queries)


def with_shared_rows(part, rows):
    first = lax.all_gather(part, SEQ, axis=0)[:HELPERS].reshape(SHARED, D)
    head_rows = jnp.where(lax.axis_index(SEQ) == 0, first.astype(rows.dtype), rows[:SHARED])
    return jnp.concatenate([head_rows, rows[SHARED:]], axis=0)


def on_any_slice(
    layer_input, segments, rand_blocks, w_qkv, w_out, w_up, w_down, gains, biases, up_bias, d_out
):
    seq_count, depth = lax.axis_size(SEQ), lax.axis_size(BATCH)
    n_dev = seq_count * depth
    own_index = lax.axis_index(SEQ)
    rows = layer_input.shape[1]
    blocks_here, length = rows // BLK, rows * seq_count
    picks = rand_blocks.reshape(-1)
    first = (own_index * blocks_here).reshape(1)

    piece = D // n_dev
    small = jnp.concatenate(
        [biases.reshape(-1, piece), gains.reshape(-1, piece), up_bias.reshape(-1, piece)], axis=0
    ).T
    small = lax.all_gather(small, (SEQ, BATCH), axis=0, tiled=True)
    segs_all = lax.all_gather(segments[0], SEQ, axis=0, tiled=True)
    weights = [
        [lax.all_gather(w[layer], (SEQ, BATCH), axis=0, tiled=True) for w in (w_qkv, w_out, w_up, w_down)]
        for layer in range(L)
    ]
    vectors, hidden_shifts = small_vectors(small, n_dev)
    shut = shut_keys(segs_all, segments, first[0], blocks_here)

    resid = layer_input[0].astype(jnp.float32)
    low = layer_input[0]
    saved = []
    for layer in range(L):
        mat_qkv, mat_out, mat_up, mat_down = weights[layer]
        bias = vectors[layer]
        proj = dot32(low, mat_qkv)
        queries = (proj[:, :D] + bias[0]).astype(jnp.bfloat16)
        kv = jnp.concatenate([proj[:, D : 2 * D], proj[:, 2 * D :] + bias[1]], axis=1).astype(jnp.bfloat16)
        kv_all, part = rows_of_all(kv, queries)
        mixed, part_mixed, *logs = attend(picks, first, queries, kv_all, shut, part)
        mixed = with_shared_rows(part_mixed, mixed)
        resid_one = resid + dot32(mixed, mat_out) + bias[2]
        middle, normed_one, inv_one = norm_rows(resid_one, bias[6], bias[3])
        middle_low = middle.astype(jnp.bfloat16)
        hidden = dot32(middle_low, mat_up) + hidden_shifts[layer]
        active = jax.nn.gelu(hidden, approximate=False).astype(jnp.bfloat16)
        resid_two = middle + dot32(active, mat_down) + bias[4]
        result, normed_two, inv_two = norm_rows(resid_two, bias[7], bias[5])
        saved.append(
            (low, queries, kv_all, part, logs, mixed, normed_one, inv_one, middle_low, hidden, active, normed_two, inv_two)
        )
        resid = result
        low = resid.astype(jnp.bfloat16)

    grad = d_out[0].astype(jnp.float32)
    owned = [None] * L
    for layer in reversed(range(L)):
        (low_in, queries, kv_all, part, logs, mixed, normed_one, inv_one, middle_low, hidden, active, normed_two, inv_two) = saved[layer]
        mat_qkv, mat_out, mat_up, mat_down = weights[layer]
        bias = vectors[layer]
        gain_two_grad = jnp.sum(grad * normed_two, axis=0)
        shift_two_grad = jnp.sum(grad, axis=0)
        grad_two = norm_back(grad, normed_two, inv_two, bias[7])
        grad_two_low = grad_two.astype(jnp.bfloat16)
        down_grad = product_tn(active, grad_two_low)
        active_grad = product_nt(grad_two_low, mat_down)
        hidden_grad = jax.vjp(partial(jax.nn.gelu, approximate=False), hidden)[1](active_grad)[0]
        hidden_grad_low = hidden_grad.astype(jnp.bfloat16)
        up_grad = product_tn(middle_low, hidden_grad_low)
        middle_grad = grad_two + product_nt(hidden_grad_low, mat_up)
        gain_one_grad = jnp.sum(middle_grad * normed_one, axis=0)
        shift_one_grad = jnp.sum(middle_grad, axis=0)
        grad_one = norm_back(middle_grad, normed_one, inv_one, bias[6])
        grad_one_low = grad_one.astype(jnp.bfloat16)
        out_grad = product_tn(mixed, grad_one_low)
        cot = product_nt(grad_one_low, mat_out).astype(jnp.bfloat16)
        part_cot = share_of(cot)
        part_cot = jnp.where(own_index < HELPERS, part_cot, 0)
        dq, dk, dv, part_dq = attend_back(picks, first, queries, kv_all, shut, cot, part, part_cot, *logs)
        dq = with_shared_rows(part_dq, dq)
        dkv = jnp.concatenate([dk, dv], axis=1).astype(jnp.float32)
        dkv = lax.psum_scatter(dkv, SEQ, scatter_dimension=0)
        dkv = jnp.moveaxis(dkv, 0, 1).reshape(rows, 2 * D)
        proj_grad = jnp.concatenate([dq, dkv.astype(jnp.bfloat16)], axis=1)
        qkv_grad = product_tn(low_in, proj_grad)
        small_rows = jnp.stack(
            [
                jnp.sum(dq.astype(jnp.float32), axis=0),
                jnp.sum(dkv[:, D:], axis=0),
                jnp.sum(grad_one, axis=0),
                shift_one_grad,
                jnp.sum(grad_two, axis=0),
                shift_two_grad,
                gain_one_grad,
                gain_two_grad,
            ]
        )
        small_rows = small_by_owner(small_rows, jnp.sum(hidden_grad, axis=0), n_dev)
        owned[layer] = [
            lax.psum_scatter(a, (SEQ, BATCH), scatter_dimension=0, tiled=True)
            for a in (qkv_grad, out_grad, up_grad, down_grad, small_rows)
        ]
        owned[layer][4] = owned[layer][4][0]
        grad = grad_one + product_nt(proj_grad, mat_qkv)
    stacked = [jnp.stack([owned[layer][i] for layer in range(L)]) for i in range(5)]
    return (low[None], grad[None], *stacked[:4], *small_outputs(stacked[4], piece, up_bias.shape[1]))


def assemble(wanted):
    parts = [part for _, parts in wanted for part in parts]

    def body(*refs):
        sources, targets = list(refs[: len(parts)]), refs[len(parts) :]
        for target, (_, held) in zip(targets, wanted):
            for array, layer, column in held:
                target[layer, :, column : column + array.shape[1]] = sources.pop(0)[...]

    return pl.pallas_call(
        body,
        out_shape=[jax.ShapeDtypeStruct(shape, jnp.float32) for shape, _ in wanted],
        in_specs=[IN_VMEM] * len(parts),
        out_specs=[IN_VMEM] * len(wanted),
        compiler_params=pltpu.CompilerParams(vmem_limit_bytes=VMEM_LIMIT),
        name="assemble",
    )(*[array for array, _, _ in parts])


def on_pairs(
    layer_input, segments, rand_blocks, w_qkv, w_out, w_up, w_down, gains, biases, up_bias, d_out
):
    seq_count, depth = lax.axis_size(SEQ), lax.axis_size(BATCH)
    n_dev = seq_count * depth
    rows, hidden = layer_input.shape[1], up_bias.shape[1] * n_dev
    blocks_here = rows // BLK
    picks = rand_blocks.reshape(-1)
    first = (lax.axis_index(SEQ) * blocks_here).reshape(1)
    piece = D // n_dev

    small = jnp.concatenate(
        [biases.reshape(-1, piece), gains.reshape(-1, piece), up_bias.reshape(-1, piece)], axis=0
    ).T
    small = jnp.pad(small, ((0, 0), (0, 128 - small.shape[1])))
    segs = jnp.pad(segments.reshape(-1, 128), ((0, 8 - rows // 128), (0, 0)))

    def flat(slabs):
        return [w.reshape(-1, w.shape[2]) for w in slabs]

    places = jnp.stack([picks // blocks_here, picks % blocks_here])

    def attention_back(got, back):
        return attend_back(
            picks, first, got.q, got.every.reshape(seq_count, 2 * PAIRS, rows, WIDE), shut, back.cot, got.part, back.part_cot, got.log, got.plog
        )

    x = layer_input[0]
    layers = [[(w, layer) for w in (w_qkv, w_out, w_up, w_down)] for layer in range(L)]
    own_segs = segments.reshape(blocks_here, BLK).astype(jnp.float32)
    own_segs = jnp.concatenate([own_segs, own_segs], axis=1)
    head_one, weights_one = first_head(x, small, segs, own_segs, places, layers[0], seq_count, depth, 0)
    weights_one = flat(weights_one)
    vectors = head_one.vectors
    shifts = head_one.table.reshape(L, 4, n_dev, piece)
    shifts = jnp.swapaxes(shifts, 1, 2).reshape(L, 1, hidden)
    shut = head_one.shut
    rows_one, weights_two = tail(
        head_one.o, head_one.po, x, vectors, shifts[0], weights_one, layers[1], shut, places, seq_count, depth, 1
    )
    weights_two = flat(weights_two)
    middle = rows_one.z_low
    rows_two = turn(rows_one.o, rows_one.po, rows_one.z, vectors, shifts[1], weights_two, d_out[0], depth, 2)
    dq, dk, dv, part = attention_back(rows_one, rows_two)
    sums_two = sum_rows(dk, dv, dq, part, rows_two, rows_two, seq_count, depth, 3)
    back_one = sum_weights(
        rows_two, middle, sums_two.proj, vectors, weights_two[0], None, (weights_one, rows_one), n_dev, depth, 4
    )
    dq, dk, dv, part = attention_back(head_one, back_one)
    sums_one = sum_rows(dk, dv, dq, part, rows_one, back_one, seq_count, depth, 5)
    small = jnp.concatenate(
        [
            small_by_owner(back.totals + sums.totals, back.hidden_totals[0], n_dev)
            for back, sums in ((back_one, sums_one), (rows_two, sums_two))
        ],
        axis=1,
    )
    last = sum_weights(
        SimpleNamespace(**{**vars(rows_one), **vars(back_one)}),
        x, sums_one.proj, None, weights_one[0], small, None, n_dev, depth, 6,
    )
    whole_outputs = assemble(
        [
            ((L, piece, 3 * D), [(last.owned0, 0, 0), (back_one.owned0, 1, 0)]),
            ((L, piece, D), [(sums_one.owned1, 0, 0), (sums_two.owned1, 1, 0)]),
            (
                (L, piece, hidden),
                [
                    (sums_one.owned2, 0, 0), (last.owned2, 0, hidden // 2),
                    (sums_two.owned2, 1, 0), (back_one.owned2, 1, hidden // 2),
                ],
            ),
            ((L, hidden // n_dev, D), [(last.owned3, 0, 0), (back_one.owned3, 1, 0)]),
            ((1, rows, D), [(last.dx, 0, 0)]),
        ]
    )
    return (
        rows_two.z_low[None],
        whole_outputs[4],
        *whole_outputs[:4],
        *small_outputs(last.owned4.reshape(L, 8, 128), piece, up_bias.shape[1]),
    )


def solution(mesh):
    placed = (
        P(BATCH, SEQ, None),
        P(BATCH, SEQ),
        P(BATCH, SEQ, None, None),
        P(None, (SEQ, BATCH), None),
        P(None, (SEQ, BATCH), None),
        P(None, (SEQ, BATCH), None),
        P(None, (SEQ, BATCH), None),
        P(None, None, (SEQ, BATCH)),
        P(None, None, (SEQ, BATCH)),
        P(None, (SEQ, BATCH)),
        P(BATCH, SEQ, None),
    )
    return jax.shard_map(
        on_pairs if mesh.shape[SEQ] == 8 and mesh.shape[BATCH] == 4 else on_any_slice,
        mesh=mesh,
        in_specs=placed,
        out_specs=(
            P(BATCH, SEQ, None),
            P(BATCH, SEQ, None),
            P(None, (SEQ, BATCH), None),
            P(None, (SEQ, BATCH), None),
            P(None, (SEQ, BATCH), None),
            P(None, (SEQ, BATCH), None),
            P(None, None, (SEQ, BATCH)),
            P(None, None, (SEQ, BATCH)),
            P(None, (SEQ, BATCH)),
        ),
        check_vma=False,
    )
```

```python
import itertools
from functools import partial
from types import SimpleNamespace

import jax
import jax.numpy as jnp
from jax import lax
from jax.experimental import pallas as pl
from jax.experimental.pallas import tpu as pltpu
from jax.sharding import PartitionSpec as P

MESH = pl.DeviceIdType.MESH
SEQ, BATCH = "seq", "batch"


HEAD_PLACES = SimpleNamespace(
    begins=(0, 3, 1, 2, 16, 28, 46, 15, 31),
    arrivals=(
        (5, 4, 17, 6, 18, 19, 32, 20, 33, 30, 54, 34, 55, 56, 77),
        (12, 13, 29),
        (7, 14, 21, 8, 22, 23, 35, 24, 36, 37, 57, 38, 58, 59, 78),
        (9, 10, 50, 11, 25, 26, 39, 27, 40, 41, 60, 42, 62, 61, 79),
        (47, 48, 72, 49, 73, 74, 102, 75, 103, 104, 125, 105, 126, 127, 143),
        (51, 52, 80, 53, 83, 81, 106, 82, 93, 107, 128, 108, 129, 130, 142),
        (76, 70, 98, 71, 99, 100, 119, 101, 120, 121, 140, 122, 144, 141, 150),
        (43, 66, 94, 44, 67, 95, 117, 45, 68, 91, 118, 69, 96, 133, 139),
        (64, 87, 115, 65, 88, 109, 136, 63, 89, 114, 137, 90, 116, 138, 147),
        (112, 113, 134),
        (123, 124, 145),
        (131, 132, 146),
        (110, 111, 135),
    ),
    project=84,
    attention=(148, 149, 151),
)
TAIL_PLACES = SimpleNamespace(
    begins=(1, 2, 0, 14, 38, 43, 4),
    arrivals=(
        (10, 11, 19, 12, 20, 21, 61, 22, 42, 33, 47, 34, 49, 48, 70),
        (32, 13, 23, 17, 26, 24, 46, 25, 35, 36, 52, 37, 53, 54, 71),
        (6, 7, 27, 8, 28, 29, 62, 31, 50, 56, 74, 51, 72, 75, 92),
        (39, 40, 63, 41, 64, 65, 93, 66, 86, 87, 108, 88, 129, 110, 128),
        (55, 59, 80, 60, 111, 89, 105, 79, 118, 98, 122, 101, 123, 124, 137),
        (67, 81, 95, 68, 82, 106, 125, 69, 83, 112, 126, 84, 107, 127, 136),
        (57, 78, 100, 73, 96, 102, 120, 58, 99, 113, 121, 91, 103, 119, 132),
        (97, 104, 130),
        (114, 115, 135),
        (133, 117, 134),
        (116, 109, 131),
    ),
    steps=(3, 5, 9, 15, 16, 18, 30, 44, 45),
    project=76,
    attention=(138, 139, 140),
)
ROWS_PLACES = SimpleNamespace(
    rows=(
        (0, 3, 4, 17, 53),
        (1, 7, 9, 25, 45),
        (11, 23, 21, 43, 52),
        (6, 13, 30, 38, 54),
    ),
    weights=(
        (5, 10, 16, 14, 15, 8, 19, 18, 12, 24, 20, 34, 31, 22, 32, 46, 55),
        (27, 28, 29, 37, 33, 39, 36, 41, 35, 47, 42, 44, 40, 49, 50, 48, 56),
    ),
    grads=(2, 26),
    collect=51,
)
BELOW_PLACES = SimpleNamespace(
    weights=(
        (9, 12, 11, 14, 47, 36, 45, 27, 66, 48, 20, 52, 70, 54, 61, 73, 77),
        (10, 37, 49, 24, 58, 26, 33, 69, 68, 30, 32, 64, 72, 40, 63, 75, 78),
        (6, 22, 18, 23, 31, 21, 39, 29, 42, 38, 43, 46, 60, 53, 62, 74, 76),
        (1, 4, 3, 2, 15, 13, 7, 19, 41, 17, 44, 28, 59, 16, 55, 67, 71),
    ),
    grads=(8, 5, 0),
    steps=(25, 34, 35, 50, 51, 56, 57, 65),
)
LAST_PLACES = SimpleNamespace(
    weights=(
        (22, 31, 32, 33, 61, 36, 57, 65, 74, 41, 63, 67, 79, 58, 72, 84, 88),
        (21, 43, 45, 47, 62, 46, 48, 75, 77, 51, 64, 78, 80, 56, 83, 81, 87),
        (11, 29, 34, 40, 49, 50, 44, 37, 52, 53, 55, 60, 68, 66, 70, 82, 86),
        (9, 13, 15, 18, 30, 35, 23, 42, 54, 25, 27, 59, 71, 39, 69, 76, 85),
        (1, 2, 5, 12, 14, 3, 4, 17, 24, 6, 7, 16, 28, 8, 19, 26, 38),
    ),
    grads=(20, 10, 0),
    steps=(73,),
)


def place():
    s = lax.axis_index(SEQ)
    return {"y": s // 4, "x": (s // 2) % 2, "c": s % 2, "z": lax.axis_index(BATCH)}


def device_of(p):
    return ((p["y"] * 2 + p["x"]) * 2 + p["c"], p["z"])


def flipped(p, axis):
    return {**p, axis: 1 - p[axis]}


def at_depth(p, z):
    return {**p, "z": z}


def number_in(depth):
    return lambda p: device_of(p)[0] * depth + p["z"]


def number_in_sequence(p):
    return device_of(p)[0]


def when(cond, action):
    if cond is None:
        action()
    else:
        pl.when(cond)(action)


def ranked(z, rank, depth):
    near = [sorted(range(depth), key=lambda q: (abs(q - k), q))[rank] for k in range(depth)]
    return sum(jnp.where(z == k, near[k], 0) for k in range(depth))


def offsets(order, depth):
    return list(itertools.product(*[range(depth if a == "z" else 2) for a in order]))


def target_of(order, offset, depth, me):
    p = me
    for axis, d in zip(order, offset):
        if d:
            p = at_depth(p, ranked(me["z"], d, depth)) if axis == "z" else flipped(p, axis)
    return p


def last_move(offset):
    return max([-1] + [i for i, d in enumerate(offset) if d])


def greet(axes, depth, spread=False, collect=False):
    me = place()
    barrier = pltpu.get_barrier_semaphore()

    def signal(device):
        pl.semaphore_signal(barrier, inc=1, device_id=device, device_id_type=MESH)

    count = 0
    for axis in axes + ("c",):
        if axis == "z":
            for step in (1, -1):
                peer = at_depth(me, me["z"] + step)
                cond = (peer["z"] >= 0) & (peer["z"] < depth)
                when(cond, lambda peer=peer: signal(device_of(peer)))
                count = count + cond.astype(jnp.int32)
        else:
            signal(device_of(flipped(me, axis)))
            count = count + 1
    if spread or collect:
        seq, z = lax.axis_index(SEQ), lax.axis_index(BATCH)
        if spread:
            when(seq != 0, lambda: signal((0, z)))
            count = count + jnp.where(seq == 0, HELPERS - 1, 0)
        if collect:

            @pl.when(seq == 0)
            def _():
                for j in range(1, HELPERS):
                    signal((j, z))

            count = count + jnp.where(seq == 0, 0, 1)
    pl.semaphore_wait(barrier, count)


class Gather:
    def __init__(self, source, target, number, order, depth, send, recv, send_at):
        self.source, self.target, self.number = source, target, number
        self.order, self.depth, self.send, self.recv = order, depth, send, recv
        self.send_at = send_at
        self.me = place()
        self.sent = []

    @staticmethod
    def sends(order, depth):
        return sum(len(order) + 2 - last_move(t) for t in offsets(order, depth))

    def onward(self, offset):
        last = last_move(offset)
        z = self.me["z"]
        moves = []
        if last >= 0 and self.order[last] == "z":
            source = ranked(z, offset[last], self.depth)
            peer = jnp.where(source < z, z + 1, z - 1)
            moves.append((at_depth(self.me, peer), (peer >= 0) & (peer < self.depth)))
        for axis in self.order[last + 1 :]:
            if axis == "z":
                moves.append((at_depth(self.me, z + 1), z + 1 < self.depth))
                moves.append((at_depth(self.me, z - 1), z > 0))
            else:
                moves.append((flipped(self.me, axis), None))
        moves.append((flipped(self.me, "c"), None))
        return moves

    def arrival(self, p):
        ref = self.target(p)
        return pltpu.make_async_remote_copy(
            src_ref=ref, dst_ref=ref, send_sem=self.send.at[0], recv_sem=self.recv.at[self.number(p)],
            device_id=device_of(self.me), device_id_type=MESH,
        )

    def handle(self, offset):
        p = target_of(self.order, offset, self.depth, self.me)
        own = not any(offset)
        if not own:
            self.arrival(p).wait_recv()
        for peer, cond in self.onward(offset):
            copy = pltpu.make_async_remote_copy(
                src_ref=self.source if own else self.target(p), dst_ref=self.target(p),
                send_sem=self.send.at[self.send_at], recv_sem=self.recv.at[self.number(p)],
                device_id=device_of(peer), device_id_type=MESH,
            )
            when(cond, copy.start)
            self.sent.append((cond, self.send_at))
            self.send_at += 1

    def begin(self):
        self.handle((0,) * len(self.order))

    def events(self, places):
        marks = [t for t in offsets(self.order, self.depth) if any(t)]
        return [(at, partial(self.handle, t)) for at, t in zip(places, marks, strict=True)]

    def siblings(self):
        for t in offsets(self.order, self.depth):
            self.arrival(flipped(target_of(self.order, t, self.depth, self.me), "c")).wait_recv()

    def drain(self):
        for cond, slot in self.sent:
            copy = pltpu.make_async_remote_copy(
                src_ref=self.source, dst_ref=self.target(self.me), send_sem=self.send.at[slot],
                recv_sem=self.recv.at[self.number(self.me)], device_id=device_of(self.me), device_id_type=MESH,
            )
            when(cond, copy.wait_send)


class Reduce:
    def __init__(self, partial_of, far_partial_of, inbox, order, depth, send, recv):
        self.partial_of, self.far_partial_of, self.inbox = partial_of, far_partial_of, inbox
        self.order, self.depth, self.send, self.recv = order, depth, send, recv
        self.me = place()
        self.base, _ = self.slots(order, depth)
        self.marks = sorted(offsets(order, depth), key=lambda t: (-sum(t), t))
        self.sent = []

    @staticmethod
    def split(order, offset):
        if "z" not in order:
            return offset, 0
        i = order.index("z")
        return offset[:i] + (0,) + offset[i + 1 :], offset[i]

    @staticmethod
    def slots(order, depth):
        base, count = {}, 0
        deep = depth if "z" in order else 1
        for t in offsets(order, depth):
            key, rank = Reduce.split(order, t)
            if rank:
                continue
            last = last_move(key)
            for i, axis in enumerate(order):
                if i <= last:
                    continue
                base[(key, axis)] = count
                if axis == "z":
                    count += deep + 1
                elif "z" in order and i > order.index("z"):
                    count += deep
                else:
                    count += 1
            base[(key, "c")] = count
            count += deep
        return base, count

    def where_(self, key, axis, z):
        deep = "z" in self.order and (axis == "c" or self.order.index(axis) > self.order.index("z"))
        return self.base[(key, axis)] + (z if deep else 0)

    def copy(self, source, edge, slot, peer):
        return pltpu.make_async_remote_copy(
            src_ref=source, dst_ref=self.inbox.at[edge], send_sem=self.send.at[slot],
            recv_sem=self.recv.at[edge], device_id=device_of(peer), device_id_type=MESH,
        )

    def start(self, offset):
        p = target_of(self.order, offset, self.depth, self.me)
        key, _ = self.split(self.order, offset)
        slot = self.marks.index(offset)
        edge = self.where_(key, "c", p["z"])
        peer = flipped(self.me, "c")
        self.copy(self.far_partial_of(flipped(p, "c")), edge, slot, peer).start()
        self.sent.append(slot)

    def kids(self, offset, p):
        key, rank = self.split(self.order, offset)
        last, z = last_move(offset), self.me["z"]
        found = [(self.where_(key, "c", p["z"]), None)]
        for axis in self.order[last + 1 :]:
            if axis == "z":
                at = self.base[(key, "z")]
                found += [(at + z, z > 0), (at + self.depth, z + 1 < self.depth)]
            else:
                found.append((self.where_(key, axis, p["z"]), None))
        if last >= 0 and self.order[last] == "z":
            far = jnp.where(p["z"] < z, z + 1, z - 1)
            found.append((self.base[(key, "z")] + p["z"], (far >= 0) & (far < self.depth)))
        return found

    def upward(self, offset, p):
        key, rank = self.split(self.order, offset)
        k, z = last_move(offset), self.me["z"]
        axis = self.order[k]
        if axis == "z":
            edge = self.base[(key, "z")] + jnp.where(p["z"] == z - 1, self.depth, p["z"])
            return edge, at_depth(self.me, jnp.where(p["z"] < z, z - 1, z + 1))
        parent = key[:k] + (0,) + key[k + 1 :]
        return self.where_(parent, axis, p["z"]), flipped(self.me, axis)

    def handle(self, offset, add, finish):
        p = target_of(self.order, offset, self.depth, self.me)
        kids = self.kids(offset, p)
        slot = len(self.marks) + self.marks.index(offset)
        for edge, cond in kids:
            when(cond, self.copy(self.inbox.at[edge], edge, slot, self.me).wait_recv)
        parts = [(self.inbox.at[edge], cond) for edge, cond in kids]
        if any(offset):
            into = parts[0][0]
            add(self.partial_of(p), parts, into)
            edge, peer = self.upward(offset, p)
            self.copy(into, edge, slot, peer).start()
            self.sent.append(slot)
        else:
            finish(self.partial_of(p), parts)

    def drain(self):
        for slot in self.sent:
            self.copy(self.inbox.at[0], 0, slot, self.me).wait_send()


D = 768
H = 12
DH = 64
BLK = 64
R = 3
GLOB = 2
L = 2
PAIRS = H // 2
WIDE = 2 * DH
SHARED = GLOB * BLK
SHARE = 16
HELPERS = SHARED // SHARE
VMEM_LIMIT = 60 * 1024 * 1024

layer_eps = 1e-06
masked_score = -1e30

Z_Y_X, Z_X_Y, X_Y_Z, Y_X_Z = ("z", "y", "x"), ("z", "x", "y"), ("x", "y", "z"), ("y", "x", "z")
Y_X, X_Y = ("y", "x"), ("x", "y")
ANYWHERE = pl.BlockSpec(memory_space=pl.ANY)
IN_SMEM = pl.BlockSpec(memory_space=pltpu.SMEM)
IN_VMEM = pl.BlockSpec(memory_space=pltpu.VMEM)
LOAD, SAVE = pl.BlockSpec(memory_space=pl.ANY), pl.BlockSpec(memory_space=pl.ANY)


def dma(*shape):
    return pltpu.SemaphoreType.DMA(shape)


def product(a, b):
    return lax.dot_general(a, b, (((1,), (0,)), ((), ())), preferred_element_type=jnp.float32)


def product_nt(a, b):
    return lax.dot_general(a, b, (((1,), (1,)), ((), ())), preferred_element_type=jnp.float32)


def product_tn(a, b):
    return lax.dot_general(a, b, (((0,), (0,)), ((), ())), preferred_element_type=jnp.float32)


def split_heads(pair_rows):
    low_lanes = lax.broadcasted_iota(jnp.int32, (1, WIDE), 1) < DH
    zero = jnp.zeros_like(pair_rows)
    return jnp.concatenate([jnp.where(low_lanes, pair_rows, zero), jnp.where(low_lanes, zero, pair_rows)], axis=0)


def join_heads(stacked):
    low_lanes = lax.broadcasted_iota(jnp.int32, (1, WIDE), 1) < DH
    rows = stacked.shape[0] // 2
    return jnp.where(low_lanes, stacked[:rows], stacked[rows:])


def row_of(block):
    return pl.multiple_of(block * BLK, BLK)


class Keys:
    def __init__(self, ref, pair=None):
        self.ref, self.pair = ref, pair
        self.held = ref.shape[2] // (BLK if pair is None else 1)
        self.blocks_all = ref.shape[0] * self.held

    def block(self, device, inner):
        if self.pair is None:
            return self.ref[device, 0, pl.ds(row_of(inner), BLK)]
        return self.ref[device, self.pair, inner]

    def whole(self):
        held = self.ref[...] if self.pair is None else self.ref[:, self.pair]
        return held.reshape(-1, WIDE)

    def with_shared(self, near):
        if self.pair is None:
            shared = self.ref[0, 0, 0:SHARED]
        else:
            shared = self.ref[0, self.pair, 0:GLOB].reshape(SHARED, WIDE)
        return jnp.concatenate([shared, near], axis=0)


def window_blocks(first, block, blocks_all):
    return [(first + block + j - 1 + blocks_all) % blocks_all for j in range(3)]


def drawn_blocks(picks_ref, pair, block, r):
    return [picks_ref[(block * H + 2 * pair + side) * R + r] for side in range(2)]


def bring(drawn, first, pairs, blocks_here):
    low_lanes = lax.broadcasted_iota(jnp.int32, (1, WIDE), 1) < DH
    for block in range(blocks_here):
        for source, target in pairs:
            for j, one in enumerate(window_blocks(first, block, source.blocks_all)):
                rows = source.block(one // source.held, one % source.held)
                target[block, j * BLK : (j + 1) * BLK] = rows
            for r in range(R):
                one, two = drawn(block, r)
                target[block, (3 + r) * BLK : (4 + r) * BLK] = jnp.where(
                    low_lanes, source.block(*one), source.block(*two)
                )


def key_scores(keys, q_heads, shut):
    scores = product_nt(keys, q_heads)
    end = SHARED + 3 * BLK
    return jnp.concatenate([scores[:SHARED], scores[SHARED:end] + shut, scores[end:]], axis=0)


def soft(scores):
    top = jnp.max(scores, axis=0, keepdims=True)
    weight = jnp.exp(scores - top)
    total = jnp.sum(weight, axis=0, keepdims=True)
    return weight * (1.0 / total), top + jnp.log(total)


def attend_pair(
    drawn, first, q_ref, keys, values, shut_ref, part_ref, o_ref, po_ref, log_ref, plog_ref, near_k, near_v
):
    blocks_here = q_ref.shape[0] // BLK
    bring(drawn, first, [(keys, near_k), (values, near_v)], blocks_here)
    scale = jnp.bfloat16(DH ** (-0.5))
    weight, logs = soft(product_nt(keys.whole(), split_heads(part_ref[...] * scale)))
    mixed = product_tn(weight.astype(jnp.bfloat16), values.whole())
    po_ref[...] = join_heads(mixed).astype(po_ref.dtype)
    plog_ref[0] = logs
    for block in range(blocks_here):
        here = slice(block * BLK, (block + 1) * BLK)
        q_heads = split_heads(q_ref[here] * scale)
        weight, logs = soft(key_scores(keys.with_shared(near_k[block]), q_heads, shut_ref[block]))
        mixed = product_tn(weight.astype(jnp.bfloat16), values.with_shared(near_v[block]))
        o_ref[here] = join_heads(mixed).astype(o_ref.dtype)
        log_ref[0, block : block + 1] = logs


def drawn_places(picks_ref, pair, held):
    def drawn(block, r):
        return [(one // held, one % held) for one in drawn_blocks(picks_ref, pair, block, r)]

    return drawn


def attend_kernel(picks_ref, first_ref, q_ref, k_ref, v_ref, *refs):
    keys, values = Keys(k_ref), Keys(v_ref)
    drawn = drawn_places(picks_ref, pl.program_id(0), keys.held)
    attend_pair(drawn, first_ref[0], q_ref, keys, values, *refs)


def near_rows(rows, dtype):
    return pltpu.VMEM((rows // BLK, 6 * BLK, WIDE), dtype)


def columns(rows, shift=0):
    return pl.BlockSpec((rows, WIDE), lambda p, *_: (0, p + shift))


def of_all(kv, shift=0):
    return pl.BlockSpec((kv.shape[0], 1, kv.shape[2], WIDE), lambda p, *_: (0, p + shift, 0, 0))


def by_pair(rows, lanes):
    return pl.BlockSpec((1, rows, lanes), lambda p, *_: (p, 0, 0))


def attend(picks, first, queries, kv, shut, part):
    rows = queries.shape[0]
    blocks = rows // BLK
    return pl.pallas_call(
        attend_kernel,
        grid_spec=pltpu.PrefetchScalarGridSpec(
            num_scalar_prefetch=2,
            grid=(PAIRS,),
            in_specs=[
                columns(rows), of_all(kv), of_all(kv, PAIRS),
                pl.BlockSpec(shut.shape, lambda p, *_: (0, 0, 0)), columns(SHARE),
            ],
            out_specs=[columns(rows), columns(SHARE), by_pair(blocks, WIDE), by_pair(1, 2 * SHARE)],
            scratch_shapes=[near_rows(rows, jnp.bfloat16)] * 2,
        ),
        out_shape=[
            jax.ShapeDtypeStruct((rows, D), jnp.bfloat16),
            jax.ShapeDtypeStruct((SHARE, D), jnp.bfloat16),
            jax.ShapeDtypeStruct((PAIRS, blocks, WIDE), jnp.float32),
            jax.ShapeDtypeStruct((PAIRS, 1, 2 * SHARE), jnp.float32),
        ],
        compiler_params=pltpu.CompilerParams(vmem_limit_bytes=VMEM_LIMIT),
        name="attend",
    )(picks, first, queries, kv, kv, shut, part)


def score_grads(weight, values, cot_heads):
    grads = product_nt(values, cot_heads)
    mean = jnp.sum(weight * grads, axis=0, keepdims=True)
    return (weight * (grads - mean)).astype(jnp.bfloat16)


def attend_back_kernel(
    picks_ref, first_ref, q_ref, k_ref, v_ref, shut_ref, do_ref, part_ref, pdo_ref, log_ref, plog_ref,
    dq_ref, dk_ref, dv_ref, pdq_ref, sum_k, sum_v, near_k, near_v, grad_k, grad_v,
):
    pair = pl.program_id(0)
    first = first_ref[0]
    blocks_here, blocks_all = q_ref.shape[0] // BLK, sum_k.shape[0] // BLK
    all_keys, all_values = Keys(k_ref), Keys(v_ref)
    drawn = drawn_places(picks_ref, pair, all_keys.held)
    bring(drawn, first, [(all_keys, near_k), (all_values, near_v)], blocks_here)
    low_lanes = lax.broadcasted_iota(jnp.int32, (1, WIDE), 1) < DH
    step = DH ** (-0.5)
    scale = jnp.bfloat16(step)
    part, cot = split_heads(part_ref[...] * scale), split_heads(pdo_ref[...])
    weight = jnp.exp(product_nt(all_keys.whole(), part) - plog_ref[0])
    grads = score_grads(weight, all_values.whole(), cot)
    pdq_ref[...] = (join_heads(product_tn(grads, all_keys.whole())) * step).astype(pdq_ref.dtype)
    sum_k[...] = product(grads, part)
    sum_v[...] = product(weight.astype(jnp.bfloat16), cot)
    shared_k = jnp.zeros((SHARED, WIDE), jnp.float32)
    shared_v = jnp.zeros((SHARED, WIDE), jnp.float32)
    for block in range(blocks_here):
        here = slice(block * BLK, (block + 1) * BLK)
        do = jnp.where(first + block < GLOB, jnp.bfloat16(0), do_ref[here])
        q_heads, do_heads = split_heads(q_ref[here] * scale), split_heads(do)
        keys, values = all_keys.with_shared(near_k[block]), all_values.with_shared(near_v[block])
        weight = jnp.exp(key_scores(keys, q_heads, shut_ref[block]) - log_ref[0, block : block + 1])
        grads = score_grads(weight, values, do_heads)
        dq_ref[here] = (join_heads(product_tn(grads, keys)) * step).astype(dq_ref.dtype)
        key_grad = product(grads, q_heads)
        value_grad = product(weight.astype(jnp.bfloat16), do_heads)
        shared_k = shared_k + key_grad[:SHARED]
        shared_v = shared_v + value_grad[:SHARED]
        grad_k[block] = key_grad[SHARED:]
        grad_v[block] = value_grad[SHARED:]
    sum_k[0:SHARED] += shared_k
    sum_v[0:SHARED] += shared_v
    for block in range(blocks_here):
        for grad, total in ((grad_k, sum_k), (grad_v, sum_v)):
            for j, one in enumerate(window_blocks(first, block, blocks_all)):
                total[pl.ds(row_of(one), BLK)] += grad[block, j * BLK : (j + 1) * BLK]
            for r in range(R):
                tile = grad[block, (3 + r) * BLK : (4 + r) * BLK]
                one, two = drawn_blocks(picks_ref, pair, block, r)
                total[pl.ds(row_of(one), BLK)] += jnp.where(low_lanes, tile, 0.0)
                total[pl.ds(row_of(two), BLK)] += jnp.where(low_lanes, 0.0, tile)
    dk_ref[...] = sum_k[...].astype(dk_ref.dtype).reshape(dk_ref.shape)
    dv_ref[...] = sum_v[...].astype(dv_ref.dtype).reshape(dv_ref.shape)


def attend_back(picks, first, queries, kv, shut, cot, part, part_cot, logs, part_logs):
    rows, grads = queries.shape[0], (kv.shape[0], PAIRS) + kv.shape[2:]
    length = kv.shape[0] * kv.shape[2]
    return pl.pallas_call(
        attend_back_kernel,
        grid_spec=pltpu.PrefetchScalarGridSpec(
            num_scalar_prefetch=2,
            grid=(PAIRS,),
            in_specs=[
                columns(rows), of_all(kv), of_all(kv, PAIRS),
                pl.BlockSpec(shut.shape, lambda p, *_: (0, 0, 0)), columns(rows), columns(SHARE), columns(SHARE),
                by_pair(rows // BLK, WIDE), by_pair(1, 2 * SHARE),
            ],
            out_specs=[columns(rows), of_all(kv), of_all(kv), columns(SHARE)],
            scratch_shapes=[pltpu.VMEM((length, WIDE), jnp.float32)] * 2
            + [near_rows(rows, jnp.bfloat16)] * 2
            + [near_rows(rows, jnp.float32)] * 2,
        ),
        out_shape=[
            jax.ShapeDtypeStruct((rows, D), jnp.bfloat16),
            jax.ShapeDtypeStruct(grads, jnp.bfloat16),
            jax.ShapeDtypeStruct(grads, jnp.bfloat16),
            jax.ShapeDtypeStruct((SHARE, D), jnp.bfloat16),
        ],
        compiler_params=pltpu.CompilerParams(vmem_limit_bytes=VMEM_LIMIT),
        name="attend_back",
    )(picks, first, queries, kv, kv, shut, cot, part, part_cot, logs, part_logs)


def call(body, name, cid, ins, outs, scratch):
    loads = [k for k, (_, where) in ins.items() if where is LOAD]
    saves = [k for k, (_, _, where) in outs.items() if where is SAVE]
    names = ["far_" + k if k in loads or k in saves else k for k in (*ins, *outs)]
    scratch = {
        **scratch,
        **{k: pltpu.VMEM(ins[k][0].shape, ins[k][0].dtype) for k in loads},
        **{k: pltpu.VMEM(outs[k][0], outs[k][1]) for k in saves},
        **dict(moves=dma(len(loads) + len(saves) + 1)),
    }

    def run(*given):
        refs = SimpleNamespace(**dict(zip(names + list(scratch), given)))
        copies = {}
        for i, k in enumerate(loads + saves):
            pair = (getattr(refs, "far_" + k), getattr(refs, k))
            copies[k] = pltpu.make_async_copy(*(pair if k in loads else pair[::-1]), refs.moves.at[i])
        coming, going = list(loads), []
        for k in loads:
            copies[k].start()

        def ready(*wanted):
            for k in wanted:
                if k in coming:
                    coming.remove(k)
                    copies[k].wait()

        def save(*given):
            for k in given:
                if k in saves:
                    going.append(k)
                    copies[k].start()

        refs.ready, refs.save = ready, save
        body(refs)
        ready(*loads)
        save(*[k for k in saves if k not in going])
        for k in saves:
            copies[k].wait()

    got = pl.pallas_call(
        run,
        out_shape=[jax.ShapeDtypeStruct(shape, dtype) for shape, dtype, _ in outs.values()],
        in_specs=[where for _, where in ins.values()],
        out_specs=[where for _, _, where in outs.values()],
        scratch_shapes=list(scratch.values()),
        compiler_params=pltpu.CompilerParams(
            collective_id=cid, has_side_effects=True, vmem_limit_bytes=VMEM_LIMIT
        ),
        name=name,
    )(*[array for array, _ in ins.values()])
    return SimpleNamespace(**dict(zip(outs, got)))


def over(count, act):
    def step(i, carry):
        act(i)
        return carry

    lax.fori_loop(0, count, step, 0)


def span(i, size, first=0):
    return pl.ds(pl.multiple_of(first + i * size, size), size)


def run_in_order(timed):
    for _, act in sorted(timed, key=lambda pair: pair[0]):
        act()


def layer_pieces(rows_in, rows_down, first):
    half, wide = rows_down // 2, 3 * D // 2
    return [
        (first, 0, rows_in, 0, wide, Z_Y_X),
        (first, 0, rows_in, wide, wide, Z_X_Y),
        (first + 1, 0, rows_in, 0, D, Z_X_Y),
        (first + 2, 0, rows_in, 0, 2 * D, Z_Y_X),
        (first + 2, 0, rows_in, 2 * D, 2 * D, Z_X_Y),
        (first + 3, 0, half, 0, D, X_Y_Z),
        (first + 3, half, half, 0, D, Y_X_Z),
    ]


class Gathering:
    def __init__(self, arrays, pieces, seq_count, depth, near):
        self.near, self.layers = near, [layer for _, layer in arrays]
        shapes = [a.shape if layer is None else a.shape[1:] for a, layer in arrays]
        self.shapes = [jax.ShapeDtypeStruct(shape, a.dtype) for shape, (a, _) in zip(shapes, arrays)]
        arrays = [a for a, _ in arrays]
        self.arrays, self.pieces, self.depth, self.n_dev = arrays, pieces, depth, seq_count * depth
        flat_only = {which for which, *_, order in pieces if "z" not in order}
        self.counts = [seq_count if i in flat_only else self.n_dev for i in range(len(arrays))]

    def ins(self):
        return {"slab%d" % i: (a, ANYWHERE) for i, a in enumerate(self.arrays)}

    def outs(self):
        return {
            "every%d" % i: ((n,) + a.shape, a.dtype, SAVE if i in self.near else ANYWHERE)
            for i, (n, a) in enumerate(zip(self.counts, self.shapes))
        }

    def scratch(self):
        total = sum(Gather.sends(order, self.depth) for *_, order in self.pieces)
        return {
            "g_send": dma(total),
            "g_recv": dma(len(self.pieces), self.n_dev),
            "g_local": dma(len(self.arrays)),
        }

    def number(self, i):
        return number_in(self.depth) if self.counts[i] == self.n_dev else number_in_sequence

    def begin(self, refs):
        slabs = [getattr(refs, "slab%d" % i) for i in range(len(self.arrays))]
        slabs = [ref if layer is None else ref.at[layer] for ref, layer in zip(slabs, self.layers)]
        every = [getattr(refs, "every%d" % i) for i in range(len(self.arrays))]
        self.jobs, at = [], 0
        for k, (which, row, rows, column, columns_, order) in enumerate(self.pieces):
            window = (pl.ds(row, rows), pl.ds(column, columns_))
            number = self.number(which)
            self.jobs.append(
                Gather(
                    slabs[which].at[window],
                    lambda p, which=which, window=window, number=number: every[which].at[(number(p),) + window],
                    number, order, self.depth, refs.g_send, refs.g_recv.at[k], at,
                )
            )
            at += Gather.sends(order, self.depth)
        me = place()
        self.own = [
            pltpu.make_async_copy(slab, all_.at[self.number(i)(me)], refs.g_local.at[i])
            for i, (slab, all_) in enumerate(zip(slabs, every))
        ]
        for copy in self.own:
            copy.start()

    def hurry(self, refs, arrays):
        for (which, *_), job in zip(self.pieces, self.jobs):
            if which in arrays:
                job.siblings()
        for i in arrays:
            self.own[i].wait()
            refs.save("every%d" % i)
        self.early = arrays

    def end(self):
        for (which, *_), job in zip(self.pieces, self.jobs):
            if which not in self.early:
                job.siblings()
        for job in self.jobs:
            job.drain()
        for i, copy in enumerate(self.own):
            if i not in self.early:
                copy.wait()

    def results(self, got):
        return [getattr(got, "every%d" % i) for i in range(len(self.arrays))]


def to_helpers(source, target, send, recv):
    seq, z = lax.axis_index(SEQ), lax.axis_index(BATCH)

    def copy(j):
        return pltpu.make_async_remote_copy(
            src_ref=source.at[pl.ds(j * SHARE, SHARE)], dst_ref=target, send_sem=send.at[j],
            recv_sem=recv, device_id=(j, z), device_id_type=MESH,
        )

    def begin():
        for j in range(1, HELPERS):
            copy(j).start()

    def own():
        pltpu.sync_copy(source.at[pl.ds(0, SHARE)], target)
        for j in range(1, HELPERS):
            copy(j).wait_send()

    def end():
        pl.when(seq == 0)(own)
        pl.when(seq != 0)(lambda: copy(1).wait_recv())

    pl.when(seq == 0)(begin)
    return end


def to_first(source, target, send, recv):
    seq, z = lax.axis_index(SEQ), lax.axis_index(BATCH)

    def copy(j):
        return pltpu.make_async_remote_copy(
            src_ref=source, dst_ref=target.at[pl.ds(j * SHARE, SHARE)], send_sem=send,
            recv_sem=recv.at[j], device_id=(0, z), device_id_type=MESH,
        )

    for j in range(1, HELPERS):
        pl.when(seq == j)(copy(j).start)

    def end():
        def mine():
            pltpu.sync_copy(source, target.at[pl.ds(0, SHARE)])
            for j in range(1, HELPERS):
                copy(j).wait_recv()

        pl.when(seq == 0)(mine)
        pl.when(seq != 0)(lambda: copy(1).wait_send())

    return end


def from_slabs(ref):
    def get(at):
        slabs = ref[:, :, at]
        return slabs.astype(jnp.float32).reshape(-1, slabs.shape[2]).astype(ref.dtype)

    return get


def project(low, w, bias, q, kv):
    def queries(i):
        at = span(i, 256)
        q[:, at] = (product(low[...], w(at)) + bias[0:1, at]).astype(q.dtype)

    def keys(i):
        keep(2 * i, product(low[...], w(span(i, 256, D))))

    def values(i):
        keep(PAIRS + 2 * i, product(low[...], w(span(i, 256, 2 * D))) + bias[1:2, span(i, 256)])

    def keep(pair, acc):
        for half in range(2):
            lanes = acc[:, half * WIDE : (half + 1) * WIDE].astype(kv.dtype)
            kv[pair + half] = lanes.reshape(kv.shape[1:])

    for act in (keys, values, queries):
        over(D // 256, act)


class Sequence:
    def __init__(self, rows, seq_count, depth, dtype):
        self.rows, self.seq_count, self.depth, self.dtype = rows, seq_count, depth, dtype

    def outs(self):
        blocks, f32 = self.rows // BLK, jnp.float32
        return dict(
            q=((self.rows, D), self.dtype, SAVE),
            every=((self.seq_count, 2 * PAIRS, blocks, BLK, WIDE), self.dtype, SAVE),
            part=((SHARE, D), self.dtype, SAVE),
            o=((self.rows, D), self.dtype, SAVE), po=((SHARE, D), self.dtype, SAVE),
            log=((PAIRS, blocks, WIDE), f32, SAVE), plog=((PAIRS, 1, 2 * SHARE), f32, SAVE),
        )

    def scratch(self):
        return dict(
            kv=pltpu.VMEM((2 * PAIRS, self.rows // BLK, BLK, WIDE), self.dtype), send=dma(4 * Gather.sends(Y_X, self.depth)),
            recv=dma(4, self.seq_count), local=dma(), give=dma(HELPERS), take=dma(),
            near_k=near_rows(self.rows, self.dtype), near_v=near_rows(self.rows, self.dtype),
        )

    def prepare(self, refs):
        count, at = PAIRS // 2, 0
        self.jobs = []
        for i in range(4):
            window = pl.ds(i * count, count)
            self.jobs.append(
                Gather(
                    refs.kv.at[window],
                    lambda p, window=window: refs.every.at[number_in_sequence(p), window],
                    number_in_sequence, (X_Y, Y_X)[i % 2], self.depth, refs.send, refs.recv.at[i], at,
                )
            )
            at += Gather.sends(Y_X, self.depth)

    def begin(self, refs):
        for job in self.jobs:
            job.begin()
        self.finish = to_helpers(refs.q, refs.part, refs.give, refs.take)
        self.own = pltpu.make_async_copy(refs.kv, refs.every.at[number_in_sequence(place())], refs.local)
        self.own.start()

    def arrived(self, refs):
        for job in self.jobs:
            job.siblings()
        self.own.wait()
        self.finish()
        refs.save("every", "part")

    def attention(self, refs, steps):
        first = lax.axis_index(SEQ) * (self.rows // BLK)
        count = PAIRS // steps

        def pair_of(pair):
            at, one = span(pair, WIDE), pl.ds(pair, 1)

            def drawn(block, r):
                first_one = (block * H + 2 * pair) * R + r
                return [(refs.picks[0, i], refs.picks[1, i]) for i in (first_one, first_one + R)]

            attend_pair(
                drawn, first, refs.q.at[:, at], Keys(refs.every, pair), Keys(refs.every, PAIRS + pair), refs.shut,
                refs.part.at[:, at], refs.o.at[:, at], refs.po.at[:, at], refs.log.at[one], refs.plog.at[one],
                refs.near_k, refs.near_v,
            )

        def step(k):
            if k == 0:
                self.arrived(refs)
                refs.ready("shut")
            over(count, lambda i: pair_of(k * count + i))
            if k == steps - 1:
                refs.save("o", "po", "log", "plog")

        return [partial(step, k) for k in range(steps)]

    def end(self):
        for job in self.jobs:
            job.drain()


def project_and_send(refs, gathering, sequence, low, which):
    def act():
        gathering.hurry(refs, [which])
        w = from_slabs(getattr(refs, "every%d" % which))
        refs.ready("low")
        project(low, w, refs.bias, refs.q, refs.kv)
        sequence.begin(refs)
        refs.save("q")

    return act


def timed_events(jobs, places):
    return [pair for job, at in zip(jobs, places, strict=True) for pair in job.events(at)]


def shut_keys_here(segs, own_segs, shut):
    me, count = lax.axis_index(SEQ), segs.shape[0]
    blocks = shut.shape[0]
    rows = blocks * BLK

    def column(device):
        held = segs[device].astype(jnp.float32).T
        return [held[:, r : r + 1] for r in range(rows // WIDE)]

    before, here, after = column((me + count - 1) % count), column(me), column((me + 1) % count)
    near = jnp.concatenate([before[-1][WIDE - BLK :]] + here + [after[0][:BLK]], axis=0)
    for block in range(blocks):
        spot = (me * blocks + block - 1) * BLK + lax.broadcasted_iota(jnp.int32, (3 * BLK, WIDE), 0)
        same = near[block * BLK : (block + 3) * BLK] == own_segs[block : block + 1]
        shut[block] = jnp.where(same & (spot >= SHARED) & (spot < count * rows), 0.0, masked_score)


def first_head(low, small, segs, own_segs, picks, weights, seq_count, depth, cid):
    rows = low.shape[0]
    pieces = [(0, 0, small.shape[0], 0, 128, Z_Y_X), (1, 0, 8, 0, 128, Y_X)]
    pieces += layer_pieces(small.shape[0], weights[3][0].shape[1], 2)
    gathering = Gathering([(small, None), (segs, None)] + weights, pieces, seq_count, depth, (0, 1, 2))
    sequence = Sequence(rows, seq_count, depth, low.dtype)

    def body(refs):
        greet(("y", "x", "z"), depth, spread=True)
        gathering.begin(refs)
        sequence.prepare(refs)
        refs.bias = refs.vectors.at[0]

        def vectors():
            gathering.hurry(refs, [0, 1])
            shut_keys_here(refs.every1, refs.own_segs, refs.shut)
            refs.save("shut")
            table = refs.every0[...].astype(jnp.float32).reshape(D, 128).T
            for layer in range(L):
                refs.vectors[layer, 0:6] = table[6 * layer : 6 * layer + 6]
                refs.vectors[layer, 6:8] = table[6 * L + 2 * layer : 6 * L + 2 * layer + 2]
            refs.table[...] = table[8 * L : 12 * L]

        def project_now():
            project_and_send(refs, gathering, sequence, refs.low, 2)()
            gathering.early = [0, 1, 2]

        at = HEAD_PLACES
        run_in_order(
            [(place_, job.begin) for place_, job in zip(at.begins, gathering.jobs, strict=True)]
            + timed_events(gathering.jobs + sequence.jobs, at.arrivals)
            + [(at.project, vectors), (at.project + 0.1, project_now)]
            + list(zip(at.attention, sequence.attention(refs, len(at.attention)), strict=True))
        )
        sequence.end()
        gathering.end()

    got = call(
        body, "first_head", cid,
        {
            **dict(low=(low, LOAD), own_segs=(own_segs, IN_VMEM), picks=(picks, IN_SMEM)), **gathering.ins(),
        },
        {
            **dict(
                vectors=((L, 8, D), jnp.float32, IN_VMEM), table=((4 * L, D), jnp.float32, IN_VMEM),
                shut=((rows // BLK, 3 * BLK, WIDE), jnp.float32, SAVE),
            ),
            **sequence.outs(), **gathering.outs(),
        },
        {**sequence.scratch(), **gathering.scratch()},
    )
    return got, gathering.results(got)[2:]


def norm_block(resid, gain, shift):
    center = resid - jnp.mean(resid, axis=1, keepdims=True)
    inv_std = lax.rsqrt(jnp.mean(center * center, axis=1, keepdims=True) + layer_eps)
    normed = center * inv_std
    return normed * gain + shift, normed, inv_std


ROW_BLOCK = 64


WIDE_D, WIDE_FF = 384, 512


def tail_steps(refs, wide_d, wide_ff):
    rows, hidden = refs.resid.shape[0], refs.shifts.shape[1]

    def out():
        refs.ready("resid", "w_out")

        def act(i):
            at = span(i, wide_d)
            own = refs.resid[:, at].astype(jnp.float32)
            refs.sum[:, at] = own + product(refs.mixed[...], refs.w_out[:, at]) + refs.bias[2:3, at]

        over(D // wide_d, act)
        refs.save("mixed")

    def norm_one():
        def act(i):
            at = span(i, ROW_BLOCK)
            y, normed, inv = norm_block(refs.sum[at], refs.bias[6:7], refs.bias[3:4])
            refs.n1[at], refs.inv1[at], refs.sum[at] = normed, inv, y
            refs.y_low[at] = y.astype(jnp.bfloat16)

        over(rows // ROW_BLOCK, act)
        refs.save("n1", "inv1", "y_low")
        refs.ready("w_up")

    def up(first, count):
        def act(i):
            at = span(first + i, wide_ff)
            u = product(refs.y_low[...], refs.w_up[:, at]) + refs.shifts[0:1, at]
            share = 0.5 + 0.5 * lax.erf(u * (0.5 ** 0.5))
            refs.a_low[:, at] = (u * share).astype(jnp.bfloat16)
            slope = share + u * jnp.exp(-0.5 * u * u) * ((2.0 * jnp.pi) ** -0.5)
            refs.slope[:, at] = slope.astype(jnp.bfloat16)

        over(count, act)

    def down():
        refs.ready("w_down")
        refs.save("a_low", "slope")

        def act(i):
            at = span(i, wide_d)
            refs.sum[:, at] = refs.sum[:, at] + product(refs.a_low[...], refs.w_down[:, at]) + refs.bias[4:5, at]

        over(D // wide_d, act)

    def norm_two():
        def act(i):
            at = span(i, ROW_BLOCK)
            z, normed, inv = norm_block(refs.sum[at], refs.bias[7:8], refs.bias[5:6])
            refs.n2[at], refs.inv2[at] = normed, inv
            if hasattr(refs, "z"):
                refs.z[at] = z
            refs.z_low[at] = z.astype(jnp.bfloat16)

        over(rows // ROW_BLOCK, act)
        refs.save("n2", "inv2", "z", "z_low")

    ends = [hidden // wide_ff * k // 4 for k in range(5)]
    ups = [partial(up, a, b - a) for a, b in zip(ends, ends[1:])]
    return [out, norm_one] + ups + [down, norm_two]


def tail_ins(mixed, part, resid, vectors, shifts, weights):
    return dict(
        generic=(mixed, LOAD), own_part=(part, ANYWHERE), resid=(resid, LOAD), vectors=(vectors, IN_VMEM),
        shifts=(shifts, IN_VMEM), w_out=(weights[1], LOAD), w_up=(weights[2], LOAD), w_down=(weights[3], LOAD),
    )


def tail_results(rows, hidden):
    f32, low = jnp.float32, jnp.bfloat16
    kept = dict(mixed=((rows, D), low), y_low=((rows, D), low), a_low=((rows, hidden), low), z_low=((rows, D), low))
    norms = dict(
        n1=((rows, D), f32), inv1=((rows, 1), f32), slope=((rows, hidden), low), n2=((rows, D), f32), inv2=((rows, 1), f32)
    )
    return kept, norms


def saved(shapes):
    return {k: (*v, SAVE) for k, v in shapes.items()}


def tail_scratch(rows):
    return dict(sum=pltpu.VMEM((rows, D), jnp.float32), t_send=dma(), t_recv=dma(HELPERS))


def tail(mixed, part, resid, vectors, shifts, weights, next_weights, shut, picks, seq_count, depth, cid):
    rows, hidden = resid.shape[0], shifts.shape[1]
    pieces = layer_pieces(next_weights[0][0].shape[1], next_weights[3][0].shape[1], 0)
    gathering = Gathering(next_weights, pieces, seq_count, depth, (0,))
    sequence = Sequence(rows, seq_count, depth, mixed.dtype)

    def body(refs):
        refs.ready("generic")
        refs.mixed[...] = refs.generic[...]
        greet(("y", "x", "z"), depth, spread=True, collect=True)
        finish = to_first(refs.own_part, refs.mixed, refs.t_send, refs.t_recv)
        gathering.begin(refs)
        sequence.prepare(refs)
        refs.bias = refs.vectors.at[0]
        steps = [finish] + tail_steps(refs, 256, 256)

        def project_now():
            refs.bias = refs.vectors.at[1]
            project_and_send(refs, gathering, sequence, refs.z_low, 0)()

        at = TAIL_PLACES
        run_in_order(
            [(place_, job.begin) for place_, job in zip(at.begins, gathering.jobs, strict=True)]
            + timed_events(gathering.jobs + sequence.jobs, at.arrivals)
            + list(zip(at.steps, steps, strict=True)) + [(at.project, project_now)]
            + list(zip(at.attention, sequence.attention(refs, len(at.attention)), strict=True))
        )
        sequence.end()
        gathering.end()

    kept, norms = tail_results(rows, hidden)
    got = call(
        body, "tail", cid,
        {
            **tail_ins(mixed, part, resid, vectors, shifts, weights),
            **dict(shut=(shut, LOAD), picks=(picks, IN_SMEM)), **gathering.ins(),
        },
        {
            **saved(kept), **saved(norms), **dict(z=((rows, D), jnp.float32, SAVE)), **sequence.outs(),
            **gathering.outs(),
        },
        {**tail_scratch(rows), **sequence.scratch(), **gathering.scratch()},
    )
    return got, gathering.results(got)


def folded(block):
    return jnp.sum(block.reshape(-1, 8, block.shape[1]), axis=0)


def norm_block_back(grad, normed, inv_std, gain):
    scaled = grad * gain
    return (
        scaled
        - jnp.mean(scaled, axis=1, keepdims=True)
        - normed * jnp.mean(scaled * normed, axis=1, keepdims=True)
    ) * inv_std


def back_steps(refs, dz, w_down, w_up, w_out, waits=(lambda: None,) * 3):
    rows, hidden = refs.n2.shape[0], refs.slope.shape[1]
    zero = jnp.zeros((8, D), jnp.float32)

    def row(k, total):
        refs.totals[k : k + 1] = jnp.sum(total, axis=0, keepdims=True)

    def norm_two():
        refs.ready("n2", "inv2", "d_out")

        def act(i, sums):
            at = span(i, ROW_BLOCK)
            grad, normed = dz(at), refs.n2[at]
            back = norm_block_back(grad, normed, refs.inv2[at], refs.bias[7:8])
            refs.work[at] = back
            refs.dr2_low[at] = back.astype(jnp.bfloat16)
            return sums[0] + folded(back), sums[1] + folded(grad), sums[2] + folded(grad * normed)

        sums = lax.fori_loop(0, rows // ROW_BLOCK, act, (zero,) * 3)
        row(4, sums[0]), row(5, sums[1]), row(7, sums[2])
        refs.save("dr2_low")
        refs.ready("slope")
        waits[0]()

    def down(first, count):
        def act(i):
            at = span(first + i, WIDE_FF)
            du = product_nt(refs.dr2_low[...], w_down[at]) * refs.slope[:, at].astype(jnp.float32)
            refs.du_low[:, at] = du.astype(jnp.bfloat16)
            refs.hidden_totals[0:1, at] = jnp.sum(du, axis=0, keepdims=True)

        over(count, act)

    def up():
        refs.save("du_low")
        waits[1]()

        def act(i):
            at = span(i, WIDE_D)
            refs.work[:, at] = refs.work[:, at] + product_nt(refs.du_low[...], w_up[at])

        over(D // WIDE_D, act)

    def norm_one():
        refs.ready("n1", "inv1")

        def act(i, sums):
            at = span(i, ROW_BLOCK)
            grad, normed = refs.work[at], refs.n1[at]
            back = norm_block_back(grad, normed, refs.inv1[at], refs.bias[6:7])
            refs.dr1[at] = back
            refs.dr1_low[at] = back.astype(jnp.bfloat16)
            return sums[0] + folded(back), sums[1] + folded(grad), sums[2] + folded(grad * normed)

        sums = lax.fori_loop(0, rows // ROW_BLOCK, act, (zero,) * 3)
        row(2, sums[0]), row(3, sums[1]), row(6, sums[2])
        refs.save("dr1", "dr1_low")

    def out():
        waits[2]()

        def act(i):
            at = span(i, WIDE_D)
            refs.cot[:, at] = product_nt(refs.dr1_low[...], w_out[at]).astype(jnp.bfloat16)

        over(D // WIDE_D, act)
        refs.save("cot")

    half = hidden // WIDE_FF // 2
    return [norm_two, partial(down, 0, half), partial(down, half, half), up, norm_one, out]


def back_outs(rows, hidden):
    f32, low = jnp.float32, jnp.bfloat16
    return dict(
        dr2_low=((rows, D), low, SAVE), du_low=((rows, hidden), low, SAVE), dr1=((rows, D), f32, SAVE),
        dr1_low=((rows, D), low, SAVE), cot=((rows, D), low, SAVE), totals=((8, D), f32, IN_VMEM),
        hidden_totals=((1, hidden), f32, IN_VMEM), part_cot=((SHARE, D), low, ANYWHERE),
    )


def turn(mixed, part, resid, vectors, shifts, weights, d_out, depth, cid):
    rows, hidden = resid.shape[0], shifts.shape[1]

    def body(refs):
        refs.ready("generic")
        refs.mixed[...] = refs.generic[...]
        refs.bias = refs.vectors.at[1]
        greet((), depth, spread=True, collect=True)
        to_first(refs.own_part, refs.mixed, refs.t_send, refs.t_recv)()
        for step in tail_steps(refs, WIDE_D, WIDE_FF):
            step()
        refs.totals[...] = jnp.zeros_like(refs.totals)
        for step in back_steps(refs, lambda at: refs.d_out[at].astype(jnp.float32), refs.w_down, refs.w_up, refs.w_out):
            step()
        to_helpers(refs.cot, refs.part_cot, refs.give, refs.take)()

    kept, norms = tail_results(rows, hidden)
    return call(
        body, "turn", cid,
        {**tail_ins(mixed, part, resid, vectors, shifts, weights), **dict(d_out=(d_out, LOAD))},
        {**saved(kept), **back_outs(rows, hidden)},
        {
            **tail_scratch(rows), **{k: pltpu.VMEM(*v) for k, v in norms.items()},
            **dict(work=pltpu.VMEM((rows, D), jnp.float32), give=dma(HELPERS), take=dma()),
        },
    )


def chunked(shape):
    rows, columns = shape
    width = columns
    while rows * width > 24 * 1024 and width % 256 == 0:
        width //= 2
    if rows * width > 24 * 1024 and width % 384 == 0:
        width //= 3
    return width, columns // width


def total_of(own, kids, window):
    total = own[window].astype(jnp.float32)
    for ref, cond in kids:
        if cond is None:
            total = total + ref[window].astype(jnp.float32)
        else:
            total = total + lax.cond(
                cond,
                lambda ref=ref: ref[window].astype(jnp.float32),
                lambda total=total: jnp.zeros_like(total),
            )
    return total


def over_chunks(shape, act):
    if len(shape) == 3:
        size = shape[1] // 2

        def part(i, carry):
            act((i // 2, span(i % 2, size)))
            return carry

        lax.fori_loop(0, 2 * shape[0], part, 0)
        return
    width, count = chunked(shape)

    def step(i, carry):
        act((slice(None), pl.ds(pl.multiple_of(i * width, width), width)))
        return carry

    lax.fori_loop(0, count, step, 0)


def add_up(own, kids, into):
    def act(window):
        into[window] = total_of(own, kids, window).astype(into.dtype)

    over_chunks(into.shape, act)


def write_total(target):
    def finish(own, kids):
        def act(window):
            target[window] = total_of(own, kids, window).astype(target.dtype)

        over_chunks(target.shape, act)

    return finish


def weight_grad(left, right, into, first=0):
    share = into.shape[1]
    width = WIDE_FF if into.shape[2] % WIDE_FF == 0 else WIDE_D
    count = 384 // share

    def act(i):
        across = into.shape[2] // width
        rows, at = i // across, span(i % across, width)
        acc = product_tn(left[:, span(rows, 384)], right[:, pl.ds(pl.multiple_of(first + i % across * width, WIDE), width)])
        for k in range(count):
            into[rows * count + k, :, at] = acc[k * share : (k + 1) * share].astype(into.dtype)

    over(left.shape[1] // 384 * (into.shape[2] // width), act)


class Sums:
    def __init__(self, tag, pieces, depth):
        self.tag, self.pieces, self.depth = tag, pieces, depth

    def name(self, what, k):
        return "%s_%s%d" % (self.tag, what, k)

    def scratch(self):
        made = {}
        for k, (_, _, shape, _, order, dtype) in enumerate(self.pieces):
            edges = Reduce.slots(order, self.depth)[1]
            made[self.name("box", k)] = pltpu.VMEM((edges,) + shape, dtype)
            made[self.name("send", k)] = dma(2 * len(offsets(order, self.depth)))
            made[self.name("recv", k)] = dma(edges)
        return made

    def prepare(self, refs):
        self.jobs = []
        for k, (source, far, _, target, order, _) in enumerate(self.pieces):
            box, send, recv = (getattr(refs, self.name(what, k)) for what in ("box", "send", "recv"))
            job = Reduce(partial(source, refs), partial(far, refs), box, order, self.depth, send, recv)
            self.jobs.append((job, target(refs)))

    def start(self, k):
        job, _ = self.jobs[k]
        for t in job.marks:
            job.start(t)

    def timed(self, places):
        timed = []
        for k, ((job, finish), at) in enumerate(zip(self.jobs, places, strict=True)):
            timed.append((at[0], partial(self.start, k)))
            acts = [partial(job.handle, t, add_up, finish) for t in job.marks]
            timed += zip(at[1:], acts, strict=True)
        return timed

    def end(self):
        for job, _ in self.jobs:
            job.drain()


def weight_sums(windows, depth, n_dev, dtypes):
    number = number_in(depth)

    def piece(which, row, rows, column, columns_, order):
        window = (pl.ds(row, rows), pl.ds(column, columns_))

        def source(refs, p):
            return getattr(refs, "grad%d" % which).at[(number(p),) + window]

        return (
            source,
            source,
            (rows, columns_),
            lambda refs: write_total(getattr(refs, "owned%d" % which).at[window]),
            order,
            dtypes[which],
        )

    return Sums("w", [piece(*w) for w in windows], depth)


def sum_rows(dk, dv, dq, part_dq, held, grads, seq_count, depth, cid):
    rows, hidden, n_dev = dq.shape[0], grads.du_low.shape[1], seq_count * depth
    low, f32 = dk.dtype, jnp.float32
    share, count = D // n_dev, PAIRS // 2

    def piece(i):
        window = pl.ds(i % 2 * count, count)

        def target(refs):
            def finish(own, kids):
                def act(at):
                    lanes = pl.ds(pl.multiple_of((PAIRS + i * count + at[0]) * WIDE, WIDE), WIDE)
                    refs.proj[at[1], lanes] = total_of(own, kids, at).astype(low)

                over_chunks((count, rows, WIDE), act)

            return finish

        return (
            lambda refs, p: (refs.dk, refs.dv)[i // 2].at[number_in_sequence(p), window],
            lambda refs, p: (refs.far_dk, refs.far_dv)[i // 2].at[number_in_sequence(p), window],
            (count, rows, WIDE),
            target,
            (X_Y, Y_X)[i % 2],
            low,
        )

    by_rows = Sums("r", [piece(i) for i in range(4)], depth)
    windows = [(1, 0, share, 0, D, X_Y_Z), (2, 0, share, 0, hidden // 2, Y_X_Z)]
    by_weights = weight_sums(windows, depth, n_dev, {1: low, 2: low})

    def body(refs):
        refs.ready("dq")
        refs.proj[:, 0:D] = refs.dq[...]
        greet(("y", "x", "z"), depth, collect=True)
        by_rows.prepare(refs)
        by_weights.prepare(refs)
        ends = [to_first(refs.part, refs.proj.at[:, pl.ds(0, D)], refs.t_send, refs.t_recv)]
        at = ROWS_PLACES

        def grad(left, right, into):
            refs.ready(left, right)
            weight_grad(getattr(refs, left), getattr(refs, right), into)

        first_block = min(place for places in at.rows for place in places[1:])
        run_in_order(
            by_rows.timed(at.rows) + by_weights.timed(at.weights)
            + [
                (at.grads[0], partial(grad, "mixed", "dr1_low", refs.grad1)),
                (at.grads[1], partial(grad, "y_low", "du_low", refs.grad2)),
                (first_block - 0.5, partial(refs.ready, "dk", "dv")),
                (at.collect, ends[0]),
            ]
        )
        by_rows.end()
        by_weights.end()

        def act(i, sums):
            at = span(i, ROW_BLOCK)
            return tuple(
                total + folded(refs.proj[at, pl.ds(first, D)].astype(f32)) for total, first in zip(sums, (0, 2 * D))
            )

        zero = jnp.zeros((8, D), f32)
        sums = lax.fori_loop(0, rows // ROW_BLOCK, act, (zero, zero))
        refs.totals[...] = jnp.zeros_like(refs.totals)
        for k in range(2):
            refs.totals[k : k + 1] = jnp.sum(sums[k], axis=0, keepdims=True)

    return call(
        body, "sum_rows", cid,
        dict(
            dq=(dq, LOAD), part=(part_dq, ANYWHERE), mixed=(held.mixed, LOAD), dr1_low=(grads.dr1_low, LOAD),
            dk=(dk, LOAD), dv=(dv, LOAD), y_low=(held.y_low, LOAD), du_low=(grads.du_low, LOAD),
        ),
        dict(
            proj=((rows, 3 * D), low, IN_VMEM), totals=((8, D), f32, IN_VMEM), owned1=((share, D), f32, IN_VMEM),
            owned2=((share, hidden // 2), f32, IN_VMEM),
        ),
        {
            **dict(
                grad1=pltpu.VMEM((n_dev, share, D), low), grad2=pltpu.VMEM((n_dev, share, hidden // 2), low),
                t_send=dma(), t_recv=dma(HELPERS),
            ),
            **by_rows.scratch(), **by_weights.scratch(),
        },
    )


def sum_weights(held, low_in, proj, vectors, w_qkv, small, below, n_dev, depth, cid):
    rows, hidden = proj.shape[0], held.du_low.shape[1]
    low, f32 = jnp.bfloat16, jnp.float32
    share, tall = D // n_dev, hidden // n_dev
    shapes = {0: (share, 3 * D), 2: (share, hidden // 2), 3: (tall, D)}
    cut = tall * 2 // 3
    windows = [
        (3, 0, cut, 0, D, Z_X_Y),
        (3, cut, tall - cut, 0, D, Z_Y_X),
        (2, 0, share, 0, hidden // 2, Y_X_Z),
        (0, 0, share, 0, 3 * D, Z_Y_X),
    ]
    ins = dict(low_in=(low_in, LOAD), proj=(proj, LOAD))
    ins.update({"up_" + k: (getattr(held, k), LOAD) for k in ("y_low", "du_low", "a_low", "dr2_low")})
    ins.update(up_dr1=(held.dr1, LOAD), w_qkv=(w_qkv, ANYWHERE))
    outs = {"owned%d" % i: (s, f32, IN_VMEM) for i, s in shapes.items()}
    scratch = {"grad%d" % i: pltpu.VMEM((n_dev,) + s, low) for i, s in shapes.items()}
    if small is not None:
        windows.append((4, 0, small.shape[1], 0, small.shape[2], Z_Y_X))
        ins.update(grad4=(small, IN_VMEM))
        outs.update(owned4=(small.shape[1:], f32, IN_VMEM))
    by_weights = weight_sums(windows, depth, n_dev, {0: low, 2: low, 3: low, 4: f32})
    scratch.update(by_weights.scratch())
    scratch.update(load=dma(4), wide=pltpu.VMEM((D, hidden), low))
    if below is not None:
        below_weights, below_held = below
        ins.update({k: (getattr(below_held, k), LOAD) for k in ("n2", "inv2", "slope", "n1", "inv1")})
        ins.update(
            vectors=(vectors, IN_VMEM), w_out=(below_weights[1], ANYWHERE), w_up=(below_weights[2], ANYWHERE),
            w_down=(below_weights[3], ANYWHERE),
        )
        outs.update(back_outs(rows, hidden))
        scratch.update(
            tall=pltpu.VMEM((hidden, D), low), work=pltpu.VMEM((rows, D), f32), give=dma(HELPERS), take=dma()
        )
    if below is None:
        outs.update(dx=((rows, D), f32, SAVE))
    else:
        scratch.update(dx=pltpu.VMEM((rows, D), f32))

    def body(refs):
        v_qkv = refs.wide.at[:, pl.ds(0, 3 * D)]
        load_qkv = pltpu.make_async_copy(refs.w_qkv, v_qkv, refs.load.at[0])
        load_qkv.start()
        if below is not None:
            refs.bias = refs.vectors.at[0]
            refs.totals[...] = jnp.zeros_like(refs.totals)
            load_down = pltpu.make_async_copy(refs.w_down, refs.tall, refs.load.at[1])
            load_down.start()
            load_up = pltpu.make_async_copy(refs.w_up, refs.wide, refs.load.at[2])
            load_out = pltpu.make_async_copy(refs.w_out, refs.tall.at[pl.ds(0, D)], refs.load.at[3])
        greet(("y", "x", "z"), depth, spread=below is not None)
        by_weights.prepare(refs)
        def dx():
            load_qkv.wait()
            refs.ready("proj", "up_dr1")

            def act(i):
                at = span(i, WIDE_D)
                refs.dx[:, at] = refs.up_dr1[:, at] + product_nt(refs.proj[...], v_qkv[at])

            over(D // WIDE_D, act)
            refs.save("dx")
            if below is not None:
                load_up.start()

        steps = [dx]
        if below is not None:

            def up_ready():
                load_out.start()
                load_up.wait()

            steps += back_steps(
                refs, lambda at: refs.dx[at], refs.tall, refs.wide, refs.tall, [load_down.wait, up_ready, load_out.wait]
            )
            ends = []
            steps.append(lambda: ends.append(to_helpers(refs.cot, refs.part_cot, refs.give, refs.take)))
        at = LAST_PLACES if below is None else BELOW_PLACES

        def grad(left, right, into, column=0):
            refs.ready(left, right)
            weight_grad(getattr(refs, left), getattr(refs, right), into, column)

        run_in_order(
            by_weights.timed(at.weights)
            + [
                (at.grads[0], partial(grad, "up_a_low", "up_dr2_low", refs.grad3)),
                (at.grads[1], partial(grad, "up_y_low", "up_du_low", refs.grad2, hidden // 2)),
                (at.grads[2], partial(grad, "low_in", "proj", refs.grad0)),
            ]
            + list(zip(at.steps, steps, strict=True))
        )
        by_weights.end()
        if below is not None:
            ends[0]()

    return call(body, "sum_weights", cid, ins, outs, scratch)


def norm_rows(resid, gain, shift):
    center = resid - jnp.mean(resid, axis=-1, keepdims=True)
    inv_std = lax.rsqrt(jnp.mean(center * center, axis=-1, keepdims=True) + layer_eps)
    normed = center * inv_std
    return (normed * gain + shift, normed, inv_std)


def norm_back(grad_rows, normed, inv_std, gain):
    scaled = grad_rows * gain
    return (
        scaled
        - jnp.mean(scaled, axis=-1, keepdims=True)
        - normed * jnp.mean(scaled * normed, axis=-1, keepdims=True)
    ) * inv_std


def dot32(a, b):
    return jnp.dot(a, b, preferred_element_type=jnp.float32)


def small_vectors(small, n_dev):
    small = small.astype(jnp.float32).T
    vectors = jnp.concatenate(
        [small[: 6 * L].reshape(L, 6, D), small[6 * L : 8 * L].reshape(L, 2, D)], axis=1
    )
    hidden_shifts = small[8 * L : 12 * L].reshape(L, 4, n_dev, D // n_dev)
    return vectors, jnp.swapaxes(hidden_shifts, 1, 2).reshape(L, -1)


def shut_keys(segs_all, segments, first, blocks_here):
    length = segs_all.shape[0]
    padding = jnp.full((BLK,), -1, jnp.int32)
    segs_all = jnp.concatenate([padding, segs_all, padding]).reshape(-1, BLK)
    segs_near = lax.dynamic_slice_in_dim(segs_all, first, blocks_here + 2, axis=0)
    seg_window = jnp.concatenate([segs_near[j : j + blocks_here] for j in range(3)], axis=1)
    spot = (first - 1 + jnp.arange(blocks_here)[:, None]) * BLK + jnp.arange(3 * BLK)[None, :]
    inside = (spot >= SHARED) & (spot < length)
    own = segments.reshape(blocks_here, 1, BLK)
    allowed = inside[:, :, None] & (seg_window[:, :, None] == jnp.concatenate([own, own], axis=2))
    return jnp.where(allowed, 0.0, masked_score)


def small_by_owner(vectors, hidden, n_dev):
    rows = jnp.moveaxis(vectors.reshape(8, n_dev, -1), 1, 0)
    rows = jnp.concatenate([rows, hidden.reshape(n_dev, 8, -1)], axis=2)
    return jnp.pad(rows, ((0, 0), (0, 0), (0, 128 - rows.shape[2])))


def small_outputs(narrow, piece, hidden):
    return (
        narrow[:, 6:8, :piece],
        narrow[:, 0:6, :piece],
        narrow[:, :, piece : piece + hidden // 8].reshape(L, -1),
    )


def share_of(rows):
    first = lax.all_gather(rows[:SHARED], SEQ, axis=0)[0]
    own = jnp.minimum(lax.axis_index(SEQ), HELPERS - 1) * SHARE
    return lax.dynamic_slice_in_dim(first, own, SHARE, axis=0)


def rows_of_all(kv, queries):
    kv = jnp.moveaxis(kv.reshape(-1, 2 * PAIRS, WIDE), 1, 0)
    return lax.all_gather(kv, SEQ, axis=0), share_of(queries)


def with_shared_rows(part, rows):
    first = lax.all_gather(part, SEQ, axis=0)[:HELPERS].reshape(SHARED, D)
    head_rows = jnp.where(lax.axis_index(SEQ) == 0, first.astype(rows.dtype), rows[:SHARED])
    return jnp.concatenate([head_rows, rows[SHARED:]], axis=0)


def on_any_slice(
    layer_input, segments, rand_blocks, w_qkv, w_out, w_up, w_down, gains, biases, up_bias, d_out
):
    seq_count, depth = lax.axis_size(SEQ), lax.axis_size(BATCH)
    n_dev = seq_count * depth
    own_index = lax.axis_index(SEQ)
    rows = layer_input.shape[1]
    blocks_here, length = rows // BLK, rows * seq_count
    picks = rand_blocks.reshape(-1)
    first = (own_index * blocks_here).reshape(1)

    piece = D // n_dev
    small = jnp.concatenate(
        [biases.reshape(-1, piece), gains.reshape(-1, piece), up_bias.reshape(-1, piece)], axis=0
    ).T
    small = lax.all_gather(small, (SEQ, BATCH), axis=0, tiled=True)
    segs_all = lax.all_gather(segments[0], SEQ, axis=0, tiled=True)
    weights = [
        [lax.all_gather(w[layer], (SEQ, BATCH), axis=0, tiled=True) for w in (w_qkv, w_out, w_up, w_down)]
        for layer in range(L)
    ]
    vectors, hidden_shifts = small_vectors(small, n_dev)
    shut = shut_keys(segs_all, segments, first[0], blocks_here)

    resid = layer_input[0].astype(jnp.float32)
    low = layer_input[0]
    saved = []
    for layer in range(L):
        mat_qkv, mat_out, mat_up, mat_down = weights[layer]
        bias = vectors[layer]
        proj = dot32(low, mat_qkv)
        queries = (proj[:, :D] + bias[0]).astype(jnp.bfloat16)
        kv = jnp.concatenate([proj[:, D : 2 * D], proj[:, 2 * D :] + bias[1]], axis=1).astype(jnp.bfloat16)
        kv_all, part = rows_of_all(kv, queries)
        mixed, part_mixed, *logs = attend(picks, first, queries, kv_all, shut, part)
        mixed = with_shared_rows(part_mixed, mixed)
        resid_one = resid + dot32(mixed, mat_out) + bias[2]
        middle, normed_one, inv_one = norm_rows(resid_one, bias[6], bias[3])
        middle_low = middle.astype(jnp.bfloat16)
        hidden = dot32(middle_low, mat_up) + hidden_shifts[layer]
        active = jax.nn.gelu(hidden, approximate=False).astype(jnp.bfloat16)
        resid_two = middle + dot32(active, mat_down) + bias[4]
        result, normed_two, inv_two = norm_rows(resid_two, bias[7], bias[5])
        saved.append(
            (low, queries, kv_all, part, logs, mixed, normed_one, inv_one, middle_low, hidden, active, normed_two, inv_two)
        )
        resid = result
        low = resid.astype(jnp.bfloat16)

    grad = d_out[0].astype(jnp.float32)
    owned = [None] * L
    for layer in reversed(range(L)):
        (low_in, queries, kv_all, part, logs, mixed, normed_one, inv_one, middle_low, hidden, active, normed_two, inv_two) = saved[layer]
        mat_qkv, mat_out, mat_up, mat_down = weights[layer]
        bias = vectors[layer]
        gain_two_grad = jnp.sum(grad * normed_two, axis=0)
        shift_two_grad = jnp.sum(grad, axis=0)
        grad_two = norm_back(grad, normed_two, inv_two, bias[7])
        grad_two_low = grad_two.astype(jnp.bfloat16)
        down_grad = product_tn(active, grad_two_low)
        active_grad = product_nt(grad_two_low, mat_down)
        hidden_grad = jax.vjp(partial(jax.nn.gelu, approximate=False), hidden)[1](active_grad)[0]
        hidden_grad_low = hidden_grad.astype(jnp.bfloat16)
        up_grad = product_tn(middle_low, hidden_grad_low)
        middle_grad = grad_two + product_nt(hidden_grad_low, mat_up)
        gain_one_grad = jnp.sum(middle_grad * normed_one, axis=0)
        shift_one_grad = jnp.sum(middle_grad, axis=0)
        grad_one = norm_back(middle_grad, normed_one, inv_one, bias[6])
        grad_one_low = grad_one.astype(jnp.bfloat16)
        out_grad = product_tn(mixed, grad_one_low)
        cot = product_nt(grad_one_low, mat_out).astype(jnp.bfloat16)
        part_cot = share_of(cot)
        part_cot = jnp.where(own_index < HELPERS, part_cot, 0)
        dq, dk, dv, part_dq = attend_back(picks, first, queries, kv_all, shut, cot, part, part_cot, *logs)
        dq = with_shared_rows(part_dq, dq)
        dkv = jnp.concatenate([dk, dv], axis=1).astype(jnp.float32)
        dkv = lax.psum_scatter(dkv, SEQ, scatter_dimension=0)
        dkv = jnp.moveaxis(dkv, 0, 1).reshape(rows, 2 * D)
        proj_grad = jnp.concatenate([dq, dkv.astype(jnp.bfloat16)], axis=1)
        qkv_grad = product_tn(low_in, proj_grad)
        small_rows = jnp.stack(
            [
                jnp.sum(dq.astype(jnp.float32), axis=0),
                jnp.sum(dkv[:, D:], axis=0),
                jnp.sum(grad_one, axis=0),
                shift_one_grad,
                jnp.sum(grad_two, axis=0),
                shift_two_grad,
                gain_one_grad,
                gain_two_grad,
            ]
        )
        small_rows = small_by_owner(small_rows, jnp.sum(hidden_grad, axis=0), n_dev)
        owned[layer] = [
            lax.psum_scatter(a, (SEQ, BATCH), scatter_dimension=0, tiled=True)
            for a in (qkv_grad, out_grad, up_grad, down_grad, small_rows)
        ]
        owned[layer][4] = owned[layer][4][0]
        grad = grad_one + product_nt(proj_grad, mat_qkv)
    stacked = [jnp.stack([owned[layer][i] for layer in range(L)]) for i in range(5)]
    return (low[None], grad[None], *stacked[:4], *small_outputs(stacked[4], piece, up_bias.shape[1]))


def assemble(wanted):
    parts = [part for _, parts in wanted for part in parts]

    def body(*refs):
        sources, targets = list(refs[: len(parts)]), refs[len(parts) :]
        for target, (_, held) in zip(targets, wanted):
            for array, layer, column in held:
                target[layer, :, column : column + array.shape[1]] = sources.pop(0)[...]

    return pl.pallas_call(
        body,
        out_shape=[jax.ShapeDtypeStruct(shape, jnp.float32) for shape, _ in wanted],
        in_specs=[IN_VMEM] * len(parts),
        out_specs=[IN_VMEM] * len(wanted),
        compiler_params=pltpu.CompilerParams(vmem_limit_bytes=VMEM_LIMIT),
        name="assemble",
    )(*[array for array, _, _ in parts])


def on_pairs(
    layer_input, segments, rand_blocks, w_qkv, w_out, w_up, w_down, gains, biases, up_bias, d_out
):
    seq_count, depth = lax.axis_size(SEQ), lax.axis_size(BATCH)
    n_dev = seq_count * depth
    rows, hidden = layer_input.shape[1], up_bias.shape[1] * n_dev
    blocks_here = rows // BLK
    picks = rand_blocks.reshape(-1)
    first = (lax.axis_index(SEQ) * blocks_here).reshape(1)
    piece = D // n_dev

    small = jnp.concatenate(
        [biases.reshape(-1, piece), gains.reshape(-1, piece), up_bias.reshape(-1, piece)], axis=0
    ).T
    small = jnp.pad(small, ((0, 0), (0, 128 - small.shape[1])))
    segs = jnp.pad(segments.reshape(-1, 128), ((0, 8 - rows // 128), (0, 0)))

    def flat(slabs):
        return [w.reshape(-1, w.shape[2]) for w in slabs]

    places = jnp.stack([picks // blocks_here, picks % blocks_here])

    def attention_back(got, back):
        return attend_back(
            picks, first, got.q, got.every.reshape(seq_count, 2 * PAIRS, rows, WIDE), shut, back.cot, got.part, back.part_cot, got.log, got.plog
        )

    x = layer_input[0]
    layers = [[(w, layer) for w in (w_qkv, w_out, w_up, w_down)] for layer in range(L)]
    own_segs = segments.reshape(blocks_here, BLK).astype(jnp.float32)
    own_segs = jnp.concatenate([own_segs, own_segs], axis=1)
    head_one, weights_one = first_head(x, small, segs, own_segs, places, layers[0], seq_count, depth, 0)
    weights_one = flat(weights_one)
    vectors = head_one.vectors
    shifts = head_one.table.reshape(L, 4, n_dev, piece)
    shifts = jnp.swapaxes(shifts, 1, 2).reshape(L, 1, hidden)
    shut = head_one.shut
    rows_one, weights_two = tail(
        head_one.o, head_one.po, x, vectors, shifts[0], weights_one, layers[1], shut, places, seq_count, depth, 1
    )
    weights_two = flat(weights_two)
    middle = rows_one.z_low
    rows_two = turn(rows_one.o, rows_one.po, rows_one.z, vectors, shifts[1], weights_two, d_out[0], depth, 2)
    dq, dk, dv, part = attention_back(rows_one, rows_two)
    sums_two = sum_rows(dk, dv, dq, part, rows_two, rows_two, seq_count, depth, 3)
    back_one = sum_weights(
        rows_two, middle, sums_two.proj, vectors, weights_two[0], None, (weights_one, rows_one), n_dev, depth, 4
    )
    dq, dk, dv, part = attention_back(head_one, back_one)
    sums_one = sum_rows(dk, dv, dq, part, rows_one, back_one, seq_count, depth, 5)
    small = jnp.concatenate(
        [
            small_by_owner(back.totals + sums.totals, back.hidden_totals[0], n_dev)
            for back, sums in ((back_one, sums_one), (rows_two, sums_two))
        ],
        axis=1,
    )
    last = sum_weights(
        SimpleNamespace(**{**vars(rows_one), **vars(back_one)}),
        x, sums_one.proj, None, weights_one[0], small, None, n_dev, depth, 6,
    )
    whole_outputs = assemble(
        [
            ((L, piece, 3 * D), [(last.owned0, 0, 0), (back_one.owned0, 1, 0)]),
            ((L, piece, D), [(sums_one.owned1, 0, 0), (sums_two.owned1, 1, 0)]),
            (
                (L, piece, hidden),
                [
                    (sums_one.owned2, 0, 0), (last.owned2, 0, hidden // 2),
                    (sums_two.owned2, 1, 0), (back_one.owned2, 1, hidden // 2),
                ],
            ),
            ((L, hidden // n_dev, D), [(last.owned3, 0, 0), (back_one.owned3, 1, 0)]),
            ((1, rows, D), [(last.dx, 0, 0)]),
        ]
    )
    return (
        rows_two.z_low[None],
        whole_outputs[4],
        *whole_outputs[:4],
        *small_outputs(last.owned4.reshape(L, 8, 128), piece, up_bias.shape[1]),
    )


def solution(mesh):
    placed = (
        P(BATCH, SEQ, None),
        P(BATCH, SEQ),
        P(BATCH, SEQ, None, None),
        P(None, (SEQ, BATCH), None),
        P(None, (SEQ, BATCH), None),
        P(None, (SEQ, BATCH), None),
        P(None, (SEQ, BATCH), None),
        P(None, None, (SEQ, BATCH)),
        P(None, None, (SEQ, BATCH)),
        P(None, (SEQ, BATCH)),
        P(BATCH, SEQ, None),
    )
    return jax.shard_map(
        on_pairs if mesh.shape[SEQ] == 8 and mesh.shape[BATCH] == 4 else on_any_slice,
        mesh=mesh,
        in_specs=placed,
        out_specs=(
            P(BATCH, SEQ, None),
            P(BATCH, SEQ, None),
            P(None, (SEQ, BATCH), None),
            P(None, (SEQ, BATCH), None),
            P(None, (SEQ, BATCH), None),
            P(None, (SEQ, BATCH), None),
            P(None, None, (SEQ, BATCH)),
            P(None, None, (SEQ, BATCH)),
            P(None, (SEQ, BATCH)),
        ),
        check_vma=False,
    )
```
